32 devices in a mesh: gx: 8 (over z, core), gy: 4 (over y, x).
Axes of the slice: x: 2, y: 2, z: 4, core: 2. Of those that a mesh axis runs over, the one named last changes fastest.
Arguments:
- right_side: float32 [2, 2, 128, 64, 128], P(None, None, 'gx', 'gy'), may hold values from -7 to 7
- slowness: float32 [128, 64, 128], P('gx', 'gy'), may hold values from 0.7 to 1.4
- source_cells: int32 [2, 16], replicated, may hold values from 0 to 1048575
- source_amplitudes: float32 [2, 16, 2], replicated, may hold values from -24 to 24
Outputs:
- wavefield: float32 [2, 2, 128, 64, 128], P(None, None, 'gx', 'gy')
- residual: float32 [2, 2, 128, 64, 128], P(None, None, 'gx', 'gy')
The draws below stay inside these ranges and needn't reach their ends.
Inputs may be any that keep to these rules, and one draw needn't show every extreme that they name: `source_cells`: flat indices (x * 64 + y) * 128 + z of cells; points may coincide.
All inputs are finite; a program needn't handle non-finite values.
Results may differ from the reference program's by a relative error of at most 0.0003.
Values sent between devices are 32-bit elements; how exact they have to be, the bound alone decides.
No kernel may reach another device: no remote copies, remote signals or barrier semaphores. Data moves between devices by JAX's collectives and lax.ppermute only.
A program may use at most 64 MiB of HBM per device.

```python
import math
import jax
import jax.numpy as jnp
from jax import lax

CX = 16
CY = 16
NZ = 128
NRHS = 2
NPT = 16
NX = 128
NY = 64
N_GX = 8
N_GY = 4


def draw_right_side(key, part):
    random_part = jnp.clip(jax.random.normal(key, (NRHS, 2, NX, NY, NZ), jnp.float32), -6.0, 6.0)
    return random_part


def plant(drawn, stream_key, smallest, largest):
    spot = [jax.random.randint(jax.random.fold_in(stream_key, axis), (), 0, length) for axis, length in enumerate(drawn.shape)]
    widest = drawn.shape.index(max(drawn.shape))
    neighbour = spot[:widest] + [(spot[widest] + 1) % drawn.shape[widest]] + spot[widest + 1:]
    return drawn.at[tuple(spot)].set(smallest).at[tuple(neighbour)].set(largest)


def levels(own_key, extent, pieces, least, largest):
    def one(dim, parts):
        draws = jax.random.uniform(jax.random.fold_in(jax.random.fold_in(own_key, 6), dim), (parts,), jnp.float32, least / len(pieces), largest / len(pieces))
        return jnp.repeat(jnp.exp(draws), extent[dim] // parts).reshape((-1,) + (1,) * (len(extent) - dim - 1))

    level = one(*pieces[0])
    for cut in pieces[1:]:
        level = level * one(*cut)
    return level


def centred(rng, shape, deviation, limit, kind=jnp.bfloat16):
    values = jax.random.normal(rng, shape, jnp.float32) * deviation
    return jnp.minimum(jnp.maximum(values, -limit), limit).astype(kind)


def setup_inputs(seed: int = 0) -> dict:
    splits = jax.random.split(jax.random.key(seed), 5)
    right_side = draw_right_side(jax.random.fold_in(splits[4], 71), 0)
    slowness = jnp.clip(jnp.exp(math.log(1.4) - 0.6931472 * jax.random.uniform(splits[1], (NX, NY, NZ), jnp.float32) ** levels(splits[1], (NX, NY, NZ), ((0, 8), (1, 4)), -0.2, 0.2)), 0.7, 1.4)
    source_cells = plant(jax.random.randint(splits[2], (NRHS, NPT), 0, NX * NY * NZ), jax.random.fold_in(splits[2], 1), 0, (NX * NY * NZ) - 1).astype(jnp.int32)
    source_amplitudes = centred(splits[3], (NRHS, NPT, 2), 4.0, 24.0, jnp.float32)
    return {"right_side": right_side, "slowness": slowness, "source_cells": source_cells, "source_amplitudes": source_amplitudes}


KAPPA = 0.12
DAMPING = 0.3
HIGHEST = lax.Precision.HIGHEST

def sine_basis(length):
    positions = jnp.arange(1, length + 1).astype(jnp.float32)
    angles = positions * (math.pi / (length + 1))
    sine_rows = math.sqrt(2.0 / (length + 1)) * jnp.sin(angles[:, None] * positions[None, :])
    return (sine_rows, angles)

def build_tables(size_x, size_y, cells_z):
    sine_x, angle_x = sine_basis(size_x)
    sine_y, angle_y = sine_basis(size_y)
    sine_z, angle_z = sine_basis(cells_z)
    symbol_x = 2.5 - 8.0 / 3.0 * jnp.cos(angle_x) + 1.0 / 6.0 * jnp.cos(2.0 * angle_x)
    symbol_y = 2.5 - 8.0 / 3.0 * jnp.cos(angle_y) + 1.0 / 6.0 * jnp.cos(2.0 * angle_y)
    symbol_z = 2.0 - 2.0 * jnp.cos(angle_z)
    real_part = symbol_x[:, None, None] + symbol_y[None, :, None] + symbol_z[None, None, :] - KAPPA
    denominator = real_part * real_part + (KAPPA * DAMPING) ** 2
    return (sine_x, sine_y, sine_z, real_part / denominator, KAPPA * DAMPING / denominator)

def transform(wavefield, sine_x, sine_y, sine_z):
    result = jnp.einsum('scxyz,zw->scxyw', wavefield, sine_z, precision=HIGHEST)
    result = jnp.einsum('scxyz,xa->scayz', result, sine_x, precision=HIGHEST)
    return jnp.einsum('scxyz,yb->scxbz', result, sine_y, precision=HIGHEST)

def fast_solve(wavefield, tables):
    sine_x, sine_y, sine_z, inverse_real, inverse_imag = tables
    spectrum = transform(wavefield, sine_x, sine_y, sine_z)
    real_part = inverse_real * spectrum[:, 0] - inverse_imag * spectrum[:, 1]
    imag_part = inverse_real * spectrum[:, 1] + inverse_imag * spectrum[:, 0]
    return transform(jnp.stack([real_part, imag_part], axis=1), sine_x, sine_y, sine_z)

def apply_operator(padded, slowness):
    size_x = padded.shape[2] - 4
    size_y = padded.shape[3] - 4
    center = padded[:, :, 2:2 + size_x, 2:2 + size_y]
    weights = (1.0, -16.0, 30.0, -16.0, 1.0)
    lateral = jnp.zeros_like(center)
    for offset in range(5):
        lateral = lateral + weights[offset] / 12.0 * (padded[:, :, offset:offset + size_x, 2:2 + size_y] + padded[:, :, 2:2 + size_x, offset:offset + size_y])
    vertical = jnp.pad(center, ((0, 0), (0, 0), (0, 0), (0, 0), (1, 1)))
    lateral = lateral + 2.0 * center - vertical[..., :-2] - vertical[..., 2:]
    scaled = KAPPA * slowness
    real_part = lateral[:, 0] - scaled * (center[:, 0] - DAMPING * center[:, 1])
    imag_part = lateral[:, 1] - scaled * (center[:, 1] + DAMPING * center[:, 0])
    return jnp.stack([real_part, imag_part], axis=1)

def tile_solve(source_term, trace_x, trace_y, slowness, tables):
    source_term = source_term.at[:, :, 0].add((16.0 * trace_x[:, :, 1] - trace_x[:, :, 0]) / 12.0)
    source_term = source_term.at[:, :, 1].add(-trace_x[:, :, 1] / 12.0)
    source_term = source_term.at[:, :, :, 0].add((16.0 * trace_y[:, :, :, 1] - trace_y[:, :, :, 0]) / 12.0)
    source_term = source_term.at[:, :, :, 1].add(-trace_y[:, :, :, 1] / 12.0)
    wavefield = fast_solve(source_term, tables)
    for sweep_step in range(2):
        padded = jnp.pad(wavefield, ((0, 0), (0, 0), (2, 2), (2, 2), (0, 0)))
        wavefield = wavefield + fast_solve(source_term - apply_operator(padded, slowness), tables)
    return wavefield

def point_sources(flat_cells, amplitudes, start_x, start_y, size_x, size_y, cells_z, total_y):
    plane_cells = total_y * cells_z
    coord_x = flat_cells // plane_cells - start_x
    coord_y = flat_cells // cells_z % total_y - start_y
    coord_z = flat_cells % cells_z
    match_x = (coord_x[:, :, None] == jnp.arange(size_x, dtype=jnp.int32)[None, None, :]).astype(jnp.float32)
    match_y = (coord_y[:, :, None] == jnp.arange(size_y, dtype=jnp.int32)[None, None, :]).astype(jnp.float32)
    match_z = (coord_z[:, :, None] == jnp.arange(cells_z, dtype=jnp.int32)[None, None, :]).astype(jnp.float32)
    return jnp.einsum('spc,spx,spy,spz->scxyz', amplitudes, match_x, match_y, match_z, precision=HIGHEST)

def reference(right_side, slowness, source_cells, source_amplitudes):
    forcing = right_side + point_sources(source_cells, source_amplitudes, 0, 0, NX, NY, NZ, NY)
    tables = build_tables(CX, CY, NZ)
    visit_order = sorted(((grid_row + grid_col, grid_row, grid_col) for grid_row in range(N_GX) for grid_col in range(N_GY)))
    tile_rows = jnp.array([triple[1] for triple in visit_order], dtype=jnp.int32)
    tile_cols = jnp.array([triple[2] for triple in visit_order], dtype=jnp.int32)
    anchor = jnp.int32(0)

    def visit(position, wavefield):
        start_x = (tile_rows[position] * CX).astype(jnp.int32)
        start_y = (tile_cols[position] * CY).astype(jnp.int32)
        padded = jnp.pad(wavefield, ((0, 0), (0, 0), (2, 0), (2, 0), (0, 0)))
        trace_x = lax.dynamic_slice(padded, (anchor, anchor, start_x, start_y + 2, anchor), (NRHS, 2, 2, CY, NZ))
        trace_y = lax.dynamic_slice(padded, (anchor, anchor, start_x + 2, start_y, anchor), (NRHS, 2, CX, 2, NZ))
        source_term = lax.dynamic_slice(forcing, (anchor, anchor, start_x, start_y, anchor), (NRHS, 2, CX, CY, NZ))
        local_slowness = lax.dynamic_slice(slowness, (start_x, start_y, anchor), (CX, CY, NZ))
        solved = tile_solve(source_term, trace_x, trace_y, local_slowness, tables)
        return lax.dynamic_update_slice(wavefield, solved, (anchor, anchor, start_x, start_y, anchor))
    wavefield = lax.fori_loop(0, N_GX * N_GY, visit, jnp.zeros_like(forcing))
    padded = jnp.pad(wavefield, ((0, 0), (0, 0), (2, 2), (2, 2), (0, 0)))

    def one_source(pair):
        block, force = pair
        return force - apply_operator(block[None], slowness)[0]
    residual = lax.map(one_source, (padded, forcing))
    return (wavefield, residual)
```

```python
import functools
import math

import jax
import jax.numpy as jnp
import ml_dtypes
import numpy as np
from jax import lax
from jax.experimental import pallas as pl
from jax.experimental.pallas import tpu as pltpu
from jax.sharding import PartitionSpec as P

KAPPA = 0.12
DAMPING = 0.3
BF16 = jnp.bfloat16
F32 = jnp.float32


def sine_matrix(length):
    index = np.arange(1, length + 1)
    angles = index * (math.pi / (length + 1))
    return math.sqrt(2.0 / (length + 1)) * np.sin(angles[:, None] * index[None, :]), angles


def halves(matrix):
    high = matrix.astype(np.float32).astype(ml_dtypes.bfloat16)
    low = (matrix - high.astype(np.float64)).astype(np.float32).astype(ml_dtypes.bfloat16)
    return high, low


def left_factor(matrix):
    high, low = halves(matrix)
    return np.concatenate(
        [np.concatenate([high, high], axis=1), np.concatenate([low, low], axis=1)], axis=0
    )


def tables(size_x, size_y, cells_z):
    sine_x, angle_x = sine_matrix(size_x)
    sine_y, angle_y = sine_matrix(size_y)
    sine_z, angle_z = sine_matrix(cells_z)
    half = size_x // 2
    order = np.concatenate([np.arange(0, size_x, 2), np.arange(1, size_x, 2)])
    cells = np.concatenate([np.arange(half), np.arange(size_x - 1, half - 1, -1)])

    def symbol(angle):
        return 2.5 - 8.0 / 3.0 * np.cos(angle) + 1.0 / 6.0 * np.cos(2.0 * angle)

    real_part = (
        symbol(angle_x)[order][:, None, None]
        + symbol(angle_y)[None, :, None]
        + (2.0 - 2.0 * np.cos(angle_z))[None, None, :]
        - KAPPA
    ).reshape(size_x * size_y, cells_z)
    denominator = real_part**2 + (KAPPA * DAMPING) ** 2
    inverse = np.stack([real_part / denominator, KAPPA * DAMPING / denominator]).astype(np.float32)

    parity = [np.kron(sine_x[order[p * half : (p + 1) * half]][:, :half], sine_y) for p in (0, 1)]
    forward = np.stack([left_factor(m) for m in parity])
    backward = np.stack([left_factor(m.T) for m in parity])
    high_z, low_z = halves(sine_z)
    right_z = np.concatenate([np.concatenate([high_z, low_z], axis=1)] * 2, axis=0)

    full = np.kron(sine_x[order], sine_y)
    by_cell = full.reshape(-1, size_x, size_y)
    enter_x = np.stack([-by_cell[:, 0] / 12.0, (16.0 * by_cell[:, 0] - by_cell[:, 1]) / 12.0], 1)
    enter_y = np.stack(
        [-by_cell[:, :, 0] / 12.0, (16.0 * by_cell[:, :, 0] - by_cell[:, :, 1]) / 12.0], 1
    )
    enter = left_factor(
        np.concatenate([enter_x.reshape(len(full), -1), enter_y.reshape(len(full), -1)], axis=1)
    )
    leave = left_factor(
        np.concatenate(
            [
                by_cell[:, size_x - 2 :].reshape(len(full), -1),
                by_cell[:, :, size_y - 2 :].transpose(0, 2, 1).reshape(len(full), -1),
            ],
            axis=1,
        ).T
    )
    edge = np.zeros((size_x, size_y, 1))
    edge[0] += 1.0 / 12.0
    edge[-1] += 1.0 / 12.0
    edge[:, 0] += 1.0 / 12.0
    edge[:, -1] += 1.0 / 12.0
    edge = edge[cells].reshape(size_x * size_y, 1).astype(np.float32)
    return dict(
        inverse=inverse, forward=forward, backward=backward, right_z=right_z,
        enter=enter, leave=leave, edge=edge,
    ), cells


def split(values):
    high = values.astype(BF16)
    return high, (values - high.astype(F32)).astype(BF16)


def left_product(matrix, values):
    high, low = split(values)
    both = jnp.dot(matrix, jnp.concatenate([high, low], axis=0), preferred_element_type=F32)
    count = both.shape[0] // 2
    return both[:count] + both[count:]


def z_transform(field, right_z):
    rows = field.shape[0]
    cells_z = field.shape[1] // 2
    high, low = split(jnp.concatenate([field[:, :cells_z], field[:, cells_z:]], axis=0))
    both = jnp.dot(jnp.concatenate([high, low], axis=1), right_z, preferred_element_type=F32)
    total = both[:, :cells_z] + both[:, cells_z:]
    return jnp.concatenate([total[:rows], total[rows:]], axis=1)


def to_modes(field, forward):
    count = field.shape[0] // 2
    first, second = field[:count], field[count:]
    return jnp.concatenate(
        [left_product(forward[0], first + second), left_product(forward[1], first - second)], axis=0
    )


def to_cells(modes, backward):
    count = modes.shape[0] // 2
    even = left_product(backward[0], modes[:count])
    odd = left_product(backward[1], modes[count:])
    return jnp.concatenate([even + odd, even - odd], axis=0)


def times(real_part, imag_part, field):
    lanes = field.shape[1] // 2
    real, imag = field[:, :lanes], field[:, lanes:]
    return jnp.concatenate(
        [real_part * real - imag_part * imag, real_part * imag + imag_part * real], axis=1
    )


def solve_modes(source_modes, contrast, t):
    term = times(t["inverse"][0], t["inverse"][1], source_modes)
    total = term
    for _ in range(2):
        cells = z_transform(to_cells(term, t["backward"]), t["right_z"])
        cells = times(contrast[0], contrast[1], cells)
        term = times(t["inverse"][0], t["inverse"][1], to_modes(z_transform(cells, t["right_z"]), t["forward"]))
        total = total + term
    return total, term


PREP = ("edge", "forward", "right_z")
BEAT = ("inverse", "forward", "backward", "right_z", "enter", "leave")
LAST = ("inverse", "forward", "backward", "right_z", "enter")


def prep_kernel(cells_x, right_ref, slow_ref, place_ref, depth_ref, amp_ref, edge_ref, forward_ref, z_ref,
                modes_ref, contrast_ref):
    sources, _, size_x, size_y, cells_z = right_ref.shape
    rows = size_x * size_y
    scaled = jnp.concatenate([slow_ref[x] for x in cells_x], axis=0)
    scaled = KAPPA * (scaled - 1.0)
    contrast_ref[0] = scaled - edge_ref[...]
    contrast_ref[1] = DAMPING * scaled
    row_ids = lax.broadcasted_iota(jnp.int32, (rows, place_ref.shape[2]), 0)
    lane_ids = lax.broadcasted_iota(jnp.int32, (cells_z, place_ref.shape[2]), 0)
    forward = (forward_ref[0], forward_ref[1])
    for s in range(sources):
        at_row = (row_ids == place_ref[s]).astype(F32).astype(BF16)
        at_lane = (lane_ids == depth_ref[s]).astype(F32)
        parts = []
        for c in range(2):
            dense = jnp.concatenate([right_ref[s, c, x] for x in cells_x], axis=0)
            amp = amp_ref[s, c]
            one = amp.astype(BF16).astype(F32)
            two = (amp - one).astype(BF16).astype(F32)
            weights = [at_lane * part for part in (one, two, amp - one - two)]
            spread = jnp.concatenate(weights, axis=1).astype(BF16)
            points = lax.dot_general(
                jnp.concatenate([at_row] * 3, axis=1), spread, (((1,), (1,)), ((), ())),
                preferred_element_type=F32,
            )
            parts.append(dense + points)
        field = z_transform(jnp.concatenate(parts, axis=1), z_ref[...])
        modes_ref[s] = to_modes(field, forward)


def source_modes(modes_ref, trace_x_ref, trace_y_ref, enter_ref, s):
    trace = jnp.concatenate([trace_x_ref[s], trace_y_ref[s]], axis=0)
    return modes_ref[s] + left_product(enter_ref[...], trace)


def beat_kernel(active_ref, modes_ref, contrast_ref, trace_x_ref, trace_y_ref, *refs):
    t = {name: ref for name, ref in zip(BEAT, refs)}
    out_x_ref, out_y_ref = refs[len(BEAT) :]

    @pl.when(active_ref[0] == 1)
    def _():
        right_z = t["right_z"][...]
        local = dict(inverse=t["inverse"], forward=t["forward"], backward=t["backward"], right_z=right_z)
        for s in range(modes_ref.shape[0]):
            total, _ = solve_modes(
                source_modes(modes_ref, trace_x_ref, trace_y_ref, t["enter"], s), contrast_ref, local
            )
            out = left_product(t["leave"][...], total)
            count = out_x_ref.shape[1]
            out_x_ref[s] = out[:count]
            out_y_ref[s] = out[count:]


def last_kernel(cells_x, modes_ref, contrast_ref, trace_x_ref, trace_y_ref, *refs):
    t = {name: ref for name, ref in zip(LAST, refs)}
    wave_ref, rest_ref = refs[len(LAST) :]
    size_y, cells_z = wave_ref.shape[3], wave_ref.shape[4]
    local = dict(t, right_z=t["right_z"][...])
    for s in range(modes_ref.shape[0]):
        total, term = solve_modes(
            source_modes(modes_ref, trace_x_ref, trace_y_ref, t["enter"], s), contrast_ref, local
        )
        wave = z_transform(to_cells(total, t["backward"]), local["right_z"])
        rest = z_transform(to_cells(term, t["backward"]), local["right_z"])
        rest = times(contrast_ref[0], contrast_ref[1], rest)
        for place, x in enumerate(cells_x):
            here = slice(place * size_y, (place + 1) * size_y)
            for c in range(2):
                there = slice(c * cells_z, (c + 1) * cells_z)
                wave_ref[s, c, x] = wave[here, there]
                rest_ref[s, c, x] = rest[here, there]


def whole():
    return pl.BlockSpec(memory_space=pltpu.VMEM)


PARAMS = pltpu.CompilerParams(vmem_limit_bytes=40 * 1024 * 1024)


def body(right_side, slowness, source_cells, source_amplitudes):
    sources, _, size_x, size_y, cells_z = right_side.shape
    grid_rows, grid_cols = lax.axis_size("gx"), lax.axis_size("gy")
    row, col = lax.axis_index("gx"), lax.axis_index("gy")
    t, cells_x = tables(size_x, size_y, cells_z)
    t = {name: jnp.asarray(value) for name, value in t.items()}
    cells_x = tuple(int(x) for x in cells_x)
    rows = size_x * size_y

    total_y = size_y * grid_cols
    near_x = source_cells // (total_y * cells_z) - row * size_x
    near_y = source_cells // cells_z % total_y - col * size_y
    inside = (near_x >= 0) & (near_x < size_x) & (near_y >= 0) & (near_y < size_y)
    place_x = jnp.where(near_x < size_x // 2, near_x, size_x + size_x // 2 - 1 - near_x)
    place = jnp.where(inside, place_x * size_y + near_y, -1)[:, None, :]
    depth = (source_cells % cells_z)[:, None, :]
    amplitudes = source_amplitudes.transpose(0, 2, 1)[:, :, None, :]

    modes, contrast = pl.pallas_call(
        functools.partial(prep_kernel, cells_x),
        out_shape=(
            jax.ShapeDtypeStruct((sources, rows, 2 * cells_z), F32),
            jax.ShapeDtypeStruct((2, rows, cells_z), F32),
        ),
        in_specs=[whole()] * 8,
        out_specs=(whole(), whole()),
        compiler_params=PARAMS,
        name="prep",
    )(right_side, slowness, place, depth, amplitudes, *[t[name] for name in PREP])

    trace_x = jnp.zeros((sources, 2 * size_y, 2 * cells_z), F32)
    trace_y = jnp.zeros((sources, 2 * size_x, 2 * cells_z), F32)
    sum_x, sum_y = [], []
    for beat in range(grid_rows + grid_cols - 2):
        active = (row + col == beat).astype(jnp.int32)[None]
        out_x, out_y = pl.pallas_call(
            beat_kernel,
            out_shape=(
                jax.ShapeDtypeStruct(trace_x.shape, F32),
                jax.ShapeDtypeStruct(trace_y.shape, F32),
            ),
            in_specs=[pl.BlockSpec(memory_space=pltpu.SMEM)] + [whole()] * (4 + len(BEAT)),
            out_specs=(whole(), whole()),
            compiler_params=PARAMS,
            name="beat",
        )(active, modes, contrast, trace_x, trace_y, *[t[name] for name in BEAT])
        pairs_x = []
        pairs_y = []
        for i in range(grid_rows):
            j = beat - i
            if 0 <= j < grid_cols:
                here = i * grid_cols + j
                if i + 1 < grid_rows:
                    pairs_x.append((here, here + grid_cols))
                if j + 1 < grid_cols:
                    pairs_y.append((here, here + 1))
        trace_x = lax.ppermute(out_x, ("gx", "gy"), pairs_x)
        trace_y = lax.ppermute(out_y, ("gx", "gy"), pairs_y)
        sum_x.append(trace_x)
        sum_y.append(trace_y)

    wavefield, rest = pl.pallas_call(
        functools.partial(last_kernel, cells_x),
        out_shape=(
            jax.ShapeDtypeStruct(right_side.shape, F32),
            jax.ShapeDtypeStruct(right_side.shape, F32),
        ),
        in_specs=[whole()] * (4 + len(LAST)),
        out_specs=(whole(), whole()),
        compiler_params=PARAMS,
        name="last",
    )(modes, contrast, sum(sum_x), sum(sum_y), *[t[name] for name in LAST])

    after_x = lax.ppermute(wavefield[:, :, :2], "gx", [(i + 1, i) for i in range(grid_rows - 1)])
    after_y = lax.ppermute(wavefield[:, :, :, :2], "gy", [(j + 1, j) for j in range(grid_cols - 1)])
    near, far = after_x[:, :, :1], after_x[:, :, 1:]
    rest = rest + jnp.pad(
        jnp.concatenate([-near, 16.0 * near - far], axis=2) / 12.0,
        ((0, 0), (0, 0), (size_x - 2, 0), (0, 0), (0, 0)),
    )
    near, far = after_y[:, :, :, :1], after_y[:, :, :, 1:]
    rest = rest + jnp.pad(
        jnp.concatenate([-near, 16.0 * near - far], axis=3) / 12.0,
        ((0, 0), (0, 0), (0, 0), (size_y - 2, 0), (0, 0)),
    )
    return wavefield, rest


def solution(mesh):
    return jax.shard_map(
        body,
        mesh=mesh,
        in_specs=(P(None, None, "gx", "gy", None), P("gx", "gy", None), P(), P()),
        out_specs=(P(None, None, "gx", "gy", None), P(None, None, "gx", "gy", None)),
        check_vma=False,
    )
```

```python
import functools
import math

import jax
import jax.numpy as jnp
import ml_dtypes
import numpy as np
from jax import lax
from jax.experimental import pallas as pl
from jax.experimental.pallas import tpu as pltpu
from jax.sharding import PartitionSpec as P

KAPPA = 0.12
DAMPING = 0.3
BF16 = jnp.bfloat16
F32 = jnp.float32


def sine_matrix(length):
    index = np.arange(1, length + 1)
    angles = index * (math.pi / (length + 1))
    return math.sqrt(2.0 / (length + 1)) * np.sin(angles[:, None] * index[None, :]), angles


def halves(matrix):
    high = matrix.astype(np.float32).astype(ml_dtypes.bfloat16)
    low = (matrix - high.astype(np.float64)).astype(np.float32).astype(ml_dtypes.bfloat16)
    return high, low


def left_factor(matrix):
    high, low = halves(matrix)
    return np.concatenate(
        [np.concatenate([high, high], axis=1), np.concatenate([low, low], axis=1)], axis=0
    )


def tables(size_x, size_y, cells_z):
    sine_x, angle_x = sine_matrix(size_x)
    sine_y, angle_y = sine_matrix(size_y)
    sine_z, angle_z = sine_matrix(cells_z)
    half = size_x // 2
    order = np.concatenate([np.arange(0, size_x, 2), np.arange(1, size_x, 2)])
    cells = np.concatenate([np.arange(half), np.arange(size_x - 1, half - 1, -1)])

    def symbol(angle):
        return 2.5 - 8.0 / 3.0 * np.cos(angle) + 1.0 / 6.0 * np.cos(2.0 * angle)

    real_part = (
        symbol(angle_x)[order][:, None, None]
        + symbol(angle_y)[None, :, None]
        + (2.0 - 2.0 * np.cos(angle_z))[None, None, :]
        - KAPPA
    ).reshape(size_x * size_y, cells_z)
    denominator = real_part**2 + (KAPPA * DAMPING) ** 2
    inverse = np.stack([real_part / denominator, KAPPA * DAMPING / denominator]).astype(np.float32)

    parity = [np.kron(sine_x[order[p * half : (p + 1) * half]][:, :half], sine_y) for p in (0, 1)]
    forward = np.stack([left_factor(m) for m in parity])
    backward = np.stack([left_factor(m.T) for m in parity])
    high_z, low_z = halves(sine_z)
    right_z = np.concatenate([np.concatenate([high_z, low_z], axis=1)] * 2, axis=0)

    full = np.kron(sine_x[order], sine_y)
    by_cell = full.reshape(-1, size_x, size_y)
    enter_x = np.stack([-by_cell[:, 0] / 12.0, (16.0 * by_cell[:, 0] - by_cell[:, 1]) / 12.0], 1)
    enter_y = np.stack(
        [-by_cell[:, :, 0] / 12.0, (16.0 * by_cell[:, :, 0] - by_cell[:, :, 1]) / 12.0], 1
    )
    enter = left_factor(
        np.concatenate([enter_x.reshape(len(full), -1), enter_y.reshape(len(full), -1)], axis=1)
    )
    leave = left_factor(
        np.concatenate(
            [
                by_cell[:, size_x - 2 :].reshape(len(full), -1),
                by_cell[:, :, size_y - 2 :].transpose(0, 2, 1).reshape(len(full), -1),
            ],
            axis=1,
        ).T
    )
    edge = np.zeros((size_x, size_y, 1))
    edge[0] += 1.0 / 12.0
    edge[-1] += 1.0 / 12.0
    edge[:, 0] += 1.0 / 12.0
    edge[:, -1] += 1.0 / 12.0
    edge = edge[cells].reshape(size_x * size_y, 1).astype(np.float32)
    return dict(
        inverse=inverse, forward=forward, backward=backward, right_z=right_z,
        enter=enter, leave=leave, edge=edge,
    ), cells


def split(values):
    high = values.astype(BF16)
    return high, (values - high.astype(F32)).astype(BF16)


def left_product(matrix, values):
    high, low = split(values)
    both = jnp.dot(matrix, jnp.concatenate([high, low], axis=0), preferred_element_type=F32)
    count = both.shape[0] // 2
    return both[:count] + both[count:]


def z_transform(field, right_z):
    rows = field.shape[0]
    cells_z = field.shape[1] // 2
    high, low = split(jnp.concatenate([field[:, :cells_z], field[:, cells_z:]], axis=0))
    both = jnp.dot(jnp.concatenate([high, low], axis=1), right_z, preferred_element_type=F32)
    total = both[:, :cells_z] + both[:, cells_z:]
    return jnp.concatenate([total[:rows], total[rows:]], axis=1)


def to_modes(field, forward):
    count = field.shape[0] // 2
    first, second = field[:count], field[count:]
    return jnp.concatenate(
        [left_product(forward[0], first + second), left_product(forward[1], first - second)], axis=0
    )


def to_cells(modes, backward):
    count = modes.shape[0] // 2
    even = left_product(backward[0], modes[:count])
    odd = left_product(backward[1], modes[count:])
    return jnp.concatenate([even + odd, even - odd], axis=0)


def times(real_part, imag_part, field):
    lanes = field.shape[1] // 2
    real, imag = field[:, :lanes], field[:, lanes:]
    return jnp.concatenate(
        [real_part * real - imag_part * imag, real_part * imag + imag_part * real], axis=1
    )


def solve_modes(source_modes, contrast, t):
    term = times(t["inverse"][0], t["inverse"][1], source_modes)
    total = term
    for _ in range(2):
        cells = z_transform(to_cells(term, t["backward"]), t["right_z"])
        cells = times(contrast[0], contrast[1], cells)
        term = times(t["inverse"][0], t["inverse"][1], to_modes(z_transform(cells, t["right_z"]), t["forward"]))
        total = total + term
    return total, term


PREP = ("edge", "forward", "right_z")
BEAT = ("inverse", "forward", "backward", "right_z", "enter", "leave")


def prep_kernel(cells_x, core_ref, right_ref, slow_ref, swap_ref, place_ref, depth_ref, amp_ref, edge_ref,
                forward_ref, z_ref, modes_ref, contrast_ref):
    _, _, size_x, size_y, cells_z = right_ref.shape
    rows = size_x * size_y
    core = core_ref[0]
    points = place_ref.shape[2]
    row_ids = lax.broadcasted_iota(jnp.int32, (rows, points), 0)
    lane_ids = lax.broadcasted_iota(jnp.int32, (cells_z, points), 0)
    at_lane = (lane_ids == depth_ref[...]).astype(F32)
    spread = []
    for c in range(2):
        amp = amp_ref[c]
        one = amp.astype(BF16).astype(F32)
        two = (amp - one).astype(BF16).astype(F32)
        parts = [at_lane * part for part in (one, two, amp - one - two)]
        spread.append(jnp.concatenate(parts, axis=1).astype(BF16))
    spread = jnp.concatenate(spread, axis=0)
    for other in range(2):
        tile = core if other == 0 else 1 - core
        if other == 0:
            slow = [slow_ref[x] for x in cells_x]
            dense = [[right_ref[core, c, x] for x in cells_x] for c in range(2)]
        else:
            slow = [swap_ref[2, x] for x in cells_x]
            dense = [[swap_ref[c, x] for x in cells_x] for c in range(2)]
        scaled = KAPPA * (jnp.concatenate(slow, axis=0) - 1.0)
        contrast_ref[tile, 0] = scaled - edge_ref[...]
        contrast_ref[tile, 1] = DAMPING * scaled
        at_row = (row_ids == place_ref[other]).astype(F32).astype(BF16)
        field = lax.dot_general(
            jnp.concatenate([at_row] * 3, axis=1), spread, (((1,), (1,)), ((), ())),
            preferred_element_type=F32,
        )
        field = field + jnp.concatenate([jnp.concatenate(d, axis=0) for d in dense], axis=1)
        modes_ref[tile] = to_modes(z_transform(field, z_ref[...]), forward_ref)


def source_modes(modes, trace_x, trace_y, enter):
    return modes + left_product(enter, jnp.concatenate([trace_x, trace_y], axis=0))


def beat_kernel(tile, active_ref, modes_ref, contrast_ref, trace_x_ref, trace_y_ref, *refs):
    t = {name: ref for name, ref in zip(BEAT, refs)}
    out_x_ref, out_y_ref = refs[len(BEAT) :]

    @pl.when(active_ref[0] == 1)
    def _():
        local = dict(t, right_z=t["right_z"][...])
        source = source_modes(modes_ref[tile], trace_x_ref[...], trace_y_ref[...], t["enter"][...])
        total, _ = solve_modes(source, contrast_ref.at[tile], local)
        out = left_product(t["leave"][...], total)
        count = out_x_ref.shape[0]
        out_x_ref[...] = out[:count]
        out_y_ref[...] = out[count:]


def last_kernel(cells_x, modes_ref, contrast_ref, trace_x_ref, trace_y0_ref, trace_y1_ref, *refs):
    t = {name: ref for name, ref in zip(BEAT, refs)}
    both_ref, edge_x_ref, edge_y_ref = refs[len(BEAT) :]
    size_y, cells_z = both_ref.shape[4], both_ref.shape[5]
    size_x = both_ref.shape[3]
    local = dict(t, right_z=t["right_z"][...])
    trace_x = trace_x_ref[...]
    for tile, trace_y_ref in enumerate((trace_y0_ref, trace_y1_ref)):
        source = source_modes(modes_ref[tile], trace_x, trace_y_ref[...], t["enter"][...])
        total, term = solve_modes(source, contrast_ref.at[tile], local)
        if tile == 0:
            trace_x = left_product(t["leave"][...], total)[: trace_x_ref.shape[0]]
        wave = z_transform(to_cells(total, t["backward"]), local["right_z"])
        rest = z_transform(to_cells(term, t["backward"]), local["right_z"])
        rest = times(contrast_ref[tile, 0], contrast_ref[tile, 1], rest)
        for place, x in enumerate(cells_x):
            here = slice(place * size_y, (place + 1) * size_y)
            for c in range(2):
                there = slice(c * cells_z, (c + 1) * cells_z)
                both_ref[tile, 0, c, x] = wave[here, there]
                both_ref[tile, 1, c, x] = rest[here, there]
                edge_y_ref[tile, c, x] = wave[place * size_y : place * size_y + 2, there]
                if tile == 0 and x < 2:
                    edge_x_ref[c, x] = wave[here, there]
                if tile == 1 and x < 2:
                    layer = wave[here, there]
                    if x == 0:
                        both_ref[0, 1, c, size_x - 2] += layer * (-1.0 / 12.0)
                        both_ref[0, 1, c, size_x - 1] += layer * (16.0 / 12.0)
                    else:
                        both_ref[0, 1, c, size_x - 1] += layer * (-1.0 / 12.0)


def fix_kernel(core_ref, both_ref, edge_x_ref, edge_y_ref, keep_ref, give_ref):
    core = core_ref[0]
    _, _, _, size_x, size_y, _ = both_ref.shape
    for out_ref, tile in ((keep_ref, core), (give_ref, 1 - core)):
        out_ref[...] = both_ref[tile]
        lower = (tile == 1).astype(F32)
        for c in range(2):
            near, far = edge_x_ref[c, 0] * lower, edge_x_ref[c, 1] * lower
            out_ref[1, c, size_x - 2] += near * (-1.0 / 12.0)
            out_ref[1, c, size_x - 1] += (16.0 * near - far) * (1.0 / 12.0)
            near, far = edge_y_ref[tile, c, :, 0:1], edge_y_ref[tile, c, :, 1:2]
            out_ref[1, c, :, size_y - 2 : size_y - 1] += near * (-1.0 / 12.0)
            out_ref[1, c, :, size_y - 1 : size_y] += (16.0 * near - far) * (1.0 / 12.0)


def place_kernel(core_ref, keep_ref, got_ref, wave_ref, rest_ref, sems):
    core = core_ref[0]
    copies = [
        pltpu.make_async_copy(source.at[which], out.at[index], sems.at[2 * pair + which])
        for pair, (source, index) in enumerate(((keep_ref, core), (got_ref, 1 - core)))
        for which, out in enumerate((wave_ref, rest_ref))
    ]
    for copy in copies:
        copy.start()
    for copy in copies:
        copy.wait()


def whole():
    return pl.BlockSpec(memory_space=pltpu.VMEM)


def scalars():
    return pl.BlockSpec(memory_space=pltpu.SMEM)


def anywhere():
    return pl.BlockSpec(memory_space=pl.ANY)


PARAMS = pltpu.CompilerParams(vmem_limit_bytes=40 * 1024 * 1024)


def shaped(*shape):
    return jax.ShapeDtypeStruct(shape, F32)


def body(right_side, slowness, source_cells, source_amplitudes):
    sources, _, size_x, size_y, cells_z = right_side.shape
    grid_rows, grid_cols = lax.axis_size("gx"), lax.axis_size("gy")
    assert sources == 2 and grid_rows % 2 == 0 and size_x % 2 == 0
    chips = grid_rows // 2
    row, col = lax.axis_index("gx"), lax.axis_index("gy")
    core = row % 2
    core_ref = core[None]
    t, cells_x = tables(size_x, size_y, cells_z)
    t = {name: jnp.asarray(value) for name, value in t.items()}
    cells_x = tuple(int(x) for x in cells_x)
    rows = size_x * size_y

    def device(chip, core, column):
        return (2 * chip + core) * grid_cols + column

    def between(pairs):
        return [
            (device(a, r, b), device(c, r, d)) for (a, b), (c, d) in pairs for r in range(2)
        ]

    own = [
        (device(k, r, j), device(k, 1 - r, j))
        for k in range(chips) for j in range(grid_cols) for r in range(2)
    ]
    axes = ("gx", "gy")
    other = lax.dynamic_index_in_dim(right_side, 1 - core, 0, keepdims=False)
    swapped = lax.ppermute(jnp.concatenate([other, slowness[None]], axis=0), axes, own)

    total_y = size_y * grid_cols
    cells = lax.dynamic_index_in_dim(source_cells, core, 0, keepdims=True)
    near_y = cells // cells_z % total_y - col * size_y
    places = []
    for tile_row in (row, row + 1 - 2 * core):
        near_x = cells // (total_y * cells_z) - tile_row * size_x
        inside = (near_x >= 0) & (near_x < size_x) & (near_y >= 0) & (near_y < size_y)
        folded = jnp.where(near_x < size_x // 2, near_x, size_x + size_x // 2 - 1 - near_x)
        places.append(jnp.where(inside, folded * size_y + near_y, -1))
    amplitudes = lax.dynamic_index_in_dim(source_amplitudes, core, 0, keepdims=False).T[:, None, :]

    modes, contrast = pl.pallas_call(
        functools.partial(prep_kernel, cells_x),
        out_shape=(shaped(2, rows, 2 * cells_z), shaped(2, 2, rows, cells_z)),
        in_specs=[scalars()] + [whole()] * 9,
        out_specs=(whole(), whole()),
        compiler_params=PARAMS,
        name="prep",
    )(core_ref, right_side, slowness, swapped, jnp.stack(places), cells % cells_z, amplitudes,
      *[t[name] for name in PREP])

    beat_tables = [t[name] for name in BEAT]

    def solve(tile, active, trace_x, trace_y):
        return pl.pallas_call(
            functools.partial(beat_kernel, tile),
            out_shape=(shaped(*zero_x.shape), shaped(*zero_y.shape)),
            in_specs=[scalars()] + [whole()] * (4 + len(BEAT)),
            out_specs=(whole(), whole()),
            compiler_params=PARAMS,
            name="upper" if tile == 0 else "lower",
        )(active, modes, contrast, trace_x, trace_y, *beat_tables)

    zero_x = jnp.zeros((2 * size_y, 2 * cells_z), F32)
    zero_y = jnp.zeros((2 * size_x, 2 * cells_z), F32)
    trace_x, trace_y0, trace_y1 = zero_x, zero_y, zero_y
    sums = ([], [], [])
    for beat in range(chips + grid_cols - 2):
        active = (row // 2 + col == beat).astype(jnp.int32)[None]
        here = [(k, beat - k) for k in range(chips) if 0 <= beat - k < grid_cols]
        along_x = between([((k, j), (k + 1, j)) for k, j in here if k + 1 < chips])
        along_y = between([((k, j), (k, j + 1)) for k, j in here if j + 1 < grid_cols])
        inner_x, out_y0 = solve(0, active, trace_x, trace_y0)
        trace_y0 = lax.ppermute(out_y0, axes, along_y)
        out_x, out_y1 = solve(1, active, inner_x, trace_y1)
        trace_x = lax.ppermute(out_x, axes, along_x)
        trace_y1 = lax.ppermute(out_y1, axes, along_y)
        for held, trace in zip(sums, (trace_x, trace_y0, trace_y1)):
            held.append(trace)

    both, edge_x, edge_y = pl.pallas_call(
        functools.partial(last_kernel, cells_x),
        out_shape=(
            shaped(2, 2, 2, size_x, size_y, cells_z),
            shaped(2, 2, size_y, cells_z),
            shaped(2, 2, size_x, 2, cells_z),
        ),
        in_specs=[whole()] * (5 + len(BEAT)),
        out_specs=(whole(),) * 3,
        compiler_params=PARAMS,
        name="last",
    )(modes, contrast, *[sum(held) for held in sums], *beat_tables)

    every = [(k, j) for k in range(chips) for j in range(grid_cols)]
    after_x = lax.ppermute(edge_x, axes, between([((k, j), (k - 1, j)) for k, j in every if k]))
    after_y = lax.ppermute(edge_y, axes, between([((k, j), (k, j - 1)) for k, j in every if j]))
    half = shaped(2, 2, size_x, size_y, cells_z)
    keep, give = pl.pallas_call(
        fix_kernel,
        out_shape=(half, half),
        in_specs=[scalars()] + [whole()] * 3,
        out_specs=(whole(), whole()),
        compiler_params=PARAMS,
        name="fix",
    )(core_ref, both, after_x, after_y)
    got = lax.ppermute(give, axes, own)
    return pl.pallas_call(
        place_kernel,
        out_shape=(shaped(*right_side.shape), shaped(*right_side.shape)),
        in_specs=[scalars(), anywhere(), anywhere()],
        out_specs=(anywhere(), anywhere()),
        scratch_shapes=[pltpu.SemaphoreType.DMA((4,))],
        compiler_params=PARAMS,
        name="place",
    )(core_ref, keep, got)


def solution(mesh):
    return jax.shard_map(
        body,
        mesh=mesh,
        in_specs=(P(None, None, "gx", "gy", None), P("gx", "gy", None), P(), P()),
        out_specs=(P(None, None, "gx", "gy", None), P(None, None, "gx", "gy", None)),
        check_vma=False,
    )
```

```python
import functools
import math

import jax
import jax.numpy as jnp
import ml_dtypes
import numpy as np
from jax import lax
from jax.experimental import pallas as pl
from jax.experimental.pallas import tpu as pltpu
from jax.sharding import PartitionSpec as P

KAPPA = 0.12
DAMPING = 0.3
BF16 = jnp.bfloat16
F32 = jnp.float32


def sine_matrix(length):
    index = np.arange(1, length + 1)
    angles = index * (math.pi / (length + 1))
    return math.sqrt(2.0 / (length + 1)) * np.sin(angles[:, None] * index[None, :]), angles


def halves(matrix):
    high = matrix.astype(np.float32).astype(ml_dtypes.bfloat16)
    low = (matrix - high.astype(np.float64)).astype(np.float32).astype(ml_dtypes.bfloat16)
    return high, low


def left_factor(matrix):
    high, low = halves(matrix)
    return np.concatenate(
        [np.concatenate([high, high], axis=1), np.concatenate([low, low], axis=1)], axis=0
    )


def tables(size_x, size_y, cells_z):
    sine_x, angle_x = sine_matrix(size_x)
    sine_y, angle_y = sine_matrix(size_y)
    sine_z, angle_z = sine_matrix(cells_z)
    half = size_x // 2
    order = np.concatenate([np.arange(0, size_x, 2), np.arange(1, size_x, 2)])
    cells = np.concatenate([np.arange(half), np.arange(size_x - 1, half - 1, -1)])

    def symbol(angle):
        return 2.5 - 8.0 / 3.0 * np.cos(angle) + 1.0 / 6.0 * np.cos(2.0 * angle)

    real_part = (
        symbol(angle_x)[order][:, None, None]
        + symbol(angle_y)[None, :, None]
        + (2.0 - 2.0 * np.cos(angle_z))[None, None, :]
        - KAPPA
    ).reshape(size_x * size_y, cells_z)
    denominator = real_part**2 + (KAPPA * DAMPING) ** 2
    inverse = np.stack([real_part / denominator, KAPPA * DAMPING / denominator]).astype(np.float32)

    parity = [np.kron(sine_x[order[p * half : (p + 1) * half]][:, :half], sine_y) for p in (0, 1)]
    forward = np.stack([left_factor(m) for m in parity])
    backward = np.stack([left_factor(m.T) for m in parity])
    high_z, low_z = halves(sine_z)
    right_z = np.concatenate([np.concatenate([high_z, low_z], axis=1)] * 2, axis=0)

    full = np.kron(sine_x[order], sine_y)
    by_cell = full.reshape(-1, size_x, size_y)
    enter_x = np.stack([-by_cell[:, 0] / 12.0, (16.0 * by_cell[:, 0] - by_cell[:, 1]) / 12.0], 1)
    enter_y = np.stack(
        [-by_cell[:, :, 0] / 12.0, (16.0 * by_cell[:, :, 0] - by_cell[:, :, 1]) / 12.0], 1
    )
    enter = left_factor(
        np.concatenate([enter_x.reshape(len(full), -1), enter_y.reshape(len(full), -1)], axis=1)
    )
    leave = left_factor(
        np.concatenate(
            [
                by_cell[:, size_x - 2 :].reshape(len(full), -1),
                by_cell[:, :, size_y - 2 :].transpose(0, 2, 1).reshape(len(full), -1),
            ],
            axis=1,
        ).T
    )
    edge = np.zeros((size_x, size_y, 1))
    edge[0] += 1.0 / 12.0
    edge[-1] += 1.0 / 12.0
    edge[:, 0] += 1.0 / 12.0
    edge[:, -1] += 1.0 / 12.0
    edge = edge[cells].reshape(size_x * size_y, 1).astype(np.float32)
    return dict(
        inverse=inverse, forward=forward, backward=backward, right_z=right_z,
        enter=enter, leave=leave, edge=edge,
    ), cells


def split(values):
    high = values.astype(BF16)
    return high, (values - high.astype(F32)).astype(BF16)


def left_product(matrix, values):
    high, low = split(values)
    both = jnp.dot(matrix, jnp.concatenate([high, low], axis=0), preferred_element_type=F32)
    count = both.shape[0] // 2
    return both[:count] + both[count:]


def z_transform(field, right_z):
    rows = field.shape[0]
    cells_z = field.shape[1] // 2
    high, low = split(jnp.concatenate([field[:, :cells_z], field[:, cells_z:]], axis=0))
    both = jnp.dot(jnp.concatenate([high, low], axis=1), right_z, preferred_element_type=F32)
    total = both[:, :cells_z] + both[:, cells_z:]
    return jnp.concatenate([total[:rows], total[rows:]], axis=1)


def to_modes(field, forward):
    count = field.shape[0] // 2
    first, second = field[:count], field[count:]
    return jnp.concatenate(
        [left_product(forward[0], first + second), left_product(forward[1], first - second)], axis=0
    )


def to_cells(modes, backward):
    count = modes.shape[0] // 2
    even = left_product(backward[0], modes[:count])
    odd = left_product(backward[1], modes[count:])
    return jnp.concatenate([even + odd, even - odd], axis=0)


def times(real_part, imag_part, field):
    lanes = field.shape[1] // 2
    real, imag = field[:, :lanes], field[:, lanes:]
    return jnp.concatenate(
        [real_part * real - imag_part * imag, real_part * imag + imag_part * real], axis=1
    )


def solve_modes(source_modes, contrast, t):
    term = times(t["inverse"][0], t["inverse"][1], source_modes)
    total = term
    for _ in range(2):
        cells = apply_contrast(to_cells(term, t["backward"]), contrast, t["right_z"])
        term = times(t["inverse"][0], t["inverse"][1], to_modes(cells, t["forward"]))
        total = total + term
    return total, term


def apply_contrast(field, contrast, right_z, block=64):
    done = []
    for start in range(0, field.shape[0], block):
        here = slice(start, start + block)
        cells = times(contrast[0, here], contrast[1, here], z_transform(field[here], right_z))
        done.append(z_transform(cells, right_z))
    return jnp.concatenate(done, axis=0)


PREP = ("edge", "forward", "right_z")
BEAT = ("inverse", "forward", "backward", "right_z", "enter", "leave")


def gather_kernel(core_ref, right_ref, slow_ref, swap_ref, sems):
    copies = [
        pltpu.make_async_copy(right_ref.at[1 - core_ref[0]], swap_ref.at[pl.ds(0, 2)], sems.at[0]),
        pltpu.make_async_copy(slow_ref, swap_ref.at[2], sems.at[1]),
    ]
    for copy in copies:
        copy.start()
    for copy in copies:
        copy.wait()


def prep_kernel(cells_x, core_ref, right_ref, slow_ref, swap_ref, place_ref, depth_ref, amp_ref, edge_ref,
                forward_ref, z_ref, modes_ref, contrast_ref):
    _, _, size_x, size_y, cells_z = right_ref.shape
    rows = size_x * size_y
    core = core_ref[0]
    points = place_ref.shape[2]
    row_ids = lax.broadcasted_iota(jnp.int32, (rows, points), 0)
    lane_ids = lax.broadcasted_iota(jnp.int32, (cells_z, points), 0)
    at_lane = (lane_ids == depth_ref[...]).astype(F32)
    spread = []
    for c in range(2):
        amp = amp_ref[c]
        one = amp.astype(BF16).astype(F32)
        two = (amp - one).astype(BF16).astype(F32)
        parts = [at_lane * part for part in (one, two, amp - one - two)]
        spread.append(jnp.concatenate(parts, axis=1).astype(BF16))
    spread = jnp.concatenate(spread, axis=0)
    for other in range(2):
        tile = core if other == 0 else 1 - core
        if other == 0:
            slow = [slow_ref[x] for x in cells_x]
            dense = [[right_ref[core, c, x] for x in cells_x] for c in range(2)]
        else:
            slow = [swap_ref[2, x] for x in cells_x]
            dense = [[swap_ref[c, x] for x in cells_x] for c in range(2)]
        scaled = KAPPA * (jnp.concatenate(slow, axis=0) - 1.0)
        contrast_ref[tile, 0] = scaled - edge_ref[...]
        contrast_ref[tile, 1] = DAMPING * scaled
        at_row = (row_ids == place_ref[other]).astype(F32).astype(BF16)
        field = lax.dot_general(
            jnp.concatenate([at_row] * 3, axis=1), spread, (((1,), (1,)), ((), ())),
            preferred_element_type=F32,
        )
        field = field + jnp.concatenate([jnp.concatenate(d, axis=0) for d in dense], axis=1)
        modes_ref[tile] = to_modes(z_transform(field, z_ref[...]), forward_ref)


def source_modes(modes, trace_x, trace_y, enter):
    return modes + left_product(enter, jnp.concatenate([trace_x, trace_y], axis=0))


def beat_kernel(tile, active_ref, modes_ref, contrast_ref, trace_x_ref, trace_y_ref, *refs):
    t = {name: ref for name, ref in zip(BEAT, refs)}
    out_x_ref, out_y_ref = refs[len(BEAT) :]

    @pl.when(active_ref[0] == 1)
    def _():
        local = dict(t, right_z=t["right_z"][...])
        source = source_modes(modes_ref[tile], trace_x_ref[...], trace_y_ref[...], t["enter"][...])
        total, _ = solve_modes(source, contrast_ref.at[tile], local)
        out = left_product(t["leave"][...], total)
        count = out_x_ref.shape[0]
        out_x_ref[...] = out[:count]
        out_y_ref[...] = out[count:]


def last_kernel(cells_x, core_ref, modes_ref, contrast_ref, trace_x_ref, trace_y0_ref, trace_y1_ref, *refs):
    t = {name: ref for name, ref in zip(BEAT, refs)}
    keep_ref, give_ref, edge_x_ref, edge_y_ref, both_ref = refs[len(BEAT) :]
    size_y, cells_z = both_ref.shape[4], both_ref.shape[5]
    size_x = both_ref.shape[3]
    local = dict(t, right_z=t["right_z"][...])
    trace_x = trace_x_ref[...]
    for tile, trace_y_ref in enumerate((trace_y0_ref, trace_y1_ref)):
        source = source_modes(modes_ref[tile], trace_x, trace_y_ref[...], t["enter"][...])
        total, term = solve_modes(source, contrast_ref.at[tile], local)
        if tile == 0:
            trace_x = left_product(t["leave"][...], total)[: trace_x_ref.shape[0]]
        wave = z_transform(to_cells(total, t["backward"]), local["right_z"])
        rest = z_transform(to_cells(term, t["backward"]), local["right_z"])
        rest = times(contrast_ref[tile, 0], contrast_ref[tile, 1], rest)
        for place, x in enumerate(cells_x):
            here = slice(place * size_y, (place + 1) * size_y)
            for c in range(2):
                there = slice(c * cells_z, (c + 1) * cells_z)
                both_ref[tile, 0, c, x] = wave[here, there]
                both_ref[tile, 1, c, x] = rest[here, there]
                edge_y_ref[tile, c, x] = wave[place * size_y : place * size_y + 2, there]
                if tile == 0 and x < 2:
                    edge_x_ref[c, x] = wave[here, there]
                if tile == 1 and x < 2:
                    layer = wave[here, there]
                    if x == 0:
                        both_ref[0, 1, c, size_x - 2] += layer * (-1.0 / 12.0)
                        both_ref[0, 1, c, size_x - 1] += layer * (16.0 / 12.0)
                    else:
                        both_ref[0, 1, c, size_x - 1] += layer * (-1.0 / 12.0)
    keep_ref[...] = both_ref[core_ref[0]]
    give_ref[...] = both_ref[1 - core_ref[0]]


def place_kernel(core_ref, keep_ref, got_ref, keep_x_ref, keep_y_ref, got_x_ref, got_y_ref,
                 wave_ref, rest_ref, work_ref, sems):
    core = core_ref[0]
    _, _, size_x, size_y, _ = keep_ref.shape
    lower = (core == 1).astype(F32)
    parts = ((keep_ref, keep_x_ref, keep_y_ref, core), (got_ref, got_x_ref, got_y_ref, 1 - core))
    copies = []
    for n, (part, _, _, index) in enumerate(parts):
        copies.append(pltpu.make_async_copy(part.at[0], wave_ref.at[index], sems.at[n]))
        copies[-1].start()
    for n, (part, edge_x, edge_y, index) in enumerate(parts):
        work_ref[n] = part[1]
        for c in range(2):
            near, far = edge_x[c, 0] * lower, edge_x[c, 1] * lower
            work_ref[n, c, size_x - 2] += near * (-1.0 / 12.0)
            work_ref[n, c, size_x - 1] += (16.0 * near - far) * (1.0 / 12.0)
            near, far = edge_y[c, :, 0:1], edge_y[c, :, 1:2]
            work_ref[n, c, :, size_y - 2 : size_y - 1] += near * (-1.0 / 12.0)
            work_ref[n, c, :, size_y - 1 : size_y] += (16.0 * near - far) * (1.0 / 12.0)
        copies.append(pltpu.make_async_copy(work_ref.at[n], rest_ref.at[index], sems.at[2 + n]))
        copies[-1].start()
    for copy in copies:
        copy.wait()


def whole():
    return pl.BlockSpec(memory_space=pltpu.VMEM)


def scalars():
    return pl.BlockSpec(memory_space=pltpu.SMEM)


def anywhere():
    return pl.BlockSpec(memory_space=pl.ANY)


PARAMS = pltpu.CompilerParams(vmem_limit_bytes=40 * 1024 * 1024)


def shaped(*shape):
    return jax.ShapeDtypeStruct(shape, F32)


def body(right_side, slowness, source_cells, source_amplitudes):
    sources, _, size_x, size_y, cells_z = right_side.shape
    grid_rows, grid_cols = lax.axis_size("gx"), lax.axis_size("gy")
    assert sources == 2 and grid_rows % 2 == 0 and size_x % 2 == 0
    chips = grid_rows // 2
    row, col = lax.axis_index("gx"), lax.axis_index("gy")
    core = row % 2
    core_ref = core[None]
    t, cells_x = tables(size_x, size_y, cells_z)
    t = {name: jnp.asarray(value) for name, value in t.items()}
    cells_x = tuple(int(x) for x in cells_x)
    rows = size_x * size_y

    def device(chip, core, column):
        return (2 * chip + core) * grid_cols + column

    def between(pairs):
        return [
            (device(a, r, b), device(c, r, d)) for (a, b), (c, d) in pairs for r in range(2)
        ]

    own = [
        (device(k, r, j), device(k, 1 - r, j))
        for k in range(chips) for j in range(grid_cols) for r in range(2)
    ]
    axes = ("gx", "gy")
    swapped = pl.pallas_call(
        gather_kernel,
        out_shape=shaped(3, size_x, size_y, cells_z),
        in_specs=[scalars(), anywhere(), anywhere()],
        out_specs=anywhere(),
        scratch_shapes=[pltpu.SemaphoreType.DMA((2,))],
        compiler_params=PARAMS,
        name="gather",
    )(core_ref, right_side, slowness)
    swapped = lax.ppermute(swapped, axes, own)

    total_y = size_y * grid_cols
    cells = lax.dynamic_index_in_dim(source_cells, core, 0, keepdims=True)
    near_y = cells // cells_z % total_y - col * size_y
    places = []
    for tile_row in (row, row + 1 - 2 * core):
        near_x = cells // (total_y * cells_z) - tile_row * size_x
        inside = (near_x >= 0) & (near_x < size_x) & (near_y >= 0) & (near_y < size_y)
        folded = jnp.where(near_x < size_x // 2, near_x, size_x + size_x // 2 - 1 - near_x)
        places.append(jnp.where(inside, folded * size_y + near_y, -1))
    amplitudes = lax.dynamic_index_in_dim(source_amplitudes, core, 0, keepdims=False).T[:, None, :]

    modes, contrast = pl.pallas_call(
        functools.partial(prep_kernel, cells_x),
        out_shape=(shaped(2, rows, 2 * cells_z), shaped(2, 2, rows, cells_z)),
        in_specs=[scalars()] + [whole()] * 9,
        out_specs=(whole(), whole()),
        compiler_params=PARAMS,
        name="prep",
    )(core_ref, right_side, slowness, swapped, jnp.stack(places), cells % cells_z, amplitudes,
      *[t[name] for name in PREP])

    beat_tables = [t[name] for name in BEAT]

    def solve(tile, active, trace_x, trace_y):
        return pl.pallas_call(
            functools.partial(beat_kernel, tile),
            out_shape=(shaped(*zero_x.shape), shaped(*zero_y.shape)),
            in_specs=[scalars()] + [whole()] * (4 + len(BEAT)),
            out_specs=(whole(), whole()),
            compiler_params=PARAMS,
            name="upper" if tile == 0 else "lower",
        )(active, modes, contrast, trace_x, trace_y, *beat_tables)

    zero_x = jnp.zeros((2 * size_y, 2 * cells_z), F32)
    zero_y = jnp.zeros((2 * size_x, 2 * cells_z), F32)
    trace_x, trace_y0, trace_y1 = zero_x, zero_y, zero_y
    sums = ([], [], [])
    for beat in range(chips + grid_cols - 2):
        active = (row // 2 + col == beat).astype(jnp.int32)[None]
        here = [(k, beat - k) for k in range(chips) if 0 <= beat - k < grid_cols]
        along_x = between([((k, j), (k + 1, j)) for k, j in here if k + 1 < chips])
        along_y = between([((k, j), (k, j + 1)) for k, j in here if j + 1 < grid_cols])
        inner_x, out_y0 = solve(0, active, trace_x, trace_y0)
        trace_y0 = lax.ppermute(out_y0, axes, along_y)
        out_x, out_y1 = solve(1, active, inner_x, trace_y1)
        out_x, trace_y0 = lax.optimization_barrier((out_x, trace_y0))
        trace_x = lax.ppermute(out_x, axes, along_x)
        trace_y1 = lax.ppermute(out_y1, axes, along_y)
        for held, trace in zip(sums, (trace_x, trace_y0, trace_y1)):
            held.append(trace)

    half = shaped(2, 2, size_x, size_y, cells_z)
    keep, give, edge_x, edge_y = pl.pallas_call(
        functools.partial(last_kernel, cells_x),
        out_shape=(
            half,
            half,
            shaped(2, 2, size_y, cells_z),
            shaped(2, 2, size_x, 2, cells_z),
        ),
        in_specs=[scalars()] + [whole()] * (5 + len(BEAT)),
        out_specs=(whole(),) * 4,
        scratch_shapes=[pltpu.VMEM((2, 2, 2, size_x, size_y, cells_z), F32)],
        compiler_params=PARAMS,
        name="last",
    )(core_ref, modes, contrast, *[sum(held) for held in sums], *beat_tables)

    every = [(k, j) for k in range(chips) for j in range(grid_cols)]
    after_x = lax.ppermute(edge_x, axes, between([((k, j), (k - 1, j)) for k, j in every if k]))
    after_y = lax.ppermute(edge_y, axes, between([((k, j), (k, j - 1)) for k, j in every if j]))
    got = lax.ppermute(give, axes, own)
    keep_y = lax.dynamic_index_in_dim(after_y, core, 0, keepdims=False)
    pass_y = lax.dynamic_index_in_dim(after_y, 1 - core, 0, keepdims=False)
    passed = jnp.concatenate([after_x, pass_y.transpose(0, 2, 1, 3)], axis=2)
    passed = lax.ppermute(passed, axes, own)
    got_x = passed[:, :, :size_y]
    got_y = passed[:, :, size_y:].transpose(0, 2, 1, 3)
    return pl.pallas_call(
        place_kernel,
        out_shape=(shaped(*right_side.shape), shaped(*right_side.shape)),
        in_specs=[scalars()] + [whole()] * 6,
        out_specs=(anywhere(), anywhere()),
        scratch_shapes=[
            pltpu.VMEM((2, 2, size_x, size_y, cells_z), F32),
            pltpu.SemaphoreType.DMA((4,)),
        ],
        compiler_params=PARAMS,
        name="place",
    )(core_ref, keep, got, after_x, keep_y, got_x, got_y)


def solution(mesh):
    return jax.shard_map(
        body,
        mesh=mesh,
        in_specs=(P(None, None, "gx", "gy", None), P("gx", "gy", None), P(), P()),
        out_specs=(P(None, None, "gx", "gy", None), P(None, None, "gx", "gy", None)),
        check_vma=False,
    )
```

```python
import functools
import math

import jax
import jax.numpy as jnp
import ml_dtypes
import numpy as np
from jax import lax
from jax.experimental import pallas as pl
from jax.experimental.pallas import tpu as pltpu
from jax.sharding import PartitionSpec as P

KAPPA = 0.12
DAMPING = 0.3
BF16 = jnp.bfloat16
F32 = jnp.float32


def sine_matrix(length):
    index = np.arange(1, length + 1)
    angles = index * (math.pi / (length + 1))
    return math.sqrt(2.0 / (length + 1)) * np.sin(angles[:, None] * index[None, :]), angles


def halves(matrix):
    high = matrix.astype(np.float32).astype(ml_dtypes.bfloat16)
    low = (matrix - high.astype(np.float64)).astype(np.float32).astype(ml_dtypes.bfloat16)
    return high, low


def left_factor(matrix):
    high, low = halves(matrix)
    return np.concatenate(
        [np.concatenate([high, high], axis=1), np.concatenate([low, low], axis=1)], axis=0
    )


def tables(size_x, size_y, cells_z):
    sine_x, angle_x = sine_matrix(size_x)
    sine_y, angle_y = sine_matrix(size_y)
    sine_z, angle_z = sine_matrix(cells_z)
    half = size_x // 2
    order = np.concatenate([np.arange(0, size_x, 2), np.arange(1, size_x, 2)])
    cells = np.concatenate([np.arange(half), np.arange(size_x - 1, half - 1, -1)])

    def symbol(angle):
        return 2.5 - 8.0 / 3.0 * np.cos(angle) + 1.0 / 6.0 * np.cos(2.0 * angle)

    real_part = (
        symbol(angle_x)[order][:, None, None]
        + symbol(angle_y)[None, :, None]
        + (2.0 - 2.0 * np.cos(angle_z))[None, None, :]
        - KAPPA
    ).reshape(size_x * size_y, cells_z)
    denominator = real_part**2 + (KAPPA * DAMPING) ** 2
    inverse = np.stack([real_part / denominator, KAPPA * DAMPING / denominator]).astype(np.float32)

    parity = [np.kron(sine_x[order[p * half : (p + 1) * half]][:, :half], sine_y) for p in (0, 1)]
    forward = np.stack([left_factor(m) for m in parity])
    backward = np.stack([left_factor(m.T) for m in parity])
    high_z, low_z = halves(sine_z)
    right_z = np.concatenate([np.concatenate([high_z, low_z], axis=1)] * 2, axis=0)

    full = np.kron(sine_x[order], sine_y)
    by_cell = full.reshape(-1, size_x, size_y)
    enter_x = np.stack([-by_cell[:, 0] / 12.0, (16.0 * by_cell[:, 0] - by_cell[:, 1]) / 12.0], 1)
    enter_y = np.stack(
        [-by_cell[:, :, 0] / 12.0, (16.0 * by_cell[:, :, 0] - by_cell[:, :, 1]) / 12.0], 1
    )
    enter = left_factor(
        np.concatenate([enter_x.reshape(len(full), -1), enter_y.reshape(len(full), -1)], axis=1)
    )
    leave = left_factor(
        np.concatenate(
            [
                by_cell[:, size_x - 2 :].reshape(len(full), -1),
                by_cell[:, :, size_y - 2 :].transpose(0, 2, 1).reshape(len(full), -1),
            ],
            axis=1,
        ).T
    )
    first = left_factor(
        np.concatenate(
            [
                by_cell[:, :2].reshape(len(full), -1),
                by_cell[:, :, :2].transpose(0, 2, 1).reshape(len(full), -1),
            ],
            axis=1,
        ).T
    )
    edge = np.zeros((size_x, size_y, 1))
    edge[0] += 1.0 / 12.0
    edge[-1] += 1.0 / 12.0
    edge[:, 0] += 1.0 / 12.0
    edge[:, -1] += 1.0 / 12.0
    edge = edge[cells].reshape(size_x * size_y, 1).astype(np.float32)
    return dict(
        inverse=inverse, forward=forward, backward=backward, right_z=right_z,
        enter=enter, leave=leave, first=first, edge=edge,
    ), cells


def split(values):
    high = values.astype(BF16)
    return high, (values - high.astype(F32)).astype(BF16)


def left_product(matrix, values):
    high, low = split(values)
    both = jnp.dot(matrix, jnp.concatenate([high, low], axis=0), preferred_element_type=F32)
    count = both.shape[0] // 2
    return both[:count] + both[count:]


def z_transform(field, right_z):
    rows = field.shape[0]
    cells_z = field.shape[1] // 2
    high, low = split(jnp.concatenate([field[:, :cells_z], field[:, cells_z:]], axis=0))
    both = jnp.dot(jnp.concatenate([high, low], axis=1), right_z, preferred_element_type=F32)
    total = both[:, :cells_z] + both[:, cells_z:]
    return jnp.concatenate([total[:rows], total[rows:]], axis=1)


def to_modes(field, forward):
    count = field.shape[0] // 2
    first, second = field[:count], field[count:]
    return jnp.concatenate(
        [left_product(forward[0], first + second), left_product(forward[1], first - second)], axis=0
    )


def to_cells(modes, backward):
    count = modes.shape[0] // 2
    even = left_product(backward[0], modes[:count])
    odd = left_product(backward[1], modes[count:])
    return jnp.concatenate([even + odd, even - odd], axis=0)


def times(real_part, imag_part, field):
    lanes = field.shape[1] // 2
    real, imag = field[:, :lanes], field[:, lanes:]
    return jnp.concatenate(
        [real_part * real - imag_part * imag, real_part * imag + imag_part * real], axis=1
    )


def solve_modes(source_modes, contrast, t):
    term = times(t["inverse"][0], t["inverse"][1], source_modes)
    total = term
    for _ in range(2):
        cells = apply_contrast(to_cells(term, t["backward"]), contrast, t["right_z"])
        term = times(t["inverse"][0], t["inverse"][1], to_modes(cells, t["forward"]))
        total = total + term
    return total, term


def apply_contrast(field, contrast, right_z, block=64):
    done = []
    for start in range(0, field.shape[0], block):
        here = slice(start, start + block)
        cells = times(contrast[0, here], contrast[1, here], z_transform(field[here], right_z))
        done.append(z_transform(cells, right_z))
    return jnp.concatenate(done, axis=0)


PREP = ("edge", "forward", "right_z")
BEAT = ("inverse", "forward", "backward", "right_z", "enter", "leave")


def hand_on_kernel(in_ref, out_ref):
    out_ref[...] = in_ref[...]


def prepare(dense, slow, place, depth, amplitude, edge, forward, right_z, modes_ref, contrast_ref):
    rows, cells_z = contrast_ref.shape[1:]
    points = place.shape[1]
    row_ids = lax.broadcasted_iota(jnp.int32, (rows, points), 0)
    lane_ids = lax.broadcasted_iota(jnp.int32, (cells_z, points), 0)
    at_lane = (lane_ids == depth).astype(F32)
    spread = []
    for c in range(2):
        amp = amplitude[c]
        one = amp.astype(BF16).astype(F32)
        two = (amp - one).astype(BF16).astype(F32)
        parts = [at_lane * part for part in (one, two, amp - one - two)]
        spread.append(jnp.concatenate(parts, axis=1).astype(BF16))
    scaled = KAPPA * (slow - 1.0)
    contrast_ref[0] = scaled - edge
    contrast_ref[1] = DAMPING * scaled
    at_row = (row_ids == place).astype(F32).astype(BF16)
    field = lax.dot_general(
        jnp.concatenate([at_row] * 3, axis=1), jnp.concatenate(spread, axis=0),
        (((1,), (1,)), ((), ())), preferred_element_type=F32,
    )
    modes_ref[...] = to_modes(z_transform(field + dense, right_z), forward)


def prep_kernel(cells_x, core_ref, right_ref, slow_ref, place_ref, depth_ref, amp_ref, edge_ref,
                forward_ref, z_ref, modes_ref, contrast_ref):
    dense = [jnp.concatenate([right_ref[core_ref[0], c, x] for x in cells_x], axis=0) for c in range(2)]
    slow = jnp.concatenate([slow_ref[x] for x in cells_x], axis=0)
    prepare(
        jnp.concatenate(dense, axis=1), slow, place_ref[...], depth_ref[...], amp_ref, edge_ref[...],
        forward_ref, z_ref[...], modes_ref, contrast_ref,
    )


def prep_other_kernel(cells_x, core_ref, swap_ref, own_modes_ref, own_contrast_ref, place_ref, depth_ref,
                      amp_ref, edge_ref, forward_ref, z_ref, modes_ref, contrast_ref):
    core = core_ref[0]
    other = 1 - core
    modes_ref[core] = own_modes_ref[...]
    contrast_ref[core] = own_contrast_ref[...]
    parts = [jnp.concatenate([swap_ref[c, x] for x in cells_x], axis=0) for c in range(3)]
    prepare(
        jnp.concatenate(parts[:2], axis=1), parts[2], place_ref[...], depth_ref[...], amp_ref,
        edge_ref[...], forward_ref, z_ref[...], modes_ref.at[other], contrast_ref.at[other],
    )


def source_modes(modes, trace_x, trace_y, enter):
    return modes + left_product(enter, jnp.concatenate([trace_x, trace_y], axis=0))


def beat_kernel(tile, active_ref, modes_ref, contrast_ref, trace_x_ref, trace_y_ref, *refs):
    t = {name: ref for name, ref in zip(BEAT, refs)}
    out_x_ref, out_y_ref = refs[len(BEAT) :]

    @pl.when(active_ref[0] == 1)
    def _():
        local = dict(t, right_z=t["right_z"][...])
        source = source_modes(modes_ref[tile], trace_x_ref[...], trace_y_ref[...], t["enter"][...])
        total, _ = solve_modes(source, contrast_ref.at[tile], local)
        out = left_product(t["leave"][...], total)
        count = out_x_ref.shape[0]
        out_x_ref[...] = out[:count]
        out_y_ref[...] = out[count:]


LAST = BEAT + ("first",)
FINISH = ("backward", "right_z")


def last_kernel(tile, modes_ref, contrast_ref, trace_x_ref, trace_y_ref, *refs):
    t = {name: ref for name, ref in zip(LAST, refs)}
    total_ref, term_ref, edge_x_ref, edge_y_ref, out_x_ref = refs[len(LAST) :]
    local = dict(t, right_z=t["right_z"][...])
    count = trace_x_ref.shape[0]
    source = source_modes(modes_ref[tile], trace_x_ref[...], trace_y_ref[...], t["enter"][...])
    total, term = solve_modes(source, contrast_ref.at[tile], local)
    total_ref[...] = total
    term_ref[...] = term
    edges = z_transform(left_product(t["first"][...], total), local["right_z"])
    edge_x_ref[...] = edges[:count]
    edge_y_ref[...] = edges[count:]
    if tile == 0:
        out_x_ref[...] = left_product(t["leave"][...], total)[:count]


def finish_kernel(cells_x, core_ref, total0_ref, term0_ref, total1_ref, term1_ref, contrast_ref, backward_ref,
                  z_ref, keep_ref, give_ref, both_ref):
    _, _, _, size_x, size_y, cells_z = both_ref.shape
    right_z = z_ref[...]
    for tile, (total_ref, term_ref) in enumerate(((total0_ref, term0_ref), (total1_ref, term1_ref))):
        wave = z_transform(to_cells(total_ref[...], backward_ref), right_z)
        rest = z_transform(to_cells(term_ref[...], backward_ref), right_z)
        rest = times(contrast_ref[tile, 0], contrast_ref[tile, 1], rest)
        for place, x in enumerate(cells_x):
            here = slice(place * size_y, (place + 1) * size_y)
            for c in range(2):
                there = slice(c * cells_z, (c + 1) * cells_z)
                both_ref[tile, 0, c, x] = wave[here, there]
                both_ref[tile, 1, c, x] = rest[here, there]
                if tile == 1 and x < 2:
                    layer = wave[here, there]
                    if x == 0:
                        both_ref[0, 1, c, size_x - 2] += layer * (-1.0 / 12.0)
                        both_ref[0, 1, c, size_x - 1] += layer * (16.0 / 12.0)
                    else:
                        both_ref[0, 1, c, size_x - 1] += layer * (-1.0 / 12.0)
    keep_ref[...] = both_ref[core_ref[0]]
    give_ref[...] = both_ref[1 - core_ref[0]]


def add_later(rest_ref, edge_x, edge_y, lower):
    _, size_x, size_y, cells_z = rest_ref.shape
    for c in range(2):
        there = slice(c * cells_z, (c + 1) * cells_z)
        near, far = edge_x[:size_y, there] * lower, edge_x[size_y:, there] * lower
        rest_ref[c, size_x - 2] += near * (-1.0 / 12.0)
        rest_ref[c, size_x - 1] += (16.0 * near - far) * (1.0 / 12.0)
        near, far = edge_y[:size_x, there], edge_y[size_x:, there]
        two = jnp.stack([near * (-1.0 / 12.0), (16.0 * near - far) * (1.0 / 12.0)], axis=1)
        rest_ref[c, :, size_y - 2 :] += two


def keep_kernel(core_ref, keep_ref, edge_x_ref, edge_y_ref, rest_ref):
    rest_ref[...] = keep_ref[1]
    add_later(rest_ref, edge_x_ref[...], edge_y_ref[...], (core_ref[0] == 1).astype(F32))


def place_kernel(core_ref, keep_ref, keep_rest_ref, got_ref, got_edge_ref, wave_ref, rest_ref, work_ref, sems):
    core = core_ref[0]
    count = got_edge_ref.shape[0] // 2
    copies = [
        pltpu.make_async_copy(keep_ref.at[0], wave_ref.at[core], sems.at[0]),
        pltpu.make_async_copy(got_ref.at[0], wave_ref.at[1 - core], sems.at[1]),
        pltpu.make_async_copy(keep_rest_ref, rest_ref.at[core], sems.at[2]),
    ]
    for copy in copies:
        copy.start()
    work_ref[...] = got_ref[1]
    add_later(work_ref, got_edge_ref[:count], got_edge_ref[count:], (core == 1).astype(F32))
    copies.append(pltpu.make_async_copy(work_ref, rest_ref.at[1 - core], sems.at[3]))
    copies[-1].start()
    for copy in copies:
        copy.wait()


def whole():
    return pl.BlockSpec(memory_space=pltpu.VMEM)


def scalars():
    return pl.BlockSpec(memory_space=pltpu.SMEM)


def anywhere():
    return pl.BlockSpec(memory_space=pl.ANY)


SOLVE_COST = pl.CostEstimate(flops=2 * 10**9, bytes_accessed=2 * 10**6, transcendentals=0)
KEEP_COST = pl.CostEstimate(flops=10**10, bytes_accessed=10**6, transcendentals=0)
PARAMS = pltpu.CompilerParams(vmem_limit_bytes=40 * 1024 * 1024)


def shaped(*shape):
    return jax.ShapeDtypeStruct(shape, F32)


def body(right_side, slowness, source_cells, source_amplitudes):
    sources, _, size_x, size_y, cells_z = right_side.shape
    grid_rows, grid_cols = lax.axis_size("gx"), lax.axis_size("gy")
    assert sources == 2 and grid_rows % 2 == 0 and size_x % 2 == 0
    chips = grid_rows // 2
    row, col = lax.axis_index("gx"), lax.axis_index("gy")
    core = row % 2
    core_ref = core[None]
    t, cells_x = tables(size_x, size_y, cells_z)
    t = {name: jnp.asarray(value) for name, value in t.items()}
    cells_x = tuple(int(x) for x in cells_x)
    rows = size_x * size_y

    def device(chip, core, column):
        return (2 * chip + core) * grid_cols + column

    def between(pairs):
        return [
            (device(a, r, b), device(c, r, d)) for (a, b), (c, d) in pairs for r in range(2)
        ]

    own = [
        (device(k, r, j), device(k, 1 - r, j))
        for k in range(chips) for j in range(grid_cols) for r in range(2)
    ]
    axes = ("gx", "gy")
    other = lax.dynamic_index_in_dim(right_side, 1 - core, 0, keepdims=False)
    swapped = lax.ppermute(jnp.concatenate([other, slowness[None]], axis=0), axes, own)

    total_y = size_y * grid_cols
    cells = lax.dynamic_index_in_dim(source_cells, core, 0, keepdims=True)
    near_y = cells // cells_z % total_y - col * size_y
    places = []
    for tile_row in (row, row + 1 - 2 * core):
        near_x = cells // (total_y * cells_z) - tile_row * size_x
        inside = (near_x >= 0) & (near_x < size_x) & (near_y >= 0) & (near_y < size_y)
        folded = jnp.where(near_x < size_x // 2, near_x, size_x + size_x // 2 - 1 - near_x)
        places.append(jnp.where(inside, folded * size_y + near_y, -1))
    amplitudes = lax.dynamic_index_in_dim(source_amplitudes, core, 0, keepdims=False).T[:, None, :]

    depth = cells % cells_z
    prep_tables = [t[name] for name in PREP]
    one = (shaped(rows, 2 * cells_z), shaped(2, rows, cells_z))
    own_modes, own_contrast = pl.pallas_call(
        functools.partial(prep_kernel, cells_x),
        out_shape=one,
        in_specs=[scalars()] + [whole()] * 8,
        out_specs=(whole(), whole()),
        compiler_params=PARAMS,
        name="prep",
    )(core_ref, right_side, slowness, places[0], depth, amplitudes, *prep_tables)
    modes, contrast = pl.pallas_call(
        functools.partial(prep_other_kernel, cells_x),
        out_shape=(shaped(2, rows, 2 * cells_z), shaped(2, 2, rows, cells_z)),
        in_specs=[scalars()] + [whole()] * 9,
        out_specs=(whole(), whole()),
        compiler_params=PARAMS,
        name="prep_other",
    )(core_ref, swapped, own_modes, own_contrast, places[1], depth, amplitudes, *prep_tables)

    beat_tables = [t[name] for name in BEAT]

    def solve(tile, active, trace_x, trace_y):
        return pl.pallas_call(
            functools.partial(beat_kernel, tile),
            out_shape=(shaped(*zero_x.shape), shaped(*zero_y.shape)),
            in_specs=[scalars()] + [whole()] * (4 + len(BEAT)),
            out_specs=(whole(), whole()),
            compiler_params=PARAMS,
            cost_estimate=SOLVE_COST,
            name="upper" if tile == 0 else "lower",
        )(active, modes, contrast, trace_x, trace_y, *beat_tables)

    def hand_on(trace):
        return pl.pallas_call(
            hand_on_kernel,
            out_shape=shaped(*trace.shape),
            in_specs=[whole()],
            out_specs=whole(),
            compiler_params=PARAMS,
            name="hand_on",
        )(trace)

    zero_x = jnp.zeros((2 * size_y, 2 * cells_z), F32)
    zero_y = jnp.zeros((2 * size_x, 2 * cells_z), F32)
    trace_x, trace_y0, trace_y1 = zero_x, zero_y, zero_y
    sums = ([], [], [])
    for beat in range(chips + grid_cols - 2):
        active = (row // 2 + col == beat).astype(jnp.int32)[None]
        here = [(k, beat - k) for k in range(chips) if 0 <= beat - k < grid_cols]
        along_x = between([((k, j), (k + 1, j)) for k, j in here if k + 1 < chips])
        along_y = between([((k, j), (k, j + 1)) for k, j in here if j + 1 < grid_cols])
        inner_x, out_y0 = solve(0, active, trace_x, trace_y0)
        trace_y0 = hand_on(lax.ppermute(out_y0, axes, along_y))
        out_x, out_y1 = solve(1, active, inner_x, trace_y1)
        trace_x = lax.ppermute(out_x, axes, along_x)
        trace_y1 = lax.ppermute(out_y1, axes, along_y)
        for held, trace in zip(sums, (trace_x, trace_y0, trace_y1)):
            held.append(trace)

    def solve_last(tile, trace_x, trace_y):
        return pl.pallas_call(
            functools.partial(last_kernel, tile),
            out_shape=(
                shaped(rows, 2 * cells_z),
                shaped(rows, 2 * cells_z),
                shaped(*zero_x.shape),
                shaped(*zero_y.shape),
                shaped(*zero_x.shape),
            ),
            in_specs=[whole()] * (4 + len(LAST)),
            out_specs=(whole(),) * 5,
            compiler_params=PARAMS,
            cost_estimate=SOLVE_COST,
            name="last_upper" if tile == 0 else "last_lower",
        )(modes, contrast, trace_x, trace_y, *[t[name] for name in LAST])

    all_x, all_y0, all_y1 = [sum(held) for held in sums]
    total0, term0, edge_x, edge_y0, inner_x = solve_last(0, all_x, all_y0)
    total1, term1, _, edge_y1, _ = solve_last(1, inner_x, all_y1)

    every = [(k, j) for k in range(chips) for j in range(grid_cols)]
    after_x = lax.ppermute(edge_x, axes, between([((k, j), (k - 1, j)) for k, j in every if k]))
    after_y = lax.ppermute(
        jnp.stack([edge_y0, edge_y1]), axes, between([((k, j), (k, j - 1)) for k, j in every if j])
    )

    half = shaped(2, 2, size_x, size_y, cells_z)
    keep, give = pl.pallas_call(
        functools.partial(finish_kernel, cells_x),
        out_shape=(half, half),
        in_specs=[scalars()] + [whole()] * (5 + len(FINISH)),
        out_specs=(whole(), whole()),
        scratch_shapes=[pltpu.VMEM((2, 2, 2, size_x, size_y, cells_z), F32)],
        compiler_params=PARAMS,
        name="finish",
    )(core_ref, total0, term0, total1, term1, contrast, *[t[name] for name in FINISH])
    got = lax.ppermute(give, axes, own)

    keep_y = lax.dynamic_index_in_dim(after_y, core, 0, keepdims=False)
    pass_y = lax.dynamic_index_in_dim(after_y, 1 - core, 0, keepdims=False)
    got_edge = lax.ppermute(jnp.concatenate([after_x, pass_y], axis=0), axes, own)
    keep_rest = pl.pallas_call(
        keep_kernel,
        out_shape=shaped(*half.shape[1:]),
        in_specs=[scalars()] + [whole()] * 3,
        out_specs=whole(),
        compiler_params=PARAMS,
        cost_estimate=KEEP_COST,
        name="keep",
    )(core_ref, keep, after_x, keep_y)
    return pl.pallas_call(
        place_kernel,
        out_shape=(shaped(*right_side.shape), shaped(*right_side.shape)),
        in_specs=[scalars()] + [whole()] * 4,
        out_specs=(anywhere(), anywhere()),
        scratch_shapes=[
            pltpu.VMEM((2, size_x, size_y, cells_z), F32),
            pltpu.SemaphoreType.DMA((4,)),
        ],
        compiler_params=PARAMS,
        name="place",
    )(core_ref, keep, keep_rest, got, got_edge)


def solution(mesh):
    return jax.shard_map(
        body,
        mesh=mesh,
        in_specs=(P(None, None, "gx", "gy", None), P("gx", "gy", None), P(), P()),
        out_specs=(P(None, None, "gx", "gy", None), P(None, None, "gx", "gy", None)),
        check_vma=False,
    )
```

```python
import functools
import math

import jax
import jax.numpy as jnp
import ml_dtypes
import numpy as np
from jax import lax
from jax.experimental import pallas as pl
from jax.experimental.pallas import tpu as pltpu
from jax.sharding import PartitionSpec as P

KAPPA = 0.12
DAMPING = 0.3
BF16 = jnp.bfloat16
F32 = jnp.float32


def sine_matrix(length):
    index = np.arange(1, length + 1)
    angles = index * (math.pi / (length + 1))
    return math.sqrt(2.0 / (length + 1)) * np.sin(angles[:, None] * index[None, :]), angles


def halves(matrix):
    high = matrix.astype(np.float32).astype(ml_dtypes.bfloat16)
    low = (matrix - high.astype(np.float64)).astype(np.float32).astype(ml_dtypes.bfloat16)
    return high, low


def left_factor(matrix):
    high, low = halves(matrix)
    return np.concatenate(
        [np.concatenate([high, high], axis=1), np.concatenate([low, low], axis=1)], axis=0
    )


def tables(size_x, size_y, cells_z):
    sine_x, angle_x = sine_matrix(size_x)
    sine_y, angle_y = sine_matrix(size_y)
    sine_z, angle_z = sine_matrix(cells_z)
    half = size_x // 2
    order = np.concatenate([np.arange(0, size_x, 2), np.arange(1, size_x, 2)])
    cells = np.concatenate([np.arange(half), np.arange(size_x - 1, half - 1, -1)])

    def symbol(angle):
        return 2.5 - 8.0 / 3.0 * np.cos(angle) + 1.0 / 6.0 * np.cos(2.0 * angle)

    real_part = (
        symbol(angle_x)[order][:, None, None]
        + symbol(angle_y)[None, :, None]
        + (2.0 - 2.0 * np.cos(angle_z))[None, None, :]
        - KAPPA
    ).reshape(size_x * size_y, cells_z)
    denominator = real_part**2 + (KAPPA * DAMPING) ** 2
    inverse = np.stack([real_part / denominator, KAPPA * DAMPING / denominator]).astype(np.float32)

    parity = [np.kron(sine_x[order[p * half : (p + 1) * half]][:, :half], sine_y) for p in (0, 1)]
    forward = np.stack([left_factor(m) for m in parity])
    backward = np.stack([left_factor(m.T) for m in parity])
    high_z, low_z = halves(sine_z)
    right_z = np.concatenate([np.concatenate([high_z, low_z], axis=1)] * 2, axis=0)

    full = np.kron(sine_x[order], sine_y)
    by_cell = full.reshape(-1, size_x, size_y)
    enter_x = np.stack([-by_cell[:, 0] / 12.0, (16.0 * by_cell[:, 0] - by_cell[:, 1]) / 12.0], 1)
    enter_y = np.stack(
        [-by_cell[:, :, 0] / 12.0, (16.0 * by_cell[:, :, 0] - by_cell[:, :, 1]) / 12.0], 1
    )
    enter = left_factor(
        np.concatenate([enter_x.reshape(len(full), -1), enter_y.reshape(len(full), -1)], axis=1)
    )
    leave = left_factor(
        np.concatenate(
            [
                by_cell[:, size_x - 2 :].reshape(len(full), -1),
                by_cell[:, :, size_y - 2 :].transpose(0, 2, 1).reshape(len(full), -1),
            ],
            axis=1,
        ).T
    )
    first = left_factor(
        np.concatenate(
            [
                by_cell[:, :2].reshape(len(full), -1),
                by_cell[:, :, :2].transpose(0, 2, 1).reshape(len(full), -1),
            ],
            axis=1,
        ).T
    )
    edge = np.zeros((size_x, size_y, 1))
    edge[0] += 1.0 / 12.0
    edge[-1] += 1.0 / 12.0
    edge[:, 0] += 1.0 / 12.0
    edge[:, -1] += 1.0 / 12.0
    edge = edge[cells].reshape(size_x * size_y, 1).astype(np.float32)
    return dict(
        inverse=inverse, forward=forward, backward=backward, right_z=right_z,
        enter=enter, leave=leave, first=first, edge=edge,
    ), cells


def split(values):
    high = values.astype(BF16)
    return high, (values - high.astype(F32)).astype(BF16)


def left_product(matrix, values):
    high, low = split(values)
    both = jnp.dot(matrix, jnp.concatenate([high, low], axis=0), preferred_element_type=F32)
    count = both.shape[0] // 2
    return both[:count] + both[count:]


def z_transform(field, right_z):
    rows = field.shape[0]
    cells_z = field.shape[1] // 2
    high, low = split(jnp.concatenate([field[:, :cells_z], field[:, cells_z:]], axis=0))
    both = jnp.dot(jnp.concatenate([high, low], axis=1), right_z, preferred_element_type=F32)
    total = both[:, :cells_z] + both[:, cells_z:]
    return jnp.concatenate([total[:rows], total[rows:]], axis=1)


def to_modes(field, forward):
    count = field.shape[0] // 2
    first, second = field[:count], field[count:]
    return jnp.concatenate(
        [left_product(forward[0], first + second), left_product(forward[1], first - second)], axis=0
    )


def to_cells(modes, backward):
    count = modes.shape[0] // 2
    even = left_product(backward[0], modes[:count])
    odd = left_product(backward[1], modes[count:])
    return jnp.concatenate([even + odd, even - odd], axis=0)


def times(real_part, imag_part, field):
    lanes = field.shape[1] // 2
    real, imag = field[:, :lanes], field[:, lanes:]
    return jnp.concatenate(
        [real_part * real - imag_part * imag, real_part * imag + imag_part * real], axis=1
    )


def solve_modes(source_modes, contrast, t):
    term = times(t["inverse"][0], t["inverse"][1], source_modes)
    total = term
    for _ in range(2):
        cells = apply_contrast(to_cells(term, t["backward"]), contrast, t["right_z"])
        term = times(t["inverse"][0], t["inverse"][1], to_modes(cells, t["forward"]))
        total = total + term
    return total, term


def apply_contrast(field, contrast, right_z, block=64):
    done = []
    for start in range(0, field.shape[0], block):
        here = slice(start, start + block)
        cells = times(contrast[0, here], contrast[1, here], z_transform(field[here], right_z))
        done.append(z_transform(cells, right_z))
    return jnp.concatenate(done, axis=0)


PREP = ("edge", "forward", "right_z")
BEAT = ("inverse", "forward", "backward", "right_z", "enter", "leave")


def hand_on_kernel(in_ref, out_ref):
    out_ref[...] = in_ref[...]


def prepare(dense, slow, place, depth, amplitude, edge, forward, right_z, modes_ref, contrast_ref):
    rows, cells_z = contrast_ref.shape[1:]
    points = place.shape[1]
    row_ids = lax.broadcasted_iota(jnp.int32, (rows, points), 0)
    lane_ids = lax.broadcasted_iota(jnp.int32, (cells_z, points), 0)
    at_lane = (lane_ids == depth).astype(F32)
    spread = []
    for c in range(2):
        amp = amplitude[c]
        one = amp.astype(BF16).astype(F32)
        two = (amp - one).astype(BF16).astype(F32)
        parts = [at_lane * part for part in (one, two, amp - one - two)]
        spread.append(jnp.concatenate(parts, axis=1).astype(BF16))
    scaled = KAPPA * (slow - 1.0)
    contrast_ref[0] = scaled - edge
    contrast_ref[1] = DAMPING * scaled
    at_row = (row_ids == place).astype(F32).astype(BF16)
    field = lax.dot_general(
        jnp.concatenate([at_row] * 3, axis=1), jnp.concatenate(spread, axis=0),
        (((1,), (1,)), ((), ())), preferred_element_type=F32,
    )
    modes_ref[...] = to_modes(z_transform(field + dense, right_z), forward)


def prep_kernel(cells_x, core_ref, right_ref, slow_ref, place_ref, depth_ref, amp_ref, edge_ref,
                forward_ref, z_ref, modes_ref, contrast_ref):
    dense = [jnp.concatenate([right_ref[core_ref[0], c, x] for x in cells_x], axis=0) for c in range(2)]
    slow = jnp.concatenate([slow_ref[x] for x in cells_x], axis=0)
    prepare(
        jnp.concatenate(dense, axis=1), slow, place_ref[...], depth_ref[...], amp_ref, edge_ref[...],
        forward_ref, z_ref[...], modes_ref, contrast_ref,
    )


def prep_other_kernel(cells_x, core_ref, swap_ref, slow_ref, own_modes_ref, own_contrast_ref, place_ref, depth_ref,
                      amp_ref, edge_ref, forward_ref, z_ref, modes_ref, contrast_ref):
    core = core_ref[0]
    other = 1 - core
    modes_ref[core] = own_modes_ref[...]
    contrast_ref[core] = own_contrast_ref[...]
    dense = [jnp.concatenate([swap_ref[core, c, x] for x in cells_x], axis=0) for c in range(2)]
    slow = jnp.concatenate([slow_ref[x] for x in cells_x], axis=0)
    prepare(
        jnp.concatenate(dense, axis=1), slow, place_ref[...], depth_ref[...], amp_ref,
        edge_ref[...], forward_ref, z_ref[...], modes_ref.at[other], contrast_ref.at[other],
    )


def source_modes(modes, trace_x, trace_y, enter):
    return modes + left_product(enter, jnp.concatenate([trace_x, trace_y], axis=0))


def beat_kernel(tile, active_ref, modes_ref, contrast_ref, trace_x_ref, trace_y_ref, total_ref, term_ref, *refs):
    t = {name: ref for name, ref in zip(BEAT, refs)}
    out_x_ref, out_y_ref, new_total_ref, new_term_ref = refs[len(BEAT) :]

    @pl.when(active_ref[0] == 1)
    def _():
        local = dict(t, right_z=t["right_z"][...])
        source = source_modes(modes_ref[tile], trace_x_ref[...], trace_y_ref[...], t["enter"][...])
        total, term = solve_modes(source, contrast_ref.at[tile], local)
        new_total_ref[...] = total
        new_term_ref[...] = term
        out = left_product(t["leave"][...], total)
        count = out_x_ref.shape[0]
        out_x_ref[...] = out[:count]
        out_y_ref[...] = out[count:]

    @pl.when(active_ref[0] == 0)
    def _():
        new_total_ref[...] = total_ref[...]
        new_term_ref[...] = term_ref[...]


def edge_kernel(total0_ref, total1_ref, first_ref, z_ref, edge_x_ref, edge_y_ref):
    count = edge_x_ref.shape[0]
    right_z = z_ref[...]
    for tile, total_ref in enumerate((total0_ref, total1_ref)):
        edges = z_transform(left_product(first_ref[...], total_ref[...]), right_z)
        edge_y_ref[tile] = edges[count:]
        if tile == 0:
            edge_x_ref[...] = edges[:count]


FINISH = ("backward", "right_z")


def finish_kernel(cells_x, core_ref, total0_ref, term0_ref, total1_ref, term1_ref, contrast_ref, backward_ref,
                  z_ref, keep_ref, give_ref, both_ref):
    _, _, _, size_x, size_y, cells_z = both_ref.shape
    right_z = z_ref[...]
    for tile, (total_ref, term_ref) in enumerate(((total0_ref, term0_ref), (total1_ref, term1_ref))):
        wave = z_transform(to_cells(total_ref[...], backward_ref), right_z)
        rest = z_transform(to_cells(term_ref[...], backward_ref), right_z)
        rest = times(contrast_ref[tile, 0], contrast_ref[tile, 1], rest)
        for place, x in enumerate(cells_x):
            here = slice(place * size_y, (place + 1) * size_y)
            for c in range(2):
                there = slice(c * cells_z, (c + 1) * cells_z)
                both_ref[tile, 0, c, x] = wave[here, there]
                both_ref[tile, 1, c, x] = rest[here, there]
                if tile == 1 and x < 2:
                    layer = wave[here, there]
                    if x == 0:
                        both_ref[0, 1, c, size_x - 2] += layer * (-1.0 / 12.0)
                        both_ref[0, 1, c, size_x - 1] += layer * (16.0 / 12.0)
                    else:
                        both_ref[0, 1, c, size_x - 1] += layer * (-1.0 / 12.0)
    keep_ref[...] = both_ref[core_ref[0]]
    give_ref[...] = both_ref[1 - core_ref[0]]


def add_later(rest_ref, edge_x, edge_y, lower):
    _, size_x, size_y, cells_z = rest_ref.shape
    for c in range(2):
        there = slice(c * cells_z, (c + 1) * cells_z)
        near, far = edge_x[:size_y, there] * lower, edge_x[size_y:, there] * lower
        rest_ref[c, size_x - 2] += near * (-1.0 / 12.0)
        rest_ref[c, size_x - 1] += (16.0 * near - far) * (1.0 / 12.0)
        near, far = edge_y[:size_x, there], edge_y[size_x:, there]
        two = jnp.stack([near * (-1.0 / 12.0), (16.0 * near - far) * (1.0 / 12.0)], axis=1)
        rest_ref[c, :, size_y - 2 :] += two


def keep_kernel(core_ref, keep_ref, edge_x_ref, edge_y_ref, rest_ref):
    rest_ref[...] = keep_ref[1]
    add_later(rest_ref, edge_x_ref[...], edge_y_ref[...], (core_ref[0] == 1).astype(F32))


def place_kernel(core_ref, keep_ref, keep_rest_ref, got_ref, got_edge_ref, wave_ref, rest_ref, work_ref, sems):
    core = core_ref[0]
    count = got_edge_ref.shape[0] // 2
    copies = [
        pltpu.make_async_copy(keep_ref.at[0], wave_ref.at[core], sems.at[0]),
        pltpu.make_async_copy(got_ref.at[0], wave_ref.at[1 - core], sems.at[1]),
        pltpu.make_async_copy(keep_rest_ref, rest_ref.at[core], sems.at[2]),
    ]
    for copy in copies:
        copy.start()
    work_ref[...] = got_ref[1]
    add_later(work_ref, got_edge_ref[:count], got_edge_ref[count:], (core == 1).astype(F32))
    copies.append(pltpu.make_async_copy(work_ref, rest_ref.at[1 - core], sems.at[3]))
    copies[-1].start()
    for copy in copies:
        copy.wait()


def whole():
    return pl.BlockSpec(memory_space=pltpu.VMEM)


def scalars():
    return pl.BlockSpec(memory_space=pltpu.SMEM)


def anywhere():
    return pl.BlockSpec(memory_space=pl.ANY)


SOLVE_COST = pl.CostEstimate(flops=2 * 10**9, bytes_accessed=2 * 10**6, transcendentals=0)
KEEP_COST = pl.CostEstimate(flops=10**10, bytes_accessed=10**6, transcendentals=0)
PARAMS = pltpu.CompilerParams(vmem_limit_bytes=40 * 1024 * 1024)


def shaped(*shape):
    return jax.ShapeDtypeStruct(shape, F32)


def body(right_side, slowness, source_cells, source_amplitudes):
    sources, _, size_x, size_y, cells_z = right_side.shape
    grid_rows, grid_cols = lax.axis_size("gx"), lax.axis_size("gy")
    assert sources == 2 and grid_rows % 2 == 0 and size_x % 2 == 0
    chips = grid_rows // 2
    row, col = lax.axis_index("gx"), lax.axis_index("gy")
    core = row % 2
    core_ref = core[None]
    t, cells_x = tables(size_x, size_y, cells_z)
    t = {name: jnp.asarray(value) for name, value in t.items()}
    cells_x = tuple(int(x) for x in cells_x)
    rows = size_x * size_y

    def device(chip, core, column):
        return (2 * chip + core) * grid_cols + column

    def between(pairs):
        return [
            (device(a, r, b), device(c, r, d)) for (a, b), (c, d) in pairs for r in range(2)
        ]

    own = [
        (device(k, r, j), device(k, 1 - r, j))
        for k in range(chips) for j in range(grid_cols) for r in range(2)
    ]
    axes = ("gx", "gy")
    swapped = lax.ppermute(right_side, axes, own)
    swapped_slow = lax.ppermute(slowness, axes, own)

    total_y = size_y * grid_cols
    cells = lax.dynamic_index_in_dim(source_cells, core, 0, keepdims=True)
    near_y = cells // cells_z % total_y - col * size_y
    places = []
    for tile_row in (row, row + 1 - 2 * core):
        near_x = cells // (total_y * cells_z) - tile_row * size_x
        inside = (near_x >= 0) & (near_x < size_x) & (near_y >= 0) & (near_y < size_y)
        folded = jnp.where(near_x < size_x // 2, near_x, size_x + size_x // 2 - 1 - near_x)
        places.append(jnp.where(inside, folded * size_y + near_y, -1))
    amplitudes = lax.dynamic_index_in_dim(source_amplitudes, core, 0, keepdims=False).T[:, None, :]

    depth = cells % cells_z
    prep_tables = [t[name] for name in PREP]
    one = (shaped(rows, 2 * cells_z), shaped(2, rows, cells_z))
    own_modes, own_contrast = pl.pallas_call(
        functools.partial(prep_kernel, cells_x),
        out_shape=one,
        in_specs=[scalars()] + [whole()] * 8,
        out_specs=(whole(), whole()),
        compiler_params=PARAMS,
        name="prep",
    )(core_ref, right_side, slowness, places[0], depth, amplitudes, *prep_tables)
    modes, contrast = pl.pallas_call(
        functools.partial(prep_other_kernel, cells_x),
        out_shape=(shaped(2, rows, 2 * cells_z), shaped(2, 2, rows, cells_z)),
        in_specs=[scalars()] + [whole()] * 10,
        out_specs=(whole(), whole()),
        compiler_params=PARAMS,
        name="prep_other",
    )(core_ref, swapped, swapped_slow, own_modes, own_contrast, places[1], depth, amplitudes, *prep_tables)

    beat_tables = [t[name] for name in BEAT]

    def solve(tile, active, trace_x, trace_y, state):
        out_x, out_y, *state = pl.pallas_call(
            functools.partial(beat_kernel, tile),
            out_shape=(shaped(*zero_x.shape), shaped(*zero_y.shape)) + (shaped(rows, 2 * cells_z),) * 2,
            in_specs=[scalars()] + [whole()] * (6 + len(BEAT)),
            out_specs=(whole(),) * 4,
            input_output_aliases={5: 2, 6: 3},
            compiler_params=PARAMS,
            cost_estimate=SOLVE_COST,
            name="upper" if tile == 0 else "lower",
        )(active, modes, contrast, trace_x, trace_y, *state, *beat_tables)
        return out_x, out_y, state

    def hand_on(trace):
        return pl.pallas_call(
            hand_on_kernel,
            out_shape=shaped(*trace.shape),
            in_specs=[whole()],
            out_specs=whole(),
            compiler_params=PARAMS,
            name="hand_on",
        )(trace)

    zero_x = jnp.zeros((2 * size_y, 2 * cells_z), F32)
    zero_y = jnp.zeros((2 * size_x, 2 * cells_z), F32)
    trace_x, trace_y0, trace_y1 = zero_x, zero_y, zero_y
    states = [[jnp.zeros((rows, 2 * cells_z), F32)] * 2 for _ in range(2)]
    for beat in range(chips + grid_cols - 1):
        active = (row // 2 + col == beat).astype(jnp.int32)[None]
        here = [(k, beat - k) for k in range(chips) if 0 <= beat - k < grid_cols]
        along_x = between([((k, j), (k + 1, j)) for k, j in here if k + 1 < chips])
        along_y = between([((k, j), (k, j + 1)) for k, j in here if j + 1 < grid_cols])
        inner_x, out_y0, states[0] = solve(0, active, trace_x, trace_y0, states[0])
        if along_y:
            trace_y0 = hand_on(lax.ppermute(out_y0, axes, along_y))
        out_x, out_y1, states[1] = solve(1, active, inner_x, trace_y1, states[1])
        if along_x:
            trace_x = lax.ppermute(out_x, axes, along_x)
        if along_y:
            trace_y1 = lax.ppermute(out_y1, axes, along_y)

    edge_x, edge_y = pl.pallas_call(
        edge_kernel,
        out_shape=(shaped(*zero_x.shape), shaped(2, *zero_y.shape)),
        in_specs=[whole()] * 4,
        out_specs=(whole(), whole()),
        compiler_params=PARAMS,
        name="edges",
    )(states[0][0], states[1][0], t["first"], t["right_z"])

    every = [(k, j) for k in range(chips) for j in range(grid_cols)]
    after_x = lax.ppermute(edge_x, axes, between([((k, j), (k - 1, j)) for k, j in every if k]))
    after_y = lax.ppermute(edge_y, axes, between([((k, j), (k, j - 1)) for k, j in every if j]))

    half = shaped(2, 2, size_x, size_y, cells_z)
    keep, give = pl.pallas_call(
        functools.partial(finish_kernel, cells_x),
        out_shape=(half, half),
        in_specs=[scalars()] + [whole()] * (5 + len(FINISH)),
        out_specs=(whole(), whole()),
        scratch_shapes=[pltpu.VMEM((2, 2, 2, size_x, size_y, cells_z), F32)],
        compiler_params=PARAMS,
        name="finish",
    )(core_ref, *states[0], *states[1], contrast, *[t[name] for name in FINISH])
    got = lax.ppermute(give, axes, own)

    keep_y = lax.dynamic_index_in_dim(after_y, core, 0, keepdims=False)
    pass_y = lax.dynamic_index_in_dim(after_y, 1 - core, 0, keepdims=False)
    got_edge = lax.ppermute(jnp.concatenate([after_x, pass_y], axis=0), axes, own)
    keep_rest = pl.pallas_call(
        keep_kernel,
        out_shape=shaped(*half.shape[1:]),
        in_specs=[scalars()] + [whole()] * 3,
        out_specs=whole(),
        compiler_params=PARAMS,
        cost_estimate=KEEP_COST,
        name="keep",
    )(core_ref, keep, after_x, keep_y)
    return pl.pallas_call(
        place_kernel,
        out_shape=(shaped(*right_side.shape), shaped(*right_side.shape)),
        in_specs=[scalars()] + [whole()] * 4,
        out_specs=(anywhere(), anywhere()),
        scratch_shapes=[
            pltpu.VMEM((2, size_x, size_y, cells_z), F32),
            pltpu.SemaphoreType.DMA((4,)),
        ],
        compiler_params=PARAMS,
        name="place",
    )(core_ref, keep, keep_rest, got, got_edge)


def solution(mesh):
    return jax.shard_map(
        body,
        mesh=mesh,
        in_specs=(P(None, None, "gx", "gy", None), P("gx", "gy", None), P(), P()),
        out_specs=(P(None, None, "gx", "gy", None), P(None, None, "gx", "gy", None)),
        check_vma=False,
    )
```

```python
import functools
import math

import jax
import jax.numpy as jnp
import ml_dtypes
import numpy as np
from jax import lax
from jax.experimental import pallas as pl
from jax.experimental.pallas import tpu as pltpu
from jax.sharding import PartitionSpec as P

KAPPA = 0.12
DAMPING = 0.3
BF16 = jnp.bfloat16
F32 = jnp.float32


def sine_matrix(length):
    index = np.arange(1, length + 1)
    angles = index * (math.pi / (length + 1))
    return math.sqrt(2.0 / (length + 1)) * np.sin(angles[:, None] * index[None, :]), angles


def halves(matrix):
    high = matrix.astype(np.float32).astype(ml_dtypes.bfloat16)
    low = (matrix - high.astype(np.float64)).astype(np.float32).astype(ml_dtypes.bfloat16)
    return high, low


def left_factor(matrix):
    high, low = halves(matrix)
    return np.concatenate([high, high, low], axis=1)


def tables(size_x, size_y, cells_z):
    sine_x, angle_x = sine_matrix(size_x)
    sine_y, angle_y = sine_matrix(size_y)
    sine_z, angle_z = sine_matrix(cells_z)
    half = size_x // 2
    order = np.concatenate([np.arange(0, size_x, 2), np.arange(1, size_x, 2)])
    cells = np.concatenate([np.arange(half), np.arange(size_x - 1, half - 1, -1)])

    def symbol(angle):
        return 2.5 - 8.0 / 3.0 * np.cos(angle) + 1.0 / 6.0 * np.cos(2.0 * angle)

    real_part = (
        symbol(angle_x)[order][:, None, None]
        + symbol(angle_y)[None, :, None]
        + (2.0 - 2.0 * np.cos(angle_z))[None, None, :]
        - KAPPA
    ).reshape(size_x * size_y, cells_z)
    denominator = real_part**2 + (KAPPA * DAMPING) ** 2
    inverse = np.stack([real_part / denominator, KAPPA * DAMPING / denominator]).astype(np.float32)

    parity = [np.kron(sine_x[order[p * half : (p + 1) * half]][:, :half], sine_y) for p in (0, 1)]
    forward = np.stack([left_factor(m) for m in parity])
    backward = np.stack([left_factor(m.T) for m in parity])
    high_z, low_z = halves(sine_z)
    right_z = np.concatenate([np.concatenate([high_z, low_z], axis=1)] * 2, axis=0)

    full = np.kron(sine_x[order], sine_y)
    by_cell = full.reshape(-1, size_x, size_y)
    enter_x = np.stack([-by_cell[:, 0] / 12.0, (16.0 * by_cell[:, 0] - by_cell[:, 1]) / 12.0], 1)
    enter_y = np.stack(
        [-by_cell[:, :, 0] / 12.0, (16.0 * by_cell[:, :, 0] - by_cell[:, :, 1]) / 12.0], 1
    )
    enter = left_factor(
        np.concatenate([enter_x.reshape(len(full), -1), enter_y.reshape(len(full), -1)], axis=1)
    )
    leave = left_factor(
        np.concatenate(
            [
                by_cell[:, size_x - 2 :].reshape(len(full), -1),
                by_cell[:, :, size_y - 2 :].transpose(0, 2, 1).reshape(len(full), -1),
            ],
            axis=1,
        ).T
    )
    first = left_factor(
        np.concatenate(
            [
                by_cell[:, :2].reshape(len(full), -1),
                by_cell[:, :, :2].transpose(0, 2, 1).reshape(len(full), -1),
            ],
            axis=1,
        ).T
    )
    edge = np.zeros((size_x, size_y, 1))
    edge[0] += 1.0 / 12.0
    edge[-1] += 1.0 / 12.0
    edge[:, 0] += 1.0 / 12.0
    edge[:, -1] += 1.0 / 12.0
    edge = edge[cells].reshape(size_x * size_y, 1).astype(np.float32)
    return dict(
        inverse=inverse, forward=forward, backward=backward, right_z=right_z,
        enter=enter, leave=leave, first=first, edge=edge,
    ), cells


def split(values):
    high = values.astype(BF16)
    return high, (values - high.astype(F32)).astype(BF16)


def left_product(matrix, values):
    high, low = split(values)
    return jnp.dot(matrix, jnp.concatenate([high, low, high], axis=0), preferred_element_type=F32)


def z_transform(field, right_z):
    rows = field.shape[0]
    cells_z = field.shape[1] // 2
    high, low = split(jnp.concatenate([field[:, :cells_z], field[:, cells_z:]], axis=0))
    both = jnp.dot(jnp.concatenate([high, low], axis=1), right_z, preferred_element_type=F32)
    total = both[:, :cells_z] + both[:, cells_z:]
    return jnp.concatenate([total[:rows], total[rows:]], axis=1)


def to_modes(field, forward):
    count = field.shape[0] // 2
    first, second = field[:count], field[count:]
    return jnp.concatenate(
        [left_product(forward[0], first + second), left_product(forward[1], first - second)], axis=0
    )


def to_cells(modes, backward):
    count = modes.shape[0] // 2
    even = left_product(backward[0], modes[:count])
    odd = left_product(backward[1], modes[count:])
    return jnp.concatenate([even + odd, even - odd], axis=0)


def times(real_part, imag_part, field):
    lanes = field.shape[1] // 2
    real, imag = field[:, :lanes], field[:, lanes:]
    return jnp.concatenate(
        [real_part * real - imag_part * imag, real_part * imag + imag_part * real], axis=1
    )


def solve_modes(source_modes, contrast, t):
    term = times(t["inverse"][0], t["inverse"][1], source_modes)
    total = term
    for _ in range(2):
        cells = apply_contrast(to_cells(term, t["backward"]), contrast, t["right_z"])
        term = times(t["inverse"][0], t["inverse"][1], to_modes(cells, t["forward"]))
        total = total + term
    return total, term


def apply_contrast(field, contrast, right_z, block=64):
    done = []
    for start in range(0, field.shape[0], block):
        here = slice(start, start + block)
        cells = times(contrast[0, here], contrast[1, here], z_transform(field[here], right_z))
        done.append(z_transform(cells, right_z))
    return jnp.concatenate(done, axis=0)


PREP = ("edge", "forward", "right_z")
BEAT = ("inverse", "forward", "backward", "right_z", "enter", "leave")


def hand_on_kernel(in_ref, out_ref):
    out_ref[...] = in_ref[...]


def prepare(dense, slow, place, depth, amplitude, edge, forward, right_z, modes_ref, contrast_ref):
    rows, cells_z = contrast_ref.shape[1:]
    points = place.shape[1]
    row_ids = lax.broadcasted_iota(jnp.int32, (rows, points), 0)
    lane_ids = lax.broadcasted_iota(jnp.int32, (cells_z, points), 0)
    at_lane = (lane_ids == depth).astype(F32)
    spread = []
    for c in range(2):
        amp = amplitude[c]
        one = amp.astype(BF16).astype(F32)
        two = (amp - one).astype(BF16).astype(F32)
        parts = [at_lane * part for part in (one, two, amp - one - two)]
        spread.append(jnp.concatenate(parts, axis=1).astype(BF16))
    scaled = KAPPA * (slow - 1.0)
    contrast_ref[0] = scaled - edge
    contrast_ref[1] = DAMPING * scaled
    at_row = (row_ids == place).astype(F32).astype(BF16)
    field = lax.dot_general(
        jnp.concatenate([at_row] * 3, axis=1), jnp.concatenate(spread, axis=0),
        (((1,), (1,)), ((), ())), preferred_element_type=F32,
    )
    modes_ref[...] = to_modes(z_transform(field + dense, right_z), forward)


def prep_kernel(cells_x, rhs_ref, right_ref, slow_ref, place_ref, depth_ref, amp_ref, edge_ref,
                forward_ref, z_ref, modes_ref, contrast_ref):
    dense = [jnp.concatenate([right_ref[rhs_ref[0], c, x] for x in cells_x], axis=0) for c in range(2)]
    slow = jnp.concatenate([slow_ref[x] for x in cells_x], axis=0)
    prepare(
        jnp.concatenate(dense, axis=1), slow, place_ref[...], depth_ref[...], amp_ref, edge_ref[...],
        forward_ref, z_ref[...], modes_ref, contrast_ref,
    )


def prep_other_kernel(cells_x, core_ref, swap_ref, own_modes_ref, own_contrast_ref, place_ref, depth_ref,
                      amp_ref, edge_ref, forward_ref, z_ref, modes_ref, contrast_ref):
    core = core_ref[0]
    other = 1 - core
    modes_ref[core] = own_modes_ref[...]
    contrast_ref[core] = own_contrast_ref[...]
    parts = [jnp.concatenate([swap_ref[c, x] for x in cells_x], axis=0) for c in range(3)]
    prepare(
        jnp.concatenate(parts[:2], axis=1), parts[2], place_ref[...], depth_ref[...], amp_ref,
        edge_ref[...], forward_ref, z_ref[...], modes_ref.at[other], contrast_ref.at[other],
    )


def source_modes(modes, trace_x, trace_y, enter):
    return modes + left_product(enter, jnp.concatenate([trace_x, trace_y], axis=0))


def beat_kernel(tile, active_ref, modes_ref, contrast_ref, trace_x_ref, trace_y_ref, total_ref, term_ref, *refs):
    t = {name: ref for name, ref in zip(BEAT, refs)}
    out_x_ref, out_y_ref, new_total_ref, new_term_ref = refs[len(BEAT) :]

    @pl.when(active_ref[0] == 1)
    def _():
        local = dict(t, right_z=t["right_z"][...])
        source = source_modes(modes_ref[tile], trace_x_ref[...], trace_y_ref[...], t["enter"][...])
        total, term = solve_modes(source, contrast_ref.at[tile], local)
        new_total_ref[...] = total
        new_term_ref[...] = term
        out = left_product(t["leave"][...], total)
        count = out_x_ref.shape[0]
        out_x_ref[...] = out[:count]
        out_y_ref[...] = out[count:]

    @pl.when(active_ref[0] == 0)
    def _():
        new_total_ref[...] = total_ref[...]
        new_term_ref[...] = term_ref[...]


def edge_kernel(total0_ref, total1_ref, first_ref, z_ref, edge_x_ref, edge_y_ref):
    count = edge_x_ref.shape[0]
    right_z = z_ref[...]
    for tile, total_ref in enumerate((total0_ref, total1_ref)):
        edges = z_transform(left_product(first_ref[...], total_ref[...]), right_z)
        edge_y_ref[tile] = edges[count:]
        if tile == 0:
            edge_x_ref[...] = edges[:count]


FINISH = ("backward", "right_z")


def finish_kernel(cells_x, core_ref, total0_ref, term0_ref, total1_ref, term1_ref, contrast_ref, backward_ref,
                  z_ref, keep_ref, give_ref, both_ref):
    _, _, _, size_x, size_y, cells_z = both_ref.shape
    right_z = z_ref[...]
    for tile, (total_ref, term_ref) in enumerate(((total0_ref, term0_ref), (total1_ref, term1_ref))):
        wave = z_transform(to_cells(total_ref[...], backward_ref), right_z)
        rest = z_transform(to_cells(term_ref[...], backward_ref), right_z)
        rest = times(contrast_ref[tile, 0], contrast_ref[tile, 1], rest)
        for place, x in enumerate(cells_x):
            here = slice(place * size_y, (place + 1) * size_y)
            for c in range(2):
                there = slice(c * cells_z, (c + 1) * cells_z)
                both_ref[tile, 0, c, x] = wave[here, there]
                both_ref[tile, 1, c, x] = rest[here, there]
                if tile == 1 and x < 2:
                    layer = wave[here, there]
                    if x == 0:
                        both_ref[0, 1, c, size_x - 2] += layer * (-1.0 / 12.0)
                        both_ref[0, 1, c, size_x - 1] += layer * (16.0 / 12.0)
                    else:
                        both_ref[0, 1, c, size_x - 1] += layer * (-1.0 / 12.0)
    keep_ref[...] = both_ref[core_ref[0]]
    give_ref[...] = both_ref[1 - core_ref[0]]


def add_later(rest_ref, edge_x, edge_y, lower):
    _, size_x, size_y, cells_z = rest_ref.shape
    for c in range(2):
        there = slice(c * cells_z, (c + 1) * cells_z)
        near, far = edge_x[:size_y, there] * lower, edge_x[size_y:, there] * lower
        rest_ref[c, size_x - 2] += near * (-1.0 / 12.0)
        rest_ref[c, size_x - 1] += (16.0 * near - far) * (1.0 / 12.0)
        near, far = edge_y[:size_x, there], edge_y[size_x:, there]
        two = jnp.stack([near * (-1.0 / 12.0), (16.0 * near - far) * (1.0 / 12.0)], axis=1)
        rest_ref[c, :, size_y - 2 :] += two


def keep_kernel(core_ref, keep_ref, edge_x_ref, edge_y_ref, rest_ref):
    rest_ref[...] = keep_ref[1]
    add_later(rest_ref, edge_x_ref[...], edge_y_ref[...], (core_ref[0] == 1).astype(F32))


def place_kernel(core_ref, rhs_ref, keep_ref, keep_rest_ref, got_ref, got_edge_ref, wave_ref, rest_ref, work_ref, sems):
    rhs = rhs_ref[0]
    count = got_edge_ref.shape[0] // 2
    copies = [
        pltpu.make_async_copy(keep_ref.at[0], wave_ref.at[rhs], sems.at[0]),
        pltpu.make_async_copy(got_ref.at[0], wave_ref.at[1 - rhs], sems.at[1]),
        pltpu.make_async_copy(keep_rest_ref, rest_ref.at[rhs], sems.at[2]),
    ]
    for copy in copies:
        copy.start()
    work_ref[...] = got_ref[1]
    add_later(work_ref, got_edge_ref[:count], got_edge_ref[count:], (core_ref[0] == 1).astype(F32))
    copies.append(pltpu.make_async_copy(work_ref, rest_ref.at[1 - rhs], sems.at[3]))
    copies[-1].start()
    for copy in copies:
        copy.wait()


def whole():
    return pl.BlockSpec(memory_space=pltpu.VMEM)


def scalars():
    return pl.BlockSpec(memory_space=pltpu.SMEM)


def anywhere():
    return pl.BlockSpec(memory_space=pl.ANY)


SOLVE_COST = pl.CostEstimate(flops=2 * 10**9, bytes_accessed=2 * 10**6, transcendentals=0)
KEEP_COST = pl.CostEstimate(flops=10**10, bytes_accessed=10**6, transcendentals=0)
PARAMS = pltpu.CompilerParams(vmem_limit_bytes=24 * 1024 * 1024)


def shaped(*shape):
    return jax.ShapeDtypeStruct(shape, F32)


def body(right_side, slowness, source_cells, source_amplitudes):
    sources, _, size_x, size_y, cells_z = right_side.shape
    grid_rows, grid_cols = lax.axis_size("gx"), lax.axis_size("gy")
    assert sources == 2 and grid_rows % 2 == 0 and size_x % 2 == 0
    chips = grid_rows // 2
    row, col = lax.axis_index("gx"), lax.axis_index("gy")
    core = row % 2
    rhs = (core + row // 2 + col) % 2
    core_ref, rhs_ref = core[None], rhs[None]
    t, cells_x = tables(size_x, size_y, cells_z)
    t = {name: jnp.asarray(value) for name, value in t.items()}
    cells_x = tuple(int(x) for x in cells_x)
    rows = size_x * size_y

    def device(chip, core, column):
        return (2 * chip + core) * grid_cols + column

    def between(pairs):
        return [
            (device(a, r, b), device(c, 1 - r, d)) for (a, b), (c, d) in pairs for r in range(2)
        ]

    own = [
        (device(k, r, j), device(k, 1 - r, j))
        for k in range(chips) for j in range(grid_cols) for r in range(2)
    ]
    axes = ("gx", "gy")
    other = lax.dynamic_index_in_dim(right_side, 1 - rhs, 0, keepdims=False)
    swapped = lax.ppermute(jnp.concatenate([other, slowness[None]], axis=0), axes, own)

    total_y = size_y * grid_cols
    cells = lax.dynamic_index_in_dim(source_cells, rhs, 0, keepdims=True)
    near_y = cells // cells_z % total_y - col * size_y
    places = []
    for tile_row in (row, row + 1 - 2 * core):
        near_x = cells // (total_y * cells_z) - tile_row * size_x
        inside = (near_x >= 0) & (near_x < size_x) & (near_y >= 0) & (near_y < size_y)
        folded = jnp.where(near_x < size_x // 2, near_x, size_x + size_x // 2 - 1 - near_x)
        places.append(jnp.where(inside, folded * size_y + near_y, -1))
    amplitudes = lax.dynamic_index_in_dim(source_amplitudes, rhs, 0, keepdims=False).T[:, None, :]

    depth = cells % cells_z
    prep_tables = [t[name] for name in PREP]
    one = (shaped(rows, 2 * cells_z), shaped(2, rows, cells_z))
    own_modes, own_contrast = pl.pallas_call(
        functools.partial(prep_kernel, cells_x),
        out_shape=one,
        in_specs=[scalars()] + [whole()] * 8,
        out_specs=(whole(), whole()),
        compiler_params=PARAMS,
        name="prep",
    )(rhs_ref, right_side, slowness, places[0], depth, amplitudes, *prep_tables)
    modes, contrast = pl.pallas_call(
        functools.partial(prep_other_kernel, cells_x),
        out_shape=(shaped(2, rows, 2 * cells_z), shaped(2, 2, rows, cells_z)),
        in_specs=[scalars()] + [whole()] * 9,
        out_specs=(whole(), whole()),
        compiler_params=PARAMS,
        name="prep_other",
    )(core_ref, swapped, own_modes, own_contrast, places[1], depth, amplitudes, *prep_tables)

    beat_tables = [t[name] for name in BEAT]

    def solve(tile, active, trace_x, trace_y, state):
        out_x, out_y, *state = pl.pallas_call(
            functools.partial(beat_kernel, tile),
            out_shape=(shaped(*zero_x.shape), shaped(*zero_y.shape)) + (shaped(rows, 2 * cells_z),) * 2,
            in_specs=[scalars()] + [whole()] * (6 + len(BEAT)),
            out_specs=(whole(),) * 4,
            input_output_aliases={5: 2, 6: 3},
            compiler_params=PARAMS,
            cost_estimate=SOLVE_COST,
            name="upper" if tile == 0 else "lower",
        )(active, modes, contrast, trace_x, trace_y, *state, *beat_tables)
        return out_x, out_y, state

    def hand_on(trace):
        return pl.pallas_call(
            hand_on_kernel,
            out_shape=shaped(*trace.shape),
            in_specs=[whole()],
            out_specs=whole(),
            compiler_params=PARAMS,
            name="hand_on",
        )(trace)

    zero_x = jnp.zeros((2 * size_y, 2 * cells_z), F32)
    zero_y = jnp.zeros((2 * size_x, 2 * cells_z), F32)
    trace_x, trace_y0, trace_y1 = zero_x, zero_y, zero_y
    states = [[jnp.zeros((rows, 2 * cells_z), F32)] * 2 for _ in range(2)]
    for beat in range(chips + grid_cols - 1):
        active = (row // 2 + col == beat).astype(jnp.int32)[None]
        here = [(k, beat - k) for k in range(chips) if 0 <= beat - k < grid_cols]
        along_x = between([((k, j), (k + 1, j)) for k, j in here if k + 1 < chips])
        along_y = between([((k, j), (k, j + 1)) for k, j in here if j + 1 < grid_cols])
        inner_x, out_y0, states[0] = solve(0, active, trace_x, trace_y0, states[0])
        if along_y:
            trace_y0 = hand_on(lax.ppermute(out_y0, axes, along_y))
        out_x, out_y1, states[1] = solve(1, active, inner_x, trace_y1, states[1])
        if along_x:
            trace_x = lax.ppermute(out_x, axes, along_x)
        if along_y:
            trace_y1 = lax.ppermute(out_y1, axes, along_y)

    edge_x, edge_y = pl.pallas_call(
        edge_kernel,
        out_shape=(shaped(*zero_x.shape), shaped(2, *zero_y.shape)),
        in_specs=[whole()] * 4,
        out_specs=(whole(), whole()),
        compiler_params=PARAMS,
        name="edges",
    )(states[0][0], states[1][0], t["first"], t["right_z"])

    every = [(k, j) for k in range(chips) for j in range(grid_cols)]
    after_x = lax.ppermute(edge_x, axes, between([((k, j), (k - 1, j)) for k, j in every if k]))
    after_y = lax.ppermute(edge_y, axes, between([((k, j), (k, j - 1)) for k, j in every if j]))

    half = shaped(2, 2, size_x, size_y, cells_z)
    keep, give = pl.pallas_call(
        functools.partial(finish_kernel, cells_x),
        out_shape=(half, half),
        in_specs=[scalars()] + [whole()] * (5 + len(FINISH)),
        out_specs=(whole(), whole()),
        scratch_shapes=[pltpu.VMEM((2, 2, 2, size_x, size_y, cells_z), F32)],
        compiler_params=PARAMS,
        name="finish",
    )(core_ref, *states[0], *states[1], contrast, *[t[name] for name in FINISH])
    got = lax.ppermute(give, axes, own)

    keep_y = lax.dynamic_index_in_dim(after_y, core, 0, keepdims=False)
    pass_y = lax.dynamic_index_in_dim(after_y, 1 - core, 0, keepdims=False)
    got_edge = lax.ppermute(jnp.concatenate([after_x, pass_y], axis=0), axes, own)
    keep_rest = pl.pallas_call(
        keep_kernel,
        out_shape=shaped(*half.shape[1:]),
        in_specs=[scalars()] + [whole()] * 3,
        out_specs=whole(),
        compiler_params=PARAMS,
        cost_estimate=KEEP_COST,
        name="keep",
    )(core_ref, keep, after_x, keep_y)
    return pl.pallas_call(
        place_kernel,
        out_shape=(shaped(*right_side.shape), shaped(*right_side.shape)),
        in_specs=[scalars()] * 2 + [whole()] * 4,
        out_specs=(anywhere(), anywhere()),
        scratch_shapes=[
            pltpu.VMEM((2, size_x, size_y, cells_z), F32),
            pltpu.SemaphoreType.DMA((4,)),
        ],
        compiler_params=PARAMS,
        name="place",
    )(core_ref, rhs_ref, keep, keep_rest, got, got_edge)


def solution(mesh):
    return jax.shard_map(
        body,
        mesh=mesh,
        in_specs=(P(None, None, "gx", "gy", None), P("gx", "gy", None), P(), P()),
        out_specs=(P(None, None, "gx", "gy", None), P(None, None, "gx", "gy", None)),
        check_vma=False,
    )
```

```python
import functools
import math

import jax
import jax.numpy as jnp
import ml_dtypes
import numpy as np
from jax import lax
from jax.experimental import pallas as pl
from jax.experimental.pallas import tpu as pltpu
from jax.sharding import PartitionSpec as P

KAPPA = 0.12
DAMPING = 0.3
BF16 = jnp.bfloat16
F32 = jnp.float32


def sine_matrix(length):
    index = np.arange(1, length + 1)
    angles = index * (math.pi / (length + 1))
    return math.sqrt(2.0 / (length + 1)) * np.sin(angles[:, None] * index[None, :]), angles


def halves(matrix):
    high = matrix.astype(np.float32).astype(ml_dtypes.bfloat16)
    low = (matrix - high.astype(np.float64)).astype(np.float32).astype(ml_dtypes.bfloat16)
    return high, low


def left_factor(matrix):
    high, low = halves(matrix)
    return np.concatenate([high, high, low], axis=1)


def tables(size_x, size_y, cells_z):
    sine_x, angle_x = sine_matrix(size_x)
    sine_y, angle_y = sine_matrix(size_y)
    sine_z, angle_z = sine_matrix(cells_z)
    half = size_x // 2
    order = np.concatenate([np.arange(0, size_x, 2), np.arange(1, size_x, 2)])
    cells = np.concatenate([np.arange(half), np.arange(size_x - 1, half - 1, -1)])

    def symbol(angle):
        return 2.5 - 8.0 / 3.0 * np.cos(angle) + 1.0 / 6.0 * np.cos(2.0 * angle)

    real_part = (
        symbol(angle_x)[order][:, None, None]
        + symbol(angle_y)[None, :, None]
        + (2.0 - 2.0 * np.cos(angle_z))[None, None, :]
        - KAPPA
    ).reshape(size_x * size_y, cells_z)
    denominator = real_part**2 + (KAPPA * DAMPING) ** 2
    inverse = np.stack([real_part / denominator, KAPPA * DAMPING / denominator]).astype(np.float32)

    parity = [np.kron(sine_x[order[p * half : (p + 1) * half]][:, :half], sine_y) for p in (0, 1)]
    cut = half * size_y // 2
    forward, backward = [
        np.stack([[left_factor(m[:, :cut]), left_factor(m[:, cut:])] for m in matrices])
        for matrices in (parity, [m.T for m in parity])
    ]
    high_z, low_z = halves(sine_z)
    right_z = np.concatenate([np.concatenate([high_z, low_z], axis=1)] * 2, axis=0)

    full = np.kron(sine_x[order], sine_y)
    by_cell = full.reshape(-1, size_x, size_y)
    enter_x = np.stack([-by_cell[:, 0] / 12.0, (16.0 * by_cell[:, 0] - by_cell[:, 1]) / 12.0], 1)
    enter_y = np.stack(
        [-by_cell[:, :, 0] / 12.0, (16.0 * by_cell[:, :, 0] - by_cell[:, :, 1]) / 12.0], 1
    )
    enter = left_factor(
        np.concatenate([enter_x.reshape(len(full), -1), enter_y.reshape(len(full), -1)], axis=1)
    )
    leave = left_factor(
        np.concatenate(
            [
                by_cell[:, size_x - 2 :].reshape(len(full), -1),
                by_cell[:, :, size_y - 2 :].transpose(0, 2, 1).reshape(len(full), -1),
            ],
            axis=1,
        ).T
    )
    first = left_factor(
        np.concatenate(
            [
                by_cell[:, :2].reshape(len(full), -1),
                by_cell[:, :, :2].transpose(0, 2, 1).reshape(len(full), -1),
            ],
            axis=1,
        ).T
    )
    edge = np.zeros((size_x, size_y, 1))
    edge[0] += 1.0 / 12.0
    edge[-1] += 1.0 / 12.0
    edge[:, 0] += 1.0 / 12.0
    edge[:, -1] += 1.0 / 12.0
    edge = edge[cells].reshape(size_x * size_y, 1).astype(np.float32)
    return dict(
        inverse=inverse, forward=forward, backward=backward, right_z=right_z,
        enter=enter, leave=leave, first=first, edge=edge,
    ), cells


def split(values):
    high = values.astype(BF16)
    return high, (values - high.astype(F32)).astype(BF16)


def stacked(values):
    high, low = split(values)
    return jnp.concatenate([high, low, high], axis=0)


def left_product(matrix, values):
    return jnp.dot(matrix, stacked(values), preferred_element_type=F32)


def z_transform(field, right_z):
    rows = field.shape[0]
    cells_z = field.shape[1] // 2
    high, low = split(jnp.concatenate([field[:, :cells_z], field[:, cells_z:]], axis=0))
    both = jnp.dot(jnp.concatenate([high, low], axis=1), right_z, preferred_element_type=F32)
    total = both[:, :cells_z] + both[:, cells_z:]
    return jnp.concatenate([total[:rows], total[rows:]], axis=1)


def to_modes(first, second, forward):
    return [
        sum(left_product(forward[p, h], join(first[h], second[h])) for h in range(2))
        for p, join in enumerate((jnp.add, jnp.subtract))
    ]


def to_cells(modes, backward):
    even, odd = [
        sum(left_product(backward[p, h], modes[p][h]) for h in range(2)) for p in range(2)
    ]
    return even + odd, even - odd


def in_two(values):
    count = values.shape[0] // 2
    return values[:count], values[count:]


def in_parities(modes):
    return [in_two(part) for part in in_two(modes)]


def whole_field(first, second):
    return jnp.concatenate([first, second], axis=0)


def times(real_part, imag_part, field):
    lanes = field.shape[1] // 2
    real, imag = field[:, :lanes], field[:, lanes:]
    return jnp.concatenate(
        [real_part * real - imag_part * imag, real_part * imag + imag_part * real], axis=1
    )


def solve_modes(source_modes, contrast, t):
    count = source_modes.shape[0] // 4
    term = in_parities(times(t["inverse"][0], t["inverse"][1], source_modes))
    total = term
    for _ in range(2):
        first, second = [in_two(cells) for cells in to_cells(term, t["backward"])]
        parts = []
        for h in range(2):
            here = [slice(at, at + count) for at in (h * count, (h + 2) * count)]
            factor = [jnp.concatenate([contrast[c, rows] for rows in here], axis=0) for c in range(2)]
            cells = z_transform(jnp.concatenate([first[h], second[h]], axis=0), t["right_z"])
            parts.append(in_two(z_transform(times(*factor, cells), t["right_z"])))
        modes = to_modes(*zip(*parts), t["forward"])
        term = []
        for p in range(2):
            halves = []
            for h, part in enumerate(in_two(modes[p])):
                here = slice((2 * p + h) * count, (2 * p + h + 1) * count)
                halves.append(times(t["inverse"][0, here], t["inverse"][1, here], part))
            term.append(halves)
        total = [[a + b for a, b in zip(*pair)] for pair in zip(total, term)]
    return [jnp.concatenate([part for pair in both for part in pair], axis=0) for both in (total, term)]


PREP = ("edge", "forward", "right_z")
BEAT = ("inverse", "forward", "backward", "right_z", "enter", "leave")


def hand_on_kernel(in_ref, out_ref):
    out_ref[...] = in_ref[...]


def prepare(dense, slow, place, depth, amplitude, edge, forward, right_z, modes_ref, contrast_ref):
    rows, cells_z = contrast_ref.shape[1:]
    points = place.shape[1]
    row_ids = lax.broadcasted_iota(jnp.int32, (rows, points), 0)
    lane_ids = lax.broadcasted_iota(jnp.int32, (cells_z, points), 0)
    at_lane = (lane_ids == depth).astype(F32)
    spread = []
    for c in range(2):
        amp = amplitude[c]
        one = amp.astype(BF16).astype(F32)
        two = (amp - one).astype(BF16).astype(F32)
        parts = [at_lane * part for part in (one, two, amp - one - two)]
        spread.append(jnp.concatenate(parts, axis=1).astype(BF16))
    scaled = KAPPA * (slow - 1.0)
    contrast_ref[0] = scaled - edge
    contrast_ref[1] = DAMPING * scaled
    at_row = (row_ids == place).astype(F32).astype(BF16)
    field = lax.dot_general(
        jnp.concatenate([at_row] * 3, axis=1), jnp.concatenate(spread, axis=0),
        (((1,), (1,)), ((), ())), preferred_element_type=F32,
    )
    first, second = [in_two(part) for part in in_two(z_transform(field + dense, right_z))]
    modes_ref[...] = jnp.concatenate(to_modes(first, second, forward), axis=0)


def prep_kernel(cells_x, rhs_ref, right_ref, slow_ref, place_ref, depth_ref, amp_ref, edge_ref,
                forward_ref, z_ref, modes_ref, contrast_ref):
    dense = [jnp.concatenate([right_ref[rhs_ref[0], c, x] for x in cells_x], axis=0) for c in range(2)]
    slow = jnp.concatenate([slow_ref[x] for x in cells_x], axis=0)
    prepare(
        jnp.concatenate(dense, axis=1), slow, place_ref[...], depth_ref[...], amp_ref, edge_ref[...],
        forward_ref, z_ref[...], modes_ref, contrast_ref,
    )


def prep_other_kernel(cells_x, core_ref, swap_ref, own_modes_ref, own_contrast_ref, place_ref, depth_ref,
                      amp_ref, edge_ref, forward_ref, z_ref, modes_ref, contrast_ref):
    core = core_ref[0]
    other = 1 - core
    modes_ref[core] = own_modes_ref[...]
    contrast_ref[core] = own_contrast_ref[...]
    parts = [jnp.concatenate([swap_ref[c, x] for x in cells_x], axis=0) for c in range(3)]
    prepare(
        jnp.concatenate(parts[:2], axis=1), parts[2], place_ref[...], depth_ref[...], amp_ref,
        edge_ref[...], forward_ref, z_ref[...], modes_ref.at[other], contrast_ref.at[other],
    )


def source_modes(modes, trace_x, trace_y, enter):
    return modes + left_product(enter, jnp.concatenate([trace_x, trace_y], axis=0))


def beat_kernel(tile, sends, active_ref, modes_ref, contrast_ref, trace_x_ref, trace_y_ref, total_ref, term_ref, *refs):
    t = {name: ref for name, ref in zip(BEAT, refs)}
    new_total_ref, new_term_ref, *out_refs = refs[len(BEAT) :]

    @pl.when(active_ref[0] == 1)
    def _():
        local = dict(t, right_z=t["right_z"][...])
        source = source_modes(modes_ref[tile], trace_x_ref[...], trace_y_ref[...], t["enter"][...])
        total, term = solve_modes(source, contrast_ref.at[tile], local)
        new_total_ref[...] = total
        new_term_ref[...] = term
        if sends:
            count = trace_x_ref.shape[0]
            out = left_product(t["leave"][...], total)
            for out_ref, part in zip(out_refs, (out[:count], out[count:])):
                out_ref[...] = part

    @pl.when(active_ref[0] == 0)
    def _():
        new_total_ref[...] = total_ref[...]
        new_term_ref[...] = term_ref[...]


def edge_kernel(total0_ref, total1_ref, first_ref, z_ref, edge_x_ref, edge_y_ref):
    count = edge_x_ref.shape[0]
    right_z = z_ref[...]
    for tile, total_ref in enumerate((total0_ref, total1_ref)):
        edges = z_transform(left_product(first_ref[...], total_ref[...]), right_z)
        edge_y_ref[tile] = edges[count:]
        if tile == 0:
            edge_x_ref[...] = edges[:count]


FINISH = ("backward", "right_z")


def finish_kernel(cells_x, core_ref, total0_ref, term0_ref, total1_ref, term1_ref, contrast_ref, backward_ref,
                  z_ref, keep_ref, give_ref, both_ref):
    _, _, _, size_x, size_y, cells_z = both_ref.shape
    right_z = z_ref[...]
    for tile, (total_ref, term_ref) in enumerate(((total0_ref, term0_ref), (total1_ref, term1_ref))):
        wave, rest = [
            z_transform(whole_field(*to_cells(in_parities(ref[...]), backward_ref)), right_z)
            for ref in (total_ref, term_ref)
        ]
        rest = times(contrast_ref[tile, 0], contrast_ref[tile, 1], rest)
        for place, x in enumerate(cells_x):
            here = slice(place * size_y, (place + 1) * size_y)
            for c in range(2):
                there = slice(c * cells_z, (c + 1) * cells_z)
                both_ref[tile, 0, c, x] = wave[here, there]
                both_ref[tile, 1, c, x] = rest[here, there]
                if tile == 1 and x < 2:
                    layer = wave[here, there]
                    if x == 0:
                        both_ref[0, 1, c, size_x - 2] += layer * (-1.0 / 12.0)
                        both_ref[0, 1, c, size_x - 1] += layer * (16.0 / 12.0)
                    else:
                        both_ref[0, 1, c, size_x - 1] += layer * (-1.0 / 12.0)
    keep_ref[...] = both_ref[core_ref[0]]
    give_ref[...] = both_ref[1 - core_ref[0]]


def add_later(rest_ref, edge_x, edge_y, lower):
    _, size_x, size_y, cells_z = rest_ref.shape
    for c in range(2):
        there = slice(c * cells_z, (c + 1) * cells_z)
        near, far = edge_x[:size_y, there] * lower, edge_x[size_y:, there] * lower
        rest_ref[c, size_x - 2] += near * (-1.0 / 12.0)
        rest_ref[c, size_x - 1] += (16.0 * near - far) * (1.0 / 12.0)
        near, far = edge_y[:size_x, there], edge_y[size_x:, there]
        two = jnp.stack([near * (-1.0 / 12.0), (16.0 * near - far) * (1.0 / 12.0)], axis=1)
        rest_ref[c, :, size_y - 2 :] += two


def keep_kernel(core_ref, keep_ref, edge_x_ref, edge_y_ref, rest_ref):
    rest_ref[...] = keep_ref[1]
    add_later(rest_ref, edge_x_ref[...], edge_y_ref[...], (core_ref[0] == 1).astype(F32))


def place_wave_kernel(rhs_ref, keep_ref, got_ref, wave_ref, sems):
    rhs = rhs_ref[0]
    copies = [
        pltpu.make_async_copy(keep_ref.at[0], wave_ref.at[rhs], sems.at[0]),
        pltpu.make_async_copy(got_ref.at[0], wave_ref.at[1 - rhs], sems.at[1]),
    ]
    for copy in copies:
        copy.start()
    for copy in copies:
        copy.wait()


def place_rest_kernel(core_ref, rhs_ref, keep_rest_ref, got_ref, got_edge_ref, rest_ref, work_ref, sems):
    rhs = rhs_ref[0]
    count = got_edge_ref.shape[0] // 2
    copies = [pltpu.make_async_copy(keep_rest_ref, rest_ref.at[rhs], sems.at[0])]
    copies[0].start()
    work_ref[...] = got_ref[1]
    add_later(work_ref, got_edge_ref[:count], got_edge_ref[count:], (core_ref[0] == 1).astype(F32))
    copies.append(pltpu.make_async_copy(work_ref, rest_ref.at[1 - rhs], sems.at[1]))
    copies[1].start()
    for copy in copies:
        copy.wait()


def whole():
    return pl.BlockSpec(memory_space=pltpu.VMEM)


def scalars():
    return pl.BlockSpec(memory_space=pltpu.SMEM)


def anywhere():
    return pl.BlockSpec(memory_space=pl.ANY)


SOLVE_COST = pl.CostEstimate(flops=2 * 10**9, bytes_accessed=2 * 10**6, transcendentals=0)
KEEP_COST = pl.CostEstimate(flops=10**10, bytes_accessed=10**6, transcendentals=0)
PARAMS = pltpu.CompilerParams(vmem_limit_bytes=24 * 1024 * 1024)


def shaped(*shape):
    return jax.ShapeDtypeStruct(shape, F32)


def body(right_side, slowness, source_cells, source_amplitudes):
    sources, _, size_x, size_y, cells_z = right_side.shape
    grid_rows, grid_cols = lax.axis_size("gx"), lax.axis_size("gy")
    assert sources == 2 and grid_rows % 2 == 0 and size_x % 2 == 0
    chips = grid_rows // 2
    row, col = lax.axis_index("gx"), lax.axis_index("gy")
    core = row % 2
    rhs = (core + row // 2 + col) % 2
    core_ref, rhs_ref = core[None], rhs[None]
    t, cells_x = tables(size_x, size_y, cells_z)
    t = {name: jnp.asarray(value) for name, value in t.items()}
    cells_x = tuple(int(x) for x in cells_x)
    rows = size_x * size_y

    def device(chip, core, column):
        return (2 * chip + core) * grid_cols + column

    def between(pairs):
        return [
            (device(a, r, b), device(c, 1 - r, d)) for (a, b), (c, d) in pairs for r in range(2)
        ]

    own = [
        (device(k, r, j), device(k, 1 - r, j))
        for k in range(chips) for j in range(grid_cols) for r in range(2)
    ]
    axes = ("gx", "gy")
    other = lax.dynamic_index_in_dim(right_side, 1 - rhs, 0, keepdims=False)
    swapped = lax.ppermute(jnp.concatenate([other, slowness[None]], axis=0), axes, own)

    total_y = size_y * grid_cols
    cells = lax.dynamic_index_in_dim(source_cells, rhs, 0, keepdims=True)
    near_y = cells // cells_z % total_y - col * size_y
    places = []
    for tile_row in (row, row + 1 - 2 * core):
        near_x = cells // (total_y * cells_z) - tile_row * size_x
        inside = (near_x >= 0) & (near_x < size_x) & (near_y >= 0) & (near_y < size_y)
        folded = jnp.where(near_x < size_x // 2, near_x, size_x + size_x // 2 - 1 - near_x)
        places.append(jnp.where(inside, folded * size_y + near_y, -1))
    amplitudes = lax.dynamic_index_in_dim(source_amplitudes, rhs, 0, keepdims=False).T[:, None, :]

    depth = cells % cells_z
    prep_tables = [t[name] for name in PREP]
    one = (shaped(rows, 2 * cells_z), shaped(2, rows, cells_z))
    own_modes, own_contrast = pl.pallas_call(
        functools.partial(prep_kernel, cells_x),
        out_shape=one,
        in_specs=[scalars()] + [whole()] * 8,
        out_specs=(whole(), whole()),
        compiler_params=PARAMS,
        cost_estimate=SOLVE_COST,
        name="prep",
    )(rhs_ref, right_side, slowness, places[0], depth, amplitudes, *prep_tables)
    modes, contrast = pl.pallas_call(
        functools.partial(prep_other_kernel, cells_x),
        out_shape=(shaped(2, rows, 2 * cells_z), shaped(2, 2, rows, cells_z)),
        in_specs=[scalars()] + [whole()] * 9,
        out_specs=(whole(), whole()),
        compiler_params=PARAMS,
        cost_estimate=SOLVE_COST,
        name="prep_other",
    )(core_ref, swapped, own_modes, own_contrast, places[1], depth, amplitudes, *prep_tables)

    beat_tables = [t[name] for name in BEAT]

    def solve(tile, active, trace_x, trace_y, state, sends):
        total, term, *out = pl.pallas_call(
            functools.partial(beat_kernel, tile, sends),
            out_shape=(shaped(rows, 2 * cells_z),) * 2 + (shaped(*zero_x.shape), shaped(*zero_y.shape))[:sends],
            in_specs=[scalars()] + [whole()] * (6 + len(BEAT)),
            out_specs=(whole(),) * (2 + sends),
            input_output_aliases={5: 0, 6: 1},
            compiler_params=PARAMS,
            cost_estimate=SOLVE_COST,
            name="upper" if tile == 0 else "lower",
        )(active, modes, contrast, trace_x, trace_y, *state, *beat_tables)
        return (total, term), out

    def hand_on(trace):
        return pl.pallas_call(
            hand_on_kernel,
            out_shape=shaped(*trace.shape),
            in_specs=[whole()],
            out_specs=whole(),
            compiler_params=PARAMS,
            name="hand_on",
        )(trace)

    zero_x = jnp.zeros((2 * size_y, 2 * cells_z), F32)
    zero_y = jnp.zeros((2 * size_x, 2 * cells_z), F32)
    trace_x, trace_y0, trace_y1 = zero_x, zero_y, zero_y
    states = [[jnp.zeros((rows, 2 * cells_z), F32)] * 2 for _ in range(2)]
    for beat in range(chips + grid_cols - 1):
        active = (row // 2 + col == beat).astype(jnp.int32)[None]
        here = [(k, beat - k) for k in range(chips) if 0 <= beat - k < grid_cols]
        along_x = between([((k, j), (k + 1, j)) for k, j in here if k + 1 < chips])
        along_y = between([((k, j), (k, j + 1)) for k, j in here if j + 1 < grid_cols])
        more = beat < chips + grid_cols - 2
        states[0], (inner_x, *out_y0) = solve(0, active, trace_x, trace_y0, states[0], 1 + more)
        if along_y:
            trace_y0 = hand_on(lax.ppermute(out_y0[0], axes, along_y))
        states[1], out = solve(1, active, inner_x, trace_y1, states[1], 2 * more)
        if along_x:
            trace_x = lax.ppermute(out[0], axes, along_x)
        if along_y:
            trace_y1 = lax.ppermute(out[1], axes, along_y)

    edge_x, edge_y = pl.pallas_call(
        edge_kernel,
        out_shape=(shaped(*zero_x.shape), shaped(2, *zero_y.shape)),
        in_specs=[whole()] * 4,
        out_specs=(whole(), whole()),
        compiler_params=PARAMS,
        name="edges",
    )(states[0][0], states[1][0], t["first"], t["right_z"])

    every = [(k, j) for k in range(chips) for j in range(grid_cols)]
    after_x = lax.ppermute(edge_x, axes, between([((k, j), (k - 1, j)) for k, j in every if k]))
    after_y = lax.ppermute(edge_y, axes, between([((k, j), (k, j - 1)) for k, j in every if j]))

    half = shaped(2, 2, size_x, size_y, cells_z)
    keep, give = pl.pallas_call(
        functools.partial(finish_kernel, cells_x),
        out_shape=(half, half),
        in_specs=[scalars()] + [whole()] * (5 + len(FINISH)),
        out_specs=(whole(), whole()),
        scratch_shapes=[pltpu.VMEM((2, 2, 2, size_x, size_y, cells_z), F32)],
        compiler_params=PARAMS,
        name="finish",
    )(core_ref, *states[0], *states[1], contrast, *[t[name] for name in FINISH])
    got = lax.ppermute(give, axes, own)

    keep_y = lax.dynamic_index_in_dim(after_y, core, 0, keepdims=False)
    pass_y = lax.dynamic_index_in_dim(after_y, 1 - core, 0, keepdims=False)
    got_edge = lax.ppermute(jnp.concatenate([after_x, pass_y], axis=0), axes, own)
    keep_rest = pl.pallas_call(
        keep_kernel,
        out_shape=shaped(*half.shape[1:]),
        in_specs=[scalars()] + [whole()] * 3,
        out_specs=whole(),
        compiler_params=PARAMS,
        cost_estimate=KEEP_COST,
        name="keep",
    )(core_ref, keep, after_x, keep_y)
    wavefield = pl.pallas_call(
        place_wave_kernel,
        out_shape=shaped(*right_side.shape),
        in_specs=[scalars()] + [whole()] * 2,
        out_specs=anywhere(),
        scratch_shapes=[pltpu.SemaphoreType.DMA((2,))],
        compiler_params=PARAMS,
        cost_estimate=KEEP_COST,
        name="place_wave",
    )(rhs_ref, keep, got)
    residual = pl.pallas_call(
        place_rest_kernel,
        out_shape=shaped(*right_side.shape),
        in_specs=[scalars()] * 2 + [whole()] * 3,
        out_specs=anywhere(),
        scratch_shapes=[
            pltpu.VMEM((2, size_x, size_y, cells_z), F32),
            pltpu.SemaphoreType.DMA((2,)),
        ],
        compiler_params=PARAMS,
        name="place_rest",
    )(core_ref, rhs_ref, keep_rest, got, got_edge)
    return wavefield, residual


def solution(mesh):
    return jax.shard_map(
        body,
        mesh=mesh,
        in_specs=(P(None, None, "gx", "gy", None), P("gx", "gy", None), P(), P()),
        out_specs=(P(None, None, "gx", "gy", None), P(None, None, "gx", "gy", None)),
        check_vma=False,
    )
```

```python
import functools
import math

import jax
import jax.numpy as jnp
import ml_dtypes
import numpy as np
from jax import lax
from jax.experimental import pallas as pl
from jax.experimental.pallas import tpu as pltpu
from jax.sharding import PartitionSpec as P

KAPPA = 0.12
DAMPING = 0.3
BF16 = jnp.bfloat16
F32 = jnp.float32


def sine_matrix(length):
    index = np.arange(1, length + 1)
    angles = index * (math.pi / (length + 1))
    return math.sqrt(2.0 / (length + 1)) * np.sin(angles[:, None] * index[None, :]), angles


def halves(matrix):
    high = matrix.astype(np.float32).astype(ml_dtypes.bfloat16)
    low = (matrix - high.astype(np.float64)).astype(np.float32).astype(ml_dtypes.bfloat16)
    return high, low


def left_factor(matrix):
    high, low = halves(matrix)
    return np.concatenate([high, high, low], axis=1)


def tables(size_x, size_y, cells_z):
    sine_x, angle_x = sine_matrix(size_x)
    sine_y, angle_y = sine_matrix(size_y)
    sine_z, angle_z = sine_matrix(cells_z)
    half = size_x // 2
    order = np.concatenate([np.arange(0, size_x, 2), np.arange(1, size_x, 2)])
    cells = np.concatenate([np.arange(half), np.arange(size_x - 1, half - 1, -1)])

    def symbol(angle):
        return 2.5 - 8.0 / 3.0 * np.cos(angle) + 1.0 / 6.0 * np.cos(2.0 * angle)

    real_part = (
        symbol(angle_x)[order][:, None, None]
        + symbol(angle_y)[None, :, None]
        + (2.0 - 2.0 * np.cos(angle_z))[None, None, :]
        - KAPPA
    ).reshape(size_x * size_y, cells_z)
    denominator = real_part**2 + (KAPPA * DAMPING) ** 2
    inverse = np.stack([real_part / denominator, KAPPA * DAMPING / denominator]).astype(np.float32)

    parity = [np.kron(sine_x[order[p * half : (p + 1) * half]][:, :half], sine_y) for p in (0, 1)]
    cut = half * size_y // 2
    forward, backward = [
        np.stack([[left_factor(m[:, :cut]), left_factor(m[:, cut:])] for m in matrices])
        for matrices in (parity, [m.T for m in parity])
    ]
    high_z, low_z = halves(sine_z)
    right_z = np.concatenate([np.concatenate([high_z, low_z], axis=1)] * 2, axis=0)

    full = np.kron(sine_x[order], sine_y)
    by_cell = full.reshape(-1, size_x, size_y)
    enter_x = np.stack([-by_cell[:, 0] / 12.0, (16.0 * by_cell[:, 0] - by_cell[:, 1]) / 12.0], 1)
    enter_y = np.stack(
        [-by_cell[:, :, 0] / 12.0, (16.0 * by_cell[:, :, 0] - by_cell[:, :, 1]) / 12.0], 1
    )
    enter = left_factor(
        np.concatenate([enter_x.reshape(len(full), -1), enter_y.reshape(len(full), -1)], axis=1)
    )
    leave = left_factor(
        np.concatenate(
            [
                by_cell[:, size_x - 2 :].reshape(len(full), -1),
                by_cell[:, :, size_y - 2 :].transpose(0, 2, 1).reshape(len(full), -1),
            ],
            axis=1,
        ).T
    )
    first = left_factor(
        np.concatenate(
            [
                by_cell[:, :2].reshape(len(full), -1),
                by_cell[:, :, :2].transpose(0, 2, 1).reshape(len(full), -1),
            ],
            axis=1,
        ).T
    )
    edge = np.zeros((size_x, size_y, 1))
    edge[0] += 1.0 / 12.0
    edge[-1] += 1.0 / 12.0
    edge[:, 0] += 1.0 / 12.0
    edge[:, -1] += 1.0 / 12.0
    edge = edge[cells].reshape(size_x * size_y, 1).astype(np.float32)
    return dict(
        inverse=inverse, forward=forward, backward=backward, right_z=right_z,
        enter=enter, leave=leave, first=first, edge=edge,
    ), cells


def split(values):
    high = values.astype(BF16)
    return high, (values - high.astype(F32)).astype(BF16)


def stacked(values):
    high, low = split(values)
    return jnp.concatenate([high, low, high], axis=0)


def left_product(matrix, values):
    return jnp.dot(matrix, stacked(values), preferred_element_type=F32)


def z_transform(field, right_z):
    rows = field.shape[0]
    cells_z = field.shape[1] // 2
    high, low = split(jnp.concatenate([field[:, :cells_z], field[:, cells_z:]], axis=0))
    both = jnp.dot(jnp.concatenate([high, low], axis=1), right_z, preferred_element_type=F32)
    total = both[:, :cells_z] + both[:, cells_z:]
    return jnp.concatenate([total[:rows], total[rows:]], axis=1)


def sum_products(matrices, values):
    products = [[left_product(matrices[p, h], values[p][h]) for p in range(2)] for h in range(2)]
    return [sum(parts) for parts in zip(*products)]


def to_modes(first, second, forward):
    folded = [[join(f, s) for f, s in zip(first, second)] for join in (jnp.add, jnp.subtract)]
    return sum_products(forward, folded)


def to_cells(modes, backward):
    even, odd = sum_products(backward, modes)
    return even + odd, even - odd


def in_two(values):
    count = values.shape[0] // 2
    return values[:count], values[count:]


def in_parities(modes):
    return [in_two(part) for part in in_two(modes)]


def whole_field(first, second):
    return jnp.concatenate([first, second], axis=0)


def times(real_part, imag_part, field):
    lanes = field.shape[1] // 2
    real, imag = field[:, :lanes], field[:, lanes:]
    return jnp.concatenate(
        [real_part * real - imag_part * imag, real_part * imag + imag_part * real], axis=1
    )


def divide(modes, inverse):
    return times(inverse[0], inverse[1], modes)


def solve_modes(start, contrast, t):
    count = start.shape[0] // 4
    term = in_parities(start)
    total = term
    for _ in range(2):
        first, second = [in_two(cells) for cells in to_cells(term, t["backward"])]
        blocks = [z_transform(jnp.concatenate(pair, axis=0), t["right_z"]) for pair in zip(first, second)]
        parts = []
        for h, block in enumerate(blocks):
            here = [slice(at, at + count) for at in (h * count, (h + 2) * count)]
            factor = [jnp.concatenate([contrast[c, rows] for rows in here], axis=0) for c in range(2)]
            parts.append(in_two(z_transform(times(*factor, block), t["right_z"])))
        modes = to_modes(*zip(*parts), t["forward"])
        term = []
        for p in range(2):
            halves = []
            for h, part in enumerate(in_two(modes[p])):
                here = slice((2 * p + h) * count, (2 * p + h + 1) * count)
                halves.append(times(t["inverse"][0, here], t["inverse"][1, here], part))
            term.append(halves)
        total = [[a + b for a, b in zip(*pair)] for pair in zip(total, term)]
    return [jnp.concatenate([part for pair in both for part in pair], axis=0) for both in (total, term)]


PREP = ("edge", "inverse", "forward", "right_z")
BEAT = ("inverse", "forward", "backward", "right_z", "enter", "leave")


def hand_on_kernel(in_ref, out_ref):
    out_ref[...] = in_ref[...]


def prepare(dense, slow, place, depth, amplitude, edge, inverse, forward, right_z, modes_ref, contrast_ref):
    rows, cells_z = contrast_ref.shape[1:]
    points = place.shape[1]
    row_ids = lax.broadcasted_iota(jnp.int32, (rows, points), 0)
    lane_ids = lax.broadcasted_iota(jnp.int32, (cells_z, points), 0)
    at_lane = (lane_ids == depth).astype(F32)
    spread = []
    for c in range(2):
        amp = amplitude[c]
        one = amp.astype(BF16).astype(F32)
        two = (amp - one).astype(BF16).astype(F32)
        parts = [at_lane * part for part in (one, two, amp - one - two)]
        spread.append(jnp.concatenate(parts, axis=1).astype(BF16))
    scaled = KAPPA * (slow - 1.0)
    contrast_ref[0] = scaled - edge
    contrast_ref[1] = DAMPING * scaled
    at_row = (row_ids == place).astype(F32).astype(BF16)
    field = lax.dot_general(
        jnp.concatenate([at_row] * 3, axis=1), jnp.concatenate(spread, axis=0),
        (((1,), (1,)), ((), ())), preferred_element_type=F32,
    )
    first, second = [in_two(part) for part in in_two(z_transform(field + dense, right_z))]
    modes_ref[...] = divide(jnp.concatenate(to_modes(first, second, forward), axis=0), inverse)


def prep_kernel(cells_x, rhs_ref, right_ref, slow_ref, place_ref, depth_ref, amp_ref, edge_ref,
                inverse_ref, forward_ref, z_ref, modes_ref, contrast_ref):
    dense = [jnp.concatenate([right_ref[rhs_ref[0], c, x] for x in cells_x], axis=0) for c in range(2)]
    slow = jnp.concatenate([slow_ref[x] for x in cells_x], axis=0)
    prepare(
        jnp.concatenate(dense, axis=1), slow, place_ref[...], depth_ref[...], amp_ref, edge_ref[...],
        inverse_ref, forward_ref, z_ref[...], modes_ref, contrast_ref,
    )


def prep_other_kernel(cells_x, core_ref, swap_ref, own_modes_ref, own_contrast_ref, place_ref, depth_ref,
                      amp_ref, edge_ref, inverse_ref, forward_ref, z_ref, modes_ref, contrast_ref):
    core = core_ref[0]
    other = 1 - core
    modes_ref[core] = own_modes_ref[...]
    contrast_ref[core] = own_contrast_ref[...]
    parts = [jnp.concatenate([swap_ref[c, x] for x in cells_x], axis=0) for c in range(3)]
    prepare(
        jnp.concatenate(parts[:2], axis=1), parts[2], place_ref[...], depth_ref[...], amp_ref,
        edge_ref[...], inverse_ref, forward_ref, z_ref[...], modes_ref.at[other], contrast_ref.at[other],
    )


def beat_kernel(tile, final, active_ref, modes_ref, contrast_ref, trace_x_ref, trace_y_ref, total_ref, term_ref,
                *refs):
    names = LAST if final else BEAT
    t = {name: ref for name, ref in zip(names, refs)}
    new_total_ref, new_term_ref, *out_refs = refs[len(names) :]
    count = trace_x_ref.shape[0]

    @pl.when(active_ref[0] == 1)
    def _():
        local = dict(t, right_z=t["right_z"][...])
        trace = jnp.concatenate([trace_x_ref[...], trace_y_ref[...]], axis=0)
        start = modes_ref[tile] + divide(left_product(t["enter"][...], trace), t["inverse"])
        total, term = solve_modes(start, contrast_ref.at[tile], local)
        new_total_ref[...] = total
        new_term_ref[...] = term
        if not (final and tile == 1):
            out = left_product(t["leave"][...], total)
            for out_ref, part in zip(out_refs[:1] if final else out_refs, (out[:count], out[count:])):
                out_ref[...] = part

    @pl.when(active_ref[0] == 0)
    def _():
        new_total_ref[...] = total_ref[...]
        new_term_ref[...] = term_ref[...]

    if final:
        out = left_product(t["first"][...], new_total_ref[...])
        edge_refs = out_refs[1 - tile :]
        edge_refs[-1][...] = out[count:]
        if tile == 0:
            edge_refs[0][...] = out[:count]


LAST = BEAT + ("first",)
FINISH = ("backward", "right_z")


def finish_kernel(cells_x, core_ref, total0_ref, term0_ref, total1_ref, term1_ref, contrast_ref, backward_ref,
                  z_ref, keep_ref, give_ref, both_ref):
    _, _, _, size_x, size_y, cells_z = both_ref.shape
    right_z = z_ref[...]
    for tile, (total_ref, term_ref) in enumerate(((total0_ref, term0_ref), (total1_ref, term1_ref))):
        wave, rest = [
            z_transform(whole_field(*to_cells(in_parities(ref[...]), backward_ref)), right_z)
            for ref in (total_ref, term_ref)
        ]
        rest = times(contrast_ref[tile, 0], contrast_ref[tile, 1], rest)
        for place, x in enumerate(cells_x):
            here = slice(place * size_y, (place + 1) * size_y)
            for c in range(2):
                there = slice(c * cells_z, (c + 1) * cells_z)
                both_ref[tile, 0, c, x] = wave[here, there]
                both_ref[tile, 1, c, x] = rest[here, there]
                if tile == 1 and x < 2:
                    layer = wave[here, there]
                    if x == 0:
                        both_ref[0, 1, c, size_x - 2] += layer * (-1.0 / 12.0)
                        both_ref[0, 1, c, size_x - 1] += layer * (16.0 / 12.0)
                    else:
                        both_ref[0, 1, c, size_x - 1] += layer * (-1.0 / 12.0)
    keep_ref[...] = both_ref[core_ref[0]]
    give_ref[...] = both_ref[1 - core_ref[0]]


def add_later(rest_ref, edge_x, edge_y, lower):
    _, size_x, size_y, cells_z = rest_ref.shape
    for c in range(2):
        there = slice(c * cells_z, (c + 1) * cells_z)
        near, far = edge_x[:size_y, there] * lower, edge_x[size_y:, there] * lower
        rest_ref[c, size_x - 2] += near * (-1.0 / 12.0)
        rest_ref[c, size_x - 1] += (16.0 * near - far) * (1.0 / 12.0)
        near, far = edge_y[:size_x, there], edge_y[size_x:, there]
        two = jnp.stack([near * (-1.0 / 12.0), (16.0 * near - far) * (1.0 / 12.0)], axis=1)
        rest_ref[c, :, size_y - 2 :] += two


def keep_kernel(core_ref, keep_ref, edge_x_ref, edge_y_ref, z_ref, rest_ref):
    rest_ref[...] = keep_ref[1]
    count = edge_x_ref.shape[0]
    edges = jnp.concatenate([edge_x_ref[...], edge_y_ref[core_ref[0]]], axis=0)
    edges = z_transform(edges, z_ref[...])
    add_later(rest_ref, edges[:count], edges[count:], (core_ref[0] == 1).astype(F32))


def place_wave_kernel(rhs_ref, keep_ref, got_ref, wave_ref, sems):
    rhs = rhs_ref[0]
    copies = [
        pltpu.make_async_copy(keep_ref.at[0], wave_ref.at[rhs], sems.at[0]),
        pltpu.make_async_copy(got_ref.at[0], wave_ref.at[1 - rhs], sems.at[1]),
    ]
    for copy in copies:
        copy.start()
    for copy in copies:
        copy.wait()


def place_rest_kernel(core_ref, rhs_ref, keep_rest_ref, got_ref, got_edge_ref, z_ref, rest_ref, work_ref, sems):
    rhs = rhs_ref[0]
    count = got_edge_ref.shape[0] // 2
    copies = [pltpu.make_async_copy(keep_rest_ref, rest_ref.at[rhs], sems.at[0])]
    copies[0].start()
    work_ref[...] = got_ref[1]
    edges = z_transform(got_edge_ref[...], z_ref[...])
    add_later(work_ref, edges[:count], edges[count:], (core_ref[0] == 1).astype(F32))
    copies.append(pltpu.make_async_copy(work_ref, rest_ref.at[1 - rhs], sems.at[1]))
    copies[1].start()
    for copy in copies:
        copy.wait()


def whole():
    return pl.BlockSpec(memory_space=pltpu.VMEM)


def scalars():
    return pl.BlockSpec(memory_space=pltpu.SMEM)


def anywhere():
    return pl.BlockSpec(memory_space=pl.ANY)


SOLVE_COST = pl.CostEstimate(flops=2 * 10**9, bytes_accessed=2 * 10**6, transcendentals=0)
KEEP_COST = pl.CostEstimate(flops=10**10, bytes_accessed=10**6, transcendentals=0)
PARAMS = pltpu.CompilerParams(vmem_limit_bytes=24 * 1024 * 1024)


def shaped(*shape):
    return jax.ShapeDtypeStruct(shape, F32)


def body(right_side, slowness, source_cells, source_amplitudes):
    sources, _, size_x, size_y, cells_z = right_side.shape
    grid_rows, grid_cols = lax.axis_size("gx"), lax.axis_size("gy")
    assert sources == 2 and grid_rows % 2 == 0 and size_x % 2 == 0
    chips = grid_rows // 2
    row, col = lax.axis_index("gx"), lax.axis_index("gy")
    core = row % 2
    rhs = (core + row // 2 + col) % 2
    core_ref, rhs_ref = core[None], rhs[None]
    t, cells_x = tables(size_x, size_y, cells_z)
    t = {name: jnp.asarray(value) for name, value in t.items()}
    cells_x = tuple(int(x) for x in cells_x)
    rows = size_x * size_y

    def device(chip, core, column):
        return (2 * chip + core) * grid_cols + column

    def between(pairs):
        return [
            (device(a, r, b), device(c, 1 - r, d)) for (a, b), (c, d) in pairs for r in range(2)
        ]

    own = [
        (device(k, r, j), device(k, 1 - r, j))
        for k in range(chips) for j in range(grid_cols) for r in range(2)
    ]
    axes = ("gx", "gy")
    other = lax.dynamic_index_in_dim(right_side, 1 - rhs, 0, keepdims=False)
    swapped = lax.ppermute(jnp.concatenate([other, slowness[None]], axis=0), axes, own)

    total_y = size_y * grid_cols
    cells = lax.dynamic_index_in_dim(source_cells, rhs, 0, keepdims=True)
    near_y = cells // cells_z % total_y - col * size_y
    places = []
    for tile_row in (row, row + 1 - 2 * core):
        near_x = cells // (total_y * cells_z) - tile_row * size_x
        inside = (near_x >= 0) & (near_x < size_x) & (near_y >= 0) & (near_y < size_y)
        folded = jnp.where(near_x < size_x // 2, near_x, size_x + size_x // 2 - 1 - near_x)
        places.append(jnp.where(inside, folded * size_y + near_y, -1))
    amplitudes = lax.dynamic_index_in_dim(source_amplitudes, rhs, 0, keepdims=False).T[:, None, :]

    depth = cells % cells_z
    prep_tables = [t[name] for name in PREP]
    one = (shaped(rows, 2 * cells_z), shaped(2, rows, cells_z))
    own_modes, own_contrast = pl.pallas_call(
        functools.partial(prep_kernel, cells_x),
        out_shape=one,
        in_specs=[scalars()] + [whole()] * 9,
        out_specs=(whole(), whole()),
        compiler_params=PARAMS,
        cost_estimate=SOLVE_COST,
        name="prep",
    )(rhs_ref, right_side, slowness, places[0], depth, amplitudes, *prep_tables)
    modes, contrast = pl.pallas_call(
        functools.partial(prep_other_kernel, cells_x),
        out_shape=(shaped(2, rows, 2 * cells_z), shaped(2, 2, rows, cells_z)),
        in_specs=[scalars()] + [whole()] * 10,
        out_specs=(whole(), whole()),
        compiler_params=PARAMS,
        cost_estimate=SOLVE_COST,
        name="prep_other",
    )(core_ref, swapped, own_modes, own_contrast, places[1], depth, amplitudes, *prep_tables)

    def solve(tile, active, trace_x, trace_y, state, final):
        x, y = shaped(*zero_x.shape), shaped(*zero_y.shape)
        outs = ((x, x, y), (y,))[tile] if final else (x, y)
        total, term, *outs = pl.pallas_call(
            functools.partial(beat_kernel, tile, final),
            out_shape=(shaped(rows, 2 * cells_z),) * 2 + outs,
            in_specs=[scalars()] + [whole()] * (6 + len(LAST if final else BEAT)),
            out_specs=(whole(),) * (2 + len(outs)),
            input_output_aliases={5: 0, 6: 1},
            compiler_params=PARAMS,
            cost_estimate=SOLVE_COST,
            name="upper" if tile == 0 else "lower",
        )(active, modes, contrast, trace_x, trace_y, *state, *[t[name] for name in (LAST if final else BEAT)])
        return (total, term), outs

    def hand_on(trace):
        return pl.pallas_call(
            hand_on_kernel,
            out_shape=shaped(*trace.shape),
            in_specs=[whole()],
            out_specs=whole(),
            compiler_params=PARAMS,
            name="hand_on",
        )(trace)

    zero_x = jnp.zeros((2 * size_y, 2 * cells_z), F32)
    zero_y = jnp.zeros((2 * size_x, 2 * cells_z), F32)
    trace_x, trace_y0, trace_y1 = zero_x, zero_y, zero_y
    states = [[jnp.zeros((rows, 2 * cells_z), F32)] * 2 for _ in range(2)]
    for beat in range(chips + grid_cols - 1):
        active = (row // 2 + col == beat).astype(jnp.int32)[None]
        here = [(k, beat - k) for k in range(chips) if 0 <= beat - k < grid_cols]
        along_x = between([((k, j), (k + 1, j)) for k, j in here if k + 1 < chips])
        along_y = between([((k, j), (k, j + 1)) for k, j in here if j + 1 < grid_cols])
        final = beat == chips + grid_cols - 2
        states[0], (inner_x, *outs0) = solve(0, active, trace_x, trace_y0, states[0], final)
        if along_y:
            trace_y0 = hand_on(lax.ppermute(outs0[0], axes, along_y))
        states[1], outs1 = solve(1, active, inner_x, trace_y1, states[1], final)
        if along_x:
            trace_x = lax.ppermute(outs1[0], axes, along_x)
        if along_y:
            trace_y1 = lax.ppermute(outs1[1], axes, along_y)
    edge_x, edge_y0 = outs0
    edge_y = jnp.stack([edge_y0, outs1[0]])

    every = [(k, j) for k in range(chips) for j in range(grid_cols)]
    after_x = lax.ppermute(edge_x, axes, between([((k, j), (k - 1, j)) for k, j in every if k]))
    after_y = lax.ppermute(edge_y, axes, between([((k, j), (k, j - 1)) for k, j in every if j]))

    half = shaped(2, 2, size_x, size_y, cells_z)
    keep, give = pl.pallas_call(
        functools.partial(finish_kernel, cells_x),
        out_shape=(half, half),
        in_specs=[scalars()] + [whole()] * (5 + len(FINISH)),
        out_specs=(whole(), whole()),
        scratch_shapes=[pltpu.VMEM((2, 2, 2, size_x, size_y, cells_z), F32)],
        compiler_params=PARAMS,
        name="finish",
    )(core_ref, *states[0], *states[1], contrast, *[t[name] for name in FINISH])
    got = lax.ppermute(give, axes, own)

    pass_y = lax.dynamic_index_in_dim(after_y, 1 - core, 0, keepdims=False)
    got_edge = lax.ppermute(jnp.concatenate([after_x, pass_y], axis=0), axes, own)
    keep_rest = pl.pallas_call(
        keep_kernel,
        out_shape=shaped(*half.shape[1:]),
        in_specs=[scalars()] + [whole()] * 4,
        out_specs=whole(),
        compiler_params=PARAMS,
        cost_estimate=KEEP_COST,
        name="keep",
    )(core_ref, keep, after_x, after_y, t["right_z"])
    wavefield = pl.pallas_call(
        place_wave_kernel,
        out_shape=shaped(*right_side.shape),
        in_specs=[scalars()] + [whole()] * 2,
        out_specs=anywhere(),
        scratch_shapes=[pltpu.SemaphoreType.DMA((2,))],
        compiler_params=PARAMS,
        cost_estimate=KEEP_COST,
        name="place_wave",
    )(rhs_ref, keep, got)
    residual = pl.pallas_call(
        place_rest_kernel,
        out_shape=shaped(*right_side.shape),
        in_specs=[scalars()] * 2 + [whole()] * 4,
        out_specs=anywhere(),
        scratch_shapes=[
            pltpu.VMEM((2, size_x, size_y, cells_z), F32),
            pltpu.SemaphoreType.DMA((2,)),
        ],
        compiler_params=PARAMS,
        name="place_rest",
    )(core_ref, rhs_ref, keep_rest, got, got_edge, t["right_z"])
    return wavefield, residual


def solution(mesh):
    return jax.shard_map(
        body,
        mesh=mesh,
        in_specs=(P(None, None, "gx", "gy", None), P("gx", "gy", None), P(), P()),
        out_specs=(P(None, None, "gx", "gy", None), P(None, None, "gx", "gy", None)),
        check_vma=False,
    )
```

```python
import functools
import math

import jax
import jax.numpy as jnp
import ml_dtypes
import numpy as np
from jax import lax
from jax.experimental import pallas as pl
from jax.experimental.pallas import tpu as pltpu
from jax.sharding import PartitionSpec as P

KAPPA = 0.12
DAMPING = 0.3
BF16 = jnp.bfloat16
F32 = jnp.float32


def sine_matrix(length):
    index = np.arange(1, length + 1)
    angles = index * (math.pi / (length + 1))
    return math.sqrt(2.0 / (length + 1)) * np.sin(angles[:, None] * index[None, :]), angles


def halves(matrix):
    high = matrix.astype(np.float32).astype(ml_dtypes.bfloat16)
    low = (matrix - high.astype(np.float64)).astype(np.float32).astype(ml_dtypes.bfloat16)
    return high, low


def left_factor(matrix):
    high, low = halves(matrix)
    return np.concatenate([high, high, low], axis=1)


def tables(size_x, size_y, cells_z):
    sine_x, angle_x = sine_matrix(size_x)
    sine_y, angle_y = sine_matrix(size_y)
    sine_z, angle_z = sine_matrix(cells_z)
    half = size_x // 2
    order = np.concatenate([np.arange(0, size_x, 2), np.arange(1, size_x, 2)])
    cells = np.concatenate([np.arange(half), np.arange(size_x - 1, half - 1, -1)])

    def symbol(angle):
        return 2.5 - 8.0 / 3.0 * np.cos(angle) + 1.0 / 6.0 * np.cos(2.0 * angle)

    real_part = (
        symbol(angle_x)[order][:, None, None]
        + symbol(angle_y)[None, :, None]
        + (2.0 - 2.0 * np.cos(angle_z))[None, None, :]
        - KAPPA
    ).reshape(size_x * size_y, cells_z)
    denominator = real_part**2 + (KAPPA * DAMPING) ** 2
    inverse = np.stack([real_part / denominator, KAPPA * DAMPING / denominator]).astype(np.float32)

    parity = [np.kron(sine_x[order[p * half : (p + 1) * half]][:, :half], sine_y) for p in (0, 1)]
    forward = [left_factor(m) for m in parity]
    backward = [left_factor(m.T) for m in parity]
    high_z, low_z = halves(sine_z)
    right_z = np.concatenate([np.concatenate([high_z, low_z], axis=1)] * 2, axis=0)

    full = np.kron(sine_x[order], sine_y)
    by_cell = full.reshape(-1, size_x, size_y)
    enter_x = np.stack([-by_cell[:, 0] / 12.0, (16.0 * by_cell[:, 0] - by_cell[:, 1]) / 12.0], 1)
    enter_y = np.stack(
        [-by_cell[:, :, 0] / 12.0, (16.0 * by_cell[:, :, 0] - by_cell[:, :, 1]) / 12.0], 1
    )
    enter = left_factor(
        np.concatenate([enter_x.reshape(len(full), -1), enter_y.reshape(len(full), -1)], axis=1)
    )
    leave = left_factor(
        np.concatenate(
            [
                by_cell[:, size_x - 2 :].reshape(len(full), -1),
                by_cell[:, :, size_y - 2 :].transpose(0, 2, 1).reshape(len(full), -1),
            ],
            axis=1,
        ).T
    )
    first = left_factor(
        np.concatenate(
            [
                by_cell[:, :2].reshape(len(full), -1),
                by_cell[:, :, :2].transpose(0, 2, 1).reshape(len(full), -1),
            ],
            axis=1,
        ).T
    )
    edge = np.zeros((size_x, size_y, 1))
    edge[0] += 1.0 / 12.0
    edge[-1] += 1.0 / 12.0
    edge[:, 0] += 1.0 / 12.0
    edge[:, -1] += 1.0 / 12.0
    edge = edge[cells].reshape(1, size_x * size_y, 1) + np.zeros((1, 1, cells_z))
    fields = np.concatenate([inverse, edge.astype(np.float32)], axis=0)

    matrices = dict(
        forward0=forward[0], forward1=forward[1], backward0=backward[0], backward1=backward[1],
        right_z=right_z, enter=enter, leave=leave, first=first,
    )
    width = 128 * max(-(-m.shape[1] // 128) for m in matrices.values())
    places, rows, at = {}, 0, 0
    height = 0
    for name, m in sorted(matrices.items(), key=lambda item: -item[1].shape[0]):
        if at + m.shape[1] > width:
            rows, at, height = rows + height, 0, 0
        places[name] = (rows, at, *m.shape)
        height = max(height, -(-m.shape[0] // 16) * 16)
        at += -(-m.shape[1] // 128) * 128
    packed = np.zeros((rows + height, width), ml_dtypes.bfloat16)
    for name, (row, lane, count, lanes) in places.items():
        packed[row : row + count, lane : lane + lanes] = matrices[name]
    return fields, packed, places, tuple(int(x) for x in cells)


class Tables:
    def __init__(self, places, fields_ref, packed_ref):
        self.places, self.fields, self.packed = places, fields_ref, packed_ref

    def __getitem__(self, name):
        row, lane, count, lanes = self.places[name]
        return self.packed[row : row + count, lane : lane + lanes]

    def divide(self, modes):
        return times(self.fields[0], self.fields[1], modes)


def split(values):
    high = values.astype(BF16)
    return high, (values - high.astype(F32)).astype(BF16)


def stacked(values):
    high, low = split(values)
    return jnp.concatenate([high, low, high], axis=0)


def left_product(matrix, values):
    return jnp.dot(matrix, stacked(values), preferred_element_type=F32)


def z_transform(field, t):
    rows = field.shape[0]
    cells_z = field.shape[1] // 2
    high, low = split(jnp.concatenate([field[:, :cells_z], field[:, cells_z:]], axis=0))
    both = jnp.dot(jnp.concatenate([high, low], axis=1), t["right_z"], preferred_element_type=F32)
    total = both[:, :cells_z] + both[:, cells_z:]
    return jnp.concatenate([total[:rows], total[rows:]], axis=1)


def to_modes(field, t):
    count = field.shape[0] // 2
    first, second = field[:count], field[count:]
    return jnp.concatenate(
        [left_product(t["forward0"], first + second), left_product(t["forward1"], first - second)], axis=0
    )


def to_cells(modes, t):
    count = modes.shape[0] // 2
    even = left_product(t["backward0"], modes[:count])
    odd = left_product(t["backward1"], modes[count:])
    return jnp.concatenate([even + odd, even - odd], axis=0)


def times(real_part, imag_part, field):
    lanes = field.shape[1] // 2
    real, imag = field[:, :lanes], field[:, lanes:]
    return jnp.concatenate(
        [real_part * real - imag_part * imag, real_part * imag + imag_part * real], axis=1
    )


def apply_contrast(field, contrast, t, block=64):
    done = []
    for start in range(0, field.shape[0], block):
        here = slice(start, start + block)
        cells = times(contrast[0, here], contrast[1, here], z_transform(field[here], t))
        done.append(z_transform(cells, t))
    return jnp.concatenate(done, axis=0)


def solve_modes(start, contrast, t):
    term = total = start
    for _ in range(2):
        term = t.divide(to_modes(apply_contrast(to_cells(term, t), contrast, t), t))
        total = total + term
    return total, term


def prepare(dense, slow, place, depth, amplitude, t, modes_ref, contrast_ref):
    rows, cells_z = contrast_ref.shape[1:]
    points = place.shape[1]
    row_ids = lax.broadcasted_iota(jnp.int32, (rows, points), 0)
    lane_ids = lax.broadcasted_iota(jnp.int32, (cells_z, points), 0)
    at_lane = (lane_ids == depth).astype(F32)
    spread = []
    for c in range(2):
        amp = amplitude[c]
        one = amp.astype(BF16).astype(F32)
        two = (amp - one).astype(BF16).astype(F32)
        parts = [at_lane * part for part in (one, two, amp - one - two)]
        spread.append(jnp.concatenate(parts, axis=1).astype(BF16))
    scaled = KAPPA * (slow - 1.0)
    contrast_ref[0] = scaled - t.fields[2]
    contrast_ref[1] = DAMPING * scaled
    at_row = (row_ids == place).astype(F32).astype(BF16)
    field = lax.dot_general(
        jnp.concatenate([at_row] * 3, axis=1), jnp.concatenate(spread, axis=0),
        (((1,), (1,)), ((), ())), preferred_element_type=F32,
    )
    modes_ref[...] = t.divide(to_modes(z_transform(field + dense, t), t))


def hand_on_kernel(in_ref, out_ref):
    out_ref[...] = in_ref[...]


def prep_kernel(cells_x, places, rhs_ref, right_ref, slow_ref, place_ref, depth_ref, amp_ref, fields_ref,
                packed_ref, modes_ref, contrast_ref):
    dense = [jnp.concatenate([right_ref[rhs_ref[0], c, x] for x in cells_x], axis=0) for c in range(2)]
    slow = jnp.concatenate([slow_ref[x] for x in cells_x], axis=0)
    prepare(
        jnp.concatenate(dense, axis=1), slow, place_ref[...], depth_ref[...], amp_ref,
        Tables(places, fields_ref, packed_ref), modes_ref, contrast_ref,
    )


def prep_other_kernel(cells_x, places, core_ref, swap_ref, own_modes_ref, own_contrast_ref, place_ref, depth_ref,
                      amp_ref, fields_ref, packed_ref, modes_ref, contrast_ref):
    core = core_ref[0]
    other = 1 - core
    modes_ref[core] = own_modes_ref[...]
    contrast_ref[core] = own_contrast_ref[...]
    parts = [jnp.concatenate([swap_ref[c, x] for x in cells_x], axis=0) for c in range(3)]
    prepare(
        jnp.concatenate(parts[:2], axis=1), parts[2], place_ref[...], depth_ref[...], amp_ref,
        Tables(places, fields_ref, packed_ref), modes_ref.at[other], contrast_ref.at[other],
    )


def beat_kernel(tile, final, places, active_ref, modes_ref, contrast_ref, trace_x_ref, trace_y_ref, total_ref,
                term_ref, fields_ref, packed_ref, new_total_ref, new_term_ref, *out_refs):
    t = Tables(places, fields_ref, packed_ref)
    count = trace_x_ref.shape[0]

    @pl.when(active_ref[0] == 1)
    def _():
        trace = jnp.concatenate([trace_x_ref[...], trace_y_ref[...]], axis=0)
        start = modes_ref[tile] + t.divide(left_product(t["enter"], trace))
        total, term = solve_modes(start, contrast_ref.at[tile], t)
        new_total_ref[...] = total
        new_term_ref[...] = term
        if not (final and tile == 1):
            out = left_product(t["leave"], total)
            for out_ref, part in zip(out_refs[:1] if final else out_refs, (out[:count], out[count:])):
                out_ref[...] = part

    @pl.when(active_ref[0] == 0)
    def _():
        new_total_ref[...] = total_ref[...]
        new_term_ref[...] = term_ref[...]

    if final:
        out = left_product(t["first"], new_total_ref[...])
        edge_refs = out_refs[1 - tile :]
        edge_refs[-1][...] = out[count:]
        if tile == 0:
            edge_refs[0][...] = out[:count]


def finish_kernel(cells_x, places, core_ref, total0_ref, term0_ref, total1_ref, term1_ref, contrast_ref,
                  fields_ref, packed_ref, keep_ref, give_ref, both_ref):
    _, _, _, size_x, size_y, cells_z = both_ref.shape
    t = Tables(places, fields_ref, packed_ref)
    for tile, (total_ref, term_ref) in enumerate(((total0_ref, term0_ref), (total1_ref, term1_ref))):
        wave, rest = [z_transform(to_cells(ref[...], t), t) for ref in (total_ref, term_ref)]
        rest = times(contrast_ref[tile, 0], contrast_ref[tile, 1], rest)
        for place, x in enumerate(cells_x):
            here = slice(place * size_y, (place + 1) * size_y)
            for c in range(2):
                there = slice(c * cells_z, (c + 1) * cells_z)
                both_ref[tile, 0, c, x] = wave[here, there]
                both_ref[tile, 1, c, x] = rest[here, there]
                if tile == 1 and x < 2:
                    layer = wave[here, there]
                    if x == 0:
                        both_ref[0, 1, c, size_x - 2] += layer * (-1.0 / 12.0)
                        both_ref[0, 1, c, size_x - 1] += layer * (16.0 / 12.0)
                    else:
                        both_ref[0, 1, c, size_x - 1] += layer * (-1.0 / 12.0)
    keep_ref[...] = both_ref[core_ref[0]]
    give_ref[...] = both_ref[1 - core_ref[0]]


def add_later(rest_ref, edge_x, edge_y, lower):
    _, size_x, size_y, cells_z = rest_ref.shape
    for c in range(2):
        there = slice(c * cells_z, (c + 1) * cells_z)
        near, far = edge_x[:size_y, there] * lower, edge_x[size_y:, there] * lower
        rest_ref[c, size_x - 2] += near * (-1.0 / 12.0)
        rest_ref[c, size_x - 1] += (16.0 * near - far) * (1.0 / 12.0)
        near, far = edge_y[:size_x, there], edge_y[size_x:, there]
        two = jnp.stack([near * (-1.0 / 12.0), (16.0 * near - far) * (1.0 / 12.0)], axis=1)
        rest_ref[c, :, size_y - 2 :] += two


def keep_kernel(places, core_ref, keep_ref, edge_x_ref, edge_y_ref, packed_ref, rest_ref):
    rest_ref[...] = keep_ref[1]
    count = edge_x_ref.shape[0]
    edges = jnp.concatenate([edge_x_ref[...], edge_y_ref[core_ref[0]]], axis=0)
    edges = z_transform(edges, Tables(places, None, packed_ref))
    add_later(rest_ref, edges[:count], edges[count:], (core_ref[0] == 1).astype(F32))


def place_wave_kernel(rhs_ref, keep_ref, got_ref, wave_ref, sems):
    rhs = rhs_ref[0]
    copies = [
        pltpu.make_async_copy(keep_ref.at[0], wave_ref.at[rhs], sems.at[0]),
        pltpu.make_async_copy(got_ref.at[0], wave_ref.at[1 - rhs], sems.at[1]),
    ]
    for copy in copies:
        copy.start()
    for copy in copies:
        copy.wait()


def place_rest_kernel(places, core_ref, rhs_ref, keep_rest_ref, got_ref, got_edge_ref, packed_ref, rest_ref, work_ref,
                      sems):
    rhs = rhs_ref[0]
    count = got_edge_ref.shape[0] // 2
    copies = [pltpu.make_async_copy(keep_rest_ref, rest_ref.at[rhs], sems.at[0])]
    copies[0].start()
    work_ref[...] = got_ref[1]
    edges = z_transform(got_edge_ref[...], Tables(places, None, packed_ref))
    add_later(work_ref, edges[:count], edges[count:], (core_ref[0] == 1).astype(F32))
    copies.append(pltpu.make_async_copy(work_ref, rest_ref.at[1 - rhs], sems.at[1]))
    copies[1].start()
    for copy in copies:
        copy.wait()


def whole():
    return pl.BlockSpec(memory_space=pltpu.VMEM)


def scalars():
    return pl.BlockSpec(memory_space=pltpu.SMEM)


def anywhere():
    return pl.BlockSpec(memory_space=pl.ANY)


SOLVE_COST = pl.CostEstimate(flops=2 * 10**9, bytes_accessed=2 * 10**6, transcendentals=0)
KEEP_COST = pl.CostEstimate(flops=10**10, bytes_accessed=10**6, transcendentals=0)
PARAMS = pltpu.CompilerParams(vmem_limit_bytes=24 * 1024 * 1024)


def shaped(*shape):
    return jax.ShapeDtypeStruct(shape, F32)


def body(right_side, slowness, source_cells, source_amplitudes):
    sources, _, size_x, size_y, cells_z = right_side.shape
    grid_rows, grid_cols = lax.axis_size("gx"), lax.axis_size("gy")
    assert sources == 2 and grid_rows % 2 == 0 and size_x % 2 == 0
    chips = grid_rows // 2
    row, col = lax.axis_index("gx"), lax.axis_index("gy")
    core = row % 2
    rhs = (core + row // 2 + col) % 2
    core_ref, rhs_ref = core[None], rhs[None]
    fields, packed, table_places, cells_x = tables(size_x, size_y, cells_z)
    fields, packed = jnp.asarray(fields), jnp.asarray(packed)
    rows = size_x * size_y

    def device(chip, core, column):
        return (2 * chip + core) * grid_cols + column

    def between(pairs):
        return [
            (device(a, r, b), device(c, 1 - r, d)) for (a, b), (c, d) in pairs for r in range(2)
        ]

    own = [
        (device(k, r, j), device(k, 1 - r, j))
        for k in range(chips) for j in range(grid_cols) for r in range(2)
    ]
    axes = ("gx", "gy")
    other = lax.dynamic_index_in_dim(right_side, 1 - rhs, 0, keepdims=False)
    swapped = lax.ppermute(jnp.concatenate([other, slowness[None]], axis=0), axes, own)

    total_y = size_y * grid_cols
    cells = lax.dynamic_index_in_dim(source_cells, rhs, 0, keepdims=True)
    near_y = cells // cells_z % total_y - col * size_y
    places = []
    for tile_row in (row, row + 1 - 2 * core):
        near_x = cells // (total_y * cells_z) - tile_row * size_x
        inside = (near_x >= 0) & (near_x < size_x) & (near_y >= 0) & (near_y < size_y)
        folded = jnp.where(near_x < size_x // 2, near_x, size_x + size_x // 2 - 1 - near_x)
        places.append(jnp.where(inside, folded * size_y + near_y, -1))
    amplitudes = lax.dynamic_index_in_dim(source_amplitudes, rhs, 0, keepdims=False).T[:, None, :]

    depth = cells % cells_z
    one = (shaped(rows, 2 * cells_z), shaped(2, rows, cells_z))
    own_modes, own_contrast = pl.pallas_call(
        functools.partial(prep_kernel, cells_x, table_places),
        out_shape=one,
        in_specs=[scalars()] + [whole()] * 7,
        out_specs=(whole(), whole()),
        compiler_params=PARAMS,
        cost_estimate=SOLVE_COST,
        name="prep",
    )(rhs_ref, right_side, slowness, places[0], depth, amplitudes, fields, packed)
    modes, contrast = pl.pallas_call(
        functools.partial(prep_other_kernel, cells_x, table_places),
        out_shape=(shaped(2, rows, 2 * cells_z), shaped(2, 2, rows, cells_z)),
        in_specs=[scalars()] + [whole()] * 8,
        out_specs=(whole(), whole()),
        compiler_params=PARAMS,
        cost_estimate=SOLVE_COST,
        name="prep_other",
    )(core_ref, swapped, own_modes, own_contrast, places[1], depth, amplitudes, fields, packed)

    def solve(tile, active, trace_x, trace_y, state, final):
        x, y = shaped(*zero_x.shape), shaped(*zero_y.shape)
        outs = ((x, x, y), (y,))[tile] if final else (x, y)
        total, term, *outs = pl.pallas_call(
            functools.partial(beat_kernel, tile, final, table_places),
            out_shape=(shaped(rows, 2 * cells_z),) * 2 + outs,
            in_specs=[scalars()] + [whole()] * 8,
            out_specs=(whole(),) * (2 + len(outs)),
            input_output_aliases={5: 0, 6: 1},
            compiler_params=PARAMS,
            cost_estimate=SOLVE_COST,
            name="upper" if tile == 0 else "lower",
        )(active, modes, contrast, trace_x, trace_y, *state, fields, packed)
        return (total, term), outs

    def hand_on(trace):
        return pl.pallas_call(
            hand_on_kernel,
            out_shape=shaped(*trace.shape),
            in_specs=[whole()],
            out_specs=whole(),
            compiler_params=PARAMS,
            name="hand_on",
        )(trace)

    zero_x = jnp.zeros((2 * size_y, 2 * cells_z), F32)
    zero_y = jnp.zeros((2 * size_x, 2 * cells_z), F32)
    trace_x, trace_y0, trace_y1 = zero_x, zero_y, zero_y
    states = [[jnp.zeros((rows, 2 * cells_z), F32)] * 2 for _ in range(2)]
    for beat in range(chips + grid_cols - 1):
        active = (row // 2 + col == beat).astype(jnp.int32)[None]
        here = [(k, beat - k) for k in range(chips) if 0 <= beat - k < grid_cols]
        along_x = between([((k, j), (k + 1, j)) for k, j in here if k + 1 < chips])
        along_y = between([((k, j), (k, j + 1)) for k, j in here if j + 1 < grid_cols])
        final = beat == chips + grid_cols - 2
        states[0], (inner_x, *outs0) = solve(0, active, trace_x, trace_y0, states[0], final)
        if along_y:
            trace_y0 = hand_on(lax.ppermute(outs0[0], axes, along_y))
        states[1], outs1 = solve(1, active, inner_x, trace_y1, states[1], final)
        if along_x:
            trace_x = lax.ppermute(outs1[0], axes, along_x)
        if along_y:
            trace_y1 = lax.ppermute(outs1[1], axes, along_y)
    edge_x, edge_y0 = outs0
    edge_y = jnp.stack([edge_y0, outs1[0]])

    every = [(k, j) for k in range(chips) for j in range(grid_cols)]
    after_x = lax.ppermute(edge_x, axes, between([((k, j), (k - 1, j)) for k, j in every if k]))
    after_y = lax.ppermute(edge_y, axes, between([((k, j), (k, j - 1)) for k, j in every if j]))

    half = shaped(2, 2, size_x, size_y, cells_z)
    keep, give = pl.pallas_call(
        functools.partial(finish_kernel, cells_x, table_places),
        out_shape=(half, half),
        in_specs=[scalars()] + [whole()] * 7,
        out_specs=(whole(), whole()),
        scratch_shapes=[pltpu.VMEM((2, 2, 2, size_x, size_y, cells_z), F32)],
        compiler_params=PARAMS,
        name="finish",
    )(core_ref, *states[0], *states[1], contrast, fields, packed)
    got = lax.ppermute(give, axes, own)

    pass_y = lax.dynamic_index_in_dim(after_y, 1 - core, 0, keepdims=False)
    got_edge = lax.ppermute(jnp.concatenate([after_x, pass_y], axis=0), axes, own)
    keep_rest = pl.pallas_call(
        functools.partial(keep_kernel, table_places),
        out_shape=shaped(*half.shape[1:]),
        in_specs=[scalars()] + [whole()] * 4,
        out_specs=whole(),
        compiler_params=PARAMS,
        cost_estimate=KEEP_COST,
        name="keep",
    )(core_ref, keep, after_x, after_y, packed)
    wavefield = pl.pallas_call(
        place_wave_kernel,
        out_shape=shaped(*right_side.shape),
        in_specs=[scalars()] + [whole()] * 2,
        out_specs=anywhere(),
        scratch_shapes=[pltpu.SemaphoreType.DMA((2,))],
        compiler_params=PARAMS,
        cost_estimate=KEEP_COST,
        name="place_wave",
    )(rhs_ref, keep, got)
    residual = pl.pallas_call(
        functools.partial(place_rest_kernel, table_places),
        out_shape=shaped(*right_side.shape),
        in_specs=[scalars()] * 2 + [whole()] * 4,
        out_specs=anywhere(),
        scratch_shapes=[
            pltpu.VMEM((2, size_x, size_y, cells_z), F32),
            pltpu.SemaphoreType.DMA((2,)),
        ],
        compiler_params=PARAMS,
        name="place_rest",
    )(core_ref, rhs_ref, keep_rest, got, got_edge, packed)
    return wavefield, residual


def solution(mesh):
    return jax.shard_map(
        body,
        mesh=mesh,
        in_specs=(P(None, None, "gx", "gy", None), P("gx", "gy", None), P(), P()),
        out_specs=(P(None, None, "gx", "gy", None), P(None, None, "gx", "gy", None)),
        check_vma=False,
    )
```

```python
import functools
import math

import jax
import jax.numpy as jnp
import ml_dtypes
import numpy as np
from jax import lax
from jax.experimental import pallas as pl
from jax.experimental.pallas import tpu as pltpu
from jax.sharding import PartitionSpec as P

KAPPA = 0.12
DAMPING = 0.3
BF16 = jnp.bfloat16
F32 = jnp.float32


def sine_matrix(length):
    index = np.arange(1, length + 1)
    angles = index * (math.pi / (length + 1))
    return math.sqrt(2.0 / (length + 1)) * np.sin(angles[:, None] * index[None, :]), angles


def halves(matrix):
    high = matrix.astype(np.float32).astype(ml_dtypes.bfloat16)
    low = (matrix - high.astype(np.float64)).astype(np.float32).astype(ml_dtypes.bfloat16)
    return high, low


def left_factor(matrix):
    high, low = halves(matrix)
    return np.concatenate([high, high, low], axis=1)


def tables(size_x, size_y, cells_z):
    sine_x, angle_x = sine_matrix(size_x)
    sine_y, angle_y = sine_matrix(size_y)
    sine_z, angle_z = sine_matrix(cells_z)
    half = size_x // 2
    order = np.concatenate([np.arange(0, size_x, 2), np.arange(1, size_x, 2)])
    cells = np.concatenate([np.arange(half), np.arange(size_x - 1, half - 1, -1)])

    def symbol(angle):
        return 2.5 - 8.0 / 3.0 * np.cos(angle) + 1.0 / 6.0 * np.cos(2.0 * angle)

    real_part = (
        symbol(angle_x)[order][:, None, None]
        + symbol(angle_y)[None, :, None]
        + (2.0 - 2.0 * np.cos(angle_z))[None, None, :]
        - KAPPA
    ).reshape(size_x * size_y, cells_z)
    denominator = real_part**2 + (KAPPA * DAMPING) ** 2
    inverse = np.stack([real_part / denominator, KAPPA * DAMPING / denominator]).astype(np.float32)

    parity = [np.kron(sine_x[order[p * half : (p + 1) * half]][:, :half], sine_y) for p in (0, 1)]
    forward = [left_factor(m) for m in parity]
    backward = [left_factor(m.T) for m in parity]
    high_z, low_z = halves(sine_z)
    right_z = np.concatenate([np.concatenate([high_z, low_z], axis=1)] * 2, axis=0)

    full = np.kron(sine_x[order], sine_y)
    by_cell = full.reshape(-1, size_x, size_y)
    enter_x = np.stack([-by_cell[:, 0] / 12.0, (16.0 * by_cell[:, 0] - by_cell[:, 1]) / 12.0], 1)
    enter_y = np.stack(
        [-by_cell[:, :, 0] / 12.0, (16.0 * by_cell[:, :, 0] - by_cell[:, :, 1]) / 12.0], 1
    )
    enter = left_factor(
        np.concatenate([enter_x.reshape(len(full), -1), enter_y.reshape(len(full), -1)], axis=1)
    )
    leave = left_factor(
        np.concatenate(
            [
                by_cell[:, size_x - 2 :].reshape(len(full), -1),
                by_cell[:, :, size_y - 2 :].transpose(0, 2, 1).reshape(len(full), -1),
            ],
            axis=1,
        ).T
    )
    first = left_factor(
        np.concatenate(
            [
                by_cell[:, :2].reshape(len(full), -1),
                by_cell[:, :, :2].transpose(0, 2, 1).reshape(len(full), -1),
            ],
            axis=1,
        ).T
    )
    edge = np.zeros((size_x, size_y, 1))
    edge[0] += 1.0 / 12.0
    edge[-1] += 1.0 / 12.0
    edge[:, 0] += 1.0 / 12.0
    edge[:, -1] += 1.0 / 12.0
    edge = edge[cells].reshape(size_x * size_y, 1).astype(np.float32)
    return dict(
        inverse=inverse, edge=edge, forward=np.stack(forward), backward=np.stack(backward),
        right_z=right_z, enter=enter, leave=leave, first=first,
    ), tuple(int(x) for x in cells)


def divide(modes, t):
    return times(t["inverse"][0], t["inverse"][1], modes)


def split(values):
    high = values.astype(BF16)
    return high, (values - high.astype(F32)).astype(BF16)


def stacked(values):
    high, low = split(values)
    return jnp.concatenate([high, low, high], axis=0)


def left_product(matrix, values):
    return jnp.dot(matrix, stacked(values), preferred_element_type=F32)


def z_transform(field, t):
    rows = field.shape[0]
    cells_z = field.shape[1] // 2
    high, low = split(jnp.concatenate([field[:, :cells_z], field[:, cells_z:]], axis=0))
    both = jnp.dot(jnp.concatenate([high, low], axis=1), t["right_z"][...], preferred_element_type=F32)
    total = both[:, :cells_z] + both[:, cells_z:]
    return jnp.concatenate([total[:rows], total[rows:]], axis=1)


def to_modes(field, t):
    count = field.shape[0] // 2
    first, second = field[:count], field[count:]
    return jnp.concatenate(
        [left_product(t["forward"][0], first + second), left_product(t["forward"][1], first - second)], axis=0
    )


def to_cells(modes, t):
    count = modes.shape[0] // 2
    even = left_product(t["backward"][0], modes[:count])
    odd = left_product(t["backward"][1], modes[count:])
    return jnp.concatenate([even + odd, even - odd], axis=0)


def times(real_part, imag_part, field):
    lanes = field.shape[1] // 2
    real, imag = field[:, :lanes], field[:, lanes:]
    return jnp.concatenate(
        [real_part * real - imag_part * imag, real_part * imag + imag_part * real], axis=1
    )


def apply_contrast(field, contrast, t, block=64):
    done = []
    for start in range(0, field.shape[0], block):
        here = slice(start, start + block)
        cells = times(contrast[0, here], contrast[1, here], z_transform(field[here], t))
        done.append(z_transform(cells, t))
    return jnp.concatenate(done, axis=0)


def solve_modes(start, contrast, t):
    term = total = start
    for _ in range(2):
        term = divide(to_modes(apply_contrast(to_cells(term, t), contrast, t), t), t)
        total = total + term
    return total, term


def prepare(dense, slow, place, depth, amplitude, t, modes_ref, contrast_ref):
    rows, cells_z = contrast_ref.shape[1:]
    points = place.shape[1]
    row_ids = lax.broadcasted_iota(jnp.int32, (rows, points), 0)
    lane_ids = lax.broadcasted_iota(jnp.int32, (cells_z, points), 0)
    at_lane = (lane_ids == depth).astype(F32)
    spread = []
    for c in range(2):
        amp = amplitude[c]
        one = amp.astype(BF16).astype(F32)
        two = (amp - one).astype(BF16).astype(F32)
        parts = [at_lane * part for part in (one, two, amp - one - two)]
        spread.append(jnp.concatenate(parts, axis=1).astype(BF16))
    scaled = KAPPA * (slow - 1.0)
    contrast_ref[0] = scaled - t["edge"][...]
    contrast_ref[1] = DAMPING * scaled
    at_row = (row_ids == place).astype(F32).astype(BF16)
    field = lax.dot_general(
        jnp.concatenate([at_row] * 3, axis=1), jnp.concatenate(spread, axis=0),
        (((1,), (1,)), ((), ())), preferred_element_type=F32,
    )
    modes_ref[...] = divide(to_modes(z_transform(field + dense, t), t), t)


def hand_on_kernel(in_ref, out_ref):
    out_ref[...] = in_ref[...]


PREP = ("inverse", "edge", "forward", "right_z", "backward", "enter", "leave")
BEAT = ("inverse", "forward", "right_z", "backward", "enter", "leave")
FINAL = BEAT + ("first",)
FINISH = ("right_z", "backward")


def named(names, refs):
    return dict(zip(names, refs))


def prep_kernel(cells_x, mine_ref, slow_ref, place_ref, depth_ref, amp_ref, *refs):
    modes_ref, contrast_ref = refs[len(PREP) :]
    dense = [jnp.concatenate([mine_ref[c, x] for x in cells_x], axis=0) for c in range(2)]
    slow = jnp.concatenate([slow_ref[x] for x in cells_x], axis=0)
    prepare(
        jnp.concatenate(dense, axis=1), slow, place_ref[...], depth_ref[...], amp_ref, named(PREP, refs),
        modes_ref, contrast_ref,
    )


def prep_other_kernel(cells_x, core_ref, rhs_ref, swap_ref, slow_ref, own_modes_ref, own_contrast_ref, place_ref,
                      depth_ref, amp_ref, *refs):
    modes_ref, contrast_ref = refs[len(PREP) :]
    core, rhs = core_ref[0], rhs_ref[0]
    other = 1 - core
    modes_ref[core] = own_modes_ref[...]
    contrast_ref[core] = own_contrast_ref[...]
    dense = [jnp.concatenate([swap_ref[rhs, c, x] for x in cells_x], axis=0) for c in range(2)]
    slow = jnp.concatenate([slow_ref[x] for x in cells_x], axis=0)
    prepare(
        jnp.concatenate(dense, axis=1), slow, place_ref[...], depth_ref[...], amp_ref, named(PREP, refs),
        modes_ref.at[other], contrast_ref.at[other],
    )


def beat_kernel(tile, final, active_ref, modes_ref, contrast_ref, trace_x_ref, trace_y_ref, total_ref, term_ref,
                *refs):
    names = FINAL if final else BEAT
    t = named(names, refs)
    new_total_ref, new_term_ref, *out_refs = refs[len(names) :]
    count = trace_x_ref.shape[0]

    @pl.when(active_ref[0] == 1)
    def _():
        trace = jnp.concatenate([trace_x_ref[...], trace_y_ref[...]], axis=0)
        start = modes_ref[tile] + divide(left_product(t["enter"][...], trace), t)
        total, term = solve_modes(start, contrast_ref.at[tile], t)
        new_total_ref[...] = total
        new_term_ref[...] = term
        if not (final and tile == 1):
            out = left_product(t["leave"][...], total)
            for out_ref, part in zip(out_refs[:1] if final else out_refs, (out[:count], out[count:])):
                out_ref[...] = part

    @pl.when(active_ref[0] == 0)
    def _():
        new_total_ref[...] = total_ref[...]
        new_term_ref[...] = term_ref[...]

    if final:
        out = left_product(t["first"][...], new_total_ref[...])
        edge_refs = out_refs[1 - tile :]
        edge_refs[-1][...] = out[count:]
        if tile == 0:
            edge_refs[0][...] = out[:count]


def finish_kernel(cells_x, core_ref, total0_ref, term0_ref, total1_ref, term1_ref, contrast_ref,
                  z_ref, backward_ref, keep_ref, give_ref, both_ref):
    _, _, _, size_x, size_y, cells_z = both_ref.shape
    t = named(FINISH, (z_ref, backward_ref))
    for tile, (total_ref, term_ref) in enumerate(((total0_ref, term0_ref), (total1_ref, term1_ref))):
        wave, rest = [z_transform(to_cells(ref[...], t), t) for ref in (total_ref, term_ref)]
        rest = times(contrast_ref[tile, 0], contrast_ref[tile, 1], rest)
        for place, x in enumerate(cells_x):
            here = slice(place * size_y, (place + 1) * size_y)
            for c in range(2):
                there = slice(c * cells_z, (c + 1) * cells_z)
                both_ref[tile, 0, c, x] = wave[here, there]
                both_ref[tile, 1, c, x] = rest[here, there]
                if tile == 1 and x < 2:
                    layer = wave[here, there]
                    if x == 0:
                        both_ref[0, 1, c, size_x - 2] += layer * (-1.0 / 12.0)
                        both_ref[0, 1, c, size_x - 1] += layer * (16.0 / 12.0)
                    else:
                        both_ref[0, 1, c, size_x - 1] += layer * (-1.0 / 12.0)
    keep_ref[...] = both_ref[core_ref[0]]
    give_ref[...] = both_ref[1 - core_ref[0]]


def add_later(rest_ref, edge_x, edge_y, lower):
    _, size_x, size_y, cells_z = rest_ref.shape
    for c in range(2):
        there = slice(c * cells_z, (c + 1) * cells_z)
        near, far = edge_x[:size_y, there] * lower, edge_x[size_y:, there] * lower
        rest_ref[c, size_x - 2] += near * (-1.0 / 12.0)
        rest_ref[c, size_x - 1] += (16.0 * near - far) * (1.0 / 12.0)
        near, far = edge_y[:size_x, there], edge_y[size_x:, there]
        two = jnp.stack([near * (-1.0 / 12.0), (16.0 * near - far) * (1.0 / 12.0)], axis=1)
        rest_ref[c, :, size_y - 2 :] += two


def keep_kernel(core_ref, keep_ref, edge_x_ref, edge_y_ref, z_ref, rest_ref):
    rest_ref[...] = keep_ref[1]
    count = edge_x_ref.shape[0]
    edges = jnp.concatenate([edge_x_ref[...], edge_y_ref[core_ref[0]]], axis=0)
    edges = z_transform(edges, dict(right_z=z_ref))
    add_later(rest_ref, edges[:count], edges[count:], (core_ref[0] == 1).astype(F32))


def place_wave_kernel(rhs_ref, keep_ref, got_ref, wave_ref, sems):
    rhs = rhs_ref[0]
    copies = [
        pltpu.make_async_copy(keep_ref.at[0], wave_ref.at[rhs], sems.at[0]),
        pltpu.make_async_copy(got_ref.at[0], wave_ref.at[1 - rhs], sems.at[1]),
    ]
    for copy in copies:
        copy.start()
    for copy in copies:
        copy.wait()


def place_rest_kernel(core_ref, rhs_ref, keep_rest_ref, got_ref, got_edge_ref, z_ref, rest_ref, work_ref, sems):
    rhs = rhs_ref[0]
    count = got_edge_ref.shape[0] // 2
    copies = [pltpu.make_async_copy(keep_rest_ref, rest_ref.at[rhs], sems.at[0])]
    copies[0].start()
    work_ref[...] = got_ref[1]
    edges = z_transform(got_edge_ref[...], dict(right_z=z_ref))
    add_later(work_ref, edges[:count], edges[count:], (core_ref[0] == 1).astype(F32))
    copies.append(pltpu.make_async_copy(work_ref, rest_ref.at[1 - rhs], sems.at[1]))
    copies[1].start()
    for copy in copies:
        copy.wait()


def whole():
    return pl.BlockSpec(memory_space=pltpu.VMEM)


def scalars():
    return pl.BlockSpec(memory_space=pltpu.SMEM)


def anywhere():
    return pl.BlockSpec(memory_space=pl.ANY)


SOLVE_COST = pl.CostEstimate(flops=2 * 10**9, bytes_accessed=2 * 10**6, transcendentals=0)
KEEP_COST = pl.CostEstimate(flops=10**10, bytes_accessed=10**6, transcendentals=0)
PARAMS = pltpu.CompilerParams(vmem_limit_bytes=24 * 1024 * 1024)


def shaped(*shape):
    return jax.ShapeDtypeStruct(shape, F32)


def body(right_side, slowness, source_cells, source_amplitudes):
    sources, _, size_x, size_y, cells_z = right_side.shape
    grid_rows, grid_cols = lax.axis_size("gx"), lax.axis_size("gy")
    assert sources == 2 and grid_rows % 2 == 0 and size_x % 2 == 0
    chips = grid_rows // 2
    row, col = lax.axis_index("gx"), lax.axis_index("gy")
    core = row % 2
    rhs = (core + row // 2 + col) % 2
    core_ref, rhs_ref = core[None], rhs[None]
    t, cells_x = tables(size_x, size_y, cells_z)
    t = {name: jnp.asarray(value) for name, value in t.items()}
    rows = size_x * size_y

    def device(chip, core, column):
        return (2 * chip + core) * grid_cols + column

    def between(pairs):
        return [
            (device(a, r, b), device(c, 1 - r, d)) for (a, b), (c, d) in pairs for r in range(2)
        ]

    own = [
        (device(k, r, j), device(k, 1 - r, j))
        for k in range(chips) for j in range(grid_cols) for r in range(2)
    ]
    axes = ("gx", "gy")
    swapped = lax.ppermute(right_side, axes, own)
    swapped_slow = lax.ppermute(slowness, axes, own)
    mine = lax.dynamic_index_in_dim(right_side, rhs, 0, keepdims=False)

    total_y = size_y * grid_cols
    cells = lax.dynamic_index_in_dim(source_cells, rhs, 0, keepdims=True)
    near_y = cells // cells_z % total_y - col * size_y
    places = []
    for tile_row in (row, row + 1 - 2 * core):
        near_x = cells // (total_y * cells_z) - tile_row * size_x
        inside = (near_x >= 0) & (near_x < size_x) & (near_y >= 0) & (near_y < size_y)
        folded = jnp.where(near_x < size_x // 2, near_x, size_x + size_x // 2 - 1 - near_x)
        places.append(jnp.where(inside, folded * size_y + near_y, -1))
    amplitudes = lax.dynamic_index_in_dim(source_amplitudes, rhs, 0, keepdims=False).T[:, None, :]

    depth = cells % cells_z
    prep_tables = [t[name] for name in PREP]
    own_modes, own_contrast = pl.pallas_call(
        functools.partial(prep_kernel, cells_x),
        out_shape=(shaped(rows, 2 * cells_z), shaped(2, rows, cells_z)),
        in_specs=[whole()] * (5 + len(PREP)),
        out_specs=(whole(), whole()),
        compiler_params=PARAMS,
        cost_estimate=SOLVE_COST,
        name="prep",
    )(mine, slowness, places[0], depth, amplitudes, *prep_tables)
    modes, contrast = pl.pallas_call(
        functools.partial(prep_other_kernel, cells_x),
        out_shape=(shaped(2, rows, 2 * cells_z), shaped(2, 2, rows, cells_z)),
        in_specs=[scalars()] * 2 + [whole()] * (7 + len(PREP)),
        out_specs=(whole(), whole()),
        compiler_params=PARAMS,
        cost_estimate=SOLVE_COST,
        name="prep_other",
    )(core_ref, rhs_ref, swapped, swapped_slow, own_modes, own_contrast, places[1], depth, amplitudes, *prep_tables)

    def solve(tile, active, trace_x, trace_y, state, final):
        names = FINAL if final else BEAT
        x, y = shaped(*zero_x.shape), shaped(*zero_y.shape)
        outs = ((x, x, y), (y,))[tile] if final else (x, y)
        total, term, *outs = pl.pallas_call(
            functools.partial(beat_kernel, tile, final),
            out_shape=(shaped(rows, 2 * cells_z),) * 2 + outs,
            in_specs=[scalars()] + [whole()] * (6 + len(names)),
            out_specs=(whole(),) * (2 + len(outs)),
            input_output_aliases={5: 0, 6: 1},
            compiler_params=PARAMS,
            cost_estimate=SOLVE_COST,
            name="upper" if tile == 0 else "lower",
        )(active, modes, contrast, trace_x, trace_y, *state, *[t[name] for name in names])
        return (total, term), outs

    def hand_on(trace):
        return pl.pallas_call(
            hand_on_kernel,
            out_shape=shaped(*trace.shape),
            in_specs=[whole()],
            out_specs=whole(),
            compiler_params=PARAMS,
            name="hand_on",
        )(trace)

    zero_x = jnp.zeros((2 * size_y, 2 * cells_z), F32)
    zero_y = jnp.zeros((2 * size_x, 2 * cells_z), F32)
    trace_x, trace_y0, trace_y1 = zero_x, zero_y, zero_y
    states = [[jnp.zeros((rows, 2 * cells_z), F32)] * 2 for _ in range(2)]
    for beat in range(chips + grid_cols - 1):
        active = (row // 2 + col == beat).astype(jnp.int32)[None]
        here = [(k, beat - k) for k in range(chips) if 0 <= beat - k < grid_cols]
        along_x = between([((k, j), (k + 1, j)) for k, j in here if k + 1 < chips])
        along_y = between([((k, j), (k, j + 1)) for k, j in here if j + 1 < grid_cols])
        final = beat == chips + grid_cols - 2
        states[0], (inner_x, *outs0) = solve(0, active, trace_x, trace_y0, states[0], final)
        if along_y:
            trace_y0 = hand_on(lax.ppermute(outs0[0], axes, along_y))
        states[1], outs1 = solve(1, active, inner_x, trace_y1, states[1], final)
        if along_x:
            trace_x = lax.ppermute(outs1[0], axes, along_x)
        if along_y:
            trace_y1 = lax.ppermute(outs1[1], axes, along_y)
    edge_x, edge_y0 = outs0
    edge_y = jnp.stack([edge_y0, outs1[0]])

    every = [(k, j) for k in range(chips) for j in range(grid_cols)]
    after_x = lax.ppermute(edge_x, axes, between([((k, j), (k - 1, j)) for k, j in every if k]))
    after_y = lax.ppermute(edge_y, axes, between([((k, j), (k, j - 1)) for k, j in every if j]))

    half = shaped(2, 2, size_x, size_y, cells_z)
    keep, give = pl.pallas_call(
        functools.partial(finish_kernel, cells_x),
        out_shape=(half, half),
        in_specs=[scalars()] + [whole()] * 7,
        out_specs=(whole(), whole()),
        scratch_shapes=[pltpu.VMEM((2, 2, 2, size_x, size_y, cells_z), F32)],
        compiler_params=PARAMS,
        name="finish",
    )(core_ref, *states[0], *states[1], contrast, *[t[name] for name in FINISH])
    got = lax.ppermute(give, axes, own)

    pass_y = lax.dynamic_index_in_dim(after_y, 1 - core, 0, keepdims=False)
    got_edge = lax.ppermute(jnp.concatenate([after_x, pass_y], axis=0), axes, own)
    keep_rest = pl.pallas_call(
        keep_kernel,
        out_shape=shaped(*half.shape[1:]),
        in_specs=[scalars()] + [whole()] * 4,
        out_specs=whole(),
        compiler_params=PARAMS,
        cost_estimate=KEEP_COST,
        name="keep",
    )(core_ref, keep, after_x, after_y, t["right_z"])
    wavefield = pl.pallas_call(
        place_wave_kernel,
        out_shape=shaped(*right_side.shape),
        in_specs=[scalars()] + [whole()] * 2,
        out_specs=anywhere(),
        scratch_shapes=[pltpu.SemaphoreType.DMA((2,))],
        compiler_params=PARAMS,
        cost_estimate=KEEP_COST,
        name="place_wave",
    )(rhs_ref, keep, got)
    residual = pl.pallas_call(
        place_rest_kernel,
        out_shape=shaped(*right_side.shape),
        in_specs=[scalars()] * 2 + [whole()] * 4,
        out_specs=anywhere(),
        scratch_shapes=[
            pltpu.VMEM((2, size_x, size_y, cells_z), F32),
            pltpu.SemaphoreType.DMA((2,)),
        ],
        compiler_params=PARAMS,
        name="place_rest",
    )(core_ref, rhs_ref, keep_rest, got, got_edge, t["right_z"])
    return wavefield, residual


def solution(mesh):
    return jax.shard_map(
        body,
        mesh=mesh,
        in_specs=(P(None, None, "gx", "gy", None), P("gx", "gy", None), P(), P()),
        out_specs=(P(None, None, "gx", "gy", None), P(None, None, "gx", "gy", None)),
        check_vma=False,
    )
```

```python
import functools
import math

import jax
import jax.numpy as jnp
import ml_dtypes
import numpy as np
from jax import lax
from jax.experimental import pallas as pl
from jax.experimental.pallas import tpu as pltpu
from jax.sharding import PartitionSpec as P

KAPPA = 0.12
DAMPING = 0.3
BF16 = jnp.bfloat16
F32 = jnp.float32


def sine_matrix(length):
    index = np.arange(1, length + 1)
    angles = index * (math.pi / (length + 1))
    return math.sqrt(2.0 / (length + 1)) * np.sin(angles[:, None] * index[None, :]), angles


def halves(matrix):
    high = matrix.astype(np.float32).astype(ml_dtypes.bfloat16)
    low = (matrix - high.astype(np.float64)).astype(np.float32).astype(ml_dtypes.bfloat16)
    return high, low


def left_factor(matrix):
    high, low = halves(matrix)
    return np.concatenate([high, high, low], axis=1)


def slabs(matrices, rows, lanes):
    pieces, free = [], 0
    for matrix in matrices:
        for row in range(0, matrix.shape[0], rows):
            for lane in range(0, matrix.shape[1], lanes):
                piece = matrix[row : row + rows, lane : lane + lanes]
                if free + piece.shape[0] > rows or not pieces:
                    pieces.append(np.zeros((rows, lanes), matrix.dtype))
                    free = 0
                pieces[-1][free : free + piece.shape[0], : piece.shape[1]] = piece
                free += piece.shape[0]
    return np.stack(pieces)


def enter_matrix(t, depth):
    return jnp.concatenate([t["later"][2, :, :depth], t["later"][3, :, :depth]], axis=0)


def leave_matrix(t):
    count = t["later"].shape[1] // 2
    return jnp.concatenate([t["later"][4, :count], t["later"][4, count:]], axis=1)


def tables(size_x, size_y, cells_z):
    sine_x, angle_x = sine_matrix(size_x)
    sine_y, angle_y = sine_matrix(size_y)
    sine_z, angle_z = sine_matrix(cells_z)
    half = size_x // 2
    order = np.concatenate([np.arange(0, size_x, 2), np.arange(1, size_x, 2)])
    cells = np.concatenate([np.arange(half), np.arange(size_x - 1, half - 1, -1)])

    def symbol(angle):
        return 2.5 - 8.0 / 3.0 * np.cos(angle) + 1.0 / 6.0 * np.cos(2.0 * angle)

    real_part = (
        symbol(angle_x)[order][:, None, None]
        + symbol(angle_y)[None, :, None]
        + (2.0 - 2.0 * np.cos(angle_z))[None, None, :]
        - KAPPA
    ).reshape(size_x * size_y, cells_z)
    denominator = real_part**2 + (KAPPA * DAMPING) ** 2
    inverse = np.stack([real_part / denominator, KAPPA * DAMPING / denominator]).astype(np.float32)

    parity = [np.kron(sine_x[order[p * half : (p + 1) * half]][:, :half], sine_y) for p in (0, 1)]
    forward = [left_factor(m) for m in parity]
    backward = [left_factor(m.T) for m in parity]
    high_z, low_z = halves(sine_z)
    right_z = np.concatenate([np.concatenate([high_z, low_z], axis=1)] * 2, axis=0)

    full = np.kron(sine_x[order], sine_y)
    by_cell = full.reshape(-1, size_x, size_y)
    enter_x = np.stack([-by_cell[:, 0] / 12.0, (16.0 * by_cell[:, 0] - by_cell[:, 1]) / 12.0], 1)
    enter_y = np.stack(
        [-by_cell[:, :, 0] / 12.0, (16.0 * by_cell[:, :, 0] - by_cell[:, :, 1]) / 12.0], 1
    )
    enter = left_factor(
        np.concatenate([enter_x.reshape(len(full), -1), enter_y.reshape(len(full), -1)], axis=1)
    )
    leave = left_factor(
        np.concatenate(
            [
                by_cell[:, size_x - 2 :].reshape(len(full), -1),
                by_cell[:, :, size_y - 2 :].transpose(0, 2, 1).reshape(len(full), -1),
            ],
            axis=1,
        ).T
    )
    first = left_factor(
        np.concatenate(
            [
                by_cell[:, :2].reshape(len(full), -1),
                by_cell[:, :, :2].transpose(0, 2, 1).reshape(len(full), -1),
            ],
            axis=1,
        ).T
    )
    assert enter.shape[0] == 2 * half * size_y and enter.shape[1] <= forward[0].shape[1]
    assert 2 * leave.shape[0] == half * size_y and leave.shape[1] == 2 * forward[0].shape[1]
    return dict(
        inverse=inverse, forward=np.stack(forward), right_z=right_z, first=first,
        later=slabs(backward + [enter, leave], half * size_y, forward[0].shape[1]),
    ), tuple(int(x) for x in cells)


def divide(modes, t):
    return times(t["inverse"][0], t["inverse"][1], modes)


def split(values):
    high = values.astype(BF16)
    return high, (values - high.astype(F32)).astype(BF16)


def stacked(values):
    high, low = split(values)
    return jnp.concatenate([high, low, high], axis=0)


def left_product(matrix, values):
    return jnp.dot(matrix, stacked(values), preferred_element_type=F32)


def z_transform(field, t):
    rows = field.shape[0]
    cells_z = field.shape[1] // 2
    high, low = split(jnp.concatenate([field[:, :cells_z], field[:, cells_z:]], axis=0))
    both = jnp.dot(jnp.concatenate([high, low], axis=1), t["right_z"][...], preferred_element_type=F32)
    total = both[:, :cells_z] + both[:, cells_z:]
    return jnp.concatenate([total[:rows], total[rows:]], axis=1)


def to_modes(field, t):
    count = field.shape[0] // 2
    first, second = field[:count], field[count:]
    return jnp.concatenate(
        [left_product(t["forward"][0], first + second), left_product(t["forward"][1], first - second)], axis=0
    )


def to_cells(modes, t):
    count = modes.shape[0] // 2
    even = left_product(t["later"][0], modes[:count])
    odd = left_product(t["later"][1], modes[count:])
    return jnp.concatenate([even + odd, even - odd], axis=0)


def times(real_part, imag_part, field):
    lanes = field.shape[1] // 2
    real, imag = field[:, :lanes], field[:, lanes:]
    return jnp.concatenate(
        [real_part * real - imag_part * imag, real_part * imag + imag_part * real], axis=1
    )


def apply_contrast(field, contrast, t, block=64):
    done = []
    for start in range(0, field.shape[0], block):
        here = slice(start, start + block)
        cells = times(contrast[0, here], contrast[1, here], z_transform(field[here], t))
        done.append(z_transform(cells, t))
    return jnp.concatenate(done, axis=0)


def solve_modes(start, contrast, t):
    term = total = start
    for _ in range(2):
        term = divide(to_modes(apply_contrast(to_cells(term, t), contrast, t), t), t)
        total = total + term
    return total, term


def edges(rows, lanes, layers):
    place = lax.broadcasted_iota(jnp.int32, (rows, lanes), 0)
    size_y = rows // layers
    along_y = lax.rem(place, size_y)
    outer = lax.rem(place, rows // 2) < size_y
    return (outer.astype(F32) + ((along_y == 0) | (along_y == size_y - 1)).astype(F32)) * (1.0 / 12.0)


def prepare(dense, slow, layers, place, depth, amplitude, t, modes_ref, contrast_ref):
    rows, cells_z = contrast_ref.shape[1:]
    points = place.shape[1]
    row_ids = lax.broadcasted_iota(jnp.int32, (rows, points), 0)
    lane_ids = lax.broadcasted_iota(jnp.int32, (cells_z, points), 0)
    at_lane = (lane_ids == depth).astype(F32)
    spread = []
    for c in range(2):
        amp = amplitude[c]
        one = amp.astype(BF16).astype(F32)
        two = (amp - one).astype(BF16).astype(F32)
        parts = [at_lane * part for part in (one, two, amp - one - two)]
        spread.append(jnp.concatenate(parts, axis=1).astype(BF16))
    scaled = KAPPA * (slow - 1.0)
    contrast_ref[0] = scaled - edges(rows, cells_z, layers)
    contrast_ref[1] = DAMPING * scaled
    at_row = (row_ids == place).astype(F32).astype(BF16)
    field = lax.dot_general(
        jnp.concatenate([at_row] * 3, axis=1), jnp.concatenate(spread, axis=0),
        (((1,), (1,)), ((), ())), preferred_element_type=F32,
    )
    modes_ref[...] = divide(to_modes(z_transform(field + dense, t), t), t)


def hand_on_kernel(in_ref, out_ref):
    out_ref[...] = in_ref[...]


PREP = ("inverse", "forward", "right_z")
BEAT = ("inverse", "forward", "right_z", "later")
FINAL = BEAT + ("first",)
LATER = ("later",)
FINISH = ("right_z", "later")


def named(names, refs):
    return dict(zip(names, refs))


def prep_kernel(cells_x, right_ref, slow_ref, place_ref, depth_ref, amp_ref, *refs):
    later_refs = refs[len(PREP) : len(PREP) + len(LATER)]
    modes_ref, contrast_ref, *held_refs, sems = refs[len(PREP) + len(LATER) :]
    copies = [
        pltpu.make_async_copy(later_ref, held_ref, sems.at[n])
        for n, (later_ref, held_ref) in enumerate(zip(later_refs, held_refs))
    ]
    for copy in copies:
        copy.start()
    dense = [jnp.concatenate([right_ref[0, c, x] for x in cells_x], axis=0) for c in range(2)]
    slow = jnp.concatenate([slow_ref[x] for x in cells_x], axis=0)
    prepare(
        jnp.concatenate(dense, axis=1), slow, len(cells_x), place_ref[...], depth_ref[...], amp_ref, named(PREP, refs),
        modes_ref, contrast_ref,
    )
    for copy in copies:
        copy.wait()


def prep_other_kernel(cells_x, core_ref, swap_ref, own_modes_ref, own_contrast_ref, place_ref, depth_ref, amp_ref,
                      *refs):
    modes_ref, contrast_ref = refs[len(PREP) :]
    core = core_ref[0]
    other = 1 - core
    modes_ref[core] = own_modes_ref[...]
    contrast_ref[core] = own_contrast_ref[...]
    *dense, slow = [jnp.concatenate([swap_ref[c, x] for x in cells_x], axis=0) for c in range(3)]
    prepare(
        jnp.concatenate(dense, axis=1), slow, len(cells_x), place_ref[...], depth_ref[...], amp_ref, named(PREP, refs),
        modes_ref.at[other], contrast_ref.at[other],
    )


def beat_kernel(tile, final, active_ref, modes_ref, contrast_ref, trace_x_ref, trace_y_ref, total_ref, term_ref,
                *refs):
    names = FINAL if final else BEAT
    t = named(names, refs)
    new_total_ref, new_term_ref, *out_refs = refs[len(names) :]
    count = trace_x_ref.shape[0]

    @pl.when(active_ref[0] == 1)
    def _():
        trace = jnp.concatenate([trace_x_ref[...], trace_y_ref[...]], axis=0)
        start = modes_ref[tile] + divide(left_product(enter_matrix(t, 3 * trace.shape[0]), trace), t)
        total, term = solve_modes(start, contrast_ref.at[tile], t)
        new_total_ref[...] = total
        new_term_ref[...] = term
        if not (final and tile == 1):
            out = left_product(leave_matrix(t), total)
            for out_ref, part in zip(out_refs[:1] if final else out_refs, (out[:count], out[count:])):
                out_ref[...] = part

    @pl.when(active_ref[0] == 0)
    def _():
        new_total_ref[...] = total_ref[...]
        new_term_ref[...] = term_ref[...]

    if final:
        out = left_product(t["first"][...], new_total_ref[...])
        edge_refs = out_refs[1 - tile :]
        edge_refs[-1][...] = out[count:]
        if tile == 0:
            edge_refs[0][...] = out[:count]


def finish_kernel(cells_x, core_ref, total0_ref, term0_ref, total1_ref, term1_ref, contrast_ref,
                  z_ref, later_ref, keep_ref, give_ref, both_ref):
    _, _, _, size_x, size_y, cells_z = both_ref.shape
    t = named(FINISH, (z_ref, later_ref))
    for tile, (total_ref, term_ref) in enumerate(((total0_ref, term0_ref), (total1_ref, term1_ref))):
        wave, rest = [z_transform(to_cells(ref[...], t), t) for ref in (total_ref, term_ref)]
        rest = times(contrast_ref[tile, 0], contrast_ref[tile, 1], rest)
        for place, x in enumerate(cells_x):
            here = slice(place * size_y, (place + 1) * size_y)
            for c in range(2):
                there = slice(c * cells_z, (c + 1) * cells_z)
                both_ref[tile, 0, c, x] = wave[here, there]
                both_ref[tile, 1, c, x] = rest[here, there]
                if tile == 1 and x < 2:
                    layer = wave[here, there]
                    if x == 0:
                        both_ref[0, 1, c, size_x - 2] += layer * (-1.0 / 12.0)
                        both_ref[0, 1, c, size_x - 1] += layer * (16.0 / 12.0)
                    else:
                        both_ref[0, 1, c, size_x - 1] += layer * (-1.0 / 12.0)
    keep_ref[...] = both_ref[core_ref[0]]
    give_ref[...] = both_ref[1 - core_ref[0]]


def add_later(rest_ref, edge_x, edge_y, lower):
    _, size_x, size_y, cells_z = rest_ref.shape
    for c in range(2):
        there = slice(c * cells_z, (c + 1) * cells_z)
        near, far = edge_x[:size_y, there] * lower, edge_x[size_y:, there] * lower
        rest_ref[c, size_x - 2] += near * (-1.0 / 12.0)
        rest_ref[c, size_x - 1] += (16.0 * near - far) * (1.0 / 12.0)
        near, far = edge_y[:size_x, there], edge_y[size_x:, there]
        two = jnp.stack([near * (-1.0 / 12.0), (16.0 * near - far) * (1.0 / 12.0)], axis=1)
        rest_ref[c, :, size_y - 2 :] += two


def keep_kernel(core_ref, keep_ref, edge_x_ref, edge_y_ref, z_ref, rest_ref):
    rest_ref[...] = keep_ref[1]
    count = edge_x_ref.shape[0]
    edges = jnp.concatenate([edge_x_ref[...], edge_y_ref[core_ref[0]]], axis=0)
    edges = z_transform(edges, dict(right_z=z_ref))
    add_later(rest_ref, edges[:count], edges[count:], (core_ref[0] == 1).astype(F32))


def place_wave_kernel(rhs_ref, keep_ref, got_ref, wave_ref, sems):
    rhs = rhs_ref[0]
    copies = [
        pltpu.make_async_copy(keep_ref.at[0], wave_ref.at[rhs], sems.at[0]),
        pltpu.make_async_copy(got_ref.at[0], wave_ref.at[1 - rhs], sems.at[1]),
    ]
    for copy in copies:
        copy.start()
    for copy in copies:
        copy.wait()


def place_rest_kernel(core_ref, rhs_ref, keep_rest_ref, got_ref, got_edge_ref, z_ref, rest_ref, work_ref, sems):
    rhs = rhs_ref[0]
    count = got_edge_ref.shape[0] // 2
    copies = [pltpu.make_async_copy(keep_rest_ref, rest_ref.at[rhs], sems.at[0])]
    copies[0].start()
    work_ref[...] = got_ref[1]
    edges = z_transform(got_edge_ref[...], dict(right_z=z_ref))
    add_later(work_ref, edges[:count], edges[count:], (core_ref[0] == 1).astype(F32))
    copies.append(pltpu.make_async_copy(work_ref, rest_ref.at[1 - rhs], sems.at[1]))
    copies[1].start()
    for copy in copies:
        copy.wait()


def whole():
    return pl.BlockSpec(memory_space=pltpu.VMEM)


def scalars():
    return pl.BlockSpec(memory_space=pltpu.SMEM)


def anywhere():
    return pl.BlockSpec(memory_space=pl.ANY)


SOLVE_COST = pl.CostEstimate(flops=2 * 10**9, bytes_accessed=2 * 10**6, transcendentals=0)
KEEP_COST = pl.CostEstimate(flops=10**10, bytes_accessed=10**6, transcendentals=0)
PARAMS = pltpu.CompilerParams(vmem_limit_bytes=24 * 1024 * 1024)


def shaped(*shape):
    return jax.ShapeDtypeStruct(shape, F32)


def body(right_side, slowness, source_cells, source_amplitudes):
    sources, _, size_x, size_y, cells_z = right_side.shape
    grid_rows, grid_cols = lax.axis_size("gx"), lax.axis_size("gy")
    assert sources == 2 and grid_rows % 2 == 0 and size_x % 2 == 0
    chips = grid_rows // 2
    row, col = lax.axis_index("gx"), lax.axis_index("gy")
    core = row % 2
    rhs = (core + row // 2 + col) % 2
    core_ref, rhs_ref = core[None], rhs[None]
    t, cells_x = tables(size_x, size_y, cells_z)
    t = {name: jnp.asarray(value) for name, value in t.items()}
    rows = size_x * size_y

    def device(chip, core, column):
        return (2 * chip + core) * grid_cols + column

    def between(pairs):
        return [
            (device(a, r, b), device(c, 1 - r, d)) for (a, b), (c, d) in pairs for r in range(2)
        ]

    own = [
        (device(k, r, j), device(k, 1 - r, j))
        for k in range(chips) for j in range(grid_cols) for r in range(2)
    ]
    axes = ("gx", "gy")
    ordered = jnp.where(rhs == 0, right_side, right_side[::-1])
    swapped = lax.ppermute(jnp.concatenate([ordered[1], slowness[None]], axis=0), axes, own)

    total_y = size_y * grid_cols
    cells = lax.dynamic_index_in_dim(source_cells, rhs, 0, keepdims=True)
    near_y = cells // cells_z % total_y - col * size_y
    places = []
    for tile_row in (row, row + 1 - 2 * core):
        near_x = cells // (total_y * cells_z) - tile_row * size_x
        inside = (near_x >= 0) & (near_x < size_x) & (near_y >= 0) & (near_y < size_y)
        folded = jnp.where(near_x < size_x // 2, near_x, size_x + size_x // 2 - 1 - near_x)
        places.append(jnp.where(inside, folded * size_y + near_y, -1))
    amplitudes = lax.dynamic_index_in_dim(source_amplitudes, rhs, 0, keepdims=False).T[:, None, :]

    depth = cells % cells_z
    prep_tables = [t[name] for name in PREP]
    own_modes, own_contrast, *held = pl.pallas_call(
        functools.partial(prep_kernel, cells_x),
        out_shape=(shaped(rows, 2 * cells_z), shaped(2, rows, cells_z))
        + tuple(jax.ShapeDtypeStruct(t[name].shape, BF16) for name in LATER),
        in_specs=[whole()] * (5 + len(PREP)) + [anywhere()] * len(LATER),
        out_specs=(whole(),) * (2 + len(LATER)),
        scratch_shapes=[pltpu.SemaphoreType.DMA((len(LATER),))],
        compiler_params=PARAMS,
        cost_estimate=SOLVE_COST,
        name="prep",
    )(ordered, slowness, places[0], depth, amplitudes, *prep_tables, *[t[name] for name in LATER])
    t.update(zip(LATER, held))
    modes, contrast = pl.pallas_call(
        functools.partial(prep_other_kernel, cells_x),
        out_shape=(shaped(2, rows, 2 * cells_z), shaped(2, 2, rows, cells_z)),
        in_specs=[scalars()] + [whole()] * (6 + len(PREP)),
        out_specs=(whole(), whole()),
        compiler_params=PARAMS,
        cost_estimate=SOLVE_COST,
        name="prep_other",
    )(core_ref, swapped, own_modes, own_contrast, places[1], depth, amplitudes, *prep_tables)

    def solve(tile, active, trace_x, trace_y, state, final):
        names = FINAL if final else BEAT
        x, y = shaped(*zero_x.shape), shaped(*zero_y.shape)
        outs = ((x, x, y), (y,))[tile] if final else (x, y)
        total, term, *outs = pl.pallas_call(
            functools.partial(beat_kernel, tile, final),
            out_shape=(shaped(rows, 2 * cells_z),) * 2 + outs,
            in_specs=[scalars()] + [whole()] * (6 + len(names)),
            out_specs=(whole(),) * (2 + len(outs)),
            input_output_aliases={5: 0, 6: 1},
            compiler_params=PARAMS,
            cost_estimate=SOLVE_COST,
            name="upper" if tile == 0 else "lower",
        )(active, modes, contrast, trace_x, trace_y, *state, *[t[name] for name in names])
        return (total, term), outs

    def hand_on(trace):
        return pl.pallas_call(
            hand_on_kernel,
            out_shape=shaped(*trace.shape),
            in_specs=[whole()],
            out_specs=whole(),
            compiler_params=PARAMS,
            name="hand_on",
        )(trace)

    zero_x = jnp.zeros((2 * size_y, 2 * cells_z), F32)
    zero_y = jnp.zeros((2 * size_x, 2 * cells_z), F32)
    trace_x, trace_y0, trace_y1 = zero_x, zero_y, zero_y
    states = [[jnp.zeros((rows, 2 * cells_z), F32)] * 2 for _ in range(2)]
    for beat in range(chips + grid_cols - 1):
        active = (row // 2 + col == beat).astype(jnp.int32)[None]
        here = [(k, beat - k) for k in range(chips) if 0 <= beat - k < grid_cols]
        along_x = between([((k, j), (k + 1, j)) for k, j in here if k + 1 < chips])
        along_y = between([((k, j), (k, j + 1)) for k, j in here if j + 1 < grid_cols])
        final = beat == chips + grid_cols - 2
        states[0], (inner_x, *outs0) = solve(0, active, trace_x, trace_y0, states[0], final)
        if along_y:
            trace_y0 = hand_on(lax.ppermute(outs0[0], axes, along_y))
        states[1], outs1 = solve(1, active, inner_x, trace_y1, states[1], final)
        if along_x:
            trace_x = lax.ppermute(outs1[0], axes, along_x)
        if along_y:
            trace_y1 = lax.ppermute(outs1[1], axes, along_y)
    edge_x, edge_y0 = outs0
    edge_y = jnp.stack([edge_y0, outs1[0]])

    every = [(k, j) for k in range(chips) for j in range(grid_cols)]
    after_x = lax.ppermute(edge_x, axes, between([((k, j), (k - 1, j)) for k, j in every if k]))
    after_y = lax.ppermute(edge_y, axes, between([((k, j), (k, j - 1)) for k, j in every if j]))

    half = shaped(2, 2, size_x, size_y, cells_z)
    keep, give = pl.pallas_call(
        functools.partial(finish_kernel, cells_x),
        out_shape=(half, half),
        in_specs=[scalars()] + [whole()] * 7,
        out_specs=(whole(), whole()),
        scratch_shapes=[pltpu.VMEM((2, 2, 2, size_x, size_y, cells_z), F32)],
        compiler_params=PARAMS,
        name="finish",
    )(core_ref, *states[0], *states[1], contrast, *[t[name] for name in FINISH])
    got = lax.ppermute(give, axes, own)

    pass_y = lax.dynamic_index_in_dim(after_y, 1 - core, 0, keepdims=False)
    got_edge = lax.ppermute(jnp.concatenate([after_x, pass_y], axis=0), axes, own)
    keep_rest = pl.pallas_call(
        keep_kernel,
        out_shape=shaped(*half.shape[1:]),
        in_specs=[scalars()] + [whole()] * 4,
        out_specs=whole(),
        compiler_params=PARAMS,
        cost_estimate=KEEP_COST,
        name="keep",
    )(core_ref, keep, after_x, after_y, t["right_z"])
    wavefield = pl.pallas_call(
        place_wave_kernel,
        out_shape=shaped(*right_side.shape),
        in_specs=[scalars()] + [whole()] * 2,
        out_specs=anywhere(),
        scratch_shapes=[pltpu.SemaphoreType.DMA((2,))],
        compiler_params=PARAMS,
        cost_estimate=KEEP_COST,
        name="place_wave",
    )(rhs_ref, keep, got)
    residual = pl.pallas_call(
        place_rest_kernel,
        out_shape=shaped(*right_side.shape),
        in_specs=[scalars()] * 2 + [whole()] * 4,
        out_specs=anywhere(),
        scratch_shapes=[
            pltpu.VMEM((2, size_x, size_y, cells_z), F32),
            pltpu.SemaphoreType.DMA((2,)),
        ],
        compiler_params=PARAMS,
        name="place_rest",
    )(core_ref, rhs_ref, keep_rest, got, got_edge, t["right_z"])
    return wavefield, residual


def solution(mesh):
    return jax.shard_map(
        body,
        mesh=mesh,
        in_specs=(P(None, None, "gx", "gy", None), P("gx", "gy", None), P(), P()),
        out_specs=(P(None, None, "gx", "gy", None), P(None, None, "gx", "gy", None)),
        check_vma=False,
    )
```

```python
import functools
import math

import jax
import jax.numpy as jnp
import ml_dtypes
import numpy as np
from jax import lax
from jax.experimental import pallas as pl
from jax.experimental.pallas import tpu as pltpu
from jax.sharding import PartitionSpec as P

KAPPA = 0.12
DAMPING = 0.3
BF16 = jnp.bfloat16
F32 = jnp.float32


def sine_matrix(length):
    index = np.arange(1, length + 1)
    angles = index * (math.pi / (length + 1))
    return math.sqrt(2.0 / (length + 1)) * np.sin(angles[:, None] * index[None, :]), angles


def halves(matrix):
    high = matrix.astype(np.float32).astype(ml_dtypes.bfloat16)
    low = (matrix - high.astype(np.float64)).astype(np.float32).astype(ml_dtypes.bfloat16)
    return high, low


def left_factor(matrix):
    high, low = halves(matrix)
    return np.concatenate([high, high, low], axis=1)


def slabs(matrices, rows, lanes):
    pieces, free = [], 0
    for matrix in matrices:
        for row in range(0, matrix.shape[0], rows):
            for lane in range(0, matrix.shape[1], lanes):
                piece = matrix[row : row + rows, lane : lane + lanes]
                if free + piece.shape[0] > rows or not pieces:
                    pieces.append(np.zeros((rows, lanes), matrix.dtype))
                    free = 0
                pieces[-1][free : free + piece.shape[0], : piece.shape[1]] = piece
                free += piece.shape[0]
    return np.stack(pieces)


def z_matrix(t, depth):
    rows = t["onward"].shape[1]
    pieces = [t["onward"][2 + n, :, :depth] for n in range(-(-depth // rows))]
    return jnp.concatenate(pieces, axis=0)


def enter_matrix(t, depth):
    return jnp.concatenate([t["later"][2, :, :depth], t["later"][3, :, :depth]], axis=0)


def leave_matrix(t):
    count = t["later"].shape[1] // 2
    return jnp.concatenate([t["later"][4, :count], t["later"][4, count:]], axis=1)


def tables(size_x, size_y, cells_z):
    sine_x, angle_x = sine_matrix(size_x)
    sine_y, angle_y = sine_matrix(size_y)
    sine_z, angle_z = sine_matrix(cells_z)
    half = size_x // 2
    order = np.concatenate([np.arange(0, size_x, 2), np.arange(1, size_x, 2)])
    cells = np.concatenate([np.arange(half), np.arange(size_x - 1, half - 1, -1)])

    def symbol(angle):
        return 2.5 - 8.0 / 3.0 * np.cos(angle) + 1.0 / 6.0 * np.cos(2.0 * angle)

    real_part = (
        symbol(angle_x)[order][:, None, None]
        + symbol(angle_y)[None, :, None]
        + (2.0 - 2.0 * np.cos(angle_z))[None, None, :]
        - KAPPA
    ).reshape(size_x * size_y, cells_z)

    parity = [np.kron(sine_x[order[p * half : (p + 1) * half]][:, :half], sine_y) for p in (0, 1)]
    forward = [left_factor(m) for m in parity]
    backward = [left_factor(m.T) for m in parity]
    high_z, low_z = halves(sine_z)
    right_z = np.concatenate([np.concatenate([high_z, low_z], axis=1)] * 2, axis=0)

    full = np.kron(sine_x[order], sine_y)
    by_cell = full.reshape(-1, size_x, size_y)
    enter_x = np.stack([-by_cell[:, 0] / 12.0, (16.0 * by_cell[:, 0] - by_cell[:, 1]) / 12.0], 1)
    enter_y = np.stack(
        [-by_cell[:, :, 0] / 12.0, (16.0 * by_cell[:, :, 0] - by_cell[:, :, 1]) / 12.0], 1
    )
    enter = left_factor(
        np.concatenate([enter_x.reshape(len(full), -1), enter_y.reshape(len(full), -1)], axis=1)
    )
    leave = left_factor(
        np.concatenate(
            [
                by_cell[:, size_x - 2 :].reshape(len(full), -1),
                by_cell[:, :, size_y - 2 :].transpose(0, 2, 1).reshape(len(full), -1),
            ],
            axis=1,
        ).T
    )
    first = left_factor(
        np.concatenate(
            [
                by_cell[:, :2].reshape(len(full), -1),
                by_cell[:, :, :2].transpose(0, 2, 1).reshape(len(full), -1),
            ],
            axis=1,
        ).T
    )
    assert 2 * cells_z % (half * size_y) == 0 and 2 * cells_z <= forward[0].shape[1]
    assert enter.shape[0] == 2 * half * size_y and enter.shape[1] <= forward[0].shape[1]
    assert 2 * leave.shape[0] == half * size_y and leave.shape[1] == 2 * forward[0].shape[1]
    return dict(
        symbol=real_part.astype(np.float32), first=first,
        onward=slabs(forward + [right_z], half * size_y, forward[0].shape[1]),
        later=slabs(backward + [enter, leave], half * size_y, forward[0].shape[1]),
    ), tuple(int(x) for x in cells)


def divide(modes, t):
    return times(t["inverse"][0], t["inverse"][1], modes)


def split(values):
    high = values.astype(BF16)
    return high, (values - high.astype(F32)).astype(BF16)


def stacked(values):
    high, low = split(values)
    return jnp.concatenate([high, low, high], axis=0)


def left_product(matrix, values):
    return jnp.dot(matrix, stacked(values), preferred_element_type=F32)


def z_transform(field, t):
    rows = field.shape[0]
    cells_z = field.shape[1] // 2
    high, low = split(jnp.concatenate([field[:, :cells_z], field[:, cells_z:]], axis=0))
    both = jnp.dot(jnp.concatenate([high, low], axis=1), z_matrix(t, 2 * cells_z), preferred_element_type=F32)
    total = both[:, :cells_z] + both[:, cells_z:]
    return jnp.concatenate([total[:rows], total[rows:]], axis=1)


def to_modes(field, t):
    count = field.shape[0] // 2
    first, second = field[:count], field[count:]
    return jnp.concatenate(
        [left_product(t["onward"][0], first + second), left_product(t["onward"][1], first - second)], axis=0
    )


def to_cells(modes, t):
    count = modes.shape[0] // 2
    even = left_product(t["later"][0], modes[:count])
    odd = left_product(t["later"][1], modes[count:])
    return jnp.concatenate([even + odd, even - odd], axis=0)


def times(real_part, imag_part, field):
    lanes = field.shape[1] // 2
    real, imag = field[:, :lanes], field[:, lanes:]
    return jnp.concatenate(
        [real_part * real - imag_part * imag, real_part * imag + imag_part * real], axis=1
    )


def apply_contrast(field, contrast, t, block=64):
    done = []
    for start in range(0, field.shape[0], block):
        here = slice(start, start + block)
        cells = times(contrast[0, here], contrast[1, here], z_transform(field[here], t))
        done.append(z_transform(cells, t))
    return jnp.concatenate(done, axis=0)


def solve_modes(start, contrast, t):
    term = total = start
    for _ in range(2):
        term = divide(to_modes(apply_contrast(to_cells(term, t), contrast, t), t), t)
        total = total + term
    return total, term


def edges(rows, lanes, layers):
    place = lax.broadcasted_iota(jnp.int32, (rows, lanes), 0)
    size_y = rows // layers
    along_y = lax.rem(place, size_y)
    outer = lax.rem(place, rows // 2) < size_y
    return (outer.astype(F32) + ((along_y == 0) | (along_y == size_y - 1)).astype(F32)) * (1.0 / 12.0)


def prepare(dense, slow, layers, place, depth, amplitude, t, modes_ref, contrast_ref):
    rows, cells_z = contrast_ref.shape[1:]
    points = place.shape[1]
    row_ids = lax.broadcasted_iota(jnp.int32, (rows, points), 0)
    lane_ids = lax.broadcasted_iota(jnp.int32, (cells_z, points), 0)
    at_lane = (lane_ids == depth).astype(F32)
    spread = []
    for c in range(2):
        amp = amplitude[c]
        one = amp.astype(BF16).astype(F32)
        two = (amp - one).astype(BF16).astype(F32)
        parts = [at_lane * part for part in (one, two, amp - one - two)]
        spread.append(jnp.concatenate(parts, axis=1).astype(BF16))
    scaled = KAPPA * (slow - 1.0)
    contrast_ref[0] = scaled - edges(rows, cells_z, layers)
    contrast_ref[1] = DAMPING * scaled
    at_row = (row_ids == place).astype(F32).astype(BF16)
    field = lax.dot_general(
        jnp.concatenate([at_row] * 3, axis=1), jnp.concatenate(spread, axis=0),
        (((1,), (1,)), ((), ())), preferred_element_type=F32,
    )
    modes_ref[...] = divide(to_modes(z_transform(field + dense, t), t), t)


def hand_on_kernel(in_ref, out_ref):
    out_ref[...] = in_ref[...]


PREP = ("symbol", "onward")
PREP_OTHER = ("inverse", "onward")
BEAT = ("inverse", "onward", "later")
FINAL = BEAT + ("first",)
LATER = ("later",)
FINISH = ("onward", "later")


def named(names, refs):
    return dict(zip(names, refs))


def prep_kernel(cells_x, right_ref, slow_ref, place_ref, depth_ref, amp_ref, *refs):
    later_refs = refs[len(PREP) : len(PREP) + len(LATER)]
    modes_ref, contrast_ref, inverse_ref, *held_refs, sems = refs[len(PREP) + len(LATER) :]
    copies = [
        pltpu.make_async_copy(later_ref, held_ref, sems.at[n])
        for n, (later_ref, held_ref) in enumerate(zip(later_refs, held_refs))
    ]
    for copy in copies:
        copy.start()
    t = named(PREP, refs)
    symbol = t["symbol"][...]
    damping = KAPPA * DAMPING
    scale = 1.0 / (symbol * symbol + damping * damping)
    inverse_ref[0] = symbol * scale
    inverse_ref[1] = damping * scale
    t["inverse"] = inverse_ref
    dense = [jnp.concatenate([right_ref[c, x] for x in cells_x], axis=0) for c in range(2)]
    slow = jnp.concatenate([slow_ref[x] for x in cells_x], axis=0)
    prepare(
        jnp.concatenate(dense, axis=1), slow, len(cells_x), place_ref[...], depth_ref[...], amp_ref, t,
        modes_ref, contrast_ref,
    )
    for copy in copies:
        copy.wait()


def prep_other_kernel(cells_x, core_ref, rhs_ref, swap_ref, slow_ref, own_modes_ref, own_contrast_ref, place_ref, depth_ref, amp_ref,
                      *refs):
    modes_ref, contrast_ref = refs[len(PREP_OTHER) :]
    core = core_ref[0]
    other = 1 - core
    modes_ref[core] = own_modes_ref[...]
    contrast_ref[core] = own_contrast_ref[...]
    dense = [jnp.concatenate([swap_ref[c, x] for x in cells_x], axis=0) for c in range(2)]
    slow = jnp.concatenate([slow_ref[x] for x in cells_x], axis=0)
    prepare(
        jnp.concatenate(dense, axis=1), slow, len(cells_x), place_ref[...], depth_ref[...], amp_ref, named(PREP_OTHER, refs),
        modes_ref.at[other], contrast_ref.at[other],
    )


def beat_kernel(tile, final, active_ref, modes_ref, contrast_ref, trace_x_ref, trace_y_ref, total_ref, term_ref,
                *refs):
    names = FINAL if final else BEAT
    t = named(names, refs)
    new_total_ref, new_term_ref, *out_refs = refs[len(names) :]
    count = trace_x_ref.shape[0]

    @pl.when(active_ref[0] == 1)
    def _():
        trace = jnp.concatenate([trace_x_ref[...], trace_y_ref[...]], axis=0)
        start = modes_ref[tile] + divide(left_product(enter_matrix(t, 3 * trace.shape[0]), trace), t)
        total, term = solve_modes(start, contrast_ref.at[tile], t)
        new_total_ref[...] = total
        new_term_ref[...] = term
        if not (final and tile == 1):
            out = left_product(leave_matrix(t), total)
            for out_ref, part in zip(out_refs[:1] if final else out_refs, (out[:count], out[count:])):
                out_ref[...] = part

    @pl.when(active_ref[0] == 0)
    def _():
        new_total_ref[...] = total_ref[...]
        new_term_ref[...] = term_ref[...]

    if final:
        out = left_product(t["first"][...], new_total_ref[...])
        edge_refs = out_refs[1 - tile :]
        edge_refs[-1][...] = out[count:]
        if tile == 0:
            edge_refs[0][...] = out[:count]


def finish_kernel(cells_x, core_ref, total0_ref, term0_ref, total1_ref, term1_ref, contrast_ref,
                  z_ref, later_ref, keep_ref, give_ref, both_ref):
    _, _, _, size_x, size_y, cells_z = both_ref.shape
    t = named(FINISH, (z_ref, later_ref))
    for tile, (total_ref, term_ref) in enumerate(((total0_ref, term0_ref), (total1_ref, term1_ref))):
        wave, rest = [z_transform(to_cells(ref[...], t), t) for ref in (total_ref, term_ref)]
        rest = times(contrast_ref[tile, 0], contrast_ref[tile, 1], rest)
        for place, x in enumerate(cells_x):
            here = slice(place * size_y, (place + 1) * size_y)
            for c in range(2):
                there = slice(c * cells_z, (c + 1) * cells_z)
                both_ref[tile, 0, c, x] = wave[here, there]
                both_ref[tile, 1, c, x] = rest[here, there]
                if tile == 1 and x < 2:
                    layer = wave[here, there]
                    if x == 0:
                        both_ref[0, 1, c, size_x - 2] += layer * (-1.0 / 12.0)
                        both_ref[0, 1, c, size_x - 1] += layer * (16.0 / 12.0)
                    else:
                        both_ref[0, 1, c, size_x - 1] += layer * (-1.0 / 12.0)
    keep_ref[...] = both_ref[core_ref[0]]
    give_ref[...] = both_ref[1 - core_ref[0]]


def add_later(rest_ref, edge_x, edge_y, lower):
    _, size_x, size_y, cells_z = rest_ref.shape
    for c in range(2):
        there = slice(c * cells_z, (c + 1) * cells_z)
        near, far = edge_x[:size_y, there] * lower, edge_x[size_y:, there] * lower
        rest_ref[c, size_x - 2] += near * (-1.0 / 12.0)
        rest_ref[c, size_x - 1] += (16.0 * near - far) * (1.0 / 12.0)
        near, far = edge_y[:size_x, there], edge_y[size_x:, there]
        two = jnp.stack([near * (-1.0 / 12.0), (16.0 * near - far) * (1.0 / 12.0)], axis=1)
        rest_ref[c, :, size_y - 2 :] += two


def keep_kernel(core_ref, keep_ref, edge_x_ref, edge_y_ref, z_ref, rest_ref):
    rest_ref[...] = keep_ref[1]
    count = edge_x_ref.shape[0]
    edges = jnp.concatenate([edge_x_ref[...], edge_y_ref[core_ref[0]]], axis=0)
    edges = z_transform(edges, dict(onward=z_ref))
    add_later(rest_ref, edges[:count], edges[count:], (core_ref[0] == 1).astype(F32))


def place_wave_kernel(rhs_ref, keep_ref, got_ref, wave_ref, sems):
    rhs = rhs_ref[0]
    copies = [
        pltpu.make_async_copy(keep_ref.at[0], wave_ref.at[rhs], sems.at[0]),
        pltpu.make_async_copy(got_ref.at[0], wave_ref.at[1 - rhs], sems.at[1]),
    ]
    for copy in copies:
        copy.start()
    for copy in copies:
        copy.wait()


def place_rest_kernel(core_ref, rhs_ref, keep_rest_ref, got_ref, got_edge_ref, z_ref, rest_ref, work_ref, sems):
    rhs = rhs_ref[0]
    count = got_edge_ref.shape[0] // 2
    copies = [pltpu.make_async_copy(keep_rest_ref, rest_ref.at[rhs], sems.at[0])]
    copies[0].start()
    work_ref[...] = got_ref[1]
    edges = z_transform(got_edge_ref[...], dict(onward=z_ref))
    add_later(work_ref, edges[:count], edges[count:], (core_ref[0] == 1).astype(F32))
    copies.append(pltpu.make_async_copy(work_ref, rest_ref.at[1 - rhs], sems.at[1]))
    copies[1].start()
    for copy in copies:
        copy.wait()


def whole():
    return pl.BlockSpec(memory_space=pltpu.VMEM)


def scalars():
    return pl.BlockSpec(memory_space=pltpu.SMEM)


def anywhere():
    return pl.BlockSpec(memory_space=pl.ANY)


SOLVE_COST = pl.CostEstimate(flops=2 * 10**9, bytes_accessed=2 * 10**6, transcendentals=0)
KEEP_COST = pl.CostEstimate(flops=10**10, bytes_accessed=10**6, transcendentals=0)
PARAMS = pltpu.CompilerParams(vmem_limit_bytes=24 * 1024 * 1024)


def shaped(*shape):
    return jax.ShapeDtypeStruct(shape, F32)


def body(right_side, slowness, source_cells, source_amplitudes):
    sources, _, size_x, size_y, cells_z = right_side.shape
    grid_rows, grid_cols = lax.axis_size("gx"), lax.axis_size("gy")
    assert sources == 2 and grid_rows % 2 == 0 and size_x % 2 == 0
    chips = grid_rows // 2
    row, col = lax.axis_index("gx"), lax.axis_index("gy")
    core = row % 2
    rhs = (core + row // 2 + col) % 2
    core_ref, rhs_ref = core[None], rhs[None]
    t, cells_x = tables(size_x, size_y, cells_z)
    t = {name: jnp.asarray(value) for name, value in t.items()}
    rows = size_x * size_y

    def device(chip, core, column):
        return (2 * chip + core) * grid_cols + column

    def between(pairs):
        return [
            (device(a, r, b), device(c, 1 - r, d)) for (a, b), (c, d) in pairs for r in range(2)
        ]

    own = [
        (device(k, r, j), device(k, 1 - r, j))
        for k in range(chips) for j in range(grid_cols) for r in range(2)
    ]
    axes = ("gx", "gy")
    other = lax.dynamic_index_in_dim(right_side, 1 - rhs, 0, keepdims=False)
    swapped = lax.ppermute(other, axes, own)
    swapped_slow = lax.ppermute(slowness, axes, own)
    mine = lax.dynamic_index_in_dim(right_side, rhs, 0, keepdims=False)

    total_y = size_y * grid_cols
    cells = lax.dynamic_index_in_dim(source_cells, rhs, 0, keepdims=True)
    near_y = cells // cells_z % total_y - col * size_y
    places = []
    for tile_row in (row, row + 1 - 2 * core):
        near_x = cells // (total_y * cells_z) - tile_row * size_x
        inside = (near_x >= 0) & (near_x < size_x) & (near_y >= 0) & (near_y < size_y)
        folded = jnp.where(near_x < size_x // 2, near_x, size_x + size_x // 2 - 1 - near_x)
        places.append(jnp.where(inside, folded * size_y + near_y, -1))
    amplitudes = lax.dynamic_index_in_dim(source_amplitudes, rhs, 0, keepdims=False).T[:, None, :]

    depth = cells % cells_z
    own_modes, own_contrast, t["inverse"], *held = pl.pallas_call(
        functools.partial(prep_kernel, cells_x),
        out_shape=(shaped(rows, 2 * cells_z), shaped(2, rows, cells_z), shaped(2, rows, cells_z))
        + tuple(jax.ShapeDtypeStruct(t[name].shape, BF16) for name in LATER),
        in_specs=[whole()] * (5 + len(PREP)) + [anywhere()] * len(LATER),
        out_specs=(whole(),) * (3 + len(LATER)),
        scratch_shapes=[pltpu.SemaphoreType.DMA((len(LATER),))],
        compiler_params=PARAMS,
        cost_estimate=SOLVE_COST,
        name="prep",
    )(mine, slowness, places[0], depth, amplitudes, *[t[name] for name in PREP + LATER])
    t.update(zip(LATER, held))
    modes, contrast = pl.pallas_call(
        functools.partial(prep_other_kernel, cells_x),
        out_shape=(shaped(2, rows, 2 * cells_z), shaped(2, 2, rows, cells_z)),
        in_specs=[scalars()] * 2 + [whole()] * (7 + len(PREP_OTHER)),
        out_specs=(whole(), whole()),
        compiler_params=PARAMS,
        cost_estimate=SOLVE_COST,
        name="prep_other",
    )(core_ref, rhs_ref, swapped, swapped_slow, own_modes, own_contrast, places[1], depth, amplitudes,
      *[t[name] for name in PREP_OTHER])

    def solve(tile, active, trace_x, trace_y, state, final):
        names = FINAL if final else BEAT
        x, y = shaped(*zero_x.shape), shaped(*zero_y.shape)
        outs = ((x, x, y), (y,))[tile] if final else (x, y)
        total, term, *outs = pl.pallas_call(
            functools.partial(beat_kernel, tile, final),
            out_shape=(shaped(rows, 2 * cells_z),) * 2 + outs,
            in_specs=[scalars()] + [whole()] * (6 + len(names)),
            out_specs=(whole(),) * (2 + len(outs)),
            input_output_aliases={5: 0, 6: 1},
            compiler_params=PARAMS,
            cost_estimate=SOLVE_COST,
            name="upper" if tile == 0 else "lower",
        )(active, modes, contrast, trace_x, trace_y, *state, *[t[name] for name in names])
        return (total, term), outs

    def hand_on(trace):
        return pl.pallas_call(
            hand_on_kernel,
            out_shape=shaped(*trace.shape),
            in_specs=[whole()],
            out_specs=whole(),
            compiler_params=PARAMS,
            name="hand_on",
        )(trace)

    zero_x = jnp.zeros((2 * size_y, 2 * cells_z), F32)
    zero_y = jnp.zeros((2 * size_x, 2 * cells_z), F32)
    trace_x, trace_y0, trace_y1 = zero_x, zero_y, zero_y
    states = [[jnp.zeros((rows, 2 * cells_z), F32)] * 2 for _ in range(2)]
    for beat in range(chips + grid_cols - 1):
        active = (row // 2 + col == beat).astype(jnp.int32)[None]
        here = [(k, beat - k) for k in range(chips) if 0 <= beat - k < grid_cols]
        along_x = between([((k, j), (k + 1, j)) for k, j in here if k + 1 < chips])
        along_y = between([((k, j), (k, j + 1)) for k, j in here if j + 1 < grid_cols])
        final = beat == chips + grid_cols - 2
        states[0], (inner_x, *outs0) = solve(0, active, trace_x, trace_y0, states[0], final)
        if along_y:
            trace_y0 = hand_on(lax.ppermute(outs0[0], axes, along_y))
        states[1], outs1 = solve(1, active, inner_x, trace_y1, states[1], final)
        if along_x:
            trace_x = lax.ppermute(outs1[0], axes, along_x)
        if along_y:
            trace_y1 = lax.ppermute(outs1[1], axes, along_y)
    edge_x, edge_y0 = outs0
    edge_y = jnp.stack([edge_y0, outs1[0]])

    every = [(k, j) for k in range(chips) for j in range(grid_cols)]
    after_x = lax.ppermute(edge_x, axes, between([((k, j), (k - 1, j)) for k, j in every if k]))
    after_y = lax.ppermute(edge_y, axes, between([((k, j), (k, j - 1)) for k, j in every if j]))

    half = shaped(2, 2, size_x, size_y, cells_z)
    keep, give = pl.pallas_call(
        functools.partial(finish_kernel, cells_x),
        out_shape=(half, half),
        in_specs=[scalars()] + [whole()] * 7,
        out_specs=(whole(), whole()),
        scratch_shapes=[pltpu.VMEM((2, 2, 2, size_x, size_y, cells_z), F32)],
        compiler_params=PARAMS,
        name="finish",
    )(core_ref, *states[0], *states[1], contrast, *[t[name] for name in FINISH])
    got = lax.ppermute(give, axes, own)

    pass_y = lax.dynamic_index_in_dim(after_y, 1 - core, 0, keepdims=False)
    got_edge = lax.ppermute(jnp.concatenate([after_x, pass_y], axis=0), axes, own)
    keep_rest = pl.pallas_call(
        keep_kernel,
        out_shape=shaped(*half.shape[1:]),
        in_specs=[scalars()] + [whole()] * 4,
        out_specs=whole(),
        compiler_params=PARAMS,
        cost_estimate=KEEP_COST,
        name="keep",
    )(core_ref, keep, after_x, after_y, t["onward"])
    wavefield = pl.pallas_call(
        place_wave_kernel,
        out_shape=shaped(*right_side.shape),
        in_specs=[scalars()] + [whole()] * 2,
        out_specs=anywhere(),
        scratch_shapes=[pltpu.SemaphoreType.DMA((2,))],
        compiler_params=PARAMS,
        cost_estimate=KEEP_COST,
        name="place_wave",
    )(rhs_ref, keep, got)
    residual = pl.pallas_call(
        place_rest_kernel,
        out_shape=shaped(*right_side.shape),
        in_specs=[scalars()] * 2 + [whole()] * 4,
        out_specs=anywhere(),
        scratch_shapes=[
            pltpu.VMEM((2, size_x, size_y, cells_z), F32),
            pltpu.SemaphoreType.DMA((2,)),
        ],
        compiler_params=PARAMS,
        name="place_rest",
    )(core_ref, rhs_ref, keep_rest, got, got_edge, t["onward"])
    return wavefield, residual


def solution(mesh):
    return jax.shard_map(
        body,
        mesh=mesh,
        in_specs=(P(None, None, "gx", "gy", None), P("gx", "gy", None), P(), P()),
        out_specs=(P(None, None, "gx", "gy", None), P(None, None, "gx", "gy", None)),
        check_vma=False,
    )
```

```python
import functools
import math

import jax
import jax.numpy as jnp
import ml_dtypes
import numpy as np
from jax import lax
from jax.experimental import pallas as pl
from jax.experimental.pallas import tpu as pltpu
from jax.sharding import PartitionSpec as P

KAPPA = 0.12
DAMPING = 0.3
BF16 = jnp.bfloat16
F32 = jnp.float32


def sine_matrix(length):
    index = np.arange(1, length + 1)
    angles = index * (math.pi / (length + 1))
    return math.sqrt(2.0 / (length + 1)) * np.sin(angles[:, None] * index[None, :]), angles


def halves(matrix):
    high = matrix.astype(np.float32).astype(ml_dtypes.bfloat16)
    low = (matrix - high.astype(np.float64)).astype(np.float32).astype(ml_dtypes.bfloat16)
    return high, low


def left_factor(matrix):
    high, low = halves(matrix)
    return np.concatenate([high, high, low], axis=1)


def slabs(matrices, rows, lanes):
    pieces, free = [], 0
    for matrix in matrices:
        for row in range(0, matrix.shape[0], rows):
            for lane in range(0, matrix.shape[1], lanes):
                piece = matrix[row : row + rows, lane : lane + lanes]
                if free + piece.shape[0] > rows or not pieces:
                    pieces.append(np.zeros((rows, lanes), matrix.dtype))
                    free = 0
                pieces[-1][free : free + piece.shape[0], : piece.shape[1]] = piece
                free += piece.shape[0]
    return np.stack(pieces)


def z_matrix(t, depth):
    rows = t["onward"].shape[1]
    pieces = [t["onward"][2 + n, :, :depth] for n in range(-(-depth // rows))]
    return jnp.concatenate(pieces, axis=0)


def enter_matrix(t, depth):
    return jnp.concatenate([t["later"][2, :, :depth], t["later"][3, :, :depth]], axis=0)


def leave_product(t, values):
    high, low = split(values)
    rest = 2 * values.shape[0] - t["later"].shape[2]
    matrix = t["later"][4]
    if rest > 0:
        matrix = jnp.concatenate([matrix, t["later"][2, :, -rest:]], axis=1)
    both = jnp.dot(matrix, jnp.concatenate([high, low], axis=0), preferred_element_type=F32)
    count = both.shape[0] // 2
    return both[:count] + both[count:]


def stacked_factor(matrix):
    high, low = halves(matrix)
    return np.concatenate([np.concatenate([part, part], axis=1) for part in (high, low)], axis=0)


def tables(size_x, size_y, cells_z):
    sine_x, angle_x = sine_matrix(size_x)
    sine_y, angle_y = sine_matrix(size_y)
    sine_z, angle_z = sine_matrix(cells_z)
    half = size_x // 2
    order = np.concatenate([np.arange(0, size_x, 2), np.arange(1, size_x, 2)])
    cells = np.concatenate([np.arange(half), np.arange(size_x - 1, half - 1, -1)])

    def symbol(angle):
        return 2.5 - 8.0 / 3.0 * np.cos(angle) + 1.0 / 6.0 * np.cos(2.0 * angle)

    real_part = (
        symbol(angle_x)[order][:, None, None]
        + symbol(angle_y)[None, :, None]
        + (2.0 - 2.0 * np.cos(angle_z))[None, None, :]
        - KAPPA
    ).reshape(size_x * size_y, cells_z)

    parity = [np.kron(sine_x[order[p * half : (p + 1) * half]][:, :half], sine_y) for p in (0, 1)]
    forward = [left_factor(m) for m in parity]
    backward = [left_factor(m.T) for m in parity]
    high_z, low_z = halves(sine_z)
    right_z = np.concatenate([np.concatenate([high_z, low_z], axis=1)] * 2, axis=0)

    full = np.kron(sine_x[order], sine_y)
    by_cell = full.reshape(-1, size_x, size_y)
    enter_x = np.stack([-by_cell[:, 0] / 12.0, (16.0 * by_cell[:, 0] - by_cell[:, 1]) / 12.0], 1)
    enter_y = np.stack(
        [-by_cell[:, :, 0] / 12.0, (16.0 * by_cell[:, :, 0] - by_cell[:, :, 1]) / 12.0], 1
    )
    enter = left_factor(
        np.concatenate([enter_x.reshape(len(full), -1), enter_y.reshape(len(full), -1)], axis=1)
    )
    leave = stacked_factor(
        np.concatenate(
            [
                by_cell[:, size_x - 2 :].reshape(len(full), -1),
                by_cell[:, :, size_y - 2 :].transpose(0, 2, 1).reshape(len(full), -1),
            ],
            axis=1,
        ).T
    )
    first = left_factor(
        np.concatenate(
            [
                by_cell[:, :2].reshape(len(full), -1),
                by_cell[:, :, :2].transpose(0, 2, 1).reshape(len(full), -1),
            ],
            axis=1,
        ).T
    )
    later = slabs(backward + [enter, leave[:, : forward[0].shape[1]]], half * size_y, forward[0].shape[1])
    rest = leave[:, forward[0].shape[1] :]
    if rest.shape[1]:
        assert enter.shape[1] <= later.shape[2] - rest.shape[1]
        later[2, :, later.shape[2] - rest.shape[1] :] = rest
    assert 2 * cells_z % (half * size_y) == 0 and 2 * cells_z <= forward[0].shape[1]
    assert enter.shape[0] == 2 * half * size_y and enter.shape[1] <= forward[0].shape[1]
    assert leave.shape[0] == half * size_y
    return dict(
        symbol=real_part.astype(np.float32), first=first,
        onward=slabs(forward + [right_z], half * size_y, forward[0].shape[1]),
        later=later,
    ), tuple(int(x) for x in cells)


def divide(modes, t):
    return times(t["inverse"][0], t["inverse"][1], modes)


def split(values):
    high = values.astype(BF16)
    return high, (values - high.astype(F32)).astype(BF16)


def stacked(values):
    high, low = split(values)
    return jnp.concatenate([high, low, high], axis=0)


def left_product(matrix, values):
    return jnp.dot(matrix, stacked(values), preferred_element_type=F32)


def z_transform(field, t):
    rows = field.shape[0]
    cells_z = field.shape[1] // 2
    high, low = split(jnp.concatenate([field[:, :cells_z], field[:, cells_z:]], axis=0))
    both = jnp.dot(jnp.concatenate([high, low], axis=1), z_matrix(t, 2 * cells_z), preferred_element_type=F32)
    total = both[:, :cells_z] + both[:, cells_z:]
    return jnp.concatenate([total[:rows], total[rows:]], axis=1)


def to_modes(field, t):
    count = field.shape[0] // 2
    first, second = field[:count], field[count:]
    return jnp.concatenate(
        [left_product(t["onward"][0], first + second), left_product(t["onward"][1], first - second)], axis=0
    )


def to_cells(modes, t):
    count = modes.shape[0] // 2
    even = left_product(t["later"][0], modes[:count])
    odd = left_product(t["later"][1], modes[count:])
    return jnp.concatenate([even + odd, even - odd], axis=0)


def times(real_part, imag_part, field):
    lanes = field.shape[1] // 2
    real, imag = field[:, :lanes], field[:, lanes:]
    return jnp.concatenate(
        [real_part * real - imag_part * imag, real_part * imag + imag_part * real], axis=1
    )


def apply_contrast(field, contrast, t, block=64):
    done = []
    for start in range(0, field.shape[0], block):
        here = slice(start, start + block)
        cells = times(contrast[0, here], contrast[1, here], z_transform(field[here], t))
        done.append(z_transform(cells, t))
    return jnp.concatenate(done, axis=0)


def solve_modes(start, contrast, t):
    term = total = start
    for _ in range(2):
        term = divide(to_modes(apply_contrast(to_cells(term, t), contrast, t), t), t)
        total = total + term
    return total, term


def edges(rows, lanes, layers):
    place = lax.broadcasted_iota(jnp.int32, (rows, lanes), 0)
    size_y = rows // layers
    along_y = lax.rem(place, size_y)
    outer = lax.rem(place, rows // 2) < size_y
    return (outer.astype(F32) + ((along_y == 0) | (along_y == size_y - 1)).astype(F32)) * (1.0 / 12.0)


def prepare(dense, slow, layers, place, depth, amplitude, t, modes_ref, contrast_ref):
    rows, cells_z = contrast_ref.shape[1:]
    points = place.shape[1]
    row_ids = lax.broadcasted_iota(jnp.int32, (rows, points), 0)
    lane_ids = lax.broadcasted_iota(jnp.int32, (cells_z, points), 0)
    at_lane = (lane_ids == depth).astype(F32)
    spread = []
    for c in range(2):
        amp = amplitude[c]
        one = amp.astype(BF16).astype(F32)
        two = (amp - one).astype(BF16).astype(F32)
        parts = [at_lane * part for part in (one, two, amp - one - two)]
        spread.append(jnp.concatenate(parts, axis=1).astype(BF16))
    scaled = KAPPA * (slow - 1.0)
    contrast_ref[0] = scaled - edges(rows, cells_z, layers)
    contrast_ref[1] = DAMPING * scaled
    at_row = (row_ids == place).astype(F32).astype(BF16)
    field = lax.dot_general(
        jnp.concatenate([at_row] * 3, axis=1), jnp.concatenate(spread, axis=0),
        (((1,), (1,)), ((), ())), preferred_element_type=F32,
    )
    modes_ref[...] = divide(to_modes(z_transform(field + dense, t), t), t)


def hand_on_kernel(in_ref, out_ref):
    out_ref[...] = in_ref[...]


PREP = ("symbol", "onward")
PREP_OTHER = ("inverse", "onward")
BEAT = ("inverse", "onward", "later")
FINAL = BEAT + ("first",)
LATER = ("later",)
FINISH = ("onward", "later")


def named(names, refs):
    return dict(zip(names, refs))


def prep_kernel(cells_x, right_ref, slow_ref, place_ref, depth_ref, amp_ref, *refs):
    later_refs = refs[len(PREP) : len(PREP) + len(LATER)]
    modes_ref, contrast_ref, inverse_ref, *held_refs, sems = refs[len(PREP) + len(LATER) :]
    copies = [
        pltpu.make_async_copy(later_ref, held_ref, sems.at[n])
        for n, (later_ref, held_ref) in enumerate(zip(later_refs, held_refs))
    ]
    for copy in copies:
        copy.start()
    t = named(PREP, refs)
    symbol = t["symbol"][...]
    damping = KAPPA * DAMPING
    scale = 1.0 / (symbol * symbol + damping * damping)
    inverse_ref[0] = symbol * scale
    inverse_ref[1] = damping * scale
    t["inverse"] = inverse_ref
    dense = [jnp.concatenate([right_ref[c, x] for x in cells_x], axis=0) for c in range(2)]
    slow = jnp.concatenate([slow_ref[x] for x in cells_x], axis=0)
    prepare(
        jnp.concatenate(dense, axis=1), slow, len(cells_x), place_ref[...], depth_ref[...], amp_ref, t,
        modes_ref, contrast_ref,
    )
    for copy in copies:
        copy.wait()


def prep_other_kernel(cells_x, core_ref, rhs_ref, swap_ref, slow_ref, own_modes_ref, own_contrast_ref, place_ref, depth_ref, amp_ref,
                      *refs):
    modes_ref, contrast_ref = refs[len(PREP_OTHER) :]
    core = core_ref[0]
    other = 1 - core
    modes_ref[core] = own_modes_ref[...]
    contrast_ref[core] = own_contrast_ref[...]
    dense = [jnp.concatenate([swap_ref[c, x] for x in cells_x], axis=0) for c in range(2)]
    slow = jnp.concatenate([slow_ref[x] for x in cells_x], axis=0)
    prepare(
        jnp.concatenate(dense, axis=1), slow, len(cells_x), place_ref[...], depth_ref[...], amp_ref, named(PREP_OTHER, refs),
        modes_ref.at[other], contrast_ref.at[other],
    )


def beat_kernel(tile, final, active_ref, modes_ref, contrast_ref, trace_x_ref, trace_y_ref, total_ref, term_ref,
                *refs):
    names = FINAL if final else BEAT
    t = named(names, refs)
    new_total_ref, new_term_ref, *out_refs = refs[len(names) :]
    count = trace_x_ref.shape[0]

    @pl.when(active_ref[0] == 1)
    def _():
        trace = jnp.concatenate([trace_x_ref[...], trace_y_ref[...]], axis=0)
        start = modes_ref[tile] + divide(left_product(enter_matrix(t, 3 * trace.shape[0]), trace), t)
        total, term = solve_modes(start, contrast_ref.at[tile], t)
        new_total_ref[...] = total
        new_term_ref[...] = term
        if not (final and tile == 1):
            out = leave_product(t, total)
            for out_ref, part in zip(out_refs[:1] if final else out_refs, (out[:count], out[count:])):
                out_ref[...] = part

    @pl.when(active_ref[0] == 0)
    def _():
        new_total_ref[...] = total_ref[...]
        new_term_ref[...] = term_ref[...]

    if final:
        out = left_product(t["first"][...], new_total_ref[...])
        edge_refs = out_refs[1 - tile :]
        edge_refs[-1][...] = out[count:]
        if tile == 0:
            edge_refs[0][...] = out[:count]


def finish_kernel(cells_x, core_ref, total0_ref, term0_ref, total1_ref, term1_ref, contrast_ref,
                  z_ref, later_ref, keep_ref, give_ref, both_ref):
    _, _, _, size_x, size_y, cells_z = both_ref.shape
    t = named(FINISH, (z_ref, later_ref))
    for tile, (total_ref, term_ref) in enumerate(((total0_ref, term0_ref), (total1_ref, term1_ref))):
        wave, rest = [z_transform(to_cells(ref[...], t), t) for ref in (total_ref, term_ref)]
        rest = times(contrast_ref[tile, 0], contrast_ref[tile, 1], rest)
        for place, x in enumerate(cells_x):
            here = slice(place * size_y, (place + 1) * size_y)
            for c in range(2):
                there = slice(c * cells_z, (c + 1) * cells_z)
                both_ref[tile, 0, c, x] = wave[here, there]
                both_ref[tile, 1, c, x] = rest[here, there]
                if tile == 1 and x < 2:
                    layer = wave[here, there]
                    if x == 0:
                        both_ref[0, 1, c, size_x - 2] += layer * (-1.0 / 12.0)
                        both_ref[0, 1, c, size_x - 1] += layer * (16.0 / 12.0)
                    else:
                        both_ref[0, 1, c, size_x - 1] += layer * (-1.0 / 12.0)
    keep_ref[...] = both_ref[core_ref[0]]
    give_ref[...] = both_ref[1 - core_ref[0]]


def add_later(rest_ref, edge_x, edge_y, lower):
    _, size_x, size_y, cells_z = rest_ref.shape
    for c in range(2):
        there = slice(c * cells_z, (c + 1) * cells_z)
        near, far = edge_x[:size_y, there] * lower, edge_x[size_y:, there] * lower
        rest_ref[c, size_x - 2] += near * (-1.0 / 12.0)
        rest_ref[c, size_x - 1] += (16.0 * near - far) * (1.0 / 12.0)
        near, far = edge_y[:size_x, there], edge_y[size_x:, there]
        two = jnp.stack([near * (-1.0 / 12.0), (16.0 * near - far) * (1.0 / 12.0)], axis=1)
        rest_ref[c, :, size_y - 2 :] += two


def keep_kernel(core_ref, keep_ref, edge_x_ref, edge_y_ref, z_ref, rest_ref):
    rest_ref[...] = keep_ref[1]
    count = edge_x_ref.shape[0]
    edges = jnp.concatenate([edge_x_ref[...], edge_y_ref[core_ref[0]]], axis=0)
    edges = z_transform(edges, dict(onward=z_ref))
    add_later(rest_ref, edges[:count], edges[count:], (core_ref[0] == 1).astype(F32))


def place_wave_kernel(rhs_ref, keep_ref, got_ref, wave_ref, sems):
    rhs = rhs_ref[0]
    copies = [
        pltpu.make_async_copy(keep_ref.at[0], wave_ref.at[rhs], sems.at[0]),
        pltpu.make_async_copy(got_ref.at[0], wave_ref.at[1 - rhs], sems.at[1]),
    ]
    for copy in copies:
        copy.start()
    for copy in copies:
        copy.wait()


def place_rest_kernel(core_ref, rhs_ref, keep_rest_ref, got_ref, got_edge_ref, z_ref, rest_ref, work_ref, sems):
    rhs = rhs_ref[0]
    count = got_edge_ref.shape[0] // 2
    copies = [pltpu.make_async_copy(keep_rest_ref, rest_ref.at[rhs], sems.at[0])]
    copies[0].start()
    work_ref[...] = got_ref[1]
    edges = z_transform(got_edge_ref[...], dict(onward=z_ref))
    add_later(work_ref, edges[:count], edges[count:], (core_ref[0] == 1).astype(F32))
    copies.append(pltpu.make_async_copy(work_ref, rest_ref.at[1 - rhs], sems.at[1]))
    copies[1].start()
    for copy in copies:
        copy.wait()


def whole():
    return pl.BlockSpec(memory_space=pltpu.VMEM)


def scalars():
    return pl.BlockSpec(memory_space=pltpu.SMEM)


def anywhere():
    return pl.BlockSpec(memory_space=pl.ANY)


SOLVE_COST = pl.CostEstimate(flops=2 * 10**9, bytes_accessed=2 * 10**6, transcendentals=0)
KEEP_COST = pl.CostEstimate(flops=10**10, bytes_accessed=10**6, transcendentals=0)
PARAMS = pltpu.CompilerParams(vmem_limit_bytes=24 * 1024 * 1024)


def shaped(*shape):
    return jax.ShapeDtypeStruct(shape, F32)


def body(right_side, slowness, source_cells, source_amplitudes):
    sources, _, size_x, size_y, cells_z = right_side.shape
    grid_rows, grid_cols = lax.axis_size("gx"), lax.axis_size("gy")
    assert sources == 2 and grid_rows % 2 == 0 and size_x % 2 == 0
    chips = grid_rows // 2
    row, col = lax.axis_index("gx"), lax.axis_index("gy")
    core = row % 2
    rhs = (core + row // 2 + col) % 2
    core_ref, rhs_ref = core[None], rhs[None]
    t, cells_x = tables(size_x, size_y, cells_z)
    t = {name: jnp.asarray(value) for name, value in t.items()}
    rows = size_x * size_y

    def device(chip, core, column):
        return (2 * chip + core) * grid_cols + column

    def between(pairs):
        return [
            (device(a, r, b), device(c, 1 - r, d)) for (a, b), (c, d) in pairs for r in range(2)
        ]

    own = [
        (device(k, r, j), device(k, 1 - r, j))
        for k in range(chips) for j in range(grid_cols) for r in range(2)
    ]
    axes = ("gx", "gy")
    other = lax.dynamic_index_in_dim(right_side, 1 - rhs, 0, keepdims=False)
    swapped = lax.ppermute(other, axes, own)
    swapped_slow = lax.ppermute(slowness, axes, own)
    mine = lax.dynamic_index_in_dim(right_side, rhs, 0, keepdims=False)

    total_y = size_y * grid_cols
    cells = lax.dynamic_index_in_dim(source_cells, rhs, 0, keepdims=True)
    near_y = cells // cells_z % total_y - col * size_y
    places = []
    for tile_row in (row, row + 1 - 2 * core):
        near_x = cells // (total_y * cells_z) - tile_row * size_x
        inside = (near_x >= 0) & (near_x < size_x) & (near_y >= 0) & (near_y < size_y)
        folded = jnp.where(near_x < size_x // 2, near_x, size_x + size_x // 2 - 1 - near_x)
        places.append(jnp.where(inside, folded * size_y + near_y, -1))
    amplitudes = lax.dynamic_index_in_dim(source_amplitudes, rhs, 0, keepdims=False).T[:, None, :]

    depth = cells % cells_z
    own_modes, own_contrast, t["inverse"], *held = pl.pallas_call(
        functools.partial(prep_kernel, cells_x),
        out_shape=(shaped(rows, 2 * cells_z), shaped(2, rows, cells_z), shaped(2, rows, cells_z))
        + tuple(jax.ShapeDtypeStruct(t[name].shape, BF16) for name in LATER),
        in_specs=[whole()] * (5 + len(PREP)) + [anywhere()] * len(LATER),
        out_specs=(whole(),) * (3 + len(LATER)),
        scratch_shapes=[pltpu.SemaphoreType.DMA((len(LATER),))],
        compiler_params=PARAMS,
        cost_estimate=SOLVE_COST,
        name="prep",
    )(mine, slowness, places[0], depth, amplitudes, *[t[name] for name in PREP + LATER])
    t.update(zip(LATER, held))
    modes, contrast = pl.pallas_call(
        functools.partial(prep_other_kernel, cells_x),
        out_shape=(shaped(2, rows, 2 * cells_z), shaped(2, 2, rows, cells_z)),
        in_specs=[scalars()] * 2 + [whole()] * (7 + len(PREP_OTHER)),
        out_specs=(whole(), whole()),
        compiler_params=PARAMS,
        cost_estimate=SOLVE_COST,
        name="prep_other",
    )(core_ref, rhs_ref, swapped, swapped_slow, own_modes, own_contrast, places[1], depth, amplitudes,
      *[t[name] for name in PREP_OTHER])

    def solve(tile, active, trace_x, trace_y, state, final):
        names = FINAL if final else BEAT
        x, y = shaped(*zero_x.shape), shaped(*zero_y.shape)
        outs = ((x, x, y), (y,))[tile] if final else (x, y)
        total, term, *outs = pl.pallas_call(
            functools.partial(beat_kernel, tile, final),
            out_shape=(shaped(rows, 2 * cells_z),) * 2 + outs,
            in_specs=[scalars()] + [whole()] * (6 + len(names)),
            out_specs=(whole(),) * (2 + len(outs)),
            input_output_aliases={5: 0, 6: 1},
            compiler_params=PARAMS,
            cost_estimate=SOLVE_COST,
            name="upper" if tile == 0 else "lower",
        )(active, modes, contrast, trace_x, trace_y, *state, *[t[name] for name in names])
        return (total, term), outs

    def hand_on(trace, cost=None):
        return pl.pallas_call(
            hand_on_kernel,
            out_shape=shaped(*trace.shape),
            in_specs=[whole()],
            out_specs=whole(),
            compiler_params=PARAMS,
            cost_estimate=cost,
            name="hand_on",
        )(trace)

    zero_x = jnp.zeros((2 * size_y, 2 * cells_z), F32)
    zero_y = jnp.zeros((2 * size_x, 2 * cells_z), F32)
    trace_x, trace_y0, trace_y1 = zero_x, zero_y, zero_y
    states = [[jnp.zeros((rows, 2 * cells_z), F32)] * 2 for _ in range(2)]
    for beat in range(chips + grid_cols - 1):
        active = (row // 2 + col == beat).astype(jnp.int32)[None]
        here = [(k, beat - k) for k in range(chips) if 0 <= beat - k < grid_cols]
        along_x = between([((k, j), (k + 1, j)) for k, j in here if k + 1 < chips])
        along_y = between([((k, j), (k, j + 1)) for k, j in here if j + 1 < grid_cols])
        final = beat == chips + grid_cols - 2
        states[0], (inner_x, *outs0) = solve(0, active, trace_x, trace_y0, states[0], final)
        if along_y:
            trace_y0 = hand_on(lax.ppermute(outs0[0], axes, along_y))
        states[1], outs1 = solve(1, active, inner_x, trace_y1, states[1], final)
        if along_x:
            trace_x = lax.ppermute(outs1[0], axes, along_x)
        if along_y:
            trace_y1 = lax.ppermute(outs1[1], axes, along_y)
    edge_x, edge_y0 = outs0
    edge_y = jnp.stack([edge_y0, outs1[0]])

    every = [(k, j) for k in range(chips) for j in range(grid_cols)]
    after_x = hand_on(
        lax.ppermute(edge_x, axes, between([((k, j), (k - 1, j)) for k, j in every if k])), KEEP_COST
    )
    after_y = lax.ppermute(edge_y, axes, between([((k, j), (k, j - 1)) for k, j in every if j]))

    half = shaped(2, 2, size_x, size_y, cells_z)
    keep, give = pl.pallas_call(
        functools.partial(finish_kernel, cells_x),
        out_shape=(half, half),
        in_specs=[scalars()] + [whole()] * 7,
        out_specs=(whole(), whole()),
        scratch_shapes=[pltpu.VMEM((2, 2, 2, size_x, size_y, cells_z), F32)],
        compiler_params=PARAMS,
        name="finish",
    )(core_ref, *states[0], *states[1], contrast, *[t[name] for name in FINISH])
    got = lax.ppermute(give, axes, own)

    pass_y = lax.dynamic_index_in_dim(after_y, 1 - core, 0, keepdims=False)
    got_edge = lax.ppermute(jnp.concatenate([after_x, pass_y], axis=0), axes, own)
    keep_rest = pl.pallas_call(
        keep_kernel,
        out_shape=shaped(*half.shape[1:]),
        in_specs=[scalars()] + [whole()] * 4,
        out_specs=whole(),
        compiler_params=PARAMS,
        cost_estimate=KEEP_COST,
        name="keep",
    )(core_ref, keep, after_x, after_y, t["onward"])
    wavefield = pl.pallas_call(
        place_wave_kernel,
        out_shape=shaped(*right_side.shape),
        in_specs=[scalars()] + [whole()] * 2,
        out_specs=anywhere(),
        scratch_shapes=[pltpu.SemaphoreType.DMA((2,))],
        compiler_params=PARAMS,
        cost_estimate=KEEP_COST,
        name="place_wave",
    )(rhs_ref, keep, got)
    residual = pl.pallas_call(
        place_rest_kernel,
        out_shape=shaped(*right_side.shape),
        in_specs=[scalars()] * 2 + [whole()] * 4,
        out_specs=anywhere(),
        scratch_shapes=[
            pltpu.VMEM((2, size_x, size_y, cells_z), F32),
            pltpu.SemaphoreType.DMA((2,)),
        ],
        compiler_params=PARAMS,
        name="place_rest",
    )(core_ref, rhs_ref, keep_rest, got, got_edge, t["onward"])
    return wavefield, residual


def solution(mesh):
    return jax.shard_map(
        body,
        mesh=mesh,
        in_specs=(P(None, None, "gx", "gy", None), P("gx", "gy", None), P(), P()),
        out_specs=(P(None, None, "gx", "gy", None), P(None, None, "gx", "gy", None)),
        check_vma=False,
    )
```

```python
import functools
import math

import jax
import jax.numpy as jnp
import ml_dtypes
import numpy as np
from jax import lax
from jax.experimental import pallas as pl
from jax.experimental.pallas import tpu as pltpu
from jax.sharding import PartitionSpec as P

KAPPA = 0.12
DAMPING = 0.3
BF16 = jnp.bfloat16
F32 = jnp.float32


def sine_matrix(length):
    index = np.arange(1, length + 1)
    angles = index * (math.pi / (length + 1))
    return math.sqrt(2.0 / (length + 1)) * np.sin(angles[:, None] * index[None, :]), angles


def halves(matrix):
    high = matrix.astype(np.float32).astype(ml_dtypes.bfloat16)
    low = (matrix - high.astype(np.float64)).astype(np.float32).astype(ml_dtypes.bfloat16)
    return high, low


def left_factor(matrix):
    high, low = halves(matrix)
    return np.concatenate([high, high, low], axis=1)


def slabs(matrices, rows, lanes):
    pieces, free = [], 0
    for matrix in matrices:
        for row in range(0, matrix.shape[0], rows):
            for lane in range(0, matrix.shape[1], lanes):
                piece = matrix[row : row + rows, lane : lane + lanes]
                if free + piece.shape[0] > rows or not pieces:
                    pieces.append(np.zeros((rows, lanes), matrix.dtype))
                    free = 0
                pieces[-1][free : free + piece.shape[0], : piece.shape[1]] = piece
                free += piece.shape[0]
    return np.stack(pieces)


def z_matrix(t, depth):
    rows = t["onward"].shape[1]
    pieces = [t["onward"][2 + n, :, :depth] for n in range(-(-depth // rows))]
    return jnp.concatenate(pieces, axis=0)


def enter_matrix(t, depth):
    return jnp.concatenate([t["later"][2, :, :depth], t["later"][3, :, :depth]], axis=0)


def leave_product(t, values):
    high, low = split(values)
    rest = 2 * values.shape[0] - t["later"].shape[2]
    matrix = t["later"][4]
    if rest > 0:
        matrix = jnp.concatenate([matrix, t["later"][2, :, -rest:]], axis=1)
    both = jnp.dot(matrix, jnp.concatenate([high, low], axis=0), preferred_element_type=F32)
    count = both.shape[0] // 2
    return both[:count] + both[count:]


def stacked_factor(matrix):
    high, low = halves(matrix)
    return np.concatenate([np.concatenate([part, part], axis=1) for part in (high, low)], axis=0)


def tables(size_x, size_y, cells_z):
    sine_x, angle_x = sine_matrix(size_x)
    sine_y, angle_y = sine_matrix(size_y)
    sine_z, angle_z = sine_matrix(cells_z)
    half = size_x // 2
    order = np.concatenate([np.arange(0, size_x, 2), np.arange(1, size_x, 2)])
    cells = np.concatenate([np.arange(half), np.arange(size_x - 1, half - 1, -1)])

    def symbol(angle):
        return 2.5 - 8.0 / 3.0 * np.cos(angle) + 1.0 / 6.0 * np.cos(2.0 * angle)

    real_part = (
        symbol(angle_x)[order][:, None, None]
        + symbol(angle_y)[None, :, None]
        + (2.0 - 2.0 * np.cos(angle_z))[None, None, :]
        - KAPPA
    ).reshape(size_x * size_y, cells_z)

    parity = [np.kron(sine_x[order[p * half : (p + 1) * half]][:, :half], sine_y) for p in (0, 1)]
    forward = [left_factor(m) for m in parity]
    backward = [left_factor(m.T) for m in parity]
    high_z, low_z = halves(sine_z)
    right_z = np.concatenate([np.concatenate([high_z, low_z], axis=1)] * 2, axis=0)

    full = np.kron(sine_x[order], sine_y)
    by_cell = full.reshape(-1, size_x, size_y)
    enter_x = np.stack([-by_cell[:, 0] / 12.0, (16.0 * by_cell[:, 0] - by_cell[:, 1]) / 12.0], 1)
    enter_y = np.stack(
        [-by_cell[:, :, 0] / 12.0, (16.0 * by_cell[:, :, 0] - by_cell[:, :, 1]) / 12.0], 1
    )
    enter = left_factor(
        np.concatenate([enter_x.reshape(len(full), -1), enter_y.reshape(len(full), -1)], axis=1)
    )
    leave = stacked_factor(
        np.concatenate(
            [
                by_cell[:, size_x - 2 :].reshape(len(full), -1),
                by_cell[:, :, size_y - 2 :].transpose(0, 2, 1).reshape(len(full), -1),
            ],
            axis=1,
        ).T
    )
    first = left_factor(
        np.concatenate(
            [
                by_cell[:, :2].reshape(len(full), -1),
                by_cell[:, :, :2].transpose(0, 2, 1).reshape(len(full), -1),
            ],
            axis=1,
        ).T
    )
    later = slabs(backward + [enter, leave[:, : forward[0].shape[1]]], half * size_y, forward[0].shape[1])
    rest = leave[:, forward[0].shape[1] :]
    if rest.shape[1]:
        assert enter.shape[1] <= later.shape[2] - rest.shape[1]
        later[2, :, later.shape[2] - rest.shape[1] :] = rest
    assert 2 * cells_z % (half * size_y) == 0 and 2 * cells_z <= forward[0].shape[1]
    assert enter.shape[0] == 2 * half * size_y and enter.shape[1] <= forward[0].shape[1]
    assert leave.shape[0] == half * size_y
    return dict(
        symbol=real_part.astype(np.float32), first=first,
        onward=slabs(forward + [right_z], half * size_y, forward[0].shape[1]),
        later=later,
    ), tuple(int(x) for x in cells)


def divide(modes, t):
    return times(t["inverse"][0], t["inverse"][1], modes)


def split(values):
    high = values.astype(BF16)
    return high, (values - high.astype(F32)).astype(BF16)


def stacked(values):
    high, low = split(values)
    return jnp.concatenate([high, low, high], axis=0)


def left_product(matrix, values):
    return jnp.dot(matrix, stacked(values), preferred_element_type=F32)


def z_transform(field, t):
    rows = field.shape[0]
    cells_z = field.shape[1] // 2
    high, low = split(jnp.concatenate([field[:, :cells_z], field[:, cells_z:]], axis=0))
    both = jnp.dot(jnp.concatenate([high, low], axis=1), z_matrix(t, 2 * cells_z), preferred_element_type=F32)
    total = both[:, :cells_z] + both[:, cells_z:]
    return jnp.concatenate([total[:rows], total[rows:]], axis=1)


def to_modes(field, t):
    count = field.shape[0] // 2
    first, second = field[:count], field[count:]
    return jnp.concatenate(
        [left_product(t["onward"][0], first + second), left_product(t["onward"][1], first - second)], axis=0
    )


def to_cells(modes, t):
    count = modes.shape[0] // 2
    even = left_product(t["later"][0], modes[:count])
    odd = left_product(t["later"][1], modes[count:])
    return jnp.concatenate([even + odd, even - odd], axis=0)


def times(real_part, imag_part, field):
    lanes = field.shape[1] // 2
    real, imag = field[:, :lanes], field[:, lanes:]
    return jnp.concatenate(
        [real_part * real - imag_part * imag, real_part * imag + imag_part * real], axis=1
    )


def apply_contrast(field, contrast, t, block=128):
    done = []
    for start in range(0, field.shape[0], block):
        here = slice(start, start + block)
        cells = times(contrast[0, here], contrast[1, here], z_transform(field[here], t))
        done.append(z_transform(cells, t))
    return jnp.concatenate(done, axis=0)


def solve_modes(start, contrast, t):
    term = total = start
    for _ in range(2):
        term = divide(to_modes(apply_contrast(to_cells(term, t), contrast, t), t), t)
        total = total + term
    return total, term


def edges(rows, lanes, layers):
    place = lax.broadcasted_iota(jnp.int32, (rows, lanes), 0)
    size_y = rows // layers
    along_y = lax.rem(place, size_y)
    outer = lax.rem(place, rows // 2) < size_y
    return (outer.astype(F32) + ((along_y == 0) | (along_y == size_y - 1)).astype(F32)) * (1.0 / 12.0)


def prepare(dense, slow, layers, place, depth, amplitude, t, modes_ref, contrast_ref):
    rows, cells_z = contrast_ref.shape[1:]
    points = place.shape[1]
    row_ids = lax.broadcasted_iota(jnp.int32, (rows, points), 0)
    lane_ids = lax.broadcasted_iota(jnp.int32, (cells_z, points), 0)
    at_lane = (lane_ids == depth).astype(F32)
    spread = []
    for c in range(2):
        amp = amplitude[c]
        one = amp.astype(BF16).astype(F32)
        two = (amp - one).astype(BF16).astype(F32)
        parts = [at_lane * part for part in (one, two, amp - one - two)]
        spread.append(jnp.concatenate(parts, axis=1).astype(BF16))
    scaled = KAPPA * (slow - 1.0)
    contrast_ref[0] = scaled - edges(rows, cells_z, layers)
    contrast_ref[1] = DAMPING * scaled
    at_row = (row_ids == place).astype(F32).astype(BF16)
    field = lax.dot_general(
        jnp.concatenate([at_row] * 3, axis=1), jnp.concatenate(spread, axis=0),
        (((1,), (1,)), ((), ())), preferred_element_type=F32,
    )
    modes_ref[...] = divide(to_modes(z_transform(field + dense, t), t), t)


def hand_on_kernel(in_ref, out_ref):
    out_ref[...] = in_ref[...]


PREP = ("symbol", "onward")
PREP_OTHER = ("inverse", "onward")
BEAT = ("inverse", "onward", "later")
FINAL = BEAT + ("first",)
LATER = ("later",)
FINISH = ("onward", "later")


def named(names, refs):
    return dict(zip(names, refs))


def prep_kernel(cells_x, right_ref, slow_ref, place_ref, depth_ref, amp_ref, *refs):
    later_refs = refs[len(PREP) : len(PREP) + len(LATER)]
    modes_ref, contrast_ref, inverse_ref, *held_refs, sems = refs[len(PREP) + len(LATER) :]
    copies = [
        pltpu.make_async_copy(later_ref, held_ref, sems.at[n])
        for n, (later_ref, held_ref) in enumerate(zip(later_refs, held_refs))
    ]
    for copy in copies:
        copy.start()
    t = named(PREP, refs)
    symbol = t["symbol"][...]
    damping = KAPPA * DAMPING
    scale = 1.0 / (symbol * symbol + damping * damping)
    inverse_ref[0] = symbol * scale
    inverse_ref[1] = damping * scale
    t["inverse"] = inverse_ref
    dense = [jnp.concatenate([right_ref[c, x] for x in cells_x], axis=0) for c in range(2)]
    slow = jnp.concatenate([slow_ref[x] for x in cells_x], axis=0)
    prepare(
        jnp.concatenate(dense, axis=1), slow, len(cells_x), place_ref[...], depth_ref[...], amp_ref, t,
        modes_ref, contrast_ref,
    )
    for copy in copies:
        copy.wait()


def prep_other_kernel(cells_x, core_ref, rhs_ref, swap_ref, slow_ref, own_modes_ref, own_contrast_ref, place_ref, depth_ref, amp_ref,
                      *refs):
    modes_ref, contrast_ref = refs[len(PREP_OTHER) :]
    core = core_ref[0]
    other = 1 - core
    modes_ref[core] = own_modes_ref[...]
    contrast_ref[core] = own_contrast_ref[...]
    dense = [jnp.concatenate([swap_ref[c, x] for x in cells_x], axis=0) for c in range(2)]
    slow = jnp.concatenate([slow_ref[x] for x in cells_x], axis=0)
    prepare(
        jnp.concatenate(dense, axis=1), slow, len(cells_x), place_ref[...], depth_ref[...], amp_ref, named(PREP_OTHER, refs),
        modes_ref.at[other], contrast_ref.at[other],
    )


def beat_kernel(tile, final, active_ref, modes_ref, contrast_ref, trace_x_ref, trace_y_ref, total_ref, term_ref,
                *refs):
    names = FINAL if final else BEAT
    t = named(names, refs)
    new_total_ref, new_term_ref, *out_refs = refs[len(names) :]
    count = trace_x_ref.shape[0]

    @pl.when(active_ref[0] == 1)
    def _():
        trace = jnp.concatenate([trace_x_ref[...], trace_y_ref[...]], axis=0)
        start = modes_ref[tile] + divide(left_product(enter_matrix(t, 3 * trace.shape[0]), trace), t)
        total, term = solve_modes(start, contrast_ref.at[tile], t)
        new_total_ref[...] = total
        new_term_ref[...] = term
        if not (final and tile == 1):
            out = leave_product(t, total)
            for out_ref, part in zip(out_refs[:1] if final else out_refs, (out[:count], out[count:])):
                out_ref[...] = part

    @pl.when(active_ref[0] == 0)
    def _():
        new_total_ref[...] = total_ref[...]
        new_term_ref[...] = term_ref[...]

    if final:
        out = left_product(t["first"][...], new_total_ref[...])
        edge_refs = out_refs[1 - tile :]
        edge_refs[-1][...] = out[count:]
        if tile == 0:
            edge_refs[0][...] = out[:count]


def finish_kernel(cells_x, core_ref, total0_ref, term0_ref, total1_ref, term1_ref, contrast_ref,
                  z_ref, later_ref, keep_ref, give_ref, both_ref):
    _, _, _, size_x, size_y, cells_z = both_ref.shape
    t = named(FINISH, (z_ref, later_ref))
    for tile, (total_ref, term_ref) in enumerate(((total0_ref, term0_ref), (total1_ref, term1_ref))):
        wave, rest = [z_transform(to_cells(ref[...], t), t) for ref in (total_ref, term_ref)]
        rest = times(contrast_ref[tile, 0], contrast_ref[tile, 1], rest)
        for place, x in enumerate(cells_x):
            here = slice(place * size_y, (place + 1) * size_y)
            for c in range(2):
                there = slice(c * cells_z, (c + 1) * cells_z)
                both_ref[tile, 0, c, x] = wave[here, there]
                both_ref[tile, 1, c, x] = rest[here, there]
                if tile == 1 and x < 2:
                    layer = wave[here, there]
                    if x == 0:
                        both_ref[0, 1, c, size_x - 2] += layer * (-1.0 / 12.0)
                        both_ref[0, 1, c, size_x - 1] += layer * (16.0 / 12.0)
                    else:
                        both_ref[0, 1, c, size_x - 1] += layer * (-1.0 / 12.0)
    keep_ref[...] = both_ref[core_ref[0]]
    give_ref[...] = both_ref[1 - core_ref[0]]


def add_later(rest_ref, edge_x, edge_y, lower):
    _, size_x, size_y, cells_z = rest_ref.shape
    for c in range(2):
        there = slice(c * cells_z, (c + 1) * cells_z)
        near, far = edge_x[:size_y, there] * lower, edge_x[size_y:, there] * lower
        rest_ref[c, size_x - 2] += near * (-1.0 / 12.0)
        rest_ref[c, size_x - 1] += (16.0 * near - far) * (1.0 / 12.0)
        near, far = edge_y[:size_x, there], edge_y[size_x:, there]
        two = jnp.stack([near * (-1.0 / 12.0), (16.0 * near - far) * (1.0 / 12.0)], axis=1)
        rest_ref[c, :, size_y - 2 :] += two


def keep_kernel(core_ref, keep_ref, edge_x_ref, edge_y_ref, z_ref, rest_ref):
    rest_ref[...] = keep_ref[1]
    count = edge_x_ref.shape[0]
    edges = jnp.concatenate([edge_x_ref[...], edge_y_ref[core_ref[0]]], axis=0)
    edges = z_transform(edges, dict(onward=z_ref))
    add_later(rest_ref, edges[:count], edges[count:], (core_ref[0] == 1).astype(F32))


def place_wave_kernel(rhs_ref, keep_ref, got_ref, wave_ref, sems):
    rhs = rhs_ref[0]
    copies = [
        pltpu.make_async_copy(keep_ref.at[0], wave_ref.at[rhs], sems.at[0]),
        pltpu.make_async_copy(got_ref.at[0], wave_ref.at[1 - rhs], sems.at[1]),
    ]
    for copy in copies:
        copy.start()
    for copy in copies:
        copy.wait()


def place_rest_kernel(core_ref, rhs_ref, keep_rest_ref, got_ref, got_edge_ref, z_ref, rest_ref, work_ref, sems):
    rhs = rhs_ref[0]
    count = got_edge_ref.shape[0] // 2
    copies = [pltpu.make_async_copy(keep_rest_ref, rest_ref.at[rhs], sems.at[0])]
    copies[0].start()
    work_ref[...] = got_ref[1]
    edges = z_transform(got_edge_ref[...], dict(onward=z_ref))
    add_later(work_ref, edges[:count], edges[count:], (core_ref[0] == 1).astype(F32))
    copies.append(pltpu.make_async_copy(work_ref, rest_ref.at[1 - rhs], sems.at[1]))
    copies[1].start()
    for copy in copies:
        copy.wait()


def whole():
    return pl.BlockSpec(memory_space=pltpu.VMEM)


def scalars():
    return pl.BlockSpec(memory_space=pltpu.SMEM)


def anywhere():
    return pl.BlockSpec(memory_space=pl.ANY)


SOLVE_COST = pl.CostEstimate(flops=2 * 10**9, bytes_accessed=2 * 10**6, transcendentals=0)
KEEP_COST = pl.CostEstimate(flops=10**10, bytes_accessed=10**6, transcendentals=0)
PARAMS = pltpu.CompilerParams(vmem_limit_bytes=24 * 1024 * 1024)


def shaped(*shape):
    return jax.ShapeDtypeStruct(shape, F32)


def body(right_side, slowness, source_cells, source_amplitudes):
    sources, _, size_x, size_y, cells_z = right_side.shape
    grid_rows, grid_cols = lax.axis_size("gx"), lax.axis_size("gy")
    assert sources == 2 and grid_rows % 2 == 0 and size_x % 2 == 0
    chips = grid_rows // 2
    row, col = lax.axis_index("gx"), lax.axis_index("gy")
    core = row % 2
    rhs = (core + row // 2 + col) % 2
    core_ref, rhs_ref = core[None], rhs[None]
    t, cells_x = tables(size_x, size_y, cells_z)
    t = {name: jnp.asarray(value) for name, value in t.items()}
    rows = size_x * size_y

    def device(chip, core, column):
        return (2 * chip + core) * grid_cols + column

    def between(pairs):
        return [
            (device(a, r, b), device(c, 1 - r, d)) for (a, b), (c, d) in pairs for r in range(2)
        ]

    own = [
        (device(k, r, j), device(k, 1 - r, j))
        for k in range(chips) for j in range(grid_cols) for r in range(2)
    ]
    axes = ("gx", "gy")
    other = lax.dynamic_index_in_dim(right_side, 1 - rhs, 0, keepdims=False)
    swapped = lax.ppermute(other, axes, own)
    swapped_slow = lax.ppermute(slowness, axes, own)
    mine = lax.dynamic_index_in_dim(right_side, rhs, 0, keepdims=False)

    total_y = size_y * grid_cols
    cells = lax.dynamic_index_in_dim(source_cells, rhs, 0, keepdims=True)
    near_y = cells // cells_z % total_y - col * size_y
    places = []
    for tile_row in (row, row + 1 - 2 * core):
        near_x = cells // (total_y * cells_z) - tile_row * size_x
        inside = (near_x >= 0) & (near_x < size_x) & (near_y >= 0) & (near_y < size_y)
        folded = jnp.where(near_x < size_x // 2, near_x, size_x + size_x // 2 - 1 - near_x)
        places.append(jnp.where(inside, folded * size_y + near_y, -1))
    amplitudes = lax.dynamic_index_in_dim(source_amplitudes, rhs, 0, keepdims=False).T[:, None, :]

    depth = cells % cells_z
    own_modes, own_contrast, t["inverse"], *held = pl.pallas_call(
        functools.partial(prep_kernel, cells_x),
        out_shape=(shaped(rows, 2 * cells_z), shaped(2, rows, cells_z), shaped(2, rows, cells_z))
        + tuple(jax.ShapeDtypeStruct(t[name].shape, BF16) for name in LATER),
        in_specs=[whole()] * (5 + len(PREP)) + [anywhere()] * len(LATER),
        out_specs=(whole(),) * (3 + len(LATER)),
        scratch_shapes=[pltpu.SemaphoreType.DMA((len(LATER),))],
        compiler_params=PARAMS,
        cost_estimate=SOLVE_COST,
        name="prep",
    )(mine, slowness, places[0], depth, amplitudes, *[t[name] for name in PREP + LATER])
    t.update(zip(LATER, held))
    modes, contrast = pl.pallas_call(
        functools.partial(prep_other_kernel, cells_x),
        out_shape=(shaped(2, rows, 2 * cells_z), shaped(2, 2, rows, cells_z)),
        in_specs=[scalars()] * 2 + [whole()] * (7 + len(PREP_OTHER)),
        out_specs=(whole(), whole()),
        compiler_params=PARAMS,
        cost_estimate=SOLVE_COST,
        name="prep_other",
    )(core_ref, rhs_ref, swapped, swapped_slow, own_modes, own_contrast, places[1], depth, amplitudes,
      *[t[name] for name in PREP_OTHER])

    def solve(tile, active, trace_x, trace_y, state, final):
        names = FINAL if final else BEAT
        x, y = shaped(*zero_x.shape), shaped(*zero_y.shape)
        outs = ((x, x, y), (y,))[tile] if final else (x, y)
        total, term, *outs = pl.pallas_call(
            functools.partial(beat_kernel, tile, final),
            out_shape=(shaped(rows, 2 * cells_z),) * 2 + outs,
            in_specs=[scalars()] + [whole()] * (6 + len(names)),
            out_specs=(whole(),) * (2 + len(outs)),
            input_output_aliases={5: 0, 6: 1},
            compiler_params=PARAMS,
            cost_estimate=SOLVE_COST,
            name="upper" if tile == 0 else "lower",
        )(active, modes, contrast, trace_x, trace_y, *state, *[t[name] for name in names])
        return (total, term), outs

    def hand_on(trace, cost=None):
        return pl.pallas_call(
            hand_on_kernel,
            out_shape=shaped(*trace.shape),
            in_specs=[whole()],
            out_specs=whole(),
            compiler_params=PARAMS,
            cost_estimate=cost,
            name="hand_on",
        )(trace)

    zero_x = jnp.zeros((2 * size_y, 2 * cells_z), F32)
    zero_y = jnp.zeros((2 * size_x, 2 * cells_z), F32)
    trace_x, trace_y0, trace_y1 = zero_x, zero_y, zero_y
    states = [[jnp.zeros((rows, 2 * cells_z), F32)] * 2 for _ in range(2)]
    for beat in range(chips + grid_cols - 1):
        active = (row // 2 + col == beat).astype(jnp.int32)[None]
        here = [(k, beat - k) for k in range(chips) if 0 <= beat - k < grid_cols]
        along_x = between([((k, j), (k + 1, j)) for k, j in here if k + 1 < chips])
        along_y = between([((k, j), (k, j + 1)) for k, j in here if j + 1 < grid_cols])
        final = beat == chips + grid_cols - 2
        states[0], (inner_x, *outs0) = solve(0, active, trace_x, trace_y0, states[0], final)
        if along_y:
            trace_y0 = hand_on(lax.ppermute(outs0[0], axes, along_y))
        states[1], outs1 = solve(1, active, inner_x, trace_y1, states[1], final)
        if along_x:
            trace_x = lax.ppermute(outs1[0], axes, along_x)
        if along_y:
            trace_y1 = lax.ppermute(outs1[1], axes, along_y)
    edge_x, edge_y0 = outs0
    edge_y = jnp.stack([edge_y0, outs1[0]])

    every = [(k, j) for k in range(chips) for j in range(grid_cols)]
    after_x = hand_on(
        lax.ppermute(edge_x, axes, between([((k, j), (k - 1, j)) for k, j in every if k])), KEEP_COST
    )
    after_y = lax.ppermute(edge_y, axes, between([((k, j), (k, j - 1)) for k, j in every if j]))

    half = shaped(2, 2, size_x, size_y, cells_z)
    keep, give = pl.pallas_call(
        functools.partial(finish_kernel, cells_x),
        out_shape=(half, half),
        in_specs=[scalars()] + [whole()] * 7,
        out_specs=(whole(), whole()),
        scratch_shapes=[pltpu.VMEM((2, 2, 2, size_x, size_y, cells_z), F32)],
        compiler_params=PARAMS,
        name="finish",
    )(core_ref, *states[0], *states[1], contrast, *[t[name] for name in FINISH])
    got = lax.ppermute(give, axes, own)

    pass_y = lax.dynamic_index_in_dim(after_y, 1 - core, 0, keepdims=False)
    got_edge = lax.ppermute(jnp.concatenate([after_x, pass_y], axis=0), axes, own)
    keep_rest = pl.pallas_call(
        keep_kernel,
        out_shape=shaped(*half.shape[1:]),
        in_specs=[scalars()] + [whole()] * 4,
        out_specs=whole(),
        compiler_params=PARAMS,
        cost_estimate=KEEP_COST,
        name="keep",
    )(core_ref, keep, after_x, after_y, t["onward"])
    wavefield = pl.pallas_call(
        place_wave_kernel,
        out_shape=shaped(*right_side.shape),
        in_specs=[scalars()] + [whole()] * 2,
        out_specs=anywhere(),
        scratch_shapes=[pltpu.SemaphoreType.DMA((2,))],
        compiler_params=PARAMS,
        cost_estimate=KEEP_COST,
        name="place_wave",
    )(rhs_ref, keep, got)
    residual = pl.pallas_call(
        place_rest_kernel,
        out_shape=shaped(*right_side.shape),
        in_specs=[scalars()] * 2 + [whole()] * 4,
        out_specs=anywhere(),
        scratch_shapes=[
            pltpu.VMEM((2, size_x, size_y, cells_z), F32),
            pltpu.SemaphoreType.DMA((2,)),
        ],
        compiler_params=PARAMS,
        name="place_rest",
    )(core_ref, rhs_ref, keep_rest, got, got_edge, t["onward"])
    return wavefield, residual


def solution(mesh):
    return jax.shard_map(
        body,
        mesh=mesh,
        in_specs=(P(None, None, "gx", "gy", None), P("gx", "gy", None), P(), P()),
        out_specs=(P(None, None, "gx", "gy", None), P(None, None, "gx", "gy", None)),
        check_vma=False,
    )
```

```python
import functools
import math

import jax
import jax.numpy as jnp
import ml_dtypes
import numpy as np
from jax import lax
from jax.experimental import pallas as pl
from jax.experimental.pallas import tpu as pltpu
from jax.sharding import PartitionSpec as P

KAPPA = 0.12
DAMPING = 0.3
BF16 = jnp.bfloat16
F32 = jnp.float32


def sine_matrix(length):
    index = np.arange(1, length + 1)
    angles = index * (math.pi / (length + 1))
    return math.sqrt(2.0 / (length + 1)) * np.sin(angles[:, None] * index[None, :]), angles


def halves(matrix):
    high = matrix.astype(np.float32).astype(ml_dtypes.bfloat16)
    low = (matrix - high.astype(np.float64)).astype(np.float32).astype(ml_dtypes.bfloat16)
    return high, low


def left_factor(matrix):
    high, low = halves(matrix)
    return np.concatenate([high, high, low], axis=1)


def slabs(matrices, rows, lanes):
    pieces, free = [], 0
    for matrix in matrices:
        for row in range(0, matrix.shape[0], rows):
            for lane in range(0, matrix.shape[1], lanes):
                piece = matrix[row : row + rows, lane : lane + lanes]
                if free + piece.shape[0] > rows or not pieces:
                    pieces.append(np.zeros((rows, lanes), matrix.dtype))
                    free = 0
                pieces[-1][free : free + piece.shape[0], : piece.shape[1]] = piece
                free += piece.shape[0]
    return np.stack(pieces)


def z_matrix(t, depth):
    rows = t["onward"].shape[1]
    pieces = [t["onward"][2 + n, :, :depth] for n in range(-(-depth // rows))]
    return jnp.concatenate(pieces, axis=0)


def enter_matrix(t, depth):
    return jnp.concatenate([t["later"][2, :, :depth], t["later"][3, :, :depth]], axis=0)


def leave_product(t, values):
    high, low = split(values)
    rest = 2 * values.shape[0] - t["later"].shape[2]
    matrix = t["later"][4]
    if rest > 0:
        matrix = jnp.concatenate([matrix, t["later"][2, :, -rest:]], axis=1)
    both = jnp.dot(matrix, jnp.concatenate([high, low], axis=0), preferred_element_type=F32)
    count = both.shape[0] // 2
    return both[:count] + both[count:]


def stacked_factor(matrix):
    high, low = halves(matrix)
    return np.concatenate([np.concatenate([part, part], axis=1) for part in (high, low)], axis=0)


def tables(size_x, size_y, cells_z):
    sine_x, angle_x = sine_matrix(size_x)
    sine_y, angle_y = sine_matrix(size_y)
    sine_z, angle_z = sine_matrix(cells_z)
    half = size_x // 2
    order = np.concatenate([np.arange(0, size_x, 2), np.arange(1, size_x, 2)])
    cells = np.concatenate([np.arange(half), np.arange(size_x - 1, half - 1, -1)])

    def symbol(angle):
        return 2.5 - 8.0 / 3.0 * np.cos(angle) + 1.0 / 6.0 * np.cos(2.0 * angle)

    real_part = (
        symbol(angle_x)[order][:, None, None]
        + symbol(angle_y)[None, :, None]
        + (2.0 - 2.0 * np.cos(angle_z))[None, None, :]
        - KAPPA
    ).reshape(size_x * size_y, cells_z)

    parity = [np.kron(sine_x[order[p * half : (p + 1) * half]][:, :half], sine_y) for p in (0, 1)]
    forward = [left_factor(m) for m in parity]
    backward = [left_factor(m.T) for m in parity]
    high_z, low_z = halves(sine_z)
    right_z = np.concatenate([np.concatenate([high_z, low_z], axis=1)] * 2, axis=0)

    full = np.kron(sine_x[order], sine_y)
    by_cell = full.reshape(-1, size_x, size_y)
    enter_x = np.stack([-by_cell[:, 0] / 12.0, (16.0 * by_cell[:, 0] - by_cell[:, 1]) / 12.0], 1)
    enter_y = np.stack(
        [-by_cell[:, :, 0] / 12.0, (16.0 * by_cell[:, :, 0] - by_cell[:, :, 1]) / 12.0], 1
    )
    enter = left_factor(
        np.concatenate([enter_x.reshape(len(full), -1), enter_y.reshape(len(full), -1)], axis=1)
    )
    leave = stacked_factor(
        np.concatenate(
            [
                by_cell[:, size_x - 2 :].reshape(len(full), -1),
                by_cell[:, :, size_y - 2 :].transpose(0, 2, 1).reshape(len(full), -1),
            ],
            axis=1,
        ).T
    )
    first = left_factor(
        np.concatenate(
            [
                by_cell[:, :2].reshape(len(full), -1),
                by_cell[:, :, :2].transpose(0, 2, 1).reshape(len(full), -1),
            ],
            axis=1,
        ).T
    )
    later = slabs(backward + [enter, leave[:, : forward[0].shape[1]]], half * size_y, forward[0].shape[1])
    rest = leave[:, forward[0].shape[1] :]
    if rest.shape[1]:
        assert enter.shape[1] <= later.shape[2] - rest.shape[1]
        later[2, :, later.shape[2] - rest.shape[1] :] = rest
    assert 2 * cells_z % (half * size_y) == 0 and 2 * cells_z <= forward[0].shape[1]
    assert enter.shape[0] == 2 * half * size_y and enter.shape[1] <= forward[0].shape[1]
    assert leave.shape[0] == half * size_y
    return dict(
        symbol=real_part.astype(np.float32), first=first,
        onward=slabs(forward + [right_z], half * size_y, forward[0].shape[1]),
        later=later,
    ), tuple(int(x) for x in cells)


def divide(modes, t):
    return times(t["inverse"][0], t["inverse"][1], modes)


def split(values):
    high = values.astype(BF16)
    return high, (values - high.astype(F32)).astype(BF16)


def stacked(values):
    high, low = split(values)
    return jnp.concatenate([high, low, high], axis=0)


def left_product(matrix, values):
    return jnp.dot(matrix, stacked(values), preferred_element_type=F32)


def z_transform(field, t):
    rows = field.shape[0]
    cells_z = field.shape[1] // 2
    high, low = split(jnp.concatenate([field[:, :cells_z], field[:, cells_z:]], axis=0))
    both = jnp.dot(jnp.concatenate([high, low], axis=1), z_matrix(t, 2 * cells_z), preferred_element_type=F32)
    total = both[:, :cells_z] + both[:, cells_z:]
    return jnp.concatenate([total[:rows], total[rows:]], axis=1)


def to_modes(field, t):
    count = field.shape[0] // 2
    first, second = field[:count], field[count:]
    return jnp.concatenate(
        [left_product(t["onward"][0], first + second), left_product(t["onward"][1], first - second)], axis=0
    )


def to_cells(modes, t):
    count = modes.shape[0] // 2
    even = left_product(t["later"][0], modes[:count])
    odd = left_product(t["later"][1], modes[count:])
    return jnp.concatenate([even + odd, even - odd], axis=0)


def times(real_part, imag_part, field):
    lanes = field.shape[1] // 2
    real, imag = field[:, :lanes], field[:, lanes:]
    return jnp.concatenate(
        [real_part * real - imag_part * imag, real_part * imag + imag_part * real], axis=1
    )


def solve_modes(start, contrast, t, block=32):
    half = start.shape[0] // 2
    term = total = start
    for _ in range(2):
        even = left_product(t["later"][0], term[:half])
        odd = left_product(t["later"][1], term[half:])
        folded = ([], [])
        for at in range(0, half, block):
            here, there = slice(at, at + block), slice(half + at, half + at + block)
            factor = [jnp.concatenate([contrast[c, here], contrast[c, there]], axis=0) for c in range(2)]
            cells = jnp.concatenate([even[here] + odd[here], even[here] - odd[here]], axis=0)
            cells = z_transform(times(*factor, z_transform(cells, t)), t)
            folded[0].append(split(cells[:block] + cells[block:]))
            folded[1].append(split(cells[:block] - cells[block:]))
        parts = []
        for p in range(2):
            high, low = [jnp.concatenate(pieces, axis=0) for pieces in zip(*folded[p])]
            data = jnp.concatenate([high, low, high], axis=0)
            modes = jnp.dot(t["onward"][p], data, preferred_element_type=F32)
            here = slice(p * half, (p + 1) * half)
            parts.append(times(t["inverse"][0, here], t["inverse"][1, here], modes))
        term = jnp.concatenate(parts, axis=0)
        total = total + term
    return total, term


def edges(rows, lanes, layers):
    place = lax.broadcasted_iota(jnp.int32, (rows, lanes), 0)
    size_y = rows // layers
    along_y = lax.rem(place, size_y)
    outer = lax.rem(place, rows // 2) < size_y
    return (outer.astype(F32) + ((along_y == 0) | (along_y == size_y - 1)).astype(F32)) * (1.0 / 12.0)


def prepare(dense, slow, layers, place, depth, amplitude, t, modes_ref, contrast_ref):
    rows, cells_z = contrast_ref.shape[1:]
    points = place.shape[1]
    row_ids = lax.broadcasted_iota(jnp.int32, (rows, points), 0)
    lane_ids = lax.broadcasted_iota(jnp.int32, (cells_z, points), 0)
    at_lane = (lane_ids == depth).astype(F32)
    spread = []
    for c in range(2):
        amp = amplitude[c]
        one = amp.astype(BF16).astype(F32)
        two = (amp - one).astype(BF16).astype(F32)
        parts = [at_lane * part for part in (one, two, amp - one - two)]
        spread.append(jnp.concatenate(parts, axis=1).astype(BF16))
    scaled = KAPPA * (slow - 1.0)
    contrast_ref[0] = scaled - edges(rows, cells_z, layers)
    contrast_ref[1] = DAMPING * scaled
    at_row = (row_ids == place).astype(F32).astype(BF16)
    field = lax.dot_general(
        jnp.concatenate([at_row] * 3, axis=1), jnp.concatenate(spread, axis=0),
        (((1,), (1,)), ((), ())), preferred_element_type=F32,
    )
    modes_ref[...] = divide(to_modes(z_transform(field + dense, t), t), t)


def hand_on_kernel(in_ref, out_ref):
    out_ref[...] = in_ref[...]


PREP = ("symbol", "onward")
PREP_OTHER = ("inverse", "onward")
BEAT = ("inverse", "onward", "later")
FINAL = BEAT + ("first",)
LATER = ("later",)
FINISH = ("onward", "later")


def named(names, refs):
    return dict(zip(names, refs))


def prep_kernel(cells_x, right_ref, slow_ref, place_ref, depth_ref, amp_ref, *refs):
    later_refs = refs[len(PREP) : len(PREP) + len(LATER)]
    modes_ref, contrast_ref, inverse_ref, *held_refs, sems = refs[len(PREP) + len(LATER) :]
    copies = [
        pltpu.make_async_copy(later_ref, held_ref, sems.at[n])
        for n, (later_ref, held_ref) in enumerate(zip(later_refs, held_refs))
    ]
    for copy in copies:
        copy.start()
    t = named(PREP, refs)
    symbol = t["symbol"][...]
    damping = KAPPA * DAMPING
    scale = 1.0 / (symbol * symbol + damping * damping)
    inverse_ref[0] = symbol * scale
    inverse_ref[1] = damping * scale
    t["inverse"] = inverse_ref
    dense = [jnp.concatenate([right_ref[c, x] for x in cells_x], axis=0) for c in range(2)]
    slow = jnp.concatenate([slow_ref[x] for x in cells_x], axis=0)
    prepare(
        jnp.concatenate(dense, axis=1), slow, len(cells_x), place_ref[...], depth_ref[...], amp_ref, t,
        modes_ref, contrast_ref,
    )
    for copy in copies:
        copy.wait()


def prep_other_kernel(cells_x, core_ref, rhs_ref, swap_ref, slow_ref, own_modes_ref, own_contrast_ref, place_ref, depth_ref, amp_ref,
                      *refs):
    modes_ref, contrast_ref = refs[len(PREP_OTHER) :]
    core = core_ref[0]
    other = 1 - core
    modes_ref[core] = own_modes_ref[...]
    contrast_ref[core] = own_contrast_ref[...]
    dense = [jnp.concatenate([swap_ref[c, x] for x in cells_x], axis=0) for c in range(2)]
    slow = jnp.concatenate([slow_ref[x] for x in cells_x], axis=0)
    prepare(
        jnp.concatenate(dense, axis=1), slow, len(cells_x), place_ref[...], depth_ref[...], amp_ref, named(PREP_OTHER, refs),
        modes_ref.at[other], contrast_ref.at[other],
    )


def beat_kernel(tile, final, active_ref, modes_ref, contrast_ref, trace_x_ref, trace_y_ref, total_ref, term_ref,
                *refs):
    names = FINAL if final else BEAT
    t = named(names, refs)
    new_total_ref, new_term_ref, *out_refs = refs[len(names) :]
    count = trace_x_ref.shape[0]

    @pl.when(active_ref[0] == 1)
    def _():
        trace = jnp.concatenate([trace_x_ref[...], trace_y_ref[...]], axis=0)
        start = modes_ref[tile] + divide(left_product(enter_matrix(t, 3 * trace.shape[0]), trace), t)
        total, term = solve_modes(start, contrast_ref.at[tile], t)
        new_total_ref[...] = total
        new_term_ref[...] = term
        if not (final and tile == 1):
            out = leave_product(t, total)
            for out_ref, part in zip(out_refs[:1] if final else out_refs, (out[:count], out[count:])):
                out_ref[...] = part

    @pl.when(active_ref[0] == 0)
    def _():
        new_total_ref[...] = total_ref[...]
        new_term_ref[...] = term_ref[...]

    if final:
        out = left_product(t["first"][...], new_total_ref[...])
        edge_refs = out_refs[1 - tile :]
        edge_refs[-1][...] = out[count:]
        if tile == 0:
            edge_refs[0][...] = out[:count]


def finish_kernel(cells_x, core_ref, total0_ref, term0_ref, total1_ref, term1_ref, contrast_ref,
                  z_ref, later_ref, keep_ref, give_ref, both_ref):
    _, _, _, size_x, size_y, cells_z = both_ref.shape
    t = named(FINISH, (z_ref, later_ref))
    for tile, (total_ref, term_ref) in enumerate(((total0_ref, term0_ref), (total1_ref, term1_ref))):
        wave, rest = [z_transform(to_cells(ref[...], t), t) for ref in (total_ref, term_ref)]
        rest = times(contrast_ref[tile, 0], contrast_ref[tile, 1], rest)
        for place, x in enumerate(cells_x):
            here = slice(place * size_y, (place + 1) * size_y)
            for c in range(2):
                there = slice(c * cells_z, (c + 1) * cells_z)
                both_ref[tile, 0, c, x] = wave[here, there]
                both_ref[tile, 1, c, x] = rest[here, there]
                if tile == 1 and x < 2:
                    layer = wave[here, there]
                    if x == 0:
                        both_ref[0, 1, c, size_x - 2] += layer * (-1.0 / 12.0)
                        both_ref[0, 1, c, size_x - 1] += layer * (16.0 / 12.0)
                    else:
                        both_ref[0, 1, c, size_x - 1] += layer * (-1.0 / 12.0)
    keep_ref[...] = both_ref[core_ref[0]]
    give_ref[...] = both_ref[1 - core_ref[0]]


def add_later(rest_ref, edge_x, edge_y, lower):
    _, size_x, size_y, cells_z = rest_ref.shape
    for c in range(2):
        there = slice(c * cells_z, (c + 1) * cells_z)
        near, far = edge_x[:size_y, there] * lower, edge_x[size_y:, there] * lower
        rest_ref[c, size_x - 2] += near * (-1.0 / 12.0)
        rest_ref[c, size_x - 1] += (16.0 * near - far) * (1.0 / 12.0)
        near, far = edge_y[:size_x, there], edge_y[size_x:, there]
        two = jnp.stack([near * (-1.0 / 12.0), (16.0 * near - far) * (1.0 / 12.0)], axis=1)
        rest_ref[c, :, size_y - 2 :] += two


def keep_kernel(core_ref, keep_ref, edge_x_ref, edge_y_ref, z_ref, rest_ref):
    rest_ref[...] = keep_ref[1]
    count = edge_x_ref.shape[0]
    edges = jnp.concatenate([edge_x_ref[...], edge_y_ref[core_ref[0]]], axis=0)
    edges = z_transform(edges, dict(onward=z_ref))
    add_later(rest_ref, edges[:count], edges[count:], (core_ref[0] == 1).astype(F32))


def place_wave_kernel(rhs_ref, keep_ref, got_ref, wave_ref, sems):
    rhs = rhs_ref[0]
    copies = [
        pltpu.make_async_copy(keep_ref.at[0], wave_ref.at[rhs], sems.at[0]),
        pltpu.make_async_copy(got_ref.at[0], wave_ref.at[1 - rhs], sems.at[1]),
    ]
    for copy in copies:
        copy.start()
    for copy in copies:
        copy.wait()


def place_rest_kernel(core_ref, rhs_ref, keep_rest_ref, got_ref, got_edge_ref, z_ref, rest_ref, work_ref, sems):
    rhs = rhs_ref[0]
    count = got_edge_ref.shape[0] // 2
    copies = [pltpu.make_async_copy(keep_rest_ref, rest_ref.at[rhs], sems.at[0])]
    copies[0].start()
    work_ref[...] = got_ref[1]
    edges = z_transform(got_edge_ref[...], dict(onward=z_ref))
    add_later(work_ref, edges[:count], edges[count:], (core_ref[0] == 1).astype(F32))
    copies.append(pltpu.make_async_copy(work_ref, rest_ref.at[1 - rhs], sems.at[1]))
    copies[1].start()
    for copy in copies:
        copy.wait()


def whole():
    return pl.BlockSpec(memory_space=pltpu.VMEM)


def scalars():
    return pl.BlockSpec(memory_space=pltpu.SMEM)


def anywhere():
    return pl.BlockSpec(memory_space=pl.ANY)


SOLVE_COST = pl.CostEstimate(flops=2 * 10**9, bytes_accessed=2 * 10**6, transcendentals=0)
KEEP_COST = pl.CostEstimate(flops=10**10, bytes_accessed=10**6, transcendentals=0)
PARAMS = pltpu.CompilerParams(vmem_limit_bytes=24 * 1024 * 1024)


def shaped(*shape):
    return jax.ShapeDtypeStruct(shape, F32)


def body(right_side, slowness, source_cells, source_amplitudes):
    sources, _, size_x, size_y, cells_z = right_side.shape
    grid_rows, grid_cols = lax.axis_size("gx"), lax.axis_size("gy")
    assert sources == 2 and grid_rows % 2 == 0 and size_x % 2 == 0
    chips = grid_rows // 2
    row, col = lax.axis_index("gx"), lax.axis_index("gy")
    core = row % 2
    rhs = (core + row // 2 + col) % 2
    core_ref, rhs_ref = core[None], rhs[None]
    t, cells_x = tables(size_x, size_y, cells_z)
    t = {name: jnp.asarray(value) for name, value in t.items()}
    rows = size_x * size_y

    def device(chip, core, column):
        return (2 * chip + core) * grid_cols + column

    def between(pairs):
        return [
            (device(a, r, b), device(c, 1 - r, d)) for (a, b), (c, d) in pairs for r in range(2)
        ]

    own = [
        (device(k, r, j), device(k, 1 - r, j))
        for k in range(chips) for j in range(grid_cols) for r in range(2)
    ]
    axes = ("gx", "gy")
    other = lax.dynamic_index_in_dim(right_side, 1 - rhs, 0, keepdims=False)
    swapped = lax.ppermute(other, axes, own)
    swapped_slow = lax.ppermute(slowness, axes, own)
    mine = lax.dynamic_index_in_dim(right_side, rhs, 0, keepdims=False)

    total_y = size_y * grid_cols
    cells = lax.dynamic_index_in_dim(source_cells, rhs, 0, keepdims=True)
    near_y = cells // cells_z % total_y - col * size_y
    places = []
    for tile_row in (row, row + 1 - 2 * core):
        near_x = cells // (total_y * cells_z) - tile_row * size_x
        inside = (near_x >= 0) & (near_x < size_x) & (near_y >= 0) & (near_y < size_y)
        folded = jnp.where(near_x < size_x // 2, near_x, size_x + size_x // 2 - 1 - near_x)
        places.append(jnp.where(inside, folded * size_y + near_y, -1))
    amplitudes = lax.dynamic_index_in_dim(source_amplitudes, rhs, 0, keepdims=False).T[:, None, :]

    depth = cells % cells_z
    own_modes, own_contrast, t["inverse"], *held = pl.pallas_call(
        functools.partial(prep_kernel, cells_x),
        out_shape=(shaped(rows, 2 * cells_z), shaped(2, rows, cells_z), shaped(2, rows, cells_z))
        + tuple(jax.ShapeDtypeStruct(t[name].shape, BF16) for name in LATER),
        in_specs=[whole()] * (5 + len(PREP)) + [anywhere()] * len(LATER),
        out_specs=(whole(),) * (3 + len(LATER)),
        scratch_shapes=[pltpu.SemaphoreType.DMA((len(LATER),))],
        compiler_params=PARAMS,
        cost_estimate=SOLVE_COST,
        name="prep",
    )(mine, slowness, places[0], depth, amplitudes, *[t[name] for name in PREP + LATER])
    t.update(zip(LATER, held))
    modes, contrast = pl.pallas_call(
        functools.partial(prep_other_kernel, cells_x),
        out_shape=(shaped(2, rows, 2 * cells_z), shaped(2, 2, rows, cells_z)),
        in_specs=[scalars()] * 2 + [whole()] * (7 + len(PREP_OTHER)),
        out_specs=(whole(), whole()),
        compiler_params=PARAMS,
        cost_estimate=SOLVE_COST,
        name="prep_other",
    )(core_ref, rhs_ref, swapped, swapped_slow, own_modes, own_contrast, places[1], depth, amplitudes,
      *[t[name] for name in PREP_OTHER])

    def solve(tile, active, trace_x, trace_y, state, final):
        names = FINAL if final else BEAT
        x, y = shaped(*zero_x.shape), shaped(*zero_y.shape)
        outs = ((x, x, y), (y,))[tile] if final else (x, y)
        total, term, *outs = pl.pallas_call(
            functools.partial(beat_kernel, tile, final),
            out_shape=(shaped(rows, 2 * cells_z),) * 2 + outs,
            in_specs=[scalars()] + [whole()] * (6 + len(names)),
            out_specs=(whole(),) * (2 + len(outs)),
            input_output_aliases={5: 0, 6: 1},
            compiler_params=PARAMS,
            cost_estimate=SOLVE_COST,
            name="upper" if tile == 0 else "lower",
        )(active, modes, contrast, trace_x, trace_y, *state, *[t[name] for name in names])
        return (total, term), outs

    def hand_on(trace, cost=None):
        return pl.pallas_call(
            hand_on_kernel,
            out_shape=shaped(*trace.shape),
            in_specs=[whole()],
            out_specs=whole(),
            compiler_params=PARAMS,
            cost_estimate=cost,
            name="hand_on",
        )(trace)

    zero_x = jnp.zeros((2 * size_y, 2 * cells_z), F32)
    zero_y = jnp.zeros((2 * size_x, 2 * cells_z), F32)
    trace_x, trace_y0, trace_y1 = zero_x, zero_y, zero_y
    states = [[jnp.zeros((rows, 2 * cells_z), F32)] * 2 for _ in range(2)]
    for beat in range(chips + grid_cols - 1):
        active = (row // 2 + col == beat).astype(jnp.int32)[None]
        here = [(k, beat - k) for k in range(chips) if 0 <= beat - k < grid_cols]
        along_x = between([((k, j), (k + 1, j)) for k, j in here if k + 1 < chips])
        along_y = between([((k, j), (k, j + 1)) for k, j in here if j + 1 < grid_cols])
        final = beat == chips + grid_cols - 2
        states[0], (inner_x, *outs0) = solve(0, active, trace_x, trace_y0, states[0], final)
        if along_y:
            trace_y0 = hand_on(lax.ppermute(outs0[0], axes, along_y))
        states[1], outs1 = solve(1, active, inner_x, trace_y1, states[1], final)
        if along_x:
            trace_x = lax.ppermute(outs1[0], axes, along_x)
        if along_y:
            trace_y1 = lax.ppermute(outs1[1], axes, along_y)
    edge_x, edge_y0 = outs0
    edge_y = jnp.stack([edge_y0, outs1[0]])

    every = [(k, j) for k in range(chips) for j in range(grid_cols)]
    after_x = hand_on(
        lax.ppermute(edge_x, axes, between([((k, j), (k - 1, j)) for k, j in every if k])), KEEP_COST
    )
    after_y = lax.ppermute(edge_y, axes, between([((k, j), (k, j - 1)) for k, j in every if j]))

    half = shaped(2, 2, size_x, size_y, cells_z)
    keep, give = pl.pallas_call(
        functools.partial(finish_kernel, cells_x),
        out_shape=(half, half),
        in_specs=[scalars()] + [whole()] * 7,
        out_specs=(whole(), whole()),
        scratch_shapes=[pltpu.VMEM((2, 2, 2, size_x, size_y, cells_z), F32)],
        compiler_params=PARAMS,
        name="finish",
    )(core_ref, *states[0], *states[1], contrast, *[t[name] for name in FINISH])
    got = lax.ppermute(give, axes, own)

    pass_y = lax.dynamic_index_in_dim(after_y, 1 - core, 0, keepdims=False)
    got_edge = lax.ppermute(jnp.concatenate([after_x, pass_y], axis=0), axes, own)
    keep_rest = pl.pallas_call(
        keep_kernel,
        out_shape=shaped(*half.shape[1:]),
        in_specs=[scalars()] + [whole()] * 4,
        out_specs=whole(),
        compiler_params=PARAMS,
        cost_estimate=KEEP_COST,
        name="keep",
    )(core_ref, keep, after_x, after_y, t["onward"])
    wavefield = pl.pallas_call(
        place_wave_kernel,
        out_shape=shaped(*right_side.shape),
        in_specs=[scalars()] + [whole()] * 2,
        out_specs=anywhere(),
        scratch_shapes=[pltpu.SemaphoreType.DMA((2,))],
        compiler_params=PARAMS,
        cost_estimate=KEEP_COST,
        name="place_wave",
    )(rhs_ref, keep, got)
    residual = pl.pallas_call(
        place_rest_kernel,
        out_shape=shaped(*right_side.shape),
        in_specs=[scalars()] * 2 + [whole()] * 4,
        out_specs=anywhere(),
        scratch_shapes=[
            pltpu.VMEM((2, size_x, size_y, cells_z), F32),
            pltpu.SemaphoreType.DMA((2,)),
        ],
        compiler_params=PARAMS,
        name="place_rest",
    )(core_ref, rhs_ref, keep_rest, got, got_edge, t["onward"])
    return wavefield, residual


def solution(mesh):
    return jax.shard_map(
        body,
        mesh=mesh,
        in_specs=(P(None, None, "gx", "gy", None), P("gx", "gy", None), P(), P()),
        out_specs=(P(None, None, "gx", "gy", None), P(None, None, "gx", "gy", None)),
        check_vma=False,
    )
```

```python
import functools
import math

import jax
import jax.numpy as jnp
import ml_dtypes
import numpy as np
from jax import lax
from jax.experimental import pallas as pl
from jax.experimental.pallas import tpu as pltpu
from jax.sharding import PartitionSpec as P

KAPPA = 0.12
DAMPING = 0.3
BF16 = jnp.bfloat16
F32 = jnp.float32


def sine_matrix(length):
    index = np.arange(1, length + 1)
    angles = index * (math.pi / (length + 1))
    return math.sqrt(2.0 / (length + 1)) * np.sin(angles[:, None] * index[None, :]), angles


def halves(matrix):
    high = matrix.astype(np.float32).astype(ml_dtypes.bfloat16)
    low = (matrix - high.astype(np.float64)).astype(np.float32).astype(ml_dtypes.bfloat16)
    return high, low


def left_factor(matrix):
    high, low = halves(matrix)
    return np.concatenate([high, high, low], axis=1)


def slabs(matrices, rows, lanes):
    pieces, free = [], 0
    for matrix in matrices:
        for row in range(0, matrix.shape[0], rows):
            for lane in range(0, matrix.shape[1], lanes):
                piece = matrix[row : row + rows, lane : lane + lanes]
                if free + piece.shape[0] > rows or not pieces:
                    pieces.append(np.zeros((rows, lanes), matrix.dtype))
                    free = 0
                pieces[-1][free : free + piece.shape[0], : piece.shape[1]] = piece
                free += piece.shape[0]
    return np.stack(pieces)


def quarter_matrix(slabs_ref, index):
    count = slabs_ref.shape[1] // 2
    return slabs_ref[index // 2, index % 2 * count : (index % 2 + 1) * count, : 3 * count]


def z_matrix(t, depth):
    rows = t["onward"].shape[1]
    pieces = [t["onward"][2 + n, :, :depth] for n in range(-(-depth // rows))]
    return jnp.concatenate(pieces, axis=0)


def enter_matrix(t, depth):
    return jnp.concatenate([t["later"][2, :, :depth], t["later"][3, :, :depth]], axis=0)


def leave_product(t, values):
    high, low = split(values)
    rest = 2 * values.shape[0] - t["later"].shape[2]
    matrix = t["later"][4]
    if rest > 0:
        matrix = jnp.concatenate([matrix, t["later"][2, :, -rest:]], axis=1)
    both = jnp.dot(matrix, jnp.concatenate([high, low], axis=0), preferred_element_type=F32)
    count = both.shape[0] // 2
    return both[:count] + both[count:]


def stacked_factor(matrix):
    high, low = halves(matrix)
    return np.concatenate([np.concatenate([part, part], axis=1) for part in (high, low)], axis=0)


def tables(size_x, size_y, cells_z):
    sine_x, angle_x = sine_matrix(size_x)
    sine_y, angle_y = sine_matrix(size_y)
    sine_z, angle_z = sine_matrix(cells_z)
    half = size_x // 2
    assert half % 8 == 0 and size_y % 16 == 0
    order_x, order_y = [np.arange(0, n, 2).reshape(1, -1) + [[0], [1]] for n in (size_x, size_y)]
    pairs = [(x, y) for p in range(2) for q in range(2) for x in order_x[p] for y in order_y[q]]
    mode_x, mode_y = np.array(pairs).T
    cells = np.concatenate([np.arange(half), np.arange(size_x - 1, half - 1, -1)])

    def symbol(angle):
        return 2.5 - 8.0 / 3.0 * np.cos(angle) + 1.0 / 6.0 * np.cos(2.0 * angle)

    real_part = (
        symbol(angle_x)[mode_x][:, None]
        + symbol(angle_y)[mode_y][:, None]
        + (2.0 - 2.0 * np.cos(angle_z))[None, :]
        - KAPPA
    )

    slab = half * size_y
    lanes = 3 * slab
    parity = [
        np.kron(sine_x[order_x[p]][:, :half], sine_y[order_y[q]][:, : size_y // 2])
        for p in range(2) for q in range(2)
    ]
    forward = [left_factor(m) for m in parity]
    backward = [left_factor(m.T) for m in parity]
    high_z, low_z = halves(sine_z)
    right_z = np.concatenate([np.concatenate([high_z, low_z], axis=1)] * 2, axis=0)

    by_cell = sine_x[mode_x][:, :, None] * sine_y[mode_y][:, None, :]
    full = by_cell.reshape(len(by_cell), -1)
    enter_x = np.stack([-by_cell[:, 0] / 12.0, (16.0 * by_cell[:, 0] - by_cell[:, 1]) / 12.0], 1)
    enter_y = np.stack(
        [-by_cell[:, :, 0] / 12.0, (16.0 * by_cell[:, :, 0] - by_cell[:, :, 1]) / 12.0], 1
    )
    enter = left_factor(
        np.concatenate([enter_x.reshape(len(full), -1), enter_y.reshape(len(full), -1)], axis=1)
    )
    leave = stacked_factor(
        np.concatenate(
            [
                by_cell[:, size_x - 2 :].reshape(len(full), -1),
                by_cell[:, :, size_y - 2 :].transpose(0, 2, 1).reshape(len(full), -1),
            ],
            axis=1,
        ).T
    )
    first = left_factor(
        np.concatenate(
            [
                by_cell[:, :2].reshape(len(full), -1),
                by_cell[:, :, :2].transpose(0, 2, 1).reshape(len(full), -1),
            ],
            axis=1,
        ).T
    )
    later = slabs(backward + [enter, leave[:, : lanes]], slab, lanes)
    rest = leave[:, lanes :]
    if rest.shape[1]:
        assert enter.shape[1] <= later.shape[2] - rest.shape[1]
        later[2, :, later.shape[2] - rest.shape[1] :] = rest
    assert 2 * cells_z % slab == 0 and 2 * cells_z <= lanes
    assert enter.shape[0] == 2 * slab and enter.shape[1] <= lanes
    assert leave.shape[0] == slab
    return dict(
        symbol=real_part.astype(np.float32), first=first,
        onward=slabs(forward + [right_z], slab, lanes),
        later=later,
    ), tuple(int(x) for x in cells)


def divide(modes, t):
    return times(t["inverse"][0], t["inverse"][1], modes)


def split(values):
    high = values.astype(BF16)
    return high, (values - high.astype(F32)).astype(BF16)


def stacked(values):
    high, low = split(values)
    return jnp.concatenate([high, low, high], axis=0)


def left_product(matrix, values):
    return jnp.dot(matrix, stacked(values), preferred_element_type=F32)


def z_transform(field, t):
    rows = field.shape[0]
    cells_z = field.shape[1] // 2
    high, low = split(jnp.concatenate([field[:, :cells_z], field[:, cells_z:]], axis=0))
    both = jnp.dot(jnp.concatenate([high, low], axis=1), z_matrix(t, 2 * cells_z), preferred_element_type=F32)
    total = both[:, :cells_z] + both[:, cells_z:]
    return jnp.concatenate([total[:rows], total[rows:]], axis=1)


def in_four(values):
    count = values.shape[0] // 4
    return [values[n * count : (n + 1) * count] for n in range(4)]


def crossed(a, b, c, d):
    s, t, u, v = a + c, a - c, b + d, b - d
    return s + u, s - u, t + v, t - v


def to_modes(field, t):
    folded = crossed(*in_four(field))
    return jnp.concatenate(
        [left_product(quarter_matrix(t["onward"], n), part) for n, part in enumerate(folded)], axis=0
    )


def to_cells(modes, t):
    parts = [left_product(quarter_matrix(t["later"], n), part) for n, part in enumerate(in_four(modes))]
    return jnp.concatenate(crossed(*parts), axis=0)


def backwards(rows):
    return jnp.concatenate([rows[n : n + 1] for n in reversed(range(rows.shape[0]))], axis=0)


def folded_cells(load, cells_x):
    half = len(cells_x) // 2
    quarters = []
    for part in (cells_x[:half], cells_x[half:]):
        layers = [load(x) for x in part]
        middle = layers[0].shape[0] // 2
        quarters += [layer[:middle] for layer in layers]
        quarters += [backwards(layer[middle:]) for layer in layers]
    return jnp.concatenate(quarters, axis=0)


def natural_layer(field, place, layers):
    count = field.shape[0] // layers // 2
    side, within = divmod(place, layers // 2)
    start = side * (field.shape[0] // 2) + within * count
    mirror = start + field.shape[0] // 4
    return jnp.concatenate(
        [field[start : start + count], backwards(field[mirror : mirror + count])], axis=0
    )


def times(real_part, imag_part, field):
    lanes = field.shape[1] // 2
    real, imag = field[:, :lanes], field[:, lanes:]
    return jnp.concatenate(
        [real_part * real - imag_part * imag, real_part * imag + imag_part * real], axis=1
    )


def apply_contrast(field, contrast, t, block=64):
    done = []
    for start in range(0, field.shape[0], block):
        here = slice(start, start + block)
        cells = times(contrast[0, here], contrast[1, here], z_transform(field[here], t))
        done.append(z_transform(cells, t))
    return jnp.concatenate(done, axis=0)


def solve_modes(start, contrast, t):
    term = total = start
    for _ in range(2):
        term = divide(to_modes(apply_contrast(to_cells(term, t), contrast, t), t), t)
        total = total + term
    return total, term


def edges(rows, lanes, layers):
    place = lax.broadcasted_iota(jnp.int32, (rows, lanes), 0)
    count = rows // layers // 2
    outer_y = lax.rem(place, count) == 0
    outer_x = lax.rem(place, rows // 4) < count
    return (outer_x.astype(F32) + outer_y.astype(F32)) * (1.0 / 12.0)


def prepare(dense, slow, layers, place, depth, amplitude, t, modes_ref, contrast_ref):
    rows, cells_z = contrast_ref.shape[1:]
    points = place.shape[1]
    row_ids = lax.broadcasted_iota(jnp.int32, (rows, points), 0)
    lane_ids = lax.broadcasted_iota(jnp.int32, (cells_z, points), 0)
    at_lane = (lane_ids == depth).astype(F32)
    spread = []
    for c in range(2):
        amp = amplitude[c]
        one = amp.astype(BF16).astype(F32)
        two = (amp - one).astype(BF16).astype(F32)
        parts = [at_lane * part for part in (one, two, amp - one - two)]
        spread.append(jnp.concatenate(parts, axis=1).astype(BF16))
    scaled = KAPPA * (slow - 1.0)
    contrast_ref[0] = scaled - edges(rows, cells_z, layers)
    contrast_ref[1] = DAMPING * scaled
    at_row = (row_ids == place).astype(F32).astype(BF16)
    field = lax.dot_general(
        jnp.concatenate([at_row] * 3, axis=1), jnp.concatenate(spread, axis=0),
        (((1,), (1,)), ((), ())), preferred_element_type=F32,
    )
    modes_ref[...] = divide(to_modes(z_transform(field + dense, t), t), t)


def hand_on_kernel(in_ref, out_ref):
    out_ref[...] = in_ref[...]


PREP = ("symbol", "onward")
PREP_OTHER = ("inverse", "onward")
BEAT = ("inverse", "onward", "later")
FINAL = BEAT + ("first",)
LATER = ("later",)
FINISH = ("onward", "later")


def named(names, refs):
    return dict(zip(names, refs))


def prep_kernel(cells_x, right_ref, slow_ref, place_ref, depth_ref, amp_ref, *refs):
    later_refs = refs[len(PREP) : len(PREP) + len(LATER)]
    modes_ref, contrast_ref, inverse_ref, *held_refs, sems = refs[len(PREP) + len(LATER) :]
    copies = [
        pltpu.make_async_copy(later_ref, held_ref, sems.at[n])
        for n, (later_ref, held_ref) in enumerate(zip(later_refs, held_refs))
    ]
    for copy in copies:
        copy.start()
    t = named(PREP, refs)
    symbol = t["symbol"][...]
    damping = KAPPA * DAMPING
    scale = 1.0 / (symbol * symbol + damping * damping)
    inverse_ref[0] = symbol * scale
    inverse_ref[1] = damping * scale
    t["inverse"] = inverse_ref
    dense = [folded_cells(lambda x, c=c: right_ref[c, x], cells_x) for c in range(2)]
    slow = folded_cells(lambda x: slow_ref[x], cells_x)
    prepare(
        jnp.concatenate(dense, axis=1), slow, len(cells_x), place_ref[...], depth_ref[...], amp_ref, t,
        modes_ref, contrast_ref,
    )
    for copy in copies:
        copy.wait()


def prep_other_kernel(cells_x, core_ref, rhs_ref, swap_ref, slow_ref, own_modes_ref, own_contrast_ref, place_ref, depth_ref, amp_ref,
                      *refs):
    modes_ref, contrast_ref = refs[len(PREP_OTHER) :]
    core = core_ref[0]
    other = 1 - core
    modes_ref[core] = own_modes_ref[...]
    contrast_ref[core] = own_contrast_ref[...]
    dense = [folded_cells(lambda x, c=c: swap_ref[c, x], cells_x) for c in range(2)]
    slow = folded_cells(lambda x: slow_ref[x], cells_x)
    prepare(
        jnp.concatenate(dense, axis=1), slow, len(cells_x), place_ref[...], depth_ref[...], amp_ref, named(PREP_OTHER, refs),
        modes_ref.at[other], contrast_ref.at[other],
    )


def beat_kernel(tile, final, active_ref, modes_ref, contrast_ref, trace_x_ref, trace_y_ref, total_ref, term_ref,
                *refs):
    names = FINAL if final else BEAT
    t = named(names, refs)
    new_total_ref, new_term_ref, *out_refs = refs[len(names) :]
    count = trace_x_ref.shape[0]

    @pl.when(active_ref[0] == 1)
    def _():
        trace = jnp.concatenate([trace_x_ref[...], trace_y_ref[...]], axis=0)
        start = modes_ref[tile] + divide(left_product(enter_matrix(t, 3 * trace.shape[0]), trace), t)
        total, term = solve_modes(start, contrast_ref.at[tile], t)
        new_total_ref[...] = total
        new_term_ref[...] = term
        if not (final and tile == 1):
            out = leave_product(t, total)
            for out_ref, part in zip(out_refs[:1] if final else out_refs, (out[:count], out[count:])):
                out_ref[...] = part

    @pl.when(active_ref[0] == 0)
    def _():
        new_total_ref[...] = total_ref[...]
        new_term_ref[...] = term_ref[...]

    if final:
        out = left_product(t["first"][...], new_total_ref[...])
        edge_refs = out_refs[1 - tile :]
        edge_refs[-1][...] = out[count:]
        if tile == 0:
            edge_refs[0][...] = out[:count]


def finish_kernel(cells_x, core_ref, total0_ref, term0_ref, total1_ref, term1_ref, contrast_ref,
                  z_ref, later_ref, keep_ref, give_ref, both_ref):
    _, _, _, size_x, size_y, cells_z = both_ref.shape
    t = named(FINISH, (z_ref, later_ref))
    for tile, (total_ref, term_ref) in enumerate(((total0_ref, term0_ref), (total1_ref, term1_ref))):
        wave, rest = [z_transform(to_cells(ref[...], t), t) for ref in (total_ref, term_ref)]
        rest = times(contrast_ref[tile, 0], contrast_ref[tile, 1], rest)
        for place, x in enumerate(cells_x):
            wave_layer, rest_layer = [natural_layer(field, place, size_x) for field in (wave, rest)]
            for c in range(2):
                there = slice(c * cells_z, (c + 1) * cells_z)
                both_ref[tile, 0, c, x] = wave_layer[:, there]
                both_ref[tile, 1, c, x] = rest_layer[:, there]
                if tile == 1 and x < 2:
                    layer = wave_layer[:, there]
                    if x == 0:
                        both_ref[0, 1, c, size_x - 2] += layer * (-1.0 / 12.0)
                        both_ref[0, 1, c, size_x - 1] += layer * (16.0 / 12.0)
                    else:
                        both_ref[0, 1, c, size_x - 1] += layer * (-1.0 / 12.0)
    keep_ref[...] = both_ref[core_ref[0]]
    give_ref[...] = both_ref[1 - core_ref[0]]


def add_later(rest_ref, edge_x, edge_y, lower):
    _, size_x, size_y, cells_z = rest_ref.shape
    for c in range(2):
        there = slice(c * cells_z, (c + 1) * cells_z)
        near, far = edge_x[:size_y, there] * lower, edge_x[size_y:, there] * lower
        rest_ref[c, size_x - 2] += near * (-1.0 / 12.0)
        rest_ref[c, size_x - 1] += (16.0 * near - far) * (1.0 / 12.0)
        near, far = edge_y[:size_x, there], edge_y[size_x:, there]
        two = jnp.stack([near * (-1.0 / 12.0), (16.0 * near - far) * (1.0 / 12.0)], axis=1)
        rest_ref[c, :, size_y - 2 :] += two


def keep_kernel(core_ref, keep_ref, edge_x_ref, edge_y_ref, z_ref, rest_ref):
    rest_ref[...] = keep_ref[1]
    count = edge_x_ref.shape[0]
    edges = jnp.concatenate([edge_x_ref[...], edge_y_ref[core_ref[0]]], axis=0)
    edges = z_transform(edges, dict(onward=z_ref))
    add_later(rest_ref, edges[:count], edges[count:], (core_ref[0] == 1).astype(F32))


def place_wave_kernel(rhs_ref, keep_ref, got_ref, wave_ref, sems):
    rhs = rhs_ref[0]
    copies = [
        pltpu.make_async_copy(keep_ref.at[0], wave_ref.at[rhs], sems.at[0]),
        pltpu.make_async_copy(got_ref.at[0], wave_ref.at[1 - rhs], sems.at[1]),
    ]
    for copy in copies:
        copy.start()
    for copy in copies:
        copy.wait()


def place_rest_kernel(core_ref, rhs_ref, keep_rest_ref, got_ref, got_edge_ref, z_ref, rest_ref, work_ref, sems):
    rhs = rhs_ref[0]
    count = got_edge_ref.shape[0] // 2
    copies = [pltpu.make_async_copy(keep_rest_ref, rest_ref.at[rhs], sems.at[0])]
    copies[0].start()
    work_ref[...] = got_ref[1]
    edges = z_transform(got_edge_ref[...], dict(onward=z_ref))
    add_later(work_ref, edges[:count], edges[count:], (core_ref[0] == 1).astype(F32))
    copies.append(pltpu.make_async_copy(work_ref, rest_ref.at[1 - rhs], sems.at[1]))
    copies[1].start()
    for copy in copies:
        copy.wait()


def whole():
    return pl.BlockSpec(memory_space=pltpu.VMEM)


def scalars():
    return pl.BlockSpec(memory_space=pltpu.SMEM)


def anywhere():
    return pl.BlockSpec(memory_space=pl.ANY)


SOLVE_COST = pl.CostEstimate(flops=2 * 10**9, bytes_accessed=2 * 10**6, transcendentals=0)
KEEP_COST = pl.CostEstimate(flops=10**10, bytes_accessed=10**6, transcendentals=0)
PARAMS = pltpu.CompilerParams(vmem_limit_bytes=24 * 1024 * 1024)


def shaped(*shape):
    return jax.ShapeDtypeStruct(shape, F32)


def body(right_side, slowness, source_cells, source_amplitudes):
    sources, _, size_x, size_y, cells_z = right_side.shape
    grid_rows, grid_cols = lax.axis_size("gx"), lax.axis_size("gy")
    assert sources == 2 and grid_rows % 2 == 0 and size_x % 2 == 0
    chips = grid_rows // 2
    row, col = lax.axis_index("gx"), lax.axis_index("gy")
    core = row % 2
    rhs = (core + row // 2 + col) % 2
    core_ref, rhs_ref = core[None], rhs[None]
    t, cells_x = tables(size_x, size_y, cells_z)
    t = {name: jnp.asarray(value) for name, value in t.items()}
    rows = size_x * size_y

    def device(chip, core, column):
        return (2 * chip + core) * grid_cols + column

    def between(pairs):
        return [
            (device(a, r, b), device(c, 1 - r, d)) for (a, b), (c, d) in pairs for r in range(2)
        ]

    own = [
        (device(k, r, j), device(k, 1 - r, j))
        for k in range(chips) for j in range(grid_cols) for r in range(2)
    ]
    axes = ("gx", "gy")
    other = lax.dynamic_index_in_dim(right_side, 1 - rhs, 0, keepdims=False)
    swapped = lax.ppermute(other, axes, own)
    swapped_slow = lax.ppermute(slowness, axes, own)
    mine = lax.dynamic_index_in_dim(right_side, rhs, 0, keepdims=False)

    total_y = size_y * grid_cols
    cells = lax.dynamic_index_in_dim(source_cells, rhs, 0, keepdims=True)
    near_y = cells // cells_z % total_y - col * size_y
    places = []
    for tile_row in (row, row + 1 - 2 * core):
        near_x = cells // (total_y * cells_z) - tile_row * size_x
        inside = (near_x >= 0) & (near_x < size_x) & (near_y >= 0) & (near_y < size_y)
        far_x, far_y = near_x >= size_x // 2, near_y >= size_y // 2
        folded_x = jnp.where(far_x, size_x - 1 - near_x, near_x)
        folded_y = jnp.where(far_y, size_y - 1 - near_y, near_y)
        quarter = (2 * far_x + far_y) * (rows // 4)
        places.append(jnp.where(inside, quarter + folded_x * (size_y // 2) + folded_y, -1))
    amplitudes = lax.dynamic_index_in_dim(source_amplitudes, rhs, 0, keepdims=False).T[:, None, :]

    depth = cells % cells_z
    own_modes, own_contrast, t["inverse"], *held = pl.pallas_call(
        functools.partial(prep_kernel, cells_x),
        out_shape=(shaped(rows, 2 * cells_z), shaped(2, rows, cells_z), shaped(2, rows, cells_z))
        + tuple(jax.ShapeDtypeStruct(t[name].shape, BF16) for name in LATER),
        in_specs=[whole()] * (5 + len(PREP)) + [anywhere()] * len(LATER),
        out_specs=(whole(),) * (3 + len(LATER)),
        scratch_shapes=[pltpu.SemaphoreType.DMA((len(LATER),))],
        compiler_params=PARAMS,
        cost_estimate=SOLVE_COST,
        name="prep",
    )(mine, slowness, places[0], depth, amplitudes, *[t[name] for name in PREP + LATER])
    t.update(zip(LATER, held))
    modes, contrast = pl.pallas_call(
        functools.partial(prep_other_kernel, cells_x),
        out_shape=(shaped(2, rows, 2 * cells_z), shaped(2, 2, rows, cells_z)),
        in_specs=[scalars()] * 2 + [whole()] * (7 + len(PREP_OTHER)),
        out_specs=(whole(), whole()),
        compiler_params=PARAMS,
        cost_estimate=SOLVE_COST,
        name="prep_other",
    )(core_ref, rhs_ref, swapped, swapped_slow, own_modes, own_contrast, places[1], depth, amplitudes,
      *[t[name] for name in PREP_OTHER])

    def solve(tile, active, trace_x, trace_y, state, final):
        names = FINAL if final else BEAT
        x, y = shaped(*zero_x.shape), shaped(*zero_y.shape)
        outs = ((x, x, y), (y,))[tile] if final else (x, y)
        total, term, *outs = pl.pallas_call(
            functools.partial(beat_kernel, tile, final),
            out_shape=(shaped(rows, 2 * cells_z),) * 2 + outs,
            in_specs=[scalars()] + [whole()] * (6 + len(names)),
            out_specs=(whole(),) * (2 + len(outs)),
            input_output_aliases={5: 0, 6: 1},
            compiler_params=PARAMS,
            cost_estimate=SOLVE_COST,
            name="upper" if tile == 0 else "lower",
        )(active, modes, contrast, trace_x, trace_y, *state, *[t[name] for name in names])
        return (total, term), outs

    def hand_on(trace, cost=None):
        return pl.pallas_call(
            hand_on_kernel,
            out_shape=shaped(*trace.shape),
            in_specs=[whole()],
            out_specs=whole(),
            compiler_params=PARAMS,
            cost_estimate=cost,
            name="hand_on",
        )(trace)

    zero_x = jnp.zeros((2 * size_y, 2 * cells_z), F32)
    zero_y = jnp.zeros((2 * size_x, 2 * cells_z), F32)
    trace_x, trace_y0, trace_y1 = zero_x, zero_y, zero_y
    states = [[jnp.zeros((rows, 2 * cells_z), F32)] * 2 for _ in range(2)]
    for beat in range(chips + grid_cols - 1):
        active = (row // 2 + col == beat).astype(jnp.int32)[None]
        here = [(k, beat - k) for k in range(chips) if 0 <= beat - k < grid_cols]
        along_x = between([((k, j), (k + 1, j)) for k, j in here if k + 1 < chips])
        along_y = between([((k, j), (k, j + 1)) for k, j in here if j + 1 < grid_cols])
        final = beat == chips + grid_cols - 2
        states[0], (inner_x, *outs0) = solve(0, active, trace_x, trace_y0, states[0], final)
        if along_y:
            trace_y0 = hand_on(lax.ppermute(outs0[0], axes, along_y))
        states[1], outs1 = solve(1, active, inner_x, trace_y1, states[1], final)
        if along_x:
            trace_x = lax.ppermute(outs1[0], axes, along_x)
        if along_y:
            trace_y1 = lax.ppermute(outs1[1], axes, along_y)
    edge_x, edge_y0 = outs0
    edge_y = jnp.stack([edge_y0, outs1[0]])

    every = [(k, j) for k in range(chips) for j in range(grid_cols)]
    after_x = hand_on(
        lax.ppermute(edge_x, axes, between([((k, j), (k - 1, j)) for k, j in every if k])), KEEP_COST
    )
    after_y = lax.ppermute(edge_y, axes, between([((k, j), (k, j - 1)) for k, j in every if j]))

    half = shaped(2, 2, size_x, size_y, cells_z)
    keep, give = pl.pallas_call(
        functools.partial(finish_kernel, cells_x),
        out_shape=(half, half),
        in_specs=[scalars()] + [whole()] * 7,
        out_specs=(whole(), whole()),
        scratch_shapes=[pltpu.VMEM((2, 2, 2, size_x, size_y, cells_z), F32)],
        compiler_params=PARAMS,
        name="finish",
    )(core_ref, *states[0], *states[1], contrast, *[t[name] for name in FINISH])
    got = lax.ppermute(give, axes, own)

    pass_y = lax.dynamic_index_in_dim(after_y, 1 - core, 0, keepdims=False)
    got_edge = lax.ppermute(jnp.concatenate([after_x, pass_y], axis=0), axes, own)
    keep_rest = pl.pallas_call(
        keep_kernel,
        out_shape=shaped(*half.shape[1:]),
        in_specs=[scalars()] + [whole()] * 4,
        out_specs=whole(),
        compiler_params=PARAMS,
        cost_estimate=KEEP_COST,
        name="keep",
    )(core_ref, keep, after_x, after_y, t["onward"])
    wavefield = pl.pallas_call(
        place_wave_kernel,
        out_shape=shaped(*right_side.shape),
        in_specs=[scalars()] + [whole()] * 2,
        out_specs=anywhere(),
        scratch_shapes=[pltpu.SemaphoreType.DMA((2,))],
        compiler_params=PARAMS,
        cost_estimate=KEEP_COST,
        name="place_wave",
    )(rhs_ref, keep, got)
    residual = pl.pallas_call(
        place_rest_kernel,
        out_shape=shaped(*right_side.shape),
        in_specs=[scalars()] * 2 + [whole()] * 4,
        out_specs=anywhere(),
        scratch_shapes=[
            pltpu.VMEM((2, size_x, size_y, cells_z), F32),
            pltpu.SemaphoreType.DMA((2,)),
        ],
        compiler_params=PARAMS,
        name="place_rest",
    )(core_ref, rhs_ref, keep_rest, got, got_edge, t["onward"])
    return wavefield, residual


def solution(mesh):
    return jax.shard_map(
        body,
        mesh=mesh,
        in_specs=(P(None, None, "gx", "gy", None), P("gx", "gy", None), P(), P()),
        out_specs=(P(None, None, "gx", "gy", None), P(None, None, "gx", "gy", None)),
        check_vma=False,
    )
```

```python
import functools
import math

import jax
import jax.numpy as jnp
import ml_dtypes
import numpy as np
from jax import lax
from jax.experimental import pallas as pl
from jax.experimental.pallas import tpu as pltpu
from jax.sharding import PartitionSpec as P

KAPPA = 0.12
DAMPING = 0.3
BF16 = jnp.bfloat16
F32 = jnp.float32


def sine_matrix(length):
    index = np.arange(1, length + 1)
    angles = index * (math.pi / (length + 1))
    return math.sqrt(2.0 / (length + 1)) * np.sin(angles[:, None] * index[None, :]), angles


def halves(matrix):
    high = matrix.astype(np.float32).astype(ml_dtypes.bfloat16)
    low = (matrix - high.astype(np.float64)).astype(np.float32).astype(ml_dtypes.bfloat16)
    return high, low


def left_factor(matrix):
    high, low = halves(matrix)
    return np.concatenate([high, high, low], axis=1)


def slabs(matrices, rows, lanes):
    pieces, free = [], 0
    for matrix in matrices:
        for row in range(0, matrix.shape[0], rows):
            for lane in range(0, matrix.shape[1], lanes):
                piece = matrix[row : row + rows, lane : lane + lanes]
                if free + piece.shape[0] > rows or not pieces:
                    pieces.append(np.zeros((rows, lanes), matrix.dtype))
                    free = 0
                pieces[-1][free : free + piece.shape[0], : piece.shape[1]] = piece
                free += piece.shape[0]
    return np.stack(pieces)


def quarter_matrix(slabs_ref, index):
    count = slabs_ref.shape[1] // 2
    return slabs_ref[index // 2, index % 2 * count : (index % 2 + 1) * count, : 3 * count]


def z_matrix(t, depth):
    rows = t["onward"].shape[1]
    pieces = [t["onward"][2 + n, :, :depth] for n in range(-(-depth // rows))]
    return jnp.concatenate(pieces, axis=0)


def enter_matrix(t, depth):
    return jnp.concatenate([t["later"][2, :, :depth], t["later"][3, :, :depth]], axis=0)


def leave_product(t, values):
    high, low = split(values)
    rest = 2 * values.shape[0] - t["later"].shape[2]
    matrix = t["later"][4]
    if rest > 0:
        matrix = jnp.concatenate([matrix, t["later"][2, :, -rest:]], axis=1)
    both = jnp.dot(matrix, jnp.concatenate([high, low], axis=0), preferred_element_type=F32)
    count = both.shape[0] // 2
    return both[:count] + both[count:]


def stacked_factor(matrix):
    high, low = halves(matrix)
    return np.concatenate([np.concatenate([part, part], axis=1) for part in (high, low)], axis=0)


def tables(size_x, size_y, cells_z):
    sine_x, angle_x = sine_matrix(size_x)
    sine_y, angle_y = sine_matrix(size_y)
    sine_z, angle_z = sine_matrix(cells_z)
    half = size_x // 2
    assert half % 8 == 0 and size_y % 16 == 0
    order_x, order_y = [np.arange(0, n, 2).reshape(1, -1) + [[0], [1]] for n in (size_x, size_y)]
    pairs = [(x, y) for p in range(2) for q in range(2) for x in order_x[p] for y in order_y[q]]
    mode_x, mode_y = np.array(pairs).T
    cells = np.concatenate([np.arange(half), np.arange(size_x - 1, half - 1, -1)])

    def symbol(angle):
        return 2.5 - 8.0 / 3.0 * np.cos(angle) + 1.0 / 6.0 * np.cos(2.0 * angle)

    real_part = (
        symbol(angle_x)[mode_x][:, None]
        + symbol(angle_y)[mode_y][:, None]
        + (2.0 - 2.0 * np.cos(angle_z))[None, :]
        - KAPPA
    )

    slab = half * size_y
    lanes = 3 * slab
    parity = [
        np.kron(sine_x[order_x[p]][:, :half], sine_y[order_y[q]][:, : size_y // 2])
        for p in range(2) for q in range(2)
    ]
    forward = [left_factor(m) for m in parity]
    backward = [left_factor(m.T) for m in parity]
    high_z, low_z = halves(sine_z)
    right_z = np.concatenate([np.concatenate([high_z, low_z], axis=1)] * 2, axis=0)

    by_cell = sine_x[mode_x][:, :, None] * sine_y[mode_y][:, None, :]
    full = by_cell.reshape(len(by_cell), -1)
    enter_x = np.stack([-by_cell[:, 0] / 12.0, (16.0 * by_cell[:, 0] - by_cell[:, 1]) / 12.0], 1)
    enter_y = np.stack(
        [-by_cell[:, :, 0] / 12.0, (16.0 * by_cell[:, :, 0] - by_cell[:, :, 1]) / 12.0], 1
    )
    enter = left_factor(
        np.concatenate([enter_x.reshape(len(full), -1), enter_y.reshape(len(full), -1)], axis=1)
    )
    leave = stacked_factor(
        np.concatenate(
            [
                by_cell[:, size_x - 2 :].reshape(len(full), -1),
                by_cell[:, :, size_y - 2 :].transpose(0, 2, 1).reshape(len(full), -1),
            ],
            axis=1,
        ).T
    )
    first = left_factor(
        np.concatenate(
            [
                by_cell[:, :2].reshape(len(full), -1),
                by_cell[:, :, :2].transpose(0, 2, 1).reshape(len(full), -1),
            ],
            axis=1,
        ).T
    )
    later = slabs(backward + [enter, leave[:, : lanes]], slab, lanes)
    rest = leave[:, lanes :]
    if rest.shape[1]:
        assert enter.shape[1] <= later.shape[2] - rest.shape[1]
        later[2, :, later.shape[2] - rest.shape[1] :] = rest
    assert 2 * cells_z % slab == 0 and 2 * cells_z <= lanes
    assert enter.shape[0] == 2 * slab and enter.shape[1] <= lanes
    assert leave.shape[0] == slab
    return dict(
        symbol=real_part.astype(np.float32), first=first,
        onward=slabs(forward + [right_z], slab, lanes),
        later=later,
    ), tuple(int(x) for x in cells)


def divide(modes, t):
    return times(t["inverse"][0], t["inverse"][1], modes)


def split(values):
    high = values.astype(BF16)
    return high, (values - high.astype(F32)).astype(BF16)


def stacked(values):
    high, low = split(values)
    return jnp.concatenate([high, low, high], axis=0)


def left_product(matrix, values):
    return jnp.dot(matrix, stacked(values), preferred_element_type=F32)


def z_transform(field, t):
    rows = field.shape[0]
    cells_z = field.shape[1] // 2
    high, low = split(jnp.concatenate([field[:, :cells_z], field[:, cells_z:]], axis=0))
    both = jnp.dot(jnp.concatenate([high, low], axis=1), z_matrix(t, 2 * cells_z), preferred_element_type=F32)
    total = both[:, :cells_z] + both[:, cells_z:]
    return jnp.concatenate([total[:rows], total[rows:]], axis=1)


def in_four(values):
    count = values.shape[0] // 4
    return [values[n * count : (n + 1) * count] for n in range(4)]


def crossed(a, b, c, d):
    s, t, u, v = a + c, a - c, b + d, b - d
    return s + u, s - u, t + v, t - v


def to_modes(field, t):
    folded = crossed(*in_four(field))
    return jnp.concatenate(
        [left_product(quarter_matrix(t["onward"], n), part) for n, part in enumerate(folded)], axis=0
    )


def to_cells(modes, t):
    parts = [left_product(quarter_matrix(t["later"], n), part) for n, part in enumerate(in_four(modes))]
    return jnp.concatenate(crossed(*parts), axis=0)


def backwards(rows):
    return jnp.concatenate([rows[n : n + 1] for n in reversed(range(rows.shape[0]))], axis=0)


def folded_cells(load, cells_x):
    half = len(cells_x) // 2
    quarters = []
    for part in (cells_x[:half], cells_x[half:]):
        layers = [load(x) for x in part]
        middle = layers[0].shape[0] // 2
        quarters += [layer[:middle] for layer in layers]
        quarters += [backwards(layer[middle:]) for layer in layers]
    return jnp.concatenate(quarters, axis=0)


def natural_layer(field, place, layers):
    count = field.shape[0] // layers // 2
    side, within = divmod(place, layers // 2)
    start = side * (field.shape[0] // 2) + within * count
    mirror = start + field.shape[0] // 4
    return jnp.concatenate(
        [field[start : start + count], backwards(field[mirror : mirror + count])], axis=0
    )


def times(real_part, imag_part, field):
    lanes = field.shape[1] // 2
    real, imag = field[:, :lanes], field[:, lanes:]
    return jnp.concatenate(
        [real_part * real - imag_part * imag, real_part * imag + imag_part * real], axis=1
    )


def apply_contrast(field, contrast, t, block=64):
    done = []
    for start in range(0, field.shape[0], block):
        here = slice(start, start + block)
        cells = times(contrast[0, here], contrast[1, here], z_transform(field[here], t))
        done.append(z_transform(cells, t))
    return jnp.concatenate(done, axis=0)


def solve_modes(start, contrast, t):
    term = total = start
    for _ in range(2):
        term = divide(to_modes(apply_contrast(to_cells(term, t), contrast, t), t), t)
        total = total + term
    return total, term


def edges(rows, lanes, layers):
    place = lax.broadcasted_iota(jnp.int32, (rows, lanes), 0)
    count = rows // layers // 2
    outer_y = lax.rem(place, count) == 0
    outer_x = lax.rem(place, rows // 4) < count
    return (outer_x.astype(F32) + outer_y.astype(F32)) * (1.0 / 12.0)


def prepare(dense, slow, layers, place, depth, amplitude, t, modes_ref, contrast_ref):
    rows, cells_z = contrast_ref.shape[1:]
    points = place.shape[1]
    row_ids = lax.broadcasted_iota(jnp.int32, (rows, points), 0)
    lane_ids = lax.broadcasted_iota(jnp.int32, (cells_z, points), 0)
    at_lane = (lane_ids == depth).astype(F32)
    spread = []
    for c in range(2):
        amp = amplitude[c]
        one = amp.astype(BF16).astype(F32)
        two = (amp - one).astype(BF16).astype(F32)
        parts = [at_lane * part for part in (one, two, amp - one - two)]
        spread.append(jnp.concatenate(parts, axis=1).astype(BF16))
    scaled = KAPPA * (slow - 1.0)
    contrast_ref[0] = scaled - edges(rows, cells_z, layers)
    contrast_ref[1] = DAMPING * scaled
    at_row = (row_ids == place).astype(F32).astype(BF16)
    field = lax.dot_general(
        jnp.concatenate([at_row] * 3, axis=1), jnp.concatenate(spread, axis=0),
        (((1,), (1,)), ((), ())), preferred_element_type=F32,
    )
    modes_ref[...] = divide(to_modes(z_transform(field + dense, t), t), t)


def hand_on_kernel(in_ref, out_ref):
    out_ref[...] = in_ref[...]


PREP = ("symbol", "onward")
PREP_OTHER = ("inverse", "onward")
BEAT = ("inverse", "onward", "later")
FINAL = BEAT + ("first",)
LATER = ("later",)
FINISH = ("onward", "later")


def named(names, refs):
    return dict(zip(names, refs))


def prep_kernel(cells_x, right_ref, slow_ref, place_ref, depth_ref, amp_ref, *refs):
    later_refs = refs[len(PREP) : len(PREP) + len(LATER)]
    modes_ref, contrast_ref, inverse_ref, *held_refs, sems = refs[len(PREP) + len(LATER) :]
    copies = [
        pltpu.make_async_copy(later_ref.at[n], held_ref.at[n], sems.at[m, n])
        for m, (later_ref, held_ref) in enumerate(zip(later_refs, held_refs))
        for n in range(later_ref.shape[0])
    ]
    for copy in copies:
        copy.start()
    t = named(PREP, refs)
    symbol = t["symbol"][...]
    damping = KAPPA * DAMPING
    scale = 1.0 / (symbol * symbol + damping * damping)
    inverse_ref[0] = symbol * scale
    inverse_ref[1] = damping * scale
    t["inverse"] = inverse_ref
    dense = [folded_cells(lambda x, c=c: right_ref[c, x], cells_x) for c in range(2)]
    slow = folded_cells(lambda x: slow_ref[x], cells_x)
    prepare(
        jnp.concatenate(dense, axis=1), slow, len(cells_x), place_ref[...], depth_ref[...], amp_ref, t,
        modes_ref, contrast_ref,
    )
    for copy in copies:
        copy.wait()


def prep_other_kernel(cells_x, core_ref, rhs_ref, swap_ref, slow_ref, own_modes_ref, own_contrast_ref, place_ref, depth_ref, amp_ref,
                      *refs):
    modes_ref, contrast_ref = refs[len(PREP_OTHER) :]
    core = core_ref[0]
    other = 1 - core
    modes_ref[core] = own_modes_ref[...]
    contrast_ref[core] = own_contrast_ref[...]
    dense = [folded_cells(lambda x, c=c: swap_ref[c, x], cells_x) for c in range(2)]
    slow = folded_cells(lambda x: slow_ref[x], cells_x)
    prepare(
        jnp.concatenate(dense, axis=1), slow, len(cells_x), place_ref[...], depth_ref[...], amp_ref, named(PREP_OTHER, refs),
        modes_ref.at[other], contrast_ref.at[other],
    )


def beat_kernel(tile, final, active_ref, modes_ref, contrast_ref, trace_x_ref, trace_y_ref, total_ref, term_ref,
                *refs):
    names = FINAL if final else BEAT
    t = named(names, refs)
    new_total_ref, new_term_ref, *out_refs = refs[len(names) :]
    count = trace_x_ref.shape[0]

    @pl.when(active_ref[0] == 1)
    def _():
        trace = jnp.concatenate([trace_x_ref[...], trace_y_ref[...]], axis=0)
        start = modes_ref[tile] + divide(left_product(enter_matrix(t, 3 * trace.shape[0]), trace), t)
        total, term = solve_modes(start, contrast_ref.at[tile], t)
        new_total_ref[...] = total
        new_term_ref[...] = term
        if not (final and tile == 1):
            out = leave_product(t, total)
            for out_ref, part in zip(out_refs[:1] if final else out_refs, (out[:count], out[count:])):
                out_ref[...] = part

    @pl.when(active_ref[0] == 0)
    def _():
        new_total_ref[...] = total_ref[...]
        new_term_ref[...] = term_ref[...]

    if final:
        out = left_product(t["first"][...], new_total_ref[...])
        edge_refs = out_refs[1 - tile :]
        edge_refs[-1][...] = out[count:]
        if tile == 0:
            edge_refs[0][...] = out[:count]


def finish_kernel(cells_x, core_ref, total0_ref, term0_ref, total1_ref, term1_ref, contrast_ref,
                  z_ref, later_ref, keep_ref, give_ref, both_ref):
    _, _, _, size_x, size_y, cells_z = both_ref.shape
    t = named(FINISH, (z_ref, later_ref))
    for tile, (total_ref, term_ref) in enumerate(((total0_ref, term0_ref), (total1_ref, term1_ref))):
        wave, rest = [z_transform(to_cells(ref[...], t), t) for ref in (total_ref, term_ref)]
        rest = times(contrast_ref[tile, 0], contrast_ref[tile, 1], rest)
        for place, x in enumerate(cells_x):
            wave_layer, rest_layer = [natural_layer(field, place, size_x) for field in (wave, rest)]
            for c in range(2):
                there = slice(c * cells_z, (c + 1) * cells_z)
                both_ref[tile, 0, c, x] = wave_layer[:, there]
                both_ref[tile, 1, c, x] = rest_layer[:, there]
                if tile == 1 and x < 2:
                    layer = wave_layer[:, there]
                    if x == 0:
                        both_ref[0, 1, c, size_x - 2] += layer * (-1.0 / 12.0)
                        both_ref[0, 1, c, size_x - 1] += layer * (16.0 / 12.0)
                    else:
                        both_ref[0, 1, c, size_x - 1] += layer * (-1.0 / 12.0)
    keep_ref[...] = both_ref[core_ref[0]]
    give_ref[...] = both_ref[1 - core_ref[0]]


def add_later(rest_ref, edge_x, edge_y, lower):
    _, size_x, size_y, cells_z = rest_ref.shape
    for c in range(2):
        there = slice(c * cells_z, (c + 1) * cells_z)
        near, far = edge_x[:size_y, there] * lower, edge_x[size_y:, there] * lower
        rest_ref[c, size_x - 2] += near * (-1.0 / 12.0)
        rest_ref[c, size_x - 1] += (16.0 * near - far) * (1.0 / 12.0)
        near, far = edge_y[:size_x, there], edge_y[size_x:, there]
        two = jnp.stack([near * (-1.0 / 12.0), (16.0 * near - far) * (1.0 / 12.0)], axis=1)
        rest_ref[c, :, size_y - 2 :] += two


def keep_kernel(core_ref, keep_ref, edge_x_ref, edge_y_ref, z_ref, rest_ref):
    rest_ref[...] = keep_ref[1]
    count = edge_x_ref.shape[0]
    edges = jnp.concatenate([edge_x_ref[...], edge_y_ref[core_ref[0]]], axis=0)
    edges = z_transform(edges, dict(onward=z_ref))
    add_later(rest_ref, edges[:count], edges[count:], (core_ref[0] == 1).astype(F32))


def copies_in_parts(source, target, sems):
    half = source.shape[1] // 2
    return [
        pltpu.make_async_copy(
            source.at[c, pl.ds(h * half, half)], target.at[c, pl.ds(h * half, half)], sems.at[2 * c + h]
        )
        for c in range(2) for h in range(2)
    ]


def place_wave_kernel(rhs_ref, keep_ref, got_ref, wave_ref, sems):
    rhs = rhs_ref[0]
    copies = copies_in_parts(keep_ref.at[0], wave_ref.at[rhs], sems.at[0])
    copies += copies_in_parts(got_ref.at[0], wave_ref.at[1 - rhs], sems.at[1])
    for copy in copies:
        copy.start()
    for copy in copies:
        copy.wait()


def place_rest_kernel(core_ref, rhs_ref, keep_rest_ref, got_ref, got_edge_ref, z_ref, rest_ref, work_ref, sems):
    rhs = rhs_ref[0]
    count = got_edge_ref.shape[0] // 2
    copies = copies_in_parts(keep_rest_ref, rest_ref.at[rhs], sems.at[0])
    for copy in copies:
        copy.start()
    work_ref[...] = got_ref[1]
    edges = z_transform(got_edge_ref[...], dict(onward=z_ref))
    add_later(work_ref, edges[:count], edges[count:], (core_ref[0] == 1).astype(F32))
    more = copies_in_parts(work_ref, rest_ref.at[1 - rhs], sems.at[1])
    for copy in more:
        copy.start()
    for copy in copies + more:
        copy.wait()


def whole():
    return pl.BlockSpec(memory_space=pltpu.VMEM)


def scalars():
    return pl.BlockSpec(memory_space=pltpu.SMEM)


def anywhere():
    return pl.BlockSpec(memory_space=pl.ANY)


SOLVE_COST = pl.CostEstimate(flops=2 * 10**9, bytes_accessed=2 * 10**6, transcendentals=0)
KEEP_COST = pl.CostEstimate(flops=10**10, bytes_accessed=10**6, transcendentals=0)
PARAMS = pltpu.CompilerParams(vmem_limit_bytes=24 * 1024 * 1024)


def shaped(*shape):
    return jax.ShapeDtypeStruct(shape, F32)


def body(right_side, slowness, source_cells, source_amplitudes):
    sources, _, size_x, size_y, cells_z = right_side.shape
    grid_rows, grid_cols = lax.axis_size("gx"), lax.axis_size("gy")
    assert sources == 2 and grid_rows % 2 == 0 and size_x % 2 == 0
    chips = grid_rows // 2
    row, col = lax.axis_index("gx"), lax.axis_index("gy")
    core = row % 2
    rhs = (core + row // 2 + col) % 2
    core_ref, rhs_ref = core[None], rhs[None]
    t, cells_x = tables(size_x, size_y, cells_z)
    t = {name: jnp.asarray(value) for name, value in t.items()}
    rows = size_x * size_y

    def device(chip, core, column):
        return (2 * chip + core) * grid_cols + column

    def between(pairs):
        return [
            (device(a, r, b), device(c, 1 - r, d)) for (a, b), (c, d) in pairs for r in range(2)
        ]

    own = [
        (device(k, r, j), device(k, 1 - r, j))
        for k in range(chips) for j in range(grid_cols) for r in range(2)
    ]
    axes = ("gx", "gy")
    other = lax.dynamic_index_in_dim(right_side, 1 - rhs, 0, keepdims=False)
    swapped = lax.ppermute(other, axes, own)
    swapped_slow = lax.ppermute(slowness, axes, own)
    mine = lax.dynamic_index_in_dim(right_side, rhs, 0, keepdims=False)

    total_y = size_y * grid_cols
    cells = lax.dynamic_index_in_dim(source_cells, rhs, 0, keepdims=True)
    near_y = cells // cells_z % total_y - col * size_y
    places = []
    for tile_row in (row, row + 1 - 2 * core):
        near_x = cells // (total_y * cells_z) - tile_row * size_x
        inside = (near_x >= 0) & (near_x < size_x) & (near_y >= 0) & (near_y < size_y)
        far_x, far_y = near_x >= size_x // 2, near_y >= size_y // 2
        folded_x = jnp.where(far_x, size_x - 1 - near_x, near_x)
        folded_y = jnp.where(far_y, size_y - 1 - near_y, near_y)
        quarter = (2 * far_x + far_y) * (rows // 4)
        places.append(jnp.where(inside, quarter + folded_x * (size_y // 2) + folded_y, -1))
    amplitudes = lax.dynamic_index_in_dim(source_amplitudes, rhs, 0, keepdims=False).T[:, None, :]

    depth = cells % cells_z
    own_modes, own_contrast, t["inverse"], *held = pl.pallas_call(
        functools.partial(prep_kernel, cells_x),
        out_shape=(shaped(rows, 2 * cells_z), shaped(2, rows, cells_z), shaped(2, rows, cells_z))
        + tuple(jax.ShapeDtypeStruct(t[name].shape, BF16) for name in LATER),
        in_specs=[whole()] * (5 + len(PREP)) + [anywhere()] * len(LATER),
        out_specs=(whole(),) * (3 + len(LATER)),
        scratch_shapes=[pltpu.SemaphoreType.DMA((len(LATER), max(t[name].shape[0] for name in LATER)))],
        compiler_params=PARAMS,
        cost_estimate=SOLVE_COST,
        name="prep",
    )(mine, slowness, places[0], depth, amplitudes, *[t[name] for name in PREP + LATER])
    t.update(zip(LATER, held))
    modes, contrast = pl.pallas_call(
        functools.partial(prep_other_kernel, cells_x),
        out_shape=(shaped(2, rows, 2 * cells_z), shaped(2, 2, rows, cells_z)),
        in_specs=[scalars()] * 2 + [whole()] * (7 + len(PREP_OTHER)),
        out_specs=(whole(), whole()),
        compiler_params=PARAMS,
        cost_estimate=SOLVE_COST,
        name="prep_other",
    )(core_ref, rhs_ref, swapped, swapped_slow, own_modes, own_contrast, places[1], depth, amplitudes,
      *[t[name] for name in PREP_OTHER])

    def solve(tile, active, trace_x, trace_y, state, final):
        names = FINAL if final else BEAT
        x, y = shaped(*zero_x.shape), shaped(*zero_y.shape)
        outs = ((x, x, y), (y,))[tile] if final else (x, y)
        total, term, *outs = pl.pallas_call(
            functools.partial(beat_kernel, tile, final),
            out_shape=(shaped(rows, 2 * cells_z),) * 2 + outs,
            in_specs=[scalars()] + [whole()] * (6 + len(names)),
            out_specs=(whole(),) * (2 + len(outs)),
            input_output_aliases={5: 0, 6: 1},
            compiler_params=PARAMS,
            cost_estimate=SOLVE_COST,
            name="upper" if tile == 0 else "lower",
        )(active, modes, contrast, trace_x, trace_y, *state, *[t[name] for name in names])
        return (total, term), outs

    def hand_on(trace, cost=None):
        return pl.pallas_call(
            hand_on_kernel,
            out_shape=shaped(*trace.shape),
            in_specs=[whole()],
            out_specs=whole(),
            compiler_params=PARAMS,
            cost_estimate=cost,
            name="hand_on",
        )(trace)

    zero_x = jnp.zeros((2 * size_y, 2 * cells_z), F32)
    zero_y = jnp.zeros((2 * size_x, 2 * cells_z), F32)
    trace_x, trace_y0, trace_y1 = zero_x, zero_y, zero_y
    states = [[jnp.zeros((rows, 2 * cells_z), F32)] * 2 for _ in range(2)]
    for beat in range(chips + grid_cols - 1):
        active = (row // 2 + col == beat).astype(jnp.int32)[None]
        here = [(k, beat - k) for k in range(chips) if 0 <= beat - k < grid_cols]
        along_x = between([((k, j), (k + 1, j)) for k, j in here if k + 1 < chips])
        along_y = between([((k, j), (k, j + 1)) for k, j in here if j + 1 < grid_cols])
        final = beat == chips + grid_cols - 2
        states[0], (inner_x, *outs0) = solve(0, active, trace_x, trace_y0, states[0], final)
        if along_y:
            trace_y0 = hand_on(lax.ppermute(outs0[0], axes, along_y))
        states[1], outs1 = solve(1, active, inner_x, trace_y1, states[1], final)
        if along_x:
            trace_x = lax.ppermute(outs1[0], axes, along_x)
        if along_y:
            trace_y1 = lax.ppermute(outs1[1], axes, along_y)
    edge_x, edge_y0 = outs0
    edge_y = jnp.stack([edge_y0, outs1[0]])

    every = [(k, j) for k in range(chips) for j in range(grid_cols)]
    after_x = hand_on(
        lax.ppermute(edge_x, axes, between([((k, j), (k - 1, j)) for k, j in every if k])), KEEP_COST
    )
    after_y = lax.ppermute(edge_y, axes, between([((k, j), (k, j - 1)) for k, j in every if j]))

    half = shaped(2, 2, size_x, size_y, cells_z)
    keep, give = pl.pallas_call(
        functools.partial(finish_kernel, cells_x),
        out_shape=(half, half),
        in_specs=[scalars()] + [whole()] * 7,
        out_specs=(whole(), whole()),
        scratch_shapes=[pltpu.VMEM((2, 2, 2, size_x, size_y, cells_z), F32)],
        compiler_params=PARAMS,
        name="finish",
    )(core_ref, *states[0], *states[1], contrast, *[t[name] for name in FINISH])
    got = lax.ppermute(give, axes, own)

    pass_y = lax.dynamic_index_in_dim(after_y, 1 - core, 0, keepdims=False)
    got_edge = lax.ppermute(jnp.concatenate([after_x, pass_y], axis=0), axes, own)
    keep_rest = pl.pallas_call(
        keep_kernel,
        out_shape=shaped(*half.shape[1:]),
        in_specs=[scalars()] + [whole()] * 4,
        out_specs=whole(),
        compiler_params=PARAMS,
        cost_estimate=KEEP_COST,
        name="keep",
    )(core_ref, keep, after_x, after_y, t["onward"])
    wavefield = pl.pallas_call(
        place_wave_kernel,
        out_shape=shaped(*right_side.shape),
        in_specs=[scalars()] + [whole()] * 2,
        out_specs=anywhere(),
        scratch_shapes=[pltpu.SemaphoreType.DMA((2, 4))],
        compiler_params=PARAMS,
        cost_estimate=KEEP_COST,
        name="place_wave",
    )(rhs_ref, keep, got)
    residual = pl.pallas_call(
        place_rest_kernel,
        out_shape=shaped(*right_side.shape),
        in_specs=[scalars()] * 2 + [whole()] * 4,
        out_specs=anywhere(),
        scratch_shapes=[
            pltpu.VMEM((2, size_x, size_y, cells_z), F32),
            pltpu.SemaphoreType.DMA((2, 4)),
        ],
        compiler_params=PARAMS,
        name="place_rest",
    )(core_ref, rhs_ref, keep_rest, got, got_edge, t["onward"])
    return wavefield, residual


def solution(mesh):
    return jax.shard_map(
        body,
        mesh=mesh,
        in_specs=(P(None, None, "gx", "gy", None), P("gx", "gy", None), P(), P()),
        out_specs=(P(None, None, "gx", "gy", None), P(None, None, "gx", "gy", None)),
        check_vma=False,
    )
```

```python
import functools
import math

import jax
import jax.numpy as jnp
import ml_dtypes
import numpy as np
from jax import lax
from jax.experimental import pallas as pl
from jax.experimental.pallas import tpu as pltpu
from jax.sharding import PartitionSpec as P

KAPPA = 0.12
DAMPING = 0.3
BF16 = jnp.bfloat16
F32 = jnp.float32


def sine_matrix(length):
    index = np.arange(1, length + 1)
    angles = index * (math.pi / (length + 1))
    return math.sqrt(2.0 / (length + 1)) * np.sin(angles[:, None] * index[None, :]), angles


def halves(matrix):
    high = matrix.astype(np.float32).astype(ml_dtypes.bfloat16)
    low = (matrix - high.astype(np.float64)).astype(np.float32).astype(ml_dtypes.bfloat16)
    return high, low


def left_factor(matrix):
    high, low = halves(matrix)
    return np.concatenate([high, high, low], axis=1)


def slabs(matrices, rows, lanes):
    pieces, free = [], 0
    for matrix in matrices:
        for row in range(0, matrix.shape[0], rows):
            for lane in range(0, matrix.shape[1], lanes):
                piece = matrix[row : row + rows, lane : lane + lanes]
                if free + piece.shape[0] > rows or not pieces:
                    pieces.append(np.zeros((rows, lanes), matrix.dtype))
                    free = 0
                pieces[-1][free : free + piece.shape[0], : piece.shape[1]] = piece
                free += piece.shape[0]
    return np.stack(pieces)


def quarter_matrix(slabs_ref, index):
    count = slabs_ref.shape[1] // 2
    return slabs_ref[index // 2, index % 2 * count : (index % 2 + 1) * count, : 3 * count]


def z_matrix(t, depth):
    rows = t["onward"].shape[1]
    pieces = [t["onward"][2 + n, :, :depth] for n in range(-(-depth // rows))]
    return jnp.concatenate(pieces, axis=0)


def enter_matrix(t, depth):
    return jnp.concatenate([t["later"][2, :, :depth], t["later"][3, :, :depth]], axis=0)


def leave_product(t, values):
    high, low = split(values)
    rest = 2 * values.shape[0] - t["later"].shape[2]
    matrix = t["later"][4]
    if rest > 0:
        matrix = jnp.concatenate([matrix, t["later"][2, :, -rest:]], axis=1)
    both = jnp.dot(matrix, jnp.concatenate([high, low], axis=0), preferred_element_type=F32)
    count = both.shape[0] // 2
    return both[:count] + both[count:]


def stacked_factor(matrix):
    high, low = halves(matrix)
    return np.concatenate([np.concatenate([part, part], axis=1) for part in (high, low)], axis=0)


def tables(size_x, size_y, cells_z):
    sine_x, angle_x = sine_matrix(size_x)
    sine_y, angle_y = sine_matrix(size_y)
    sine_z, angle_z = sine_matrix(cells_z)
    half = size_x // 2
    assert half % 8 == 0 and size_y % 16 == 0
    order_x, order_y = [np.arange(0, n, 2).reshape(1, -1) + [[0], [1]] for n in (size_x, size_y)]
    pairs = [(x, y) for p in range(2) for q in range(2) for x in order_x[p] for y in order_y[q]]
    mode_x, mode_y = np.array(pairs).T
    cells = np.concatenate([np.arange(half), np.arange(size_x - 1, half - 1, -1)])

    def symbol(angle):
        return 2.5 - 8.0 / 3.0 * np.cos(angle) + 1.0 / 6.0 * np.cos(2.0 * angle)

    real_part = (
        symbol(angle_x)[mode_x][:, None]
        + symbol(angle_y)[mode_y][:, None]
        + (2.0 - 2.0 * np.cos(angle_z))[None, :]
        - KAPPA
    )

    slab = half * size_y
    lanes = 3 * slab
    parity = [
        np.kron(sine_x[order_x[p]][:, :half], sine_y[order_y[q]][:, : size_y // 2])
        for p in range(2) for q in range(2)
    ]
    forward = [left_factor(m) for m in parity]
    backward = [left_factor(m.T) for m in parity]
    high_z, low_z = halves(sine_z)
    right_z = np.concatenate([np.concatenate([high_z, low_z], axis=1)] * 2, axis=0)

    by_cell = sine_x[mode_x][:, :, None] * sine_y[mode_y][:, None, :]
    full = by_cell.reshape(len(by_cell), -1)
    enter_x = np.stack([-by_cell[:, 0] / 12.0, (16.0 * by_cell[:, 0] - by_cell[:, 1]) / 12.0], 1)
    enter_y = np.stack(
        [-by_cell[:, :, 0] / 12.0, (16.0 * by_cell[:, :, 0] - by_cell[:, :, 1]) / 12.0], 1
    )
    enter = left_factor(
        np.concatenate([enter_x.reshape(len(full), -1), enter_y.reshape(len(full), -1)], axis=1)
    )
    leave = stacked_factor(
        np.concatenate(
            [
                by_cell[:, size_x - 2 :].reshape(len(full), -1),
                by_cell[:, :, size_y - 2 :].transpose(0, 2, 1).reshape(len(full), -1),
            ],
            axis=1,
        ).T
    )
    first = left_factor(
        np.concatenate(
            [
                by_cell[:, :2].reshape(len(full), -1),
                by_cell[:, :, :2].transpose(0, 2, 1).reshape(len(full), -1),
            ],
            axis=1,
        ).T
    )
    later = slabs(backward + [enter, leave[:, : lanes]], slab, lanes)
    rest = leave[:, lanes :]
    if rest.shape[1]:
        assert enter.shape[1] <= later.shape[2] - rest.shape[1]
        later[2, :, later.shape[2] - rest.shape[1] :] = rest
    assert 2 * cells_z % slab == 0 and 2 * cells_z <= lanes
    assert enter.shape[0] == 2 * slab and enter.shape[1] <= lanes
    assert leave.shape[0] == slab
    return dict(
        symbol=real_part.astype(np.float32), first=first,
        onward=slabs(forward + [right_z], slab, lanes),
        later=later,
    ), tuple(int(x) for x in cells)


def divide(modes, t):
    return times(t["inverse"][0], t["inverse"][1], modes)


def split(values):
    high = values.astype(BF16)
    return high, (values - high.astype(F32)).astype(BF16)


def stacked(values):
    high, low = split(values)
    return jnp.concatenate([high, low, high], axis=0)


def left_product(matrix, values):
    return jnp.dot(matrix, stacked(values), preferred_element_type=F32)


def z_transform(field, t):
    rows = field.shape[0]
    cells_z = field.shape[1] // 2
    high, low = split(jnp.concatenate([field[:, :cells_z], field[:, cells_z:]], axis=0))
    both = jnp.dot(jnp.concatenate([high, low], axis=1), z_matrix(t, 2 * cells_z), preferred_element_type=F32)
    total = both[:, :cells_z] + both[:, cells_z:]
    return jnp.concatenate([total[:rows], total[rows:]], axis=1)


def in_four(values):
    count = values.shape[0] // 4
    return [values[n * count : (n + 1) * count] for n in range(4)]


def crossed(a, b, c, d):
    s, t, u, v = a + c, a - c, b + d, b - d
    return s + u, s - u, t + v, t - v


def to_modes(field, t):
    folded = crossed(*in_four(field))
    return jnp.concatenate(
        [left_product(quarter_matrix(t["onward"], n), part) for n, part in enumerate(folded)], axis=0
    )


def to_cells(modes, t):
    parts = [left_product(quarter_matrix(t["later"], n), part) for n, part in enumerate(in_four(modes))]
    return jnp.concatenate(crossed(*parts), axis=0)


def backwards(rows):
    return jnp.concatenate([rows[n : n + 1] for n in reversed(range(rows.shape[0]))], axis=0)


def folded_cells(load, cells_x):
    half = len(cells_x) // 2
    quarters = []
    for part in (cells_x[:half], cells_x[half:]):
        layers = [load(x) for x in part]
        middle = layers[0].shape[0] // 2
        quarters += [layer[:middle] for layer in layers]
        quarters += [backwards(layer[middle:]) for layer in layers]
    return jnp.concatenate(quarters, axis=0)


def natural_layer(field, place, layers):
    count = field.shape[0] // layers // 2
    side, within = divmod(place, layers // 2)
    start = side * (field.shape[0] // 2) + within * count
    mirror = start + field.shape[0] // 4
    return jnp.concatenate(
        [field[start : start + count], backwards(field[mirror : mirror + count])], axis=0
    )


def times(real_part, imag_part, field):
    lanes = field.shape[1] // 2
    real, imag = field[:, :lanes], field[:, lanes:]
    return jnp.concatenate(
        [real_part * real - imag_part * imag, real_part * imag + imag_part * real], axis=1
    )


def apply_contrast(field, contrast, t, block=64):
    done = []
    for start in range(0, field.shape[0], block):
        here = slice(start, start + block)
        cells = times(contrast[0, here], contrast[1, here], z_transform(field[here], t))
        done.append(z_transform(cells, t))
    return jnp.concatenate(done, axis=0)


def solve_modes(start, contrast, t):
    term = total = start
    for _ in range(2):
        term = divide(to_modes(apply_contrast(to_cells(term, t), contrast, t), t), t)
        total = total + term
    return total, term


def edges(rows, lanes, layers):
    place = lax.broadcasted_iota(jnp.int32, (rows, lanes), 0)
    count = rows // layers // 2
    outer_y = lax.rem(place, count) == 0
    outer_x = lax.rem(place, rows // 4) < count
    return (outer_x.astype(F32) + outer_y.astype(F32)) * (1.0 / 12.0)


def prepare(dense, slow, layers, place, depth, amplitude, t, modes_ref, contrast_ref):
    rows, cells_z = contrast_ref.shape[1:]
    points = place.shape[1]
    row_ids = lax.broadcasted_iota(jnp.int32, (rows, points), 0)
    lane_ids = lax.broadcasted_iota(jnp.int32, (cells_z, points), 0)
    at_lane = (lane_ids == depth).astype(F32)
    spread = []
    for c in range(2):
        amp = amplitude[c]
        one = amp.astype(BF16).astype(F32)
        two = (amp - one).astype(BF16).astype(F32)
        parts = [at_lane * part for part in (one, two, amp - one - two)]
        spread.append(jnp.concatenate(parts, axis=1).astype(BF16))
    scaled = KAPPA * (slow - 1.0)
    contrast_ref[0] = scaled - edges(rows, cells_z, layers)
    contrast_ref[1] = DAMPING * scaled
    at_row = (row_ids == place).astype(F32).astype(BF16)
    field = lax.dot_general(
        jnp.concatenate([at_row] * 3, axis=1), jnp.concatenate(spread, axis=0),
        (((1,), (1,)), ((), ())), preferred_element_type=F32,
    )
    modes_ref[...] = divide(to_modes(z_transform(field + dense, t), t), t)


def hand_on_kernel(in_ref, out_ref):
    out_ref[...] = in_ref[...]


PREP = ("symbol", "onward")
PREP_OTHER = ("inverse", "onward")
BEAT = ("inverse", "onward", "later")
FINAL = BEAT + ("first",)
LATER = ("later",)
FINISH = ("onward", "later")


def named(names, refs):
    return dict(zip(names, refs))


def prep_kernel(cells_x, right_ref, slow_ref, place_ref, depth_ref, amp_ref, *refs):
    later_refs = refs[len(PREP) : len(PREP) + len(LATER)]
    modes_ref, contrast_ref, inverse_ref, *held_refs = refs[len(PREP) + len(LATER) :]
    for later_ref, held_ref in zip(later_refs, held_refs):
        held_ref[...] = later_ref[...]
    t = named(PREP, refs)
    symbol = t["symbol"][...]
    damping = KAPPA * DAMPING
    scale = 1.0 / (symbol * symbol + damping * damping)
    inverse_ref[0] = symbol * scale
    inverse_ref[1] = damping * scale
    t["inverse"] = inverse_ref
    dense = [folded_cells(lambda x, c=c: right_ref[c, x], cells_x) for c in range(2)]
    slow = folded_cells(lambda x: slow_ref[x], cells_x)
    prepare(
        jnp.concatenate(dense, axis=1), slow, len(cells_x), place_ref[...], depth_ref[...], amp_ref, t,
        modes_ref, contrast_ref,
    )


def prep_other_kernel(cells_x, core_ref, rhs_ref, swap_ref, slow_ref, own_modes_ref, own_contrast_ref, place_ref, depth_ref, amp_ref,
                      *refs):
    modes_ref, contrast_ref = refs[len(PREP_OTHER) :]
    core = core_ref[0]
    other = 1 - core
    modes_ref[core] = own_modes_ref[...]
    contrast_ref[core] = own_contrast_ref[...]
    dense = [folded_cells(lambda x, c=c: swap_ref[c, x], cells_x) for c in range(2)]
    slow = folded_cells(lambda x: slow_ref[x], cells_x)
    prepare(
        jnp.concatenate(dense, axis=1), slow, len(cells_x), place_ref[...], depth_ref[...], amp_ref, named(PREP_OTHER, refs),
        modes_ref.at[other], contrast_ref.at[other],
    )


def beat_kernel(tile, final, active_ref, modes_ref, contrast_ref, trace_x_ref, trace_y_ref, total_ref, term_ref,
                *refs):
    names = FINAL if final else BEAT
    t = named(names, refs)
    new_total_ref, new_term_ref, *out_refs = refs[len(names) :]
    count = trace_x_ref.shape[0]

    @pl.when(active_ref[0] == 1)
    def _():
        trace = jnp.concatenate([trace_x_ref[...], trace_y_ref[...]], axis=0)
        start = modes_ref[tile] + divide(left_product(enter_matrix(t, 3 * trace.shape[0]), trace), t)
        total, term = solve_modes(start, contrast_ref.at[tile], t)
        new_total_ref[...] = total
        new_term_ref[...] = term
        if not (final and tile == 1):
            out = leave_product(t, total)
            for out_ref, part in zip(out_refs[:1] if final else out_refs, (out[:count], out[count:])):
                out_ref[...] = part

    @pl.when(active_ref[0] == 0)
    def _():
        new_total_ref[...] = total_ref[...]
        new_term_ref[...] = term_ref[...]

    if final:
        out = left_product(t["first"][...], new_total_ref[...])
        edge_refs = out_refs[1 - tile :]
        edge_refs[-1][...] = out[count:]
        if tile == 0:
            edge_refs[0][...] = out[:count]


def finish_kernel(cells_x, core_ref, total0_ref, term0_ref, total1_ref, term1_ref, contrast_ref,
                  z_ref, later_ref, keep_ref, give_ref, both_ref):
    _, _, _, size_x, size_y, cells_z = both_ref.shape
    t = named(FINISH, (z_ref, later_ref))
    for tile, (total_ref, term_ref) in enumerate(((total0_ref, term0_ref), (total1_ref, term1_ref))):
        wave, rest = [z_transform(to_cells(ref[...], t), t) for ref in (total_ref, term_ref)]
        rest = times(contrast_ref[tile, 0], contrast_ref[tile, 1], rest)
        for place, x in enumerate(cells_x):
            wave_layer, rest_layer = [natural_layer(field, place, size_x) for field in (wave, rest)]
            for c in range(2):
                there = slice(c * cells_z, (c + 1) * cells_z)
                both_ref[tile, 0, c, x] = wave_layer[:, there]
                both_ref[tile, 1, c, x] = rest_layer[:, there]
                if tile == 1 and x < 2:
                    layer = wave_layer[:, there]
                    if x == 0:
                        both_ref[0, 1, c, size_x - 2] += layer * (-1.0 / 12.0)
                        both_ref[0, 1, c, size_x - 1] += layer * (16.0 / 12.0)
                    else:
                        both_ref[0, 1, c, size_x - 1] += layer * (-1.0 / 12.0)
    keep_ref[...] = both_ref[core_ref[0]]
    give_ref[...] = both_ref[1 - core_ref[0]]


def add_later(rest_ref, edge_x, edge_y, lower):
    _, size_x, size_y, cells_z = rest_ref.shape
    for c in range(2):
        there = slice(c * cells_z, (c + 1) * cells_z)
        near, far = edge_x[:size_y, there] * lower, edge_x[size_y:, there] * lower
        rest_ref[c, size_x - 2] += near * (-1.0 / 12.0)
        rest_ref[c, size_x - 1] += (16.0 * near - far) * (1.0 / 12.0)
        near, far = edge_y[:size_x, there], edge_y[size_x:, there]
        two = jnp.stack([near * (-1.0 / 12.0), (16.0 * near - far) * (1.0 / 12.0)], axis=1)
        rest_ref[c, :, size_y - 2 :] += two


def keep_kernel(core_ref, keep_ref, edge_x_ref, edge_y_ref, z_ref, rest_ref):
    rest_ref[...] = keep_ref[1]
    count = edge_x_ref.shape[0]
    edges = jnp.concatenate([edge_x_ref[...], edge_y_ref[core_ref[0]]], axis=0)
    edges = z_transform(edges, dict(onward=z_ref))
    add_later(rest_ref, edges[:count], edges[count:], (core_ref[0] == 1).astype(F32))


def place_kernel(core_ref, rhs_ref, keep_ref, keep_rest_ref, got_ref, got_edge_ref, z_ref,
                 wave_ref, rest_ref, work_ref, sems):
    rhs = rhs_ref[0]
    count = got_edge_ref.shape[0] // 2
    copies = [
        pltpu.make_async_copy(keep_ref.at[0], wave_ref.at[rhs], sems.at[0]),
        pltpu.make_async_copy(got_ref.at[0], wave_ref.at[1 - rhs], sems.at[1]),
        pltpu.make_async_copy(keep_rest_ref, rest_ref.at[rhs], sems.at[2]),
    ]
    for copy in copies:
        copy.start()
    work_ref[...] = got_ref[1]
    edges = z_transform(got_edge_ref[...], dict(onward=z_ref))
    add_later(work_ref, edges[:count], edges[count:], (core_ref[0] == 1).astype(F32))
    copies.append(pltpu.make_async_copy(work_ref, rest_ref.at[1 - rhs], sems.at[3]))
    copies[-1].start()
    for copy in copies:
        copy.wait()


def whole():
    return pl.BlockSpec(memory_space=pltpu.VMEM)


def scalars():
    return pl.BlockSpec(memory_space=pltpu.SMEM)


def anywhere():
    return pl.BlockSpec(memory_space=pl.ANY)


SOLVE_COST = pl.CostEstimate(flops=2 * 10**9, bytes_accessed=2 * 10**6, transcendentals=0)
KEEP_COST = pl.CostEstimate(flops=10**10, bytes_accessed=10**6, transcendentals=0)
PARAMS = pltpu.CompilerParams(vmem_limit_bytes=24 * 1024 * 1024)


def shaped(*shape):
    return jax.ShapeDtypeStruct(shape, F32)


def body(right_side, slowness, source_cells, source_amplitudes):
    sources, _, size_x, size_y, cells_z = right_side.shape
    grid_rows, grid_cols = lax.axis_size("gx"), lax.axis_size("gy")
    assert sources == 2 and grid_rows % 2 == 0 and size_x % 2 == 0
    chips = grid_rows // 2
    row, col = lax.axis_index("gx"), lax.axis_index("gy")
    core = row % 2
    rhs = (core + row // 2 + col) % 2
    core_ref, rhs_ref = core[None], rhs[None]
    t, cells_x = tables(size_x, size_y, cells_z)
    t = {name: jnp.asarray(value) for name, value in t.items()}
    rows = size_x * size_y

    def device(chip, core, column):
        return (2 * chip + core) * grid_cols + column

    def between(pairs):
        return [
            (device(a, r, b), device(c, 1 - r, d)) for (a, b), (c, d) in pairs for r in range(2)
        ]

    own = [
        (device(k, r, j), device(k, 1 - r, j))
        for k in range(chips) for j in range(grid_cols) for r in range(2)
    ]
    axes = ("gx", "gy")
    other = lax.dynamic_index_in_dim(right_side, 1 - rhs, 0, keepdims=False)
    swapped = lax.ppermute(other, axes, own)
    swapped_slow = lax.ppermute(slowness, axes, own)
    mine = lax.dynamic_index_in_dim(right_side, rhs, 0, keepdims=False)

    total_y = size_y * grid_cols
    cells = lax.dynamic_index_in_dim(source_cells, rhs, 0, keepdims=True)
    near_y = cells // cells_z % total_y - col * size_y
    places = []
    for tile_row in (row, row + 1 - 2 * core):
        near_x = cells // (total_y * cells_z) - tile_row * size_x
        inside = (near_x >= 0) & (near_x < size_x) & (near_y >= 0) & (near_y < size_y)
        far_x, far_y = near_x >= size_x // 2, near_y >= size_y // 2
        folded_x = jnp.where(far_x, size_x - 1 - near_x, near_x)
        folded_y = jnp.where(far_y, size_y - 1 - near_y, near_y)
        quarter = (2 * far_x + far_y) * (rows // 4)
        places.append(jnp.where(inside, quarter + folded_x * (size_y // 2) + folded_y, -1))
    amplitudes = lax.dynamic_index_in_dim(source_amplitudes, rhs, 0, keepdims=False).T[:, None, :]

    depth = cells % cells_z
    own_modes, own_contrast, t["inverse"], *held = pl.pallas_call(
        functools.partial(prep_kernel, cells_x),
        out_shape=(shaped(rows, 2 * cells_z), shaped(2, rows, cells_z), shaped(2, rows, cells_z))
        + tuple(jax.ShapeDtypeStruct(t[name].shape, BF16) for name in LATER),
        in_specs=[whole()] * (5 + len(PREP) + len(LATER)),
        out_specs=(whole(),) * (3 + len(LATER)),
        compiler_params=PARAMS,
        cost_estimate=SOLVE_COST,
        name="prep",
    )(mine, slowness, places[0], depth, amplitudes, *[t[name] for name in PREP + LATER])
    t.update(zip(LATER, held))
    modes, contrast = pl.pallas_call(
        functools.partial(prep_other_kernel, cells_x),
        out_shape=(shaped(2, rows, 2 * cells_z), shaped(2, 2, rows, cells_z)),
        in_specs=[scalars()] * 2 + [whole()] * (7 + len(PREP_OTHER)),
        out_specs=(whole(), whole()),
        compiler_params=PARAMS,
        cost_estimate=SOLVE_COST,
        name="prep_other",
    )(core_ref, rhs_ref, swapped, swapped_slow, own_modes, own_contrast, places[1], depth, amplitudes,
      *[t[name] for name in PREP_OTHER])

    def solve(tile, active, trace_x, trace_y, state, final):
        names = FINAL if final else BEAT
        x, y = shaped(*zero_x.shape), shaped(*zero_y.shape)
        outs = ((x, x, y), (y,))[tile] if final else (x, y)
        total, term, *outs = pl.pallas_call(
            functools.partial(beat_kernel, tile, final),
            out_shape=(shaped(rows, 2 * cells_z),) * 2 + outs,
            in_specs=[scalars()] + [whole()] * (6 + len(names)),
            out_specs=(whole(),) * (2 + len(outs)),
            input_output_aliases={5: 0, 6: 1},
            compiler_params=PARAMS,
            cost_estimate=SOLVE_COST,
            name="upper" if tile == 0 else "lower",
        )(active, modes, contrast, trace_x, trace_y, *state, *[t[name] for name in names])
        return (total, term), outs

    def hand_on(trace, cost=None):
        return pl.pallas_call(
            hand_on_kernel,
            out_shape=shaped(*trace.shape),
            in_specs=[whole()],
            out_specs=whole(),
            compiler_params=PARAMS,
            cost_estimate=cost,
            name="hand_on",
        )(trace)

    zero_x = jnp.zeros((2 * size_y, 2 * cells_z), F32)
    zero_y = jnp.zeros((2 * size_x, 2 * cells_z), F32)
    trace_x, trace_y0, trace_y1 = zero_x, zero_y, zero_y
    states = [[jnp.zeros((rows, 2 * cells_z), F32)] * 2 for _ in range(2)]
    for beat in range(chips + grid_cols - 1):
        active = (row // 2 + col == beat).astype(jnp.int32)[None]
        here = [(k, beat - k) for k in range(chips) if 0 <= beat - k < grid_cols]
        along_x = between([((k, j), (k + 1, j)) for k, j in here if k + 1 < chips])
        along_y = between([((k, j), (k, j + 1)) for k, j in here if j + 1 < grid_cols])
        final = beat == chips + grid_cols - 2
        states[0], (inner_x, *outs0) = solve(0, active, trace_x, trace_y0, states[0], final)
        if along_y:
            trace_y0 = hand_on(lax.ppermute(outs0[0], axes, along_y))
        states[1], outs1 = solve(1, active, inner_x, trace_y1, states[1], final)
        if along_x:
            trace_x = lax.ppermute(outs1[0], axes, along_x)
        if along_y:
            trace_y1 = lax.ppermute(outs1[1], axes, along_y)
    edge_x, edge_y0 = outs0
    edge_y = jnp.stack([edge_y0, outs1[0]])

    every = [(k, j) for k in range(chips) for j in range(grid_cols)]
    after_x = hand_on(
        lax.ppermute(edge_x, axes, between([((k, j), (k - 1, j)) for k, j in every if k])), KEEP_COST
    )
    after_y = lax.ppermute(edge_y, axes, between([((k, j), (k, j - 1)) for k, j in every if j]))

    half = shaped(2, 2, size_x, size_y, cells_z)
    keep, give = pl.pallas_call(
        functools.partial(finish_kernel, cells_x),
        out_shape=(half, half),
        in_specs=[scalars()] + [whole()] * 7,
        out_specs=(whole(), whole()),
        scratch_shapes=[pltpu.VMEM((2, 2, 2, size_x, size_y, cells_z), F32)],
        compiler_params=PARAMS,
        name="finish",
    )(core_ref, *states[0], *states[1], contrast, *[t[name] for name in FINISH])
    got = lax.ppermute(give, axes, own)

    pass_y = lax.dynamic_index_in_dim(after_y, 1 - core, 0, keepdims=False)
    got_edge = lax.ppermute(jnp.concatenate([after_x, pass_y], axis=0), axes, own)
    keep_rest = pl.pallas_call(
        keep_kernel,
        out_shape=shaped(*half.shape[1:]),
        in_specs=[scalars()] + [whole()] * 4,
        out_specs=whole(),
        compiler_params=PARAMS,
        cost_estimate=KEEP_COST,
        name="keep",
    )(core_ref, keep, after_x, after_y, t["onward"])
    return pl.pallas_call(
        place_kernel,
        out_shape=(shaped(*right_side.shape), shaped(*right_side.shape)),
        in_specs=[scalars()] * 2 + [whole()] * 5,
        out_specs=(anywhere(), anywhere()),
        scratch_shapes=[
            pltpu.VMEM((2, size_x, size_y, cells_z), F32),
            pltpu.SemaphoreType.DMA((4,)),
        ],
        compiler_params=PARAMS,
        name="place",
    )(core_ref, rhs_ref, keep, keep_rest, got, got_edge, t["onward"])


def solution(mesh):
    return jax.shard_map(
        body,
        mesh=mesh,
        in_specs=(P(None, None, "gx", "gy", None), P("gx", "gy", None), P(), P()),
        out_specs=(P(None, None, "gx", "gy", None), P(None, None, "gx", "gy", None)),
        check_vma=False,
    )
```

```python
import functools
import math

import jax
import jax.numpy as jnp
import ml_dtypes
import numpy as np
from jax import lax
from jax.experimental import pallas as pl
from jax.experimental.pallas import tpu as pltpu
from jax.sharding import PartitionSpec as P

KAPPA = 0.12
DAMPING = 0.3
BF16 = jnp.bfloat16
F32 = jnp.float32


def sine_matrix(length):
    index = np.arange(1, length + 1)
    angles = index * (math.pi / (length + 1))
    return math.sqrt(2.0 / (length + 1)) * np.sin(angles[:, None] * index[None, :]), angles


def halves(matrix):
    high = matrix.astype(np.float32).astype(ml_dtypes.bfloat16)
    low = (matrix - high.astype(np.float64)).astype(np.float32).astype(ml_dtypes.bfloat16)
    return high, low


def left_factor(matrix):
    high, low = halves(matrix)
    return np.concatenate([high, high, low], axis=1)


def slabs(matrices, rows, lanes):
    pieces, free = [], 0
    for matrix in matrices:
        for row in range(0, matrix.shape[0], rows):
            for lane in range(0, matrix.shape[1], lanes):
                piece = matrix[row : row + rows, lane : lane + lanes]
                if free + piece.shape[0] > rows or not pieces:
                    pieces.append(np.zeros((rows, lanes), matrix.dtype))
                    free = 0
                pieces[-1][free : free + piece.shape[0], : piece.shape[1]] = piece
                free += piece.shape[0]
    return np.stack(pieces)


def quarter_matrix(slabs_ref, index):
    count = slabs_ref.shape[1] // 2
    return slabs_ref[index // 2, index % 2 * count : (index % 2 + 1) * count, : 3 * count]


def z_matrix(t, depth):
    rows = t["onward"].shape[1]
    pieces = [t["onward"][2 + n, :, :depth] for n in range(-(-depth // rows))]
    return jnp.concatenate(pieces, axis=0)


def enter_matrix(t, depth):
    return jnp.concatenate([t["later"][2, :, :depth], t["later"][3, :, :depth]], axis=0)


def leave_product(t, values):
    high, low = split(values)
    rest = 2 * values.shape[0] - t["later"].shape[2]
    matrix = t["later"][4]
    if rest > 0:
        matrix = jnp.concatenate([matrix, t["later"][2, :, -rest:]], axis=1)
    both = jnp.dot(matrix, jnp.concatenate([high, low], axis=0), preferred_element_type=F32)
    count = both.shape[0] // 2
    return both[:count] + both[count:]


def stacked_factor(matrix):
    high, low = halves(matrix)
    return np.concatenate([np.concatenate([part, part], axis=1) for part in (high, low)], axis=0)


def tables(size_x, size_y, cells_z):
    sine_x, angle_x = sine_matrix(size_x)
    sine_y, angle_y = sine_matrix(size_y)
    sine_z, angle_z = sine_matrix(cells_z)
    half = size_x // 2
    assert half % 8 == 0 and size_y % 16 == 0
    order_x, order_y = [np.arange(0, n, 2).reshape(1, -1) + [[0], [1]] for n in (size_x, size_y)]
    pairs = [(x, y) for p in range(2) for q in range(2) for x in order_x[p] for y in order_y[q]]
    mode_x, mode_y = np.array(pairs).T
    cells = np.concatenate([np.arange(half), np.arange(size_x - 1, half - 1, -1)])

    def symbol(angle):
        return 2.5 - 8.0 / 3.0 * np.cos(angle) + 1.0 / 6.0 * np.cos(2.0 * angle)

    real_part = (
        symbol(angle_x)[mode_x][:, None]
        + symbol(angle_y)[mode_y][:, None]
        + (2.0 - 2.0 * np.cos(angle_z))[None, :]
        - KAPPA
    )

    slab = half * size_y
    lanes = 3 * slab
    parity = [
        np.kron(sine_x[order_x[p]][:, :half], sine_y[order_y[q]][:, : size_y // 2])
        for p in range(2) for q in range(2)
    ]
    forward = [left_factor(m) for m in parity]
    backward = [left_factor(m.T) for m in parity]
    high_z, low_z = halves(sine_z)
    right_z = np.concatenate([np.concatenate([high_z, low_z], axis=1)] * 2, axis=0)

    by_cell = sine_x[mode_x][:, :, None] * sine_y[mode_y][:, None, :]
    full = by_cell.reshape(len(by_cell), -1)
    enter_x = np.stack([-by_cell[:, 0] / 12.0, (16.0 * by_cell[:, 0] - by_cell[:, 1]) / 12.0], 1)
    enter_y = np.stack(
        [-by_cell[:, :, 0] / 12.0, (16.0 * by_cell[:, :, 0] - by_cell[:, :, 1]) / 12.0], 1
    )
    enter = left_factor(
        np.concatenate([enter_x.reshape(len(full), -1), enter_y.reshape(len(full), -1)], axis=1)
    )
    leave = stacked_factor(
        np.concatenate(
            [
                by_cell[:, size_x - 2 :].reshape(len(full), -1),
                by_cell[:, :, size_y - 2 :].transpose(0, 2, 1).reshape(len(full), -1),
            ],
            axis=1,
        ).T
    )
    first = left_factor(
        np.concatenate(
            [
                by_cell[:, :2].reshape(len(full), -1),
                by_cell[:, :, :2].transpose(0, 2, 1).reshape(len(full), -1),
            ],
            axis=1,
        ).T
    )
    later = slabs(backward + [enter, leave[:, : lanes]], slab, lanes)
    rest = leave[:, lanes :]
    if rest.shape[1]:
        assert enter.shape[1] <= later.shape[2] - rest.shape[1]
        later[2, :, later.shape[2] - rest.shape[1] :] = rest
    assert 2 * cells_z % slab == 0 and 2 * cells_z <= lanes
    assert enter.shape[0] == 2 * slab and enter.shape[1] <= lanes
    assert leave.shape[0] == slab
    return dict(
        symbol=real_part.astype(np.float32), first=first,
        onward=slabs(forward + [right_z], slab, lanes),
        later=later,
    ), tuple(int(x) for x in cells)


def divide(modes, t):
    return times(t["inverse"][0], t["inverse"][1], modes)


def split(values):
    high = values.astype(BF16)
    return high, (values - high.astype(F32)).astype(BF16)


def stacked(values):
    high, low = split(values)
    return jnp.concatenate([high, low, high], axis=0)


def left_product(matrix, values):
    return jnp.dot(matrix, stacked(values), preferred_element_type=F32)


def z_transform(field, t):
    rows = field.shape[0]
    cells_z = field.shape[1] // 2
    high, low = split(jnp.concatenate([field[:, :cells_z], field[:, cells_z:]], axis=0))
    both = jnp.dot(jnp.concatenate([high, low], axis=1), z_matrix(t, 2 * cells_z), preferred_element_type=F32)
    total = both[:, :cells_z] + both[:, cells_z:]
    return jnp.concatenate([total[:rows], total[rows:]], axis=1)


def in_four(values):
    count = values.shape[0] // 4
    return [values[n * count : (n + 1) * count] for n in range(4)]


def crossed(a, b, c, d):
    s, t, u, v = a + c, a - c, b + d, b - d
    return s + u, s - u, t + v, t - v


def to_modes(field, t):
    folded = crossed(*in_four(field))
    return jnp.concatenate(
        [left_product(quarter_matrix(t["onward"], n), part) for n, part in enumerate(folded)], axis=0
    )


def to_cells(modes, t):
    parts = [left_product(quarter_matrix(t["later"], n), part) for n, part in enumerate(in_four(modes))]
    return jnp.concatenate(crossed(*parts), axis=0)


def backwards(rows):
    return jnp.concatenate([rows[n : n + 1] for n in reversed(range(rows.shape[0]))], axis=0)


def folded_cells(load, cells_x):
    half = len(cells_x) // 2
    quarters = []
    for part in (cells_x[:half], cells_x[half:]):
        layers = [load(x) for x in part]
        middle = layers[0].shape[0] // 2
        quarters += [layer[:middle] for layer in layers]
        quarters += [backwards(layer[middle:]) for layer in layers]
    return jnp.concatenate(quarters, axis=0)


def natural_layer(field, place, layers):
    count = field.shape[0] // layers // 2
    side, within = divmod(place, layers // 2)
    start = side * (field.shape[0] // 2) + within * count
    mirror = start + field.shape[0] // 4
    return jnp.concatenate(
        [field[start : start + count], backwards(field[mirror : mirror + count])], axis=0
    )


def times(real_part, imag_part, field):
    lanes = field.shape[1] // 2
    real, imag = field[:, :lanes], field[:, lanes:]
    return jnp.concatenate(
        [real_part * real - imag_part * imag, real_part * imag + imag_part * real], axis=1
    )


def apply_contrast(field, contrast, t, block=32):
    done = []
    for start in range(0, field.shape[0], block):
        here = slice(start, start + block)
        cells = times(contrast[0, here], contrast[1, here], z_transform(field[here], t))
        done.append(z_transform(cells, t))
    return jnp.concatenate(done, axis=0)


def solve_modes(start, contrast, t):
    term = total = start
    for _ in range(2):
        term = divide(to_modes(apply_contrast(to_cells(term, t), contrast, t), t), t)
        total = total + term
    return total, term


def edges(rows, lanes, layers):
    place = lax.broadcasted_iota(jnp.int32, (rows, lanes), 0)
    count = rows // layers // 2
    outer_y = lax.rem(place, count) == 0
    outer_x = lax.rem(place, rows // 4) < count
    return (outer_x.astype(F32) + outer_y.astype(F32)) * (1.0 / 12.0)


def prepare(dense, slow, layers, place, depth, amplitude, t, modes_ref, contrast_ref):
    rows, cells_z = contrast_ref.shape[1:]
    points = place.shape[1]
    row_ids = lax.broadcasted_iota(jnp.int32, (rows, points), 0)
    lane_ids = lax.broadcasted_iota(jnp.int32, (cells_z, points), 0)
    at_lane = (lane_ids == depth).astype(F32)
    spread = []
    for c in range(2):
        amp = amplitude[c]
        one = amp.astype(BF16).astype(F32)
        two = (amp - one).astype(BF16).astype(F32)
        parts = [at_lane * part for part in (one, two, amp - one - two)]
        spread.append(jnp.concatenate(parts, axis=1).astype(BF16))
    scaled = KAPPA * (slow - 1.0)
    contrast_ref[0] = scaled - edges(rows, cells_z, layers)
    contrast_ref[1] = DAMPING * scaled
    at_row = (row_ids == place).astype(F32).astype(BF16)
    field = lax.dot_general(
        jnp.concatenate([at_row] * 3, axis=1), jnp.concatenate(spread, axis=0),
        (((1,), (1,)), ((), ())), preferred_element_type=F32,
    )
    modes_ref[...] = divide(to_modes(z_transform(field + dense, t), t), t)


def hand_on_kernel(in_ref, out_ref):
    out_ref[...] = in_ref[...]


PREP = ("symbol", "onward")
PREP_OTHER = ("inverse", "onward")
BEAT = ("inverse", "onward", "later")
FINAL = BEAT + ("first",)
LATER = ("later",)
FINISH = ("onward", "later")


def named(names, refs):
    return dict(zip(names, refs))


def prep_kernel(cells_x, right_ref, slow_ref, place_ref, depth_ref, amp_ref, *refs):
    later_refs = refs[len(PREP) : len(PREP) + len(LATER)]
    modes_ref, contrast_ref, inverse_ref, *held_refs, sems = refs[len(PREP) + len(LATER) :]
    copies = [
        pltpu.make_async_copy(later_ref, held_ref, sems.at[n])
        for n, (later_ref, held_ref) in enumerate(zip(later_refs, held_refs))
    ]
    for copy in copies:
        copy.start()
    t = named(PREP, refs)
    symbol = t["symbol"][...]
    damping = KAPPA * DAMPING
    scale = 1.0 / (symbol * symbol + damping * damping)
    inverse_ref[0] = symbol * scale
    inverse_ref[1] = damping * scale
    t["inverse"] = inverse_ref
    dense = [folded_cells(lambda x, c=c: right_ref[c, x], cells_x) for c in range(2)]
    slow = folded_cells(lambda x: slow_ref[x], cells_x)
    prepare(
        jnp.concatenate(dense, axis=1), slow, len(cells_x), place_ref[...], depth_ref[...], amp_ref, t,
        modes_ref, contrast_ref,
    )
    for copy in copies:
        copy.wait()


def prep_other_kernel(cells_x, core_ref, rhs_ref, swap_ref, slow_ref, own_modes_ref, own_contrast_ref, place_ref, depth_ref, amp_ref,
                      *refs):
    modes_ref, contrast_ref = refs[len(PREP_OTHER) :]
    core = core_ref[0]
    other = 1 - core
    modes_ref[core] = own_modes_ref[...]
    contrast_ref[core] = own_contrast_ref[...]
    dense = [folded_cells(lambda x, c=c: swap_ref[c, x], cells_x) for c in range(2)]
    slow = folded_cells(lambda x: slow_ref[x], cells_x)
    prepare(
        jnp.concatenate(dense, axis=1), slow, len(cells_x), place_ref[...], depth_ref[...], amp_ref, named(PREP_OTHER, refs),
        modes_ref.at[other], contrast_ref.at[other],
    )


def beat_kernel(tile, final, active_ref, modes_ref, contrast_ref, trace_x_ref, trace_y_ref, total_ref, term_ref,
                *refs):
    names = FINAL if final else BEAT
    t = named(names, refs)
    new_total_ref, new_term_ref, *out_refs = refs[len(names) :]
    count = trace_x_ref.shape[0]

    @pl.when(active_ref[0] == 1)
    def _():
        trace = jnp.concatenate([trace_x_ref[...], trace_y_ref[...]], axis=0)
        start = modes_ref[tile] + divide(left_product(enter_matrix(t, 3 * trace.shape[0]), trace), t)
        total, term = solve_modes(start, contrast_ref.at[tile], t)
        new_total_ref[...] = total
        new_term_ref[...] = term
        if not (final and tile == 1):
            out = leave_product(t, total)
            for out_ref, part in zip(out_refs[:1] if final else out_refs, (out[:count], out[count:])):
                out_ref[...] = part

    @pl.when(active_ref[0] == 0)
    def _():
        new_total_ref[...] = total_ref[...]
        new_term_ref[...] = term_ref[...]

    if final:
        out = left_product(t["first"][...], new_total_ref[...])
        edge_refs = out_refs[1 - tile :]
        edge_refs[-1][...] = out[count:]
        if tile == 0:
            edge_refs[0][...] = out[:count]


def finish_kernel(cells_x, core_ref, total0_ref, term0_ref, total1_ref, term1_ref, contrast_ref,
                  z_ref, later_ref, keep_ref, give_ref, both_ref):
    _, _, _, size_x, size_y, cells_z = both_ref.shape
    t = named(FINISH, (z_ref, later_ref))
    for tile, (total_ref, term_ref) in enumerate(((total0_ref, term0_ref), (total1_ref, term1_ref))):
        wave, rest = [z_transform(to_cells(ref[...], t), t) for ref in (total_ref, term_ref)]
        rest = times(contrast_ref[tile, 0], contrast_ref[tile, 1], rest)
        for place, x in enumerate(cells_x):
            wave_layer, rest_layer = [natural_layer(field, place, size_x) for field in (wave, rest)]
            for c in range(2):
                there = slice(c * cells_z, (c + 1) * cells_z)
                both_ref[tile, 0, c, x] = wave_layer[:, there]
                both_ref[tile, 1, c, x] = rest_layer[:, there]
                if tile == 1 and x < 2:
                    layer = wave_layer[:, there]
                    if x == 0:
                        both_ref[0, 1, c, size_x - 2] += layer * (-1.0 / 12.0)
                        both_ref[0, 1, c, size_x - 1] += layer * (16.0 / 12.0)
                    else:
                        both_ref[0, 1, c, size_x - 1] += layer * (-1.0 / 12.0)
    keep_ref[...] = both_ref[core_ref[0]]
    give_ref[...] = both_ref[1 - core_ref[0]]


def add_later(rest_ref, edge_x, edge_y, lower):
    _, size_x, size_y, cells_z = rest_ref.shape
    for c in range(2):
        there = slice(c * cells_z, (c + 1) * cells_z)
        near, far = edge_x[:size_y, there] * lower, edge_x[size_y:, there] * lower
        rest_ref[c, size_x - 2] += near * (-1.0 / 12.0)
        rest_ref[c, size_x - 1] += (16.0 * near - far) * (1.0 / 12.0)
        near, far = edge_y[:size_x, there], edge_y[size_x:, there]
        two = jnp.stack([near * (-1.0 / 12.0), (16.0 * near - far) * (1.0 / 12.0)], axis=1)
        rest_ref[c, :, size_y - 2 :] += two


def keep_kernel(core_ref, keep_ref, edge_x_ref, edge_y_ref, z_ref, rest_ref):
    rest_ref[...] = keep_ref[1]
    count = edge_x_ref.shape[0]
    edges = jnp.concatenate([edge_x_ref[...], edge_y_ref[core_ref[0]]], axis=0)
    edges = z_transform(edges, dict(onward=z_ref))
    add_later(rest_ref, edges[:count], edges[count:], (core_ref[0] == 1).astype(F32))


def place_wave_kernel(rhs_ref, keep_ref, got_ref, wave_ref, sems):
    rhs = rhs_ref[0]
    copies = [
        pltpu.make_async_copy(keep_ref.at[0], wave_ref.at[rhs], sems.at[0]),
        pltpu.make_async_copy(got_ref.at[0], wave_ref.at[1 - rhs], sems.at[1]),
    ]
    for copy in copies:
        copy.start()
    for copy in copies:
        copy.wait()


def place_rest_kernel(core_ref, rhs_ref, keep_rest_ref, got_ref, got_edge_ref, z_ref, rest_ref, work_ref, sems):
    rhs = rhs_ref[0]
    count = got_edge_ref.shape[0] // 2
    copies = [pltpu.make_async_copy(keep_rest_ref, rest_ref.at[rhs], sems.at[0])]
    copies[0].start()
    work_ref[...] = got_ref[1]
    edges = z_transform(got_edge_ref[...], dict(onward=z_ref))
    add_later(work_ref, edges[:count], edges[count:], (core_ref[0] == 1).astype(F32))
    copies.append(pltpu.make_async_copy(work_ref, rest_ref.at[1 - rhs], sems.at[1]))
    copies[1].start()
    for copy in copies:
        copy.wait()


def whole():
    return pl.BlockSpec(memory_space=pltpu.VMEM)


def scalars():
    return pl.BlockSpec(memory_space=pltpu.SMEM)


def anywhere():
    return pl.BlockSpec(memory_space=pl.ANY)


SOLVE_COST = pl.CostEstimate(flops=2 * 10**9, bytes_accessed=2 * 10**6, transcendentals=0)
KEEP_COST = pl.CostEstimate(flops=10**10, bytes_accessed=10**6, transcendentals=0)
PARAMS = pltpu.CompilerParams(vmem_limit_bytes=24 * 1024 * 1024)


def shaped(*shape):
    return jax.ShapeDtypeStruct(shape, F32)


def body(right_side, slowness, source_cells, source_amplitudes):
    sources, _, size_x, size_y, cells_z = right_side.shape
    grid_rows, grid_cols = lax.axis_size("gx"), lax.axis_size("gy")
    assert sources == 2 and grid_rows % 2 == 0 and size_x % 2 == 0
    chips = grid_rows // 2
    row, col = lax.axis_index("gx"), lax.axis_index("gy")
    core = row % 2
    rhs = (core + row // 2 + col) % 2
    core_ref, rhs_ref = core[None], rhs[None]
    t, cells_x = tables(size_x, size_y, cells_z)
    t = {name: jnp.asarray(value) for name, value in t.items()}
    rows = size_x * size_y

    def device(chip, core, column):
        return (2 * chip + core) * grid_cols + column

    def between(pairs):
        return [
            (device(a, r, b), device(c, 1 - r, d)) for (a, b), (c, d) in pairs for r in range(2)
        ]

    own = [
        (device(k, r, j), device(k, 1 - r, j))
        for k in range(chips) for j in range(grid_cols) for r in range(2)
    ]
    axes = ("gx", "gy")
    other = lax.dynamic_index_in_dim(right_side, 1 - rhs, 0, keepdims=False)
    swapped = lax.ppermute(other, axes, own)
    swapped_slow = lax.ppermute(slowness, axes, own)
    mine = lax.dynamic_index_in_dim(right_side, rhs, 0, keepdims=False)

    total_y = size_y * grid_cols
    cells = lax.dynamic_index_in_dim(source_cells, rhs, 0, keepdims=True)
    near_y = cells // cells_z % total_y - col * size_y
    places = []
    for tile_row in (row, row + 1 - 2 * core):
        near_x = cells // (total_y * cells_z) - tile_row * size_x
        inside = (near_x >= 0) & (near_x < size_x) & (near_y >= 0) & (near_y < size_y)
        far_x, far_y = near_x >= size_x // 2, near_y >= size_y // 2
        folded_x = jnp.where(far_x, size_x - 1 - near_x, near_x)
        folded_y = jnp.where(far_y, size_y - 1 - near_y, near_y)
        quarter = (2 * far_x + far_y) * (rows // 4)
        places.append(jnp.where(inside, quarter + folded_x * (size_y // 2) + folded_y, -1))
    amplitudes = lax.dynamic_index_in_dim(source_amplitudes, rhs, 0, keepdims=False).T[:, None, :]

    depth = cells % cells_z
    own_modes, own_contrast, t["inverse"], *held = pl.pallas_call(
        functools.partial(prep_kernel, cells_x),
        out_shape=(shaped(rows, 2 * cells_z), shaped(2, rows, cells_z), shaped(2, rows, cells_z))
        + tuple(jax.ShapeDtypeStruct(t[name].shape, BF16) for name in LATER),
        in_specs=[whole()] * (5 + len(PREP)) + [anywhere()] * len(LATER),
        out_specs=(whole(),) * (3 + len(LATER)),
        scratch_shapes=[pltpu.SemaphoreType.DMA((len(LATER),))],
        compiler_params=PARAMS,
        cost_estimate=SOLVE_COST,
        name="prep",
    )(mine, slowness, places[0], depth, amplitudes, *[t[name] for name in PREP + LATER])
    t.update(zip(LATER, held))
    modes, contrast = pl.pallas_call(
        functools.partial(prep_other_kernel, cells_x),
        out_shape=(shaped(2, rows, 2 * cells_z), shaped(2, 2, rows, cells_z)),
        in_specs=[scalars()] * 2 + [whole()] * (7 + len(PREP_OTHER)),
        out_specs=(whole(), whole()),
        compiler_params=PARAMS,
        cost_estimate=SOLVE_COST,
        name="prep_other",
    )(core_ref, rhs_ref, swapped, swapped_slow, own_modes, own_contrast, places[1], depth, amplitudes,
      *[t[name] for name in PREP_OTHER])

    def solve(tile, active, trace_x, trace_y, state, final):
        names = FINAL if final else BEAT
        x, y = shaped(*zero_x.shape), shaped(*zero_y.shape)
        outs = ((x, x, y), (y,))[tile] if final else (x, y)
        total, term, *outs = pl.pallas_call(
            functools.partial(beat_kernel, tile, final),
            out_shape=(shaped(rows, 2 * cells_z),) * 2 + outs,
            in_specs=[scalars()] + [whole()] * (6 + len(names)),
            out_specs=(whole(),) * (2 + len(outs)),
            input_output_aliases={5: 0, 6: 1},
            compiler_params=PARAMS,
            cost_estimate=SOLVE_COST,
            name="upper" if tile == 0 else "lower",
        )(active, modes, contrast, trace_x, trace_y, *state, *[t[name] for name in names])
        return (total, term), outs

    def hand_on(trace, cost=None):
        return pl.pallas_call(
            hand_on_kernel,
            out_shape=shaped(*trace.shape),
            in_specs=[whole()],
            out_specs=whole(),
            compiler_params=PARAMS,
            cost_estimate=cost,
            name="hand_on",
        )(trace)

    zero_x = jnp.zeros((2 * size_y, 2 * cells_z), F32)
    zero_y = jnp.zeros((2 * size_x, 2 * cells_z), F32)
    trace_x, trace_y0, trace_y1 = zero_x, zero_y, zero_y
    states = [[jnp.zeros((rows, 2 * cells_z), F32)] * 2 for _ in range(2)]
    for beat in range(chips + grid_cols - 1):
        active = (row // 2 + col == beat).astype(jnp.int32)[None]
        here = [(k, beat - k) for k in range(chips) if 0 <= beat - k < grid_cols]
        along_x = between([((k, j), (k + 1, j)) for k, j in here if k + 1 < chips])
        along_y = between([((k, j), (k, j + 1)) for k, j in here if j + 1 < grid_cols])
        final = beat == chips + grid_cols - 2
        states[0], (inner_x, *outs0) = solve(0, active, trace_x, trace_y0, states[0], final)
        if along_y:
            trace_y0 = hand_on(lax.ppermute(outs0[0], axes, along_y))
        states[1], outs1 = solve(1, active, inner_x, trace_y1, states[1], final)
        if along_x:
            trace_x = lax.ppermute(outs1[0], axes, along_x)
        if along_y:
            trace_y1 = lax.ppermute(outs1[1], axes, along_y)
    edge_x, edge_y0 = outs0
    edge_y = jnp.stack([edge_y0, outs1[0]])

    every = [(k, j) for k in range(chips) for j in range(grid_cols)]
    after_x = hand_on(
        lax.ppermute(edge_x, axes, between([((k, j), (k - 1, j)) for k, j in every if k])), KEEP_COST
    )
    after_y = lax.ppermute(edge_y, axes, between([((k, j), (k, j - 1)) for k, j in every if j]))

    half = shaped(2, 2, size_x, size_y, cells_z)
    keep, give = pl.pallas_call(
        functools.partial(finish_kernel, cells_x),
        out_shape=(half, half),
        in_specs=[scalars()] + [whole()] * 7,
        out_specs=(whole(), whole()),
        scratch_shapes=[pltpu.VMEM((2, 2, 2, size_x, size_y, cells_z), F32)],
        compiler_params=PARAMS,
        name="finish",
    )(core_ref, *states[0], *states[1], contrast, *[t[name] for name in FINISH])
    got = lax.ppermute(give, axes, own)

    pass_y = lax.dynamic_index_in_dim(after_y, 1 - core, 0, keepdims=False)
    got_edge = lax.ppermute(jnp.concatenate([after_x, pass_y], axis=0), axes, own)
    keep_rest = pl.pallas_call(
        keep_kernel,
        out_shape=shaped(*half.shape[1:]),
        in_specs=[scalars()] + [whole()] * 4,
        out_specs=whole(),
        compiler_params=PARAMS,
        cost_estimate=KEEP_COST,
        name="keep",
    )(core_ref, keep, after_x, after_y, t["onward"])
    wavefield = pl.pallas_call(
        place_wave_kernel,
        out_shape=shaped(*right_side.shape),
        in_specs=[scalars()] + [whole()] * 2,
        out_specs=anywhere(),
        scratch_shapes=[pltpu.SemaphoreType.DMA((2,))],
        compiler_params=PARAMS,
        cost_estimate=KEEP_COST,
        name="place_wave",
    )(rhs_ref, keep, got)
    residual = pl.pallas_call(
        place_rest_kernel,
        out_shape=shaped(*right_side.shape),
        in_specs=[scalars()] * 2 + [whole()] * 4,
        out_specs=anywhere(),
        scratch_shapes=[
            pltpu.VMEM((2, size_x, size_y, cells_z), F32),
            pltpu.SemaphoreType.DMA((2,)),
        ],
        compiler_params=PARAMS,
        name="place_rest",
    )(core_ref, rhs_ref, keep_rest, got, got_edge, t["onward"])
    return wavefield, residual


def solution(mesh):
    return jax.shard_map(
        body,
        mesh=mesh,
        in_specs=(P(None, None, "gx", "gy", None), P("gx", "gy", None), P(), P()),
        out_specs=(P(None, None, "gx", "gy", None), P(None, None, "gx", "gy", None)),
        check_vma=False,
    )
```
